128 devices in a mesh: ax: 4 (over y), az: 32 (over z, x, core).
Axes of the slice: x: 4, y: 4, z: 4, core: 2. Of those that a mesh axis runs over, the one named last changes fastest.
Arguments:
- noise: float32 [64, 512, 512], P('ax', 'az'), may hold values from -6 to 6
- half_width: int32 [64, 512, 512], P('ax', 'az'), may hold values from 1 to 4
- owner: int32 [32768], P(('ax', 'az')), may hold values from 0 to 127, as said below
- target_cell: int32 [32768], P(('ax', 'az')), may hold values from 0 to 511
- fields: float32 [5, 128, 512, 256], P(None, 'ax', 'az'), may hold values from -6 to 6
Outputs:
- fields_next: float32 [5, 128, 512, 256], P(None, 'ax', 'az')
The draws below stay inside these ranges and needn't reach their ends.
Inputs may be any that keep to these rules, and one draw needn't show every extreme that they name: The owner of a device's column is the device itself, one of its two azimuthal neighbours (periodic), or one of its axial neighbours; among the 256 columns of one device no owner is named more than 128 times, and one owner is named exactly 128 times.
All inputs are finite; a program needn't handle non-finite values.
Results may differ from the reference program's by a relative error of at most 0.000067.
Values sent between devices are 32-bit elements; how exact they have to be, the bound alone decides.
No kernel may reach another device: no remote copies, remote signals or barrier semaphores. Data moves between devices by JAX's collectives and lax.ppermute only.
A program may use at most 128 MiB of HBM per device.

```python
import math
import jax
import jax.numpy as jnp
from jax import lax

CX = 32
CA = 16
R = 256
PX = 16
PA = 16
PR = 512
HMAX = 4
NX = 128
NA = 512
NXR = 64
NAR = 512
COLS = 256
N_AX = 4
N_AZ = 32


def draw_owner(key, part):
    key = jax.random.fold_in(key, 11)
    ndev = N_AX * N_AZ
    ncols = PX * PA
    most = ncols // 2
    key_big, key_perm, key_rest = jax.random.split(key, 3)
    device = jnp.arange(ndev, dtype=jnp.int32)
    axial = device // N_AZ
    azim = device % N_AZ
    valid = 5 - (axial == 0).astype(jnp.int32) - (axial == N_AX - 1).astype(jnp.int32)
    big = jax.random.randint(key_big, (ndev,), 0, 60, dtype=jnp.int32) % valid
    perms = jax.vmap(lambda k: jax.random.permutation(k, ncols))(jax.random.split(key_perm, ndev))
    chosen = jnp.zeros((ndev, ncols), jnp.int32).at[device[:, None], perms[:, :most]].set(1)
    spread = jax.random.randint(key_rest, (ndev, ncols), 0, 60, dtype=jnp.int32) % (valid[:, None] - 1)
    other = (big[:, None] + 1 + spread) % valid[:, None]
    slot = jnp.where(chosen == 1, big[:, None], other)
    direction = jnp.where((axial[:, None] == 0) & (slot >= 3), slot + 1, slot)
    table = jnp.stack([device, axial * N_AZ + (azim - 1) % N_AZ, axial * N_AZ + (azim + 1) % N_AZ, (axial - 1) * N_AZ + azim, (axial + 1) * N_AZ + azim], axis=1)
    owner = jnp.take_along_axis(table, direction, axis=1)
    return owner.reshape(-1).astype(jnp.int32)


def draw_fields(key, part):
    key = jax.random.fold_in(key, 23)
    key_sign, key_env, key_rough = jax.random.split(key, 3)
    shape = (5, NX, NA, R)
    axial_idx = jnp.arange(NX, dtype=jnp.int32)[:, None, None]
    azim_idx = jnp.arange(NA, dtype=jnp.int32)[None, :, None]
    radial_idx = jnp.arange(R, dtype=jnp.int32)[None, None, :]
    parity = (axial_idx + azim_idx + radial_idx) % 2
    checker = (1 - 2 * parity).astype(jnp.float32)[None]
    signs = jnp.where(jax.random.randint(key_sign, (5, 1, 1, 1), 0, 2) == 0, -1.0, 1.0).astype(jnp.float32)
    envelope = 3.0 + 0.5 * jnp.clip(jax.random.normal(key_env, shape, jnp.float32), -2.5, 2.5)
    rough = 0.8 * jnp.clip(jax.random.normal(key_rough, shape, jnp.float32), -2.5, 2.5)
    return jnp.clip(signs * checker * envelope + rough, -6.0, 6.0).astype(jnp.float32)


def plant(values, own_key, least, largest):
    index_at = [jax.random.randint(jax.random.fold_in(own_key, axis), (), 0, length) for axis, length in enumerate(values.shape)]
    longest = values.shape.index(max(values.shape))
    neighbour = index_at[:longest] + [(index_at[longest] + 1) % values.shape[longest]] + index_at[longest + 1:]
    return values.at[tuple(index_at)].set(least).at[tuple(neighbour)].set(largest)


def block_levels(stream_key, dims, pieces, smallest, high):
    def one(axis_at, parts):
        heights = jax.random.uniform(jax.random.fold_in(jax.random.fold_in(stream_key, 6), axis_at), (parts,), jnp.float32, smallest / len(pieces), high / len(pieces))
        return jnp.repeat(jnp.exp(heights), dims[axis_at] // parts).reshape((-1,) + (1,) * (len(dims) - axis_at - 1))

    level = one(*pieces[0])
    for cut in pieces[1:]:
        level = level * one(*cut)
    return level


def gaussian(rng, dims, scale, bound, pieces=(), kind=jnp.bfloat16):
    result = jax.random.normal(rng, dims, jnp.float32) * scale
    if len(pieces) > 0:
        result = block_levels(rng, dims, pieces, -0.22, 0.18) * result
    return jnp.clip(result, min=-bound, max=bound).astype(kind)


def setup_inputs(seed: int = 0) -> dict:
    arg_keys = jax.random.split(jax.random.key(seed), 6)
    noise = gaussian(arg_keys[0], (NXR, NAR, PR), 1.0, 6.0, ((0, 4), (1, 32)), jnp.float32)
    half_width = plant(jax.random.randint(arg_keys[1], (NXR, NAR, PR), 1, HMAX + 1), jax.random.fold_in(arg_keys[1], 1), 1, HMAX).astype(jnp.int32)
    owner = draw_owner(jax.random.fold_in(arg_keys[5], 71), 0)
    target_cell = plant(jax.random.randint(arg_keys[3], (N_AX * N_AZ * COLS,), 0, CX * CA), jax.random.fold_in(arg_keys[3], 1), 0, (CX * CA) - 1).astype(jnp.int32)
    fields = draw_fields(jax.random.fold_in(arg_keys[5], 71), 0)
    return {"noise": noise, "half_width": half_width, "owner": owner, "target_cell": target_cell, "fields": fields}


drp_coeffs = (0.770882380518, -0.166705904415, 0.020843142770)
mach_number = 0.5
time_step = 0.7
source_gain = 4.0
radial_step = 2.0
hub_ratio = 1.6


def drp_diff(padded, axis, length):
    total = jnp.zeros_like(lax.slice_in_dim(padded, 3, 3 + length, axis=axis))
    for shift, coeff in zip((1, 2, 3), drp_coeffs):
        upper = lax.slice_in_dim(padded, 3 + shift, 3 + shift + length, axis=axis)
        lower = lax.slice_in_dim(padded, 3 - shift, 3 - shift + length, axis=axis)
        total = total + coeff * (upper - lower)
    return total


def tendency(xpad, tpad, core, source, inv_h, inv_r):
    dx = drp_diff(xpad, 1, core.shape[1])
    dt_ = drp_diff(tpad, 2, core.shape[2]) * inv_h
    rpad = jnp.pad(core[3:5], ((0, 0), (0, 0), (0, 0), (3, 3)))
    dr = drp_diff(rpad, 3, core.shape[3]) / radial_step
    div = dx[1] + dt_[0] + dr[0] + core[3] * inv_r
    rho_t = -mach_number * dx[0] - div
    ux_t = -mach_number * dx[1] - dx[4]
    ut_t = -mach_number * dx[2] - dt_[1]
    ur_t = -mach_number * dx[3] - dr[1]
    p_t = -mach_number * dx[4] - div + source
    return jnp.stack([rho_t, ux_t, ut_t, ur_t, p_t])


def radial_factors(na_total, radial):
    base = na_total / (2.0 * math.pi)
    radius = base / hub_ratio + radial_step * (jnp.arange(radial, dtype=jnp.float32) + 0.5)
    inv_r = 1.0 / radius
    return base * inv_r, inv_r


def smooth(padded, width, axis, length, reach):
    hval = width.astype(jnp.float32)
    numer = jnp.zeros(width.shape, jnp.float32)
    denom = jnp.zeros(width.shape, jnp.float32)
    for offset in range(-reach, reach + 1):
        weight = jnp.where(abs(offset) <= hval, jnp.exp(-2.0 * offset * offset / (hval * hval)), 0.0)
        numer = numer + weight * lax.slice_in_dim(padded, reach + offset, reach + offset + length, axis=axis)
        denom = denom + weight
    return numer / denom


def reference(noise, half_width, owner, target_cell, fields):
    first = smooth(jnp.pad(noise, ((HMAX, HMAX), (0, 0), (0, 0))), half_width, 0, NXR, HMAX)
    second = smooth(jnp.pad(first, ((0, 0), (HMAX, HMAX), (0, 0)), mode="wrap"), half_width, 1, NAR, HMAX)
    filtered = smooth(jnp.pad(second, ((0, 0), (0, 0), (HMAX, HMAX))), half_width, 2, PR, HMAX)
    values = filtered.reshape(N_AX, PX, N_AZ, PA, PR).transpose(0, 2, 1, 3, 4).reshape(-1, PR)
    cell_x = (owner // N_AZ) * CX + target_cell // CA
    cell_a = (owner % N_AZ) * CA + target_cell % CA
    cell_r = (jnp.arange(PR, dtype=jnp.int32) * R) // PR
    source = jnp.zeros((NX, NA, R), jnp.float32).at[cell_x[:, None], cell_a[:, None], cell_r[None, :]].add(values) * source_gain
    inv_h, inv_r = radial_factors(float(NA), R)

    def full_tend(state):
        xpad = jnp.pad(state, ((0, 0), (3, 3), (0, 0), (0, 0)))
        tpad = jnp.pad(state[2:5:2], ((0, 0), (0, 0), (3, 3), (0, 0)), mode="wrap")
        return tendency(xpad, tpad, state, source, inv_h, inv_r)

    half_step = 0.5 * time_step
    k1 = full_tend(fields)
    k2 = full_tend(fields + half_step * k1)
    k3 = full_tend(fields + half_step * k2)
    k4 = full_tend(fields + time_step * k3)
    return fields + (time_step / 6.0) * (k1 + 2.0 * k2 + 2.0 * k3 + k4)
```

```python
import math

import numpy as np

import jax
import jax.numpy as jnp
from jax import lax
from jax.experimental import pallas as pl
from jax.experimental.pallas import tpu as pltpu
from jax.sharding import PartitionSpec as P

HMAX = 4
drp_coeffs = (0.770882380518, -0.166705904415, 0.02084314277)
mach_number = 0.5
time_step = 0.7
source_gain = 4.0
radial_step = 2.0
hub_ratio = 1.6

F32 = jnp.float32
BF16 = jnp.bfloat16
VM = pl.BlockSpec(memory_space=pltpu.VMEM)
PARAMS = pltpu.CompilerParams(vmem_limit_bytes=24 * 1024 * 1024)
GROUP = 8


def np_split(matrix):
    hi = matrix.astype(np.float32).astype(BF16)
    lo = (matrix - hi.astype(np.float64)).astype(np.float32).astype(BF16)
    return hi, lo


def filter_table():
    table = np.zeros((HMAX + 1, HMAX))
    for h in range(1, HMAX + 1):
        weights = [math.exp(-2.0 * k * k / (h * h)) if k <= h else 0.0 for k in range(HMAX + 1)]
        total = weights[0] + 2.0 * sum(weights[1:])
        table[:, h - 1] = [w / total for w in weights]
    return table


def radial_rows(na_total, radial):
    base = na_total / (2.0 * math.pi)
    radius = base / hub_ratio + radial_step * (np.arange(radial) + 0.5)
    return base / radius, 1.0 / radius


def radial_matrices(na_total, radial):
    diff = np.zeros((radial, radial))
    for s, a in zip((1, 2, 3), drp_coeffs):
        for j in range(radial):
            if j + s < radial:
                diff[j + s, j] += a / radial_step
            if j - s >= 0:
                diff[j - s, j] -= a / radial_step
    with_r = diff + np.diag(radial_rows(na_total, radial)[1])
    return np.stack([np.stack(np_split(with_r)), np.stack(np_split(diff))])


def azimuth_matrices(cols):
    full = np.zeros((2, GROUP * cols, GROUP * (cols + 16)))
    for which in range(2):
        place = {}
        for m in range(3):
            place[m - 3] = 1 + m + 4 * which
            place[cols + m] = 8 + m + 4 * which
        for x in range(GROUP):
            for i in range(cols):
                for s, a in zip((1, 2, 3), drp_coeffs):
                    for j, sign in ((i + s, 1.0), (i - s, -1.0)):
                        at = x * cols + j if 0 <= j < cols else GROUP * cols + x * 16 + place[j]
                        full[which, x * cols + i, at] += sign * a
    return np.stack([np.stack(np_split(full[w])) for w in range(2)])


def bin_matrix(fine, radial):
    at = (np.arange(fine) * radial) // fine
    return (source_gain * (at[:, None] == np.arange(radial)[None, :])).astype(np.float32).astype(BF16)


def split(x):
    hi = x.astype(BF16)
    return hi, (x - hi.astype(F32)).astype(BF16)


def dot(a, b):
    return lax.dot_general(a, b, (((1,), (0,)), ((), ())), preferred_element_type=F32)


def is_even(axis):
    return lax.rem(lax.axis_index(axis), 2) == 0


def swap(to_a, to_b, axis):
    devices = lax.axis_size(axis)
    pairs_a = [(i, i ^ 1) for i in range(devices)]
    pairs_b = [(i, (i - 1) % devices if i % 2 == 0 else (i + 1) % devices) for i in range(devices)]
    return lax.ppermute(to_a, axis, pairs_a), lax.ppermute(to_b, axis, pairs_b)


def call(body, outs, scratch=(), name=None, flops=0, moved=0):
    return pl.pallas_call(
        body,
        out_shape=[jax.ShapeDtypeStruct(s, d) for s, d in outs],
        out_specs=[VM] * len(outs),
        scratch_shapes=[pltpu.VMEM(s, d) for s, d in scratch],
        compiler_params=PARAMS,
        name=name,
        cost_estimate=pl.CostEstimate(flops=flops, bytes_accessed=moved, transcendentals=0),
    )


def full_specs(body, outs, args, scratch=(), name=None, moved=0):
    return pl.pallas_call(
        body,
        out_shape=[jax.ShapeDtypeStruct(s, d) for s, d in outs],
        in_specs=[VM] * len(args),
        out_specs=[VM] * len(outs),
        scratch_shapes=[pltpu.VMEM(s, d) for s, d in scratch],
        compiler_params=PARAMS,
        name=name,
        cost_estimate=pl.CostEstimate(flops=0, bytes_accessed=moved, transcendentals=0),
    )(*args)


def route_body(owner_ref, target_ref, upper_ref, pick_ref, cells_ref, own_ref):
    n_ax, n_az = lax.axis_size("ax"), lax.axis_size("az")
    ax, az = lax.axis_index("ax"), lax.axis_index("az")
    step_x = jnp.where(lax.rem(ax, 2) == 0, 1, -1)
    step_z = jnp.where(lax.rem(az, 2) == 0, 1, -1)
    me = ax * n_az + az
    b_x = ax - step_x
    ids = [
        (ax + step_x) * n_az + az,
        jnp.where((b_x >= 0) & (b_x < n_ax), b_x * n_az + az, -1),
        ax * n_az + lax.rem(az + step_z + n_az, n_az),
        ax * n_az + lax.rem(az - step_z + n_az, n_az),
    ]
    owner = owner_ref[...]
    target = target_ref[...]
    ncols = owner.shape[1]
    most = ncols // 2
    own_ref[...] = jnp.where(owner == me, target, -1)
    row = lax.broadcasted_iota(jnp.int32, (8, ncols), 0)
    marks = jnp.zeros((8, ncols), F32)
    for d, i in enumerate(ids):
        marks = jnp.where((row == d) & (owner == i), 1.0, marks)
    rank = dot(marks.astype(BF16), upper_ref[...])
    coarse = (target // 32).astype(F32)
    fine = (target % 32).astype(F32)
    digits = jnp.where(row == 0, coarse, jnp.where(row == 1, fine, 0.0)).astype(BF16)
    slot = lax.broadcasted_iota(jnp.int32, (most, ncols), 0).astype(F32)
    for d in range(4):
        wanted = jnp.where(marks[d : d + 1] > 0.0, rank[d : d + 1], -1.0)
        pick = jnp.where(slot == wanted, 1.0, 0.0).astype(BF16)
        pick_ref[d * most : (d + 1) * most, :] = pick
        found = lax.dot_general(digits, pick, (((1,), (1,)), ((), ())), preferred_element_type=F32)
        cells_ref[d, :, :] = jnp.zeros(cells_ref.shape[1:], F32)
        cells_ref[d, 0:1, 0:most] = found[0:1] * 32.0 + found[1:2]


def weights_of(h):
    table = filter_table()
    le = [h <= 1, h <= 2, h <= 3]
    out = []
    for k in range(HMAX + 1):
        value = jnp.full(h.shape, table[k, 3], F32)
        for j in (2, 1, 0):
            if j > 0 and table[k, j] == 0.0 and table[k, j - 1] == 0.0:
                value = jnp.where(le[j], 0.0, value)
                break
            value = jnp.where(le[j], table[k, j], value)
        out.append(value)
    return out


def first_body(noise_ref, half_ref, got_a_ref, got_b_ref, first_ref, to_a_ref, to_b_ref, halo):
    n_ax, ax = lax.axis_size("ax"), lax.axis_index("ax")
    even_x, even_z = is_even("ax"), is_even("az")
    rows = noise_ref.shape[0]
    halo[0] = jnp.where(ax > 0, jnp.where(even_x, got_b_ref[...], got_a_ref[...]), 0.0)
    halo[1] = jnp.where(ax < n_ax - 1, jnp.where(even_x, got_a_ref[...], got_b_ref[...]), 0.0)

    def row(x):
        if x < 0:
            return halo[0, x + HMAX]
        if x >= rows:
            return halo[1, x - rows]
        return noise_ref[x]

    for x in range(rows):
        w = weights_of(half_ref[x])
        total = w[0] * row(x)
        for k in range(1, HMAX + 1):
            total = total + w[k] * (row(x - k) + row(x + k))
        first_ref[x] = total
    half = rows // 2
    low = lax.broadcasted_iota(jnp.int32, (8, noise_ref.shape[2]), 0) < 4
    for x in range(half):
        last = jnp.where(low, pltpu.roll(first_ref[x, 8:16], 4, 0), first_ref[x + half, 8:16])
        begin = jnp.where(low, first_ref[x, 0:8], pltpu.roll(first_ref[x + half, 0:8], 4, 0))
        to_a_ref[x] = jnp.where(even_z, last, begin)
        to_b_ref[x] = jnp.where(even_z, begin, last)


def second_body(
    first_ref, half_ref, got_a_ref, got_b_ref, bins_ref, pick_ref, cells_ref,
    own_ref, to_xa, to_xb, to_za, to_zb, wide, fine_hi, fine_lo,
):
    even = is_even("az")
    rows, cols, fine = first_ref.shape
    half = rows // 2
    for x in range(half):
        got_a, got_b = got_a_ref[x], got_b_ref[x]
        before = jnp.where(even, got_b, got_a)
        after = jnp.where(even, got_a, got_b)
        wide[x, 0:8] = pltpu.roll(before, 4, 0)
        wide[x + half, 0:8] = before
        wide[x, 24:32] = after
        wide[x + half, 24:32] = pltpu.roll(after, 4, 0)
    lane = lax.broadcasted_iota(jnp.int32, (cols, fine), 1)
    for x in range(rows):
        wide[x, 8:24] = first_ref[x]
    for x in range(rows):
        w = weights_of(half_ref[x])
        total = w[0] * first_ref[x]
        for k in range(1, HMAX + 1):
            total = total + w[k] * (wide[x, 8 - k : 24 - k] + wide[x, 8 + k : 24 + k])
        result = w[0] * total
        for k in range(1, HMAX + 1):
            up = jnp.where(lane < fine - k, pltpu.roll(total, fine - k, 1), 0.0)
            down = jnp.where(lane >= k, pltpu.roll(total, k, 1), 0.0)
            result = result + w[k] * (up + down)
        hi, lo = split(result)
        fine_hi[x * cols : (x + 1) * cols] = hi
        fine_lo[x * cols : (x + 1) * cols] = lo
    bins = bins_ref[...]
    binned = dot(fine_hi[...], bins) + dot(fine_lo[...], bins)
    own_ref[...] = binned
    hi, lo = split(binned)
    most = pick_ref.shape[0] // 4
    for d, out in enumerate((to_xa, to_xb, to_za, to_zb)):
        pick = pick_ref[d * most : (d + 1) * most]
        out[0:most] = dot(pick, hi) + dot(pick, lo)
        out[most : most + 8] = cells_ref[d]


def gather_body(binned_ref, own_ref, xa, xb, za, zb, q_ref):
    cells, radial = q_ref.shape
    most = xa.shape[0] - 8

    def onehot(row):
        at = lax.broadcasted_iota(jnp.int32, (cells, row.shape[1]), 0)
        return jnp.where(at == row, 1.0, 0.0).astype(BF16)

    mats = [onehot(own_ref[...])]
    rows = [binned_ref[...]]
    for got in (xa, xb, za, zb):
        mats.append(onehot(got[most : most + 1, 0:most].astype(jnp.int32)))
        rows.append(got[0:most])
    mat = jnp.concatenate(mats, axis=1)
    hi, lo = split(jnp.concatenate(rows, axis=0))
    q_ref[...] = dot(mat, hi) + dot(mat, lo)


def write_sends(state, to_xa, to_xb, to_za, to_zb):
    even_x, even_z = is_even("ax"), is_even("az")
    rows = state.shape[1]
    for f in range(state.shape[0]):
        first, last = state[f, 0:3], state[f, rows - 3 : rows]
        to_xa[f] = jnp.where(even_x, last, first)
        to_xb[f] = jnp.where(even_x, first, last)
    low = lax.broadcasted_iota(jnp.int32, (8, state.shape[3]), 0) < 4
    for x in range(rows):
        last = jnp.where(low, pltpu.roll(state[2, x, 8:16], 4, 0), state[4, x, 8:16])
        first = jnp.where(low, state[2, x, 0:8], pltpu.roll(state[4, x, 0:8], 4, 0))
        to_za[x] = jnp.where(even_z, last, first)
        to_zb[x] = jnp.where(even_z, first, last)


def send_shapes(rows, cols, radial):
    ax, az = ((5, 3, cols, radial), F32), ((rows, 8, radial), F32)
    return [ax, ax, az, az]


def edges_body(state, to_xa, to_xb, to_za, to_zb):
    write_sends(state, to_xa, to_xb, to_za, to_zb)


def apply_operator(state, xa, xb, za, zb, tmat, rmat, inv_h_ref, halo, side, finish):
    n_ax, ax = lax.axis_size("ax"), lax.axis_index("ax")
    even_x, even_z = is_even("ax"), is_even("az")
    _, rows, cols, radial = state.shape
    for f in range(5):
        halo[0, f] = jnp.where(ax > 0, jnp.where(even_x, xb[f], xa[f]), 0.0)
        halo[1, f] = jnp.where(ax < n_ax - 1, jnp.where(even_x, xa[f], xb[f]), 0.0)
    side[:, 0:8] = jnp.where(even_z, zb[...], za[...])
    side[:, 8:16] = jnp.where(even_z, za[...], zb[...])
    inv_h = inv_h_ref[...]

    def row(f, x):
        if x < 0:
            return halo[0, f, x + 3]
        if x >= rows:
            return halo[1, f, x - rows]
        return state[f, x]

    def dx(f, x):
        total = drp_coeffs[0] * (row(f, x + 1) - row(f, x - 1))
        for s in (2, 3):
            total = total + drp_coeffs[s - 1] * (row(f, x + s) - row(f, x - s))
        return total

    size = GROUP * cols
    for g in range(rows // GROUP):
        at = slice(g * GROUP, (g + 1) * GROUP)
        halo_hi, halo_lo = split(side[at].reshape(GROUP * 16, radial))
        p_hi, p_lo = split(state[4, at].reshape(size, radial))
        ut_hi, ut_lo = split(state[2, at].reshape(size, radial))
        ur_hi, ur_lo = split(state[3, at].reshape(size, radial))

        def across(which, hi, lo):
            hi = jnp.concatenate([hi, halo_hi], axis=0)
            lo = jnp.concatenate([lo, halo_lo], axis=0)
            return dot(tmat[which, 0], hi) + dot(tmat[which, 0], lo) + dot(tmat[which, 1], hi)

        def outward(which, hi, lo):
            return dot(hi, rmat[which, 0]) + dot(lo, rmat[which, 0]) + dot(hi, rmat[which, 1])

        div_tr = across(0, ut_hi, ut_lo) * inv_h + outward(0, ur_hi, ur_lo)
        p_t = across(1, p_hi, p_lo) * inv_h
        p_r = outward(1, p_hi, p_lo)
        for i in range(GROUP):
            x = g * GROUP + i
            part = slice(i * cols, (i + 1) * cols)
            d = [dx(f, x) for f in range(5)]
            div = d[1] + div_tr[part]
            finish(
                x,
                [
                    -mach_number * d[0] - div,
                    -mach_number * d[1] - d[4],
                    -mach_number * d[2] - p_t[part],
                    -mach_number * d[3] - p_r[part],
                    -mach_number * d[4] - div,
                ],
            )


def start_body(state, xa, xb, za, zb, tmat, rmat, inv_h, out, halo, side):
    def finish(x, tend):
        for f in range(5):
            out[f, x] = tend[f]

    apply_operator(state, xa, xb, za, zb, tmat, rmat, inv_h, halo, side, finish)


def stage_body(factor, state, xa, xb, za, zb, tmat, rmat, inv_h, base, out, to_xa, to_xb, to_za, to_zb, halo, side):
    def finish(x, tend):
        for f in range(5):
            out[f, x] = base[f, x] + factor * tend[f]

    apply_operator(state, xa, xb, za, zb, tmat, rmat, inv_h, halo, side, finish)
    write_sends(out, to_xa, to_xb, to_za, to_zb)


def last_body(state, xa, xb, za, zb, tmat, rmat, inv_h, k, fields, out, halo, side):
    def finish(x, tend):
        for f in range(5):
            out[f, x] = fields[f, x] + time_step * k[f, x] + (0.5 * time_step * time_step) * tend[f]

    apply_operator(state, xa, xb, za, zb, tmat, rmat, inv_h, halo, side, finish)


def local(noise, half_width, owner, target_cell, fields):
    px, pa, fine = noise.shape
    cx, ca, radial = fields.shape[1:]
    ncols = px * pa
    most = ncols // 2
    n_az = lax.axis_size("az")
    even_x = is_even("ax")

    first, last = noise[:HMAX], noise[px - HMAX :]
    noise_a, noise_b = swap(jnp.where(even_x, last, first), jnp.where(even_x, first, last), "ax")
    sends = send_shapes(cx, ca, radial)
    xa, xb, za, zb = full_specs(edges_body, sends, [fields], name="edges")
    uza, uzb = swap(za, zb, "az")
    uxa, uxb = swap(xa, xb, "ax")

    upper = jnp.asarray(np.triu(np.ones((ncols, ncols), np.float32), 1).astype(BF16))
    pick, cells, own = full_specs(
        route_body,
        [((4 * most, ncols), BF16), ((4, 8, radial), F32), ((1, ncols), jnp.int32)],
        [owner.reshape(1, ncols), target_cell.reshape(1, ncols), upper],
        name="route",
    )
    filtered, to_a, to_b = full_specs(
        first_body,
        [((px, pa, fine), F32), ((px // 2, 8, fine), F32), ((px // 2, 8, fine), F32)],
        [noise, half_width, noise_a, noise_b],
        [((2, HMAX, pa, fine), F32)],
        name="filter_axial",
    )
    got_a, got_b = swap(to_a, to_b, "az")

    tmat = jnp.asarray(azimuth_matrices(ca))
    rmat = jnp.asarray(radial_matrices(float(ca * n_az), radial))
    inv_h = jnp.asarray(radial_rows(float(ca * n_az), radial)[0].astype(np.float32)[None, :])
    state = ((5, cx, ca, radial), F32)
    spare = [((2, 5, 3, ca, radial), F32), ((cx, 16, radial), F32)]
    (k,) = full_specs(start_body, [state], [fields, uxa, uxb, uza, uzb, tmat, rmat, inv_h], spare, name="operator")

    bins = jnp.asarray(bin_matrix(fine, radial))
    packet = ((most + 8, radial), F32)
    binned, xa, xb, za, zb = full_specs(
        second_body,
        [((ncols, radial), F32), packet, packet, packet, packet],
        [filtered, half_width, got_a, got_b, bins, pick, cells],
        [((px, 32, fine), F32), ((ncols, fine), BF16), ((ncols, fine), BF16)],
        name="filter_rest",
    )
    xa, xb = swap(xa, xb, "ax")
    za, zb = swap(za, zb, "az")
    (q,) = full_specs(gather_body, [((cx * ca, radial), F32)], [binned, own, xa, xb, za, zb], name="gather")

    k = k.at[4].add(q.reshape(cx, ca, radial))
    xa, xb, za, zb = full_specs(edges_body, sends, [k], name="edges_k")
    level = k
    for factor in (time_step / 4.0, time_step / 3.0):
        za, zb = swap(za, zb, "az")
        xa, xb = swap(xa, xb, "ax")

        def body(*refs, factor=factor):
            stage_body(factor, *refs)

        level, xa, xb, za, zb = full_specs(
            body, [state] + sends, [level, xa, xb, za, zb, tmat, rmat, inv_h, k], spare, name="stage"
        )
    za, zb = swap(za, zb, "az")
    xa, xb = swap(xa, xb, "ax")
    (out,) = full_specs(
        last_body, [state], [level, xa, xb, za, zb, tmat, rmat, inv_h, k, fields], spare, name="final"
    )
    return out


def solution(mesh):
    return jax.shard_map(
        local,
        mesh=mesh,
        in_specs=(
            P("ax", "az", None),
            P("ax", "az", None),
            P(("ax", "az")),
            P(("ax", "az")),
            P(None, "ax", "az", None),
        ),
        out_specs=P(None, "ax", "az", None),
        check_vma=False,
    )
```

```python
import math

import numpy as np

import jax
import jax.numpy as jnp
from jax import lax
from jax.experimental import pallas as pl
from jax.experimental.pallas import tpu as pltpu
from jax.sharding import PartitionSpec as P

HMAX = 4
drp_coeffs = (0.770882380518, -0.166705904415, 0.02084314277)
mach_number = 0.5
time_step = 0.7
source_gain = 4.0
radial_step = 2.0
hub_ratio = 1.6

F32 = jnp.float32
BF16 = jnp.bfloat16
VM = pl.BlockSpec(memory_space=pltpu.VMEM)
PARAMS = pltpu.CompilerParams(vmem_limit_bytes=24 * 1024 * 1024)
GROUP = 8


def window_matrices(span):
    one = np.zeros((span, span))
    for s, a in zip((1, 2, 3), drp_coeffs):
        one += a * (np.eye(span, k=s) - np.eye(span, k=-s))
    return np.stack(np_split(np.kron(np.eye(GROUP), one)))


def np_split(matrix):
    hi = matrix.astype(np.float32).astype(BF16)
    lo = (matrix - hi.astype(np.float64)).astype(np.float32).astype(BF16)
    return hi, lo


def filter_table():
    table = np.zeros((HMAX + 1, HMAX))
    for h in range(1, HMAX + 1):
        weights = [math.exp(-2.0 * k * k / (h * h)) if k <= h else 0.0 for k in range(HMAX + 1)]
        total = weights[0] + 2.0 * sum(weights[1:])
        table[:, h - 1] = [w / total for w in weights]
    return table


def radial_rows(na_total, radial):
    base = na_total / (2.0 * math.pi)
    radius = base / hub_ratio + radial_step * (np.arange(radial) + 0.5)
    return base / radius, 1.0 / radius


def radial_matrices(na_total, radial):
    diff = np.zeros((radial, radial))
    for s, a in zip((1, 2, 3), drp_coeffs):
        for j in range(radial):
            if j + s < radial:
                diff[j + s, j] += a / radial_step
            if j - s >= 0:
                diff[j - s, j] -= a / radial_step
    with_r = diff + np.diag(radial_rows(na_total, radial)[1])
    return np.stack([np.stack(np_split(with_r)), np.stack(np_split(diff))])


def azimuth_matrices(cols):
    full = np.zeros((2, GROUP * cols, GROUP * (cols + 16)))
    for which in range(2):
        place = {}
        for m in range(3):
            place[m - 3] = m + 4 * which
            place[cols + m] = 8 + m + 4 * which
        for x in range(GROUP):
            for i in range(cols):
                for s, a in zip((1, 2, 3), drp_coeffs):
                    for j, sign in ((i + s, 1.0), (i - s, -1.0)):
                        at = x * cols + j if 0 <= j < cols else GROUP * cols + x * 16 + place[j]
                        full[which, x * cols + i, at] += sign * a
    return np.stack([np.stack(np_split(full[w])) for w in range(2)])


def split(x):
    hi = x.astype(BF16)
    return hi, (x - hi.astype(F32)).astype(BF16)


def dot(a, b):
    return lax.dot_general(a, b, (((1,), (0,)), ((), ())), preferred_element_type=F32)


def is_even(axis):
    return lax.rem(lax.axis_index(axis), 2) == 0


def swap(to_a, to_b, axis):
    devices = lax.axis_size(axis)
    pairs_a = [(i, i ^ 1) for i in range(devices)]
    pairs_b = [(i, (i - 1) % devices if i % 2 == 0 else (i + 1) % devices) for i in range(devices)]
    return lax.ppermute(to_a, axis, pairs_a), lax.ppermute(to_b, axis, pairs_b)


def full_specs(body, outs, args, scratch=(), name=None, out_specs=None):
    return pl.pallas_call(
        body,
        out_shape=[jax.ShapeDtypeStruct(s, d) for s, d in outs],
        in_specs=[VM] * len(args),
        out_specs=out_specs or [VM] * len(outs),
        scratch_shapes=[pltpu.VMEM(*s) if isinstance(s, tuple) else s for s in scratch],
        compiler_params=PARAMS,
        name=name,
    )(*args)


def route_body(owner_ref, target_ref, pick_ref, cells_ref, own_ref):
    n_ax, n_az = lax.axis_size("ax"), lax.axis_size("az")
    ax, az = lax.axis_index("ax"), lax.axis_index("az")
    step_x = jnp.where(lax.rem(ax, 2) == 0, 1, -1)
    step_z = jnp.where(lax.rem(az, 2) == 0, 1, -1)
    me = ax * n_az + az
    b_x = ax - step_x
    ids = [
        (ax + step_x) * n_az + az,
        jnp.where((b_x >= 0) & (b_x < n_ax), b_x * n_az + az, -1),
        ax * n_az + lax.rem(az + step_z + n_az, n_az),
        ax * n_az + lax.rem(az - step_z + n_az, n_az),
    ]
    owner = owner_ref[...]
    target = target_ref[...]
    ncols = owner.shape[1]
    most = ncols // 2
    own_ref[...] = jnp.where(owner == me, target, -1)
    row = lax.broadcasted_iota(jnp.int32, (8, ncols), 0)
    marks = jnp.zeros((8, ncols), F32)
    for d, i in enumerate(ids):
        marks = jnp.where((row == d) & (owner == i), 1.0, marks)
    before = lax.broadcasted_iota(jnp.int32, (ncols, ncols), 0) < lax.broadcasted_iota(jnp.int32, (ncols, ncols), 1)
    rank = dot(marks.astype(BF16), jnp.where(before, 1.0, 0.0).astype(BF16))
    coarse = (target // 32).astype(F32)
    fine = (target % 32).astype(F32)
    digits = jnp.where(row == 0, coarse, jnp.where(row == 1, fine, 0.0)).astype(BF16)
    slot = lax.broadcasted_iota(jnp.int32, (most, ncols), 0).astype(F32)
    for d in range(4):
        wanted = jnp.where(marks[d : d + 1] > 0.0, rank[d : d + 1], -1.0)
        pick = jnp.where(slot == wanted, 1.0, 0.0).astype(BF16)
        pick_ref[d * most : (d + 1) * most, :] = pick
        found = lax.dot_general(digits, pick, (((1,), (1,)), ((), ())), preferred_element_type=F32)
        cells_ref[d, :, :] = jnp.zeros(cells_ref.shape[1:], F32)
        cells_ref[d, 0:1, 0:most] = found[0:1] * 32.0 + found[1:2]


def weights_of(h):
    table = filter_table()
    le = [h <= 1, h <= 2, h <= 3]
    out = []
    for k in range(HMAX + 1):
        value = jnp.full(h.shape, table[k, 3], F32)
        for j in (2, 1, 0):
            if j > 0 and table[k, j] == 0.0 and table[k, j - 1] == 0.0:
                value = jnp.where(le[j], 0.0, value)
                break
            value = jnp.where(le[j], table[k, j], value)
        out.append(value)
    return out


def inner_body(noise_ref, half_ref, first_ref):
    rows = noise_ref.shape[0]
    for x in range(rows):
        w = weights_of(half_ref[x])
        total = w[0] * noise_ref[x]
        for k in range(1, HMAX + 1):
            near = [noise_ref[y] for y in (x - k, x + k) if 0 <= y < rows]
            if near:
                total = total + w[k] * (near[0] + near[1] if len(near) == 2 else near[0])
        first_ref[x] = total


def first_body(inner_ref, half_ref, got_a_ref, got_b_ref, first_ref, to_a_ref, to_b_ref, halo):
    n_ax, ax = lax.axis_size("ax"), lax.axis_index("ax")
    even_x, even_z = is_even("ax"), is_even("az")
    rows = half_ref.shape[0]
    halo[0] = jnp.where(ax > 0, jnp.where(even_x, got_b_ref[...], got_a_ref[...]), 0.0)
    halo[1] = jnp.where(ax < n_ax - 1, jnp.where(even_x, got_a_ref[...], got_b_ref[...]), 0.0)
    for x in range(HMAX, rows - HMAX):
        first_ref[x] = inner_ref[x]
    for i in range(HMAX):
        w = weights_of(half_ref[i])
        total = inner_ref[i]
        for k in range(i + 1, HMAX + 1):
            total = total + w[k] * halo[0, HMAX + i - k]
        first_ref[i] = total
        x = rows - 1 - i
        w = weights_of(half_ref[x])
        total = inner_ref[x]
        for k in range(i + 1, HMAX + 1):
            total = total + w[k] * halo[1, k - i - 1]
        first_ref[x] = total
    half = rows // 2
    low = lax.broadcasted_iota(jnp.int32, (8, half_ref.shape[2]), 0) < 4
    for x in range(half):
        last = jnp.where(low, pltpu.roll(first_ref[x, 8:16], 4, 0), first_ref[x + half, 8:16])
        begin = jnp.where(low, first_ref[x, 0:8], pltpu.roll(first_ref[x + half, 0:8], 4, 0))
        to_a_ref[x] = jnp.where(even_z, last, begin)
        to_b_ref[x] = jnp.where(even_z, begin, last)


def second_body(
    first_ref, half_ref, got_a_ref, got_b_ref, pick_ref, cells_ref,
    own_ref, to_xa, to_xb, to_za, to_zb, wide, fine_hi, fine_lo,
):
    even = is_even("az")
    rows, cols, fine = first_ref.shape
    half = rows // 2
    for x in range(half):
        got_a, got_b = got_a_ref[x], got_b_ref[x]
        before = jnp.where(even, got_b, got_a)
        after = jnp.where(even, got_a, got_b)
        wide[x, 0:8] = pltpu.roll(before, 4, 0)
        wide[x + half, 0:8] = before
        wide[x, 24:32] = after
        wide[x + half, 24:32] = pltpu.roll(after, 4, 0)
    lane = lax.broadcasted_iota(jnp.int32, (cols, fine), 1)
    for x in range(rows):
        wide[x, 8:24] = first_ref[x]
    for x in range(rows):
        w = weights_of(half_ref[x])
        total = w[0] * first_ref[x]
        for k in range(1, HMAX + 1):
            total = total + w[k] * (wide[x, 8 - k : 24 - k] + wide[x, 8 + k : 24 + k])
        result = w[0] * total
        for k in range(1, HMAX + 1):
            up = jnp.where(lane < fine - k, pltpu.roll(total, fine - k, 1), 0.0)
            down = jnp.where(lane >= k, pltpu.roll(total, k, 1), 0.0)
            result = result + w[k] * (up + down)
        hi, lo = split(result)
        fine_hi[x * cols : (x + 1) * cols] = hi
        fine_lo[x * cols : (x + 1) * cols] = lo
    radial = own_ref.shape[1]
    above = lax.broadcasted_iota(jnp.int32, (fine, radial), 0) - lax.broadcasted_iota(
        jnp.int32, (fine, radial), 1
    ) * (fine // radial)
    bins = jnp.where((above >= 0) & (above < fine // radial), source_gain, 0.0).astype(BF16)
    binned = dot(fine_hi[...], bins) + dot(fine_lo[...], bins)
    own_ref[...] = binned
    hi, lo = split(binned)
    most = pick_ref.shape[0] // 4
    for d, out in enumerate((to_xa, to_xb, to_za, to_zb)):
        pick = pick_ref[d * most : (d + 1) * most]
        out[0:most] = dot(pick, hi) + dot(pick, lo)
        out[most : most + 8] = cells_ref[d]


def gather_body(binned_ref, own_ref, xa, xb, za, zb, q_ref, to_xa, to_xb):
    rows, cols, radial = q_ref.shape
    cells = rows * cols
    most = xa.shape[0] - 8
    even = is_even("ax")

    def onehot(row):
        at = lax.broadcasted_iota(jnp.int32, (cells, row.shape[1]), 0)
        return jnp.where(at == row, 1.0, 0.0).astype(BF16)

    mats = [onehot(own_ref[...])]
    packets = [binned_ref[...]]
    for got in (xa, xb, za, zb):
        mats.append(onehot(got[most : most + 1, 0:most].astype(jnp.int32)))
        packets.append(got[0:most])
    mat = jnp.concatenate(mats, axis=1)
    hi, lo = split(jnp.concatenate(packets, axis=0))
    q_ref[...] = (dot(mat, hi) + dot(mat, lo)).reshape(rows, cols, radial)
    first, last = q_ref[0:REACH], q_ref[rows - REACH :]
    to_xa[...] = jnp.where(even, last, first)
    to_xb[...] = jnp.where(even, first, last)


def join_last(ut, p):
    low = lax.broadcasted_iota(jnp.int32, ut.shape, 0) < 4
    return jnp.where(low, pltpu.roll(ut, 3, 0), pltpu.roll(p, 7, 0))


def join_first(ut, p):
    low = lax.broadcasted_iota(jnp.int32, ut.shape, 0) < 4
    return jnp.where(low, ut, pltpu.roll(p, 4, 0))


def write_sends(state, to_xa, to_xb, to_za, to_zb):
    even_x, even_z = is_even("ax"), is_even("az")
    rows = state.shape[1]
    for f in range(state.shape[0]):
        first, last = state[f, 0:3], state[f, rows - 3 : rows]
        to_xa[f] = jnp.where(even_x, last, first)
        to_xb[f] = jnp.where(even_x, first, last)
    for x in range(rows):
        last = join_last(state[2, x, 8:16], state[4, x, 8:16])[0:7]
        first = join_first(state[2, x, 0:8], state[4, x, 0:8])[0:7]
        to_za[x] = jnp.where(even_z, last, first)
        to_zb[x] = jnp.where(even_z, first, last)


def send_shapes(rows, cols, radial):
    ax, az = ((5, 3, cols, radial), F32), ((rows, 7, radial), F32)
    return [ax, ax, az, az]


def edges_body(state, to_xa, to_xb, to_za, to_zb):
    write_sends(state, to_xa, to_xb, to_za, to_zb)


def fill_side(side, za, zb):
    even = is_even("az")
    side[:, 0:7] = jnp.where(even, zb[...], za[...])
    side[:, 8:15] = jnp.where(even, za[...], zb[...])
    blank = jnp.zeros((side.shape[0], 1, side.shape[2]), F32)
    side[:, 7:8] = blank
    side[:, 15:16] = blank


def inverse_step(cols, radial):
    base = cols * lax.axis_size("az") / (2.0 * math.pi)
    at = lax.broadcasted_iota(jnp.int32, (1, radial), 1).astype(F32)
    return base / (base / hub_ratio + radial_step * (at + 0.5))


def outward(rmat, which, hi, lo):
    return dot(hi, rmat[which, 0]) + dot(lo, rmat[which, 0]) + dot(hi, rmat[which, 1])


def along(row, x):
    total = drp_coeffs[0] * (row(x + 1) - row(x - 1))
    for s in (2, 3):
        total = total + drp_coeffs[s - 1] * (row(x + s) - row(x - s))
    return total


def apply_operator(state, row, side, tmat, rmat, finish):
    _, rows, cols, radial = state.shape
    inv_h = inverse_step(cols, radial)
    size = GROUP * cols
    for g in range(rows // GROUP):
        at = slice(g * GROUP, (g + 1) * GROUP)
        halo_hi, halo_lo = split(side[at].reshape(GROUP * 16, radial))
        p_hi, p_lo = split(state[4, at].reshape(size, radial))
        ut_hi, ut_lo = split(state[2, at].reshape(size, radial))
        ur_hi, ur_lo = split(state[3, at].reshape(size, radial))

        def across(which, hi, lo):
            hi = jnp.concatenate([hi, halo_hi], axis=0)
            lo = jnp.concatenate([lo, halo_lo], axis=0)
            return dot(tmat[which, 0], hi) + dot(tmat[which, 0], lo) + dot(tmat[which, 1], hi)

        div_tr = across(0, ut_hi, ut_lo) * inv_h + outward(rmat, 0, ur_hi, ur_lo)
        p_t = across(1, p_hi, p_lo) * inv_h
        p_r = outward(rmat, 1, p_hi, p_lo)
        for i in range(GROUP):
            x = g * GROUP + i
            part = slice(i * cols, (i + 1) * cols)
            d = [along(lambda y: row(f, y), x) for f in range(5)]
            div = d[1] + div_tr[part]
            finish(
                x,
                [
                    -mach_number * d[0] - div,
                    -mach_number * d[1] - d[4],
                    -mach_number * d[2] - p_t[part],
                    -mach_number * d[3] - p_r[part],
                    -mach_number * d[4] - div,
                ],
            )


def fill_halo(halo, xa, xb):
    n_ax, ax = lax.axis_size("ax"), lax.axis_index("ax")
    even = is_even("ax")
    for f in range(halo.shape[1]):
        halo[0, f] = jnp.where(ax > 0, jnp.where(even, xb[f], xa[f]), 0.0)
        halo[1, f] = jnp.where(ax < n_ax - 1, jnp.where(even, xa[f], xb[f]), 0.0)


def with_halos(state, halo):
    rows = state.shape[1]

    def row(f, x):
        if x < 0:
            return halo[0, f, x + 3]
        if x >= rows:
            return halo[1, f, x - rows]
        return state[f, x]

    return row


def stage_body(factor, refs):
    state, za, zb, xa, xb, tmat, rmat, *rest = refs
    base = rest.pop(0) if len(rest) == 8 else None
    out, to_xa, to_xb, to_za, to_zb, halo, side = rest
    fill_halo(halo, xa, xb)
    fill_side(side, za, zb)

    def finish(x, tend):
        for f in range(5):
            out[f, x] = tend[f] if base is None else base[f, x] + factor * tend[f]

    apply_operator(state, with_halos(state, halo), side, tmat, rmat, finish)
    write_sends(out, to_xa, to_xb, to_za, to_zb)


def last_body(
    state, za, zb, xa, xb, tmat, rmat, k, fields, extra, extra_side, q, out, halo, side, both, result, sems
):
    _, rows, cols, radial = state.shape
    fill_halo(halo, xa, xb)
    fill_side(side, za, zb)
    side[...] = side[...] + extra_side[...]
    for f in range(5):
        halo[0, f] = halo[0, f] + extra[f, 0:3]
        halo[1, f] = halo[1, f] + extra[f, rows + 3 : rows + 6]
        for x in range(rows):
            both[f, x] = state[f, x] + extra[f, x + 3]

    def finish(x, tend):
        for f in range(5):
            slope = k[f, x] + q[x] if f == 4 else k[f, x]
            result[f, x] = fields[f, x] + time_step * slope + (0.5 * time_step * time_step) * tend[f]
        if x % GROUP == GROUP - 1:
            copy(x // GROUP).start()

    def copy(g):
        at = pl.ds(g * GROUP, GROUP)
        return pltpu.make_async_copy(result.at[:, at], out.at[:, at], sems.at[g])

    apply_operator(both, with_halos(both, halo), side, tmat, rmat, finish)
    for g in range(rows // GROUP):
        copy(g).wait()


REACH = 9


def widen_body(q, xa, xb, wide, to_za, to_zb):
    n_ax, ax = lax.axis_size("ax"), lax.axis_index("ax")
    even_x, even_z = is_even("ax"), is_even("az")
    rows, _, radial = q.shape
    wide[0:REACH] = jnp.where(ax > 0, jnp.where(even_x, xb[...], xa[...]), 0.0)
    wide[REACH : REACH + rows] = q[...]
    wide[REACH + rows :] = jnp.where(ax < n_ax - 1, jnp.where(even_x, xa[...], xb[...]), 0.0)
    total = rows + 2 * REACH
    place = lax.broadcasted_iota(jnp.int32, (8, radial), 0)
    for start in range(0, total, 8):
        last, first = jnp.zeros((8, radial), F32), jnp.zeros((8, radial), F32)
        for x in range(start, min(start + 8, total)):
            low, high = wide[x, 0:8], wide[x, 8:16]
            to_za[x] = jnp.where(even_z, high, low)
            to_zb[x] = jnp.where(even_z, low, high)
            at = x - start
            last = jnp.where(place == at, pltpu.roll(low, (at + 1) % 8, 0), last)
            first = jnp.where(place == at, pltpu.roll(high, at, 0) if at else high, first)
        to_za[total + start // 8] = jnp.where(even_z, last, first)
        to_zb[total + start // 8] = jnp.where(even_z, first, last)


def source_body(wide, za, zb, tmat, rmat, out, out_side, full, far, w3):
    n_ax, ax = lax.axis_size("ax"), lax.axis_index("ax")
    even = is_even("az")
    total, cols, radial = wide.shape
    rows = total - 2 * REACH

    def inside(value, x):
        if x < 0:
            return jnp.where(ax > 0, value, 0.0)
        if x >= rows:
            return jnp.where(ax < n_ax - 1, value, 0.0)
        return value

    before, after = 8, 8 + cols
    full[:, 0:8] = jnp.where(even, zb[0:total], za[0:total])
    full[:, 8:after] = wide[...]
    full[:, after : after + 8] = jnp.where(even, za[0:total], zb[0:total])
    far[0] = jnp.where(even, zb[total:], za[total:])
    far[1] = jnp.where(even, za[total:], zb[total:])
    inv_h = inverse_step(cols, radial)
    span = cols + 16
    size = GROUP * span
    place = lax.broadcasted_iota(jnp.int32, (8, radial), 0)
    edge = drp_coeffs[2]

    def across(hi, lo):
        return dot(tmat[0], hi) + dot(tmat[0], lo) + dot(tmat[1], hi)

    def groups(start, count):
        done = start
        while done < start + count:
            at = min(done, start + count - GROUP)
            yield at, range(done, at + GROUP)
            done = at + GROUP

    c = time_step / 4.0
    for at, todo in groups(3, rows + 12):
        hi, lo = split(full[at : at + GROUP].reshape(size, radial))
        q_t = across(hi, lo)
        q_r = outward(rmat, 1, hi, lo)
        for x in todo:
            part = slice((x - at) * span, (x - at + 1) * span)
            d = along(lambda y: full[y], x)
            w3[0, x - 3] = inside(-c * d, x - REACH)
            turn = q_t[part]
            low = jnp.where(place == 2, -edge * far[0, x // 8, x % 8 : x % 8 + 1], 0.0)
            high = jnp.where(place == 5, edge * far[1, x // 8, x % 8 : x % 8 + 1], 0.0)
            turn = jnp.concatenate([turn[0:8] + low, turn[8:after], turn[after:span] + high], axis=0)
            w3[1, x - 3] = inside((-c) * inv_h * turn, x - REACH)
            w3[2, x - 3] = inside(-c * q_r[part], x - REACH)
            w3[3, x - 3] = inside(full[x] - (c * mach_number) * d, x - REACH)

    c = time_step / 3.0
    for at, todo in groups(3, rows + 6):
        ut_hi, ut_lo = split(w3[1, at : at + GROUP].reshape(size, radial))
        ur_hi, ur_lo = split(w3[2, at : at + GROUP].reshape(size, radial))
        p_hi, p_lo = split(w3[3, at : at + GROUP].reshape(size, radial))
        div_tr = across(ut_hi, ut_lo) * inv_h + outward(rmat, 0, ur_hi, ur_lo)
        p_t = across(p_hi, p_lo) * inv_h
        p_r = outward(rmat, 1, p_hi, p_lo)
        for x in todo:
            o = x - 3
            begin = (x - at) * span
            part = slice(begin + 8, begin + 8 + cols)
            d = [along(lambda y: w3[f, y, 8:after], x) for f in range(4)]
            div = d[0] + div_tr[part]
            out[0, o] = inside(-c * div, o - 3)
            out[1, o] = inside(-c * (mach_number * d[0] + d[3]), o - 3)
            out[2, o] = inside(-c * (mach_number * d[1] + p_t[part]), o - 3)
            out[3, o] = inside(-c * (mach_number * d[2] + p_r[part]), o - 3)
            out[4, o] = inside(full[x + 3, 8:after] - c * (mach_number * d[3] + div), o - 3)
            if 3 <= o < 3 + rows:
                tiles = []
                for lanes in (slice(0, 8), slice(after, after + 8)):
                    part = slice(begin + lanes.start, begin + lanes.stop)
                    d0, d1, d3 = [along(lambda y: w3[f, y, lanes], x) for f in (0, 1, 3)]
                    ut = -c * (mach_number * d1 + p_t[part])
                    p = full[x + 3, lanes] - c * (mach_number * d3 + d0 + div_tr[part])
                    tiles.append((ut, p))
                out_side[o - 3, 0:8] = jnp.where(place == 7, 0.0, join_last(*tiles[0]))
                out_side[o - 3, 8:16] = jnp.where(place == 7, 0.0, join_first(*tiles[1]))


def local(noise, half_width, owner, target_cell, fields):
    px, pa, fine = noise.shape
    cx, ca, radial = fields.shape[1:]
    ncols = px * pa
    most = ncols // 2
    n_az = lax.axis_size("az")
    even_x = is_even("ax")

    first, last = noise[:HMAX], noise[px - HMAX :]
    to_a, to_b = jnp.where(even_x, last, first), jnp.where(even_x, first, last)
    to_a, to_b, late = lax.optimization_barrier((to_a, to_b, fields))
    noise_a, noise_b = swap(to_a, to_b, "ax")
    sends = send_shapes(cx, ca, radial)
    xa, xb, za, zb = full_specs(edges_body, sends, [late], name="edges")
    uza, uzb = swap(za, zb, "az")
    uxa, uxb = swap(xa, xb, "ax")

    pick, cells, own = full_specs(
        route_body,
        [((4 * most, ncols), BF16), ((4, 8, radial), F32), ((1, ncols), jnp.int32)],
        [owner.reshape(1, ncols), target_cell.reshape(1, ncols)],
        name="route",
    )
    (inner,) = full_specs(inner_body, [((px, pa, fine), F32)], [noise, half_width], name="filter_inner")
    filtered, to_a, to_b = full_specs(
        first_body,
        [((px, pa, fine), F32), ((px // 2, 8, fine), F32), ((px // 2, 8, fine), F32)],
        [inner, half_width, noise_a, noise_b],
        [((2, HMAX, pa, fine), F32)],
        name="filter_axial",
    )
    got_a, got_b = swap(to_a, to_b, "az")

    tmat = jnp.asarray(azimuth_matrices(ca))
    rmat = jnp.asarray(radial_matrices(float(ca * n_az), radial))
    state = ((5, cx, ca, radial), F32)
    spare = [((2, 5, 3, ca, radial), F32), ((cx, 16, radial), F32)]
    packet = ((most + 8, radial), F32)
    binned, xa, xb, za, zb = full_specs(
        second_body,
        [((ncols, radial), F32), packet, packet, packet, packet],
        [filtered, half_width, got_a, got_b, pick, cells],
        [((px, 32, fine), F32), ((ncols, fine), BF16), ((ncols, fine), BF16)],
        name="filter_rest",
    )
    xa, xb = swap(xa, xb, "ax")
    za, zb = swap(za, zb, "az")
    edge = ((REACH, ca, radial), F32)
    q, qxa, qxb = full_specs(
        gather_body, [((cx, ca, radial), F32), edge, edge], [binned, own, xa, xb, za, zb], name="gather"
    )
    qxa, qxb = swap(qxa, qxb, "ax")
    total = cx + 2 * REACH
    strip = ((total + pl.cdiv(total, 8), 8, radial), F32)
    wide, qza, qzb = full_specs(
        widen_body, [((total, ca, radial), F32), strip, strip], [q, qxa, qxb], name="widen"
    )
    qza, qzb = swap(qza, qzb, "az")

    def stage(factor, level, halos, base, name):
        def body(*refs):
            stage_body(factor, refs)

        args = [level, *halos, tmat, rmat] + ([] if base is None else [base])
        out, xa, xb, za, zb = full_specs(body, [state] + sends, args, spare, name=name)
        return out, (*swap(za, zb, "az"), *swap(xa, xb, "ax"))

    k, halos = stage(1.0, late, (uza, uzb, uxa, uxb), None, "operator")
    level, halos = stage(time_step / 4.0, k, halos, k, "stage")
    level, halos = stage(time_step / 3.0, level, halos, k, "stage")

    span = ca + 16
    extra, extra_side = full_specs(
        source_body,
        [((5, cx + 6, ca, radial), F32), ((cx, 16, radial), F32)],
        [wide, qza, qzb, jnp.asarray(window_matrices(span)), rmat],
        [
            ((total, span, radial), F32),
            ((2, pl.cdiv(total, 8), 8, radial), F32),
            ((4, cx + 12, span, radial), F32),
        ],
        name="source",
    )
    (out,) = full_specs(
        last_body,
        [state],
        [level, *halos, tmat, rmat, k, late, extra, extra_side, q],
        spare + [state, state, pltpu.SemaphoreType.DMA((cx // GROUP,))],
        name="final",
        out_specs=[pl.BlockSpec(memory_space=pl.ANY)],
    )
    return out


def solution(mesh):
    return jax.shard_map(
        local,
        mesh=mesh,
        in_specs=(
            P("ax", "az", None),
            P("ax", "az", None),
            P(("ax", "az")),
            P(("ax", "az")),
            P(None, "ax", "az", None),
        ),
        out_specs=P(None, "ax", "az", None),
        check_vma=False,
    )
```

```python
import math

import numpy as np

import jax
import jax.numpy as jnp
from jax import lax
from jax.experimental import pallas as pl
from jax.experimental.pallas import tpu as pltpu
from jax.sharding import PartitionSpec as P

HMAX = 4
drp_coeffs = (0.770882380518, -0.166705904415, 0.02084314277)
mach_number = 0.5
time_step = 0.7
source_gain = 4.0
radial_step = 2.0
hub_ratio = 1.6

F32 = jnp.float32
BF16 = jnp.bfloat16
VM = pl.BlockSpec(memory_space=pltpu.VMEM)
ANY = pl.BlockSpec(memory_space=pl.ANY)
PARAMS = pltpu.CompilerParams(vmem_limit_bytes=24 * 1024 * 1024)
GROUP = 8


def window_matrices(span):
    one = np.zeros((span, span))
    for s, a in zip((1, 2, 3), drp_coeffs):
        one += a * (np.eye(span, k=s) - np.eye(span, k=-s))
    return np.stack(np_split(np.kron(np.eye(GROUP), one)))


def np_split(matrix):
    hi = matrix.astype(np.float32).astype(BF16)
    lo = (matrix - hi.astype(np.float64)).astype(np.float32).astype(BF16)
    return hi, lo


def filter_table():
    table = np.zeros((HMAX + 1, HMAX))
    for h in range(1, HMAX + 1):
        weights = [math.exp(-2.0 * k * k / (h * h)) if k <= h else 0.0 for k in range(HMAX + 1)]
        total = weights[0] + 2.0 * sum(weights[1:])
        table[:, h - 1] = [w / total for w in weights]
    return table


def radial_rows(na_total, radial):
    base = na_total / (2.0 * math.pi)
    radius = base / hub_ratio + radial_step * (np.arange(radial) + 0.5)
    return base / radius, 1.0 / radius


def radial_matrices(na_total, radial):
    diff = np.zeros((radial, radial))
    for s, a in zip((1, 2, 3), drp_coeffs):
        for j in range(radial):
            if j + s < radial:
                diff[j + s, j] += a / radial_step
            if j - s >= 0:
                diff[j - s, j] -= a / radial_step
    with_r = diff + np.diag(radial_rows(na_total, radial)[1])
    return np.stack([np.stack(np_split(with_r)), np.stack(np_split(diff))])


def azimuth_matrices(cols):
    full = np.zeros((2, GROUP * cols, GROUP * (cols + 16)))
    for which in range(2):
        place = {}
        for m in range(3):
            place[m - 3] = m + 4 * which
            place[cols + m] = 8 + m + 4 * which
        for x in range(GROUP):
            for i in range(cols):
                for s, a in zip((1, 2, 3), drp_coeffs):
                    for j, sign in ((i + s, 1.0), (i - s, -1.0)):
                        at = x * cols + j if 0 <= j < cols else GROUP * cols + x * 16 + place[j]
                        full[which, x * cols + i, at] += sign * a
    return np.stack([np.stack(np_split(full[w])) for w in range(2)])


def split(x):
    hi = x.astype(BF16)
    return hi, (x - hi.astype(F32)).astype(BF16)


def dot(a, b):
    return lax.dot_general(a, b, (((1,), (0,)), ((), ())), preferred_element_type=F32)


def is_even(axis):
    return lax.rem(lax.axis_index(axis), 2) == 0


def swap(to_a, to_b, axis):
    devices = lax.axis_size(axis)
    pairs_a = [(i, i ^ 1) for i in range(devices)]
    pairs_b = [(i, (i - 1) % devices if i % 2 == 0 else (i + 1) % devices) for i in range(devices)]
    return lax.ppermute(to_a, axis, pairs_a), lax.ppermute(to_b, axis, pairs_b)


def full_specs(body, outs, args, scratch=(), name=None, out_specs=None, after=(), cost=0):
    skip = len(args)

    def run(*refs):
        body(*refs[:skip], *refs[skip + len(after) :])

    return pl.pallas_call(
        run,
        out_shape=[jax.ShapeDtypeStruct(s, d) for s, d in outs],
        in_specs=[VM] * skip + [ANY] * len(after),
        out_specs=out_specs or [VM] * len(outs),
        scratch_shapes=[pltpu.VMEM(*s) if isinstance(s, tuple) else s for s in scratch],
        compiler_params=PARAMS,
        name=name,
        cost_estimate=pl.CostEstimate(flops=0, bytes_accessed=cost, transcendentals=0),
    )(*args, *after)


def route_body(owner_ref, target_ref, pick_ref, cells_ref, own_ref):
    n_ax, n_az = lax.axis_size("ax"), lax.axis_size("az")
    ax, az = lax.axis_index("ax"), lax.axis_index("az")
    step_x = jnp.where(lax.rem(ax, 2) == 0, 1, -1)
    step_z = jnp.where(lax.rem(az, 2) == 0, 1, -1)
    me = ax * n_az + az
    b_x = ax - step_x
    ids = [
        (ax + step_x) * n_az + az,
        jnp.where((b_x >= 0) & (b_x < n_ax), b_x * n_az + az, -1),
        ax * n_az + lax.rem(az + step_z + n_az, n_az),
        ax * n_az + lax.rem(az - step_z + n_az, n_az),
    ]
    owner = owner_ref[...]
    target = target_ref[...]
    ncols = owner.shape[1]
    most = ncols // 2
    own_ref[...] = jnp.where(owner == me, target, -1)
    row = lax.broadcasted_iota(jnp.int32, (8, ncols), 0)
    marks = jnp.zeros((8, ncols), F32)
    for d, i in enumerate(ids):
        marks = jnp.where((row == d) & (owner == i), 1.0, marks)
    before = lax.broadcasted_iota(jnp.int32, (ncols, ncols), 0) < lax.broadcasted_iota(jnp.int32, (ncols, ncols), 1)
    rank = dot(marks.astype(BF16), jnp.where(before, 1.0, 0.0).astype(BF16))
    coarse = (target // 32).astype(F32)
    fine = (target % 32).astype(F32)
    digits = jnp.where(row == 0, coarse, jnp.where(row == 1, fine, 0.0)).astype(BF16)
    slot = lax.broadcasted_iota(jnp.int32, (most, ncols), 0).astype(F32)
    for d in range(4):
        wanted = jnp.where(marks[d : d + 1] > 0.0, rank[d : d + 1], -1.0)
        pick = jnp.where(slot == wanted, 1.0, 0.0).astype(BF16)
        pick_ref[d * most : (d + 1) * most, :] = pick
        found = lax.dot_general(digits, pick, (((1,), (1,)), ((), ())), preferred_element_type=F32)
        cells_ref[d, :, :] = jnp.zeros(cells_ref.shape[1:], F32)
        cells_ref[d, 0:1, 0:most] = found[0:1] * 32.0 + found[1:2]


def weights_of(h):
    table = filter_table()
    le = [h <= 1, h <= 2, h <= 3]
    out = []
    for k in range(HMAX + 1):
        value = jnp.full(h.shape, table[k, 3], F32)
        for j in (2, 1, 0):
            if j > 0 and table[k, j] == 0.0 and table[k, j - 1] == 0.0:
                value = jnp.where(le[j], 0.0, value)
                break
            value = jnp.where(le[j], table[k, j], value)
        out.append(value)
    return out


def inner_body(noise_ref, half_ref, first_ref, kept_ref):
    rows = noise_ref.shape[0]
    kept_ref[...] = half_ref[...]
    for x in range(rows):
        w = weights_of(half_ref[x])
        total = w[0] * noise_ref[x]
        for k in range(1, HMAX + 1):
            near = [noise_ref[y] for y in (x - k, x + k) if 0 <= y < rows]
            if near:
                total = total + w[k] * (near[0] + near[1] if len(near) == 2 else near[0])
        first_ref[x] = total


def first_body(inner_ref, half_ref, got_a_ref, got_b_ref, first_ref, to_a_ref, to_b_ref, halo):
    n_ax, ax = lax.axis_size("ax"), lax.axis_index("ax")
    even_x, even_z = is_even("ax"), is_even("az")
    rows = half_ref.shape[0]
    halo[0] = jnp.where(ax > 0, jnp.where(even_x, got_b_ref[...], got_a_ref[...]), 0.0)
    halo[1] = jnp.where(ax < n_ax - 1, jnp.where(even_x, got_a_ref[...], got_b_ref[...]), 0.0)
    for x in range(HMAX, rows - HMAX):
        first_ref[x] = inner_ref[x]
    for i in range(HMAX):
        w = weights_of(half_ref[i])
        total = inner_ref[i]
        for k in range(i + 1, HMAX + 1):
            total = total + w[k] * halo[0, HMAX + i - k]
        first_ref[i] = total
        x = rows - 1 - i
        w = weights_of(half_ref[x])
        total = inner_ref[x]
        for k in range(i + 1, HMAX + 1):
            total = total + w[k] * halo[1, k - i - 1]
        first_ref[x] = total
    half = rows // 2
    low = lax.broadcasted_iota(jnp.int32, (8, half_ref.shape[2]), 0) < 4
    for x in range(half):
        last = jnp.where(low, pltpu.roll(first_ref[x, 8:16], 4, 0), first_ref[x + half, 8:16])
        begin = jnp.where(low, first_ref[x, 0:8], pltpu.roll(first_ref[x + half, 0:8], 4, 0))
        to_a_ref[x] = jnp.where(even_z, last, begin)
        to_b_ref[x] = jnp.where(even_z, begin, last)


def second_body(
    first_ref, half_ref, got_a_ref, got_b_ref, pick_ref, cells_ref,
    own_ref, to_xa, to_xb, to_za, to_zb, wide, fine_hi, fine_lo,
):
    even = is_even("az")
    rows, cols, fine = first_ref.shape
    half = rows // 2
    for x in range(half):
        got_a, got_b = got_a_ref[x], got_b_ref[x]
        before = jnp.where(even, got_b, got_a)
        after = jnp.where(even, got_a, got_b)
        wide[x, 0:8] = pltpu.roll(before, 4, 0)
        wide[x + half, 0:8] = before
        wide[x, 24:32] = after
        wide[x + half, 24:32] = pltpu.roll(after, 4, 0)
    lane = lax.broadcasted_iota(jnp.int32, (cols, fine), 1)
    for x in range(rows):
        wide[x, 8:24] = first_ref[x]
    for x in range(rows):
        w = weights_of(half_ref[x])
        total = w[0] * first_ref[x]
        for k in range(1, HMAX + 1):
            total = total + w[k] * (wide[x, 8 - k : 24 - k] + wide[x, 8 + k : 24 + k])
        result = w[0] * total
        for k in range(1, HMAX + 1):
            up = jnp.where(lane < fine - k, pltpu.roll(total, fine - k, 1), 0.0)
            down = jnp.where(lane >= k, pltpu.roll(total, k, 1), 0.0)
            result = result + w[k] * (up + down)
        hi, lo = split(result)
        fine_hi[x * cols : (x + 1) * cols] = hi
        fine_lo[x * cols : (x + 1) * cols] = lo
    radial = own_ref.shape[1]
    above = lax.broadcasted_iota(jnp.int32, (fine, radial), 0) - lax.broadcasted_iota(
        jnp.int32, (fine, radial), 1
    ) * (fine // radial)
    bins = jnp.where((above >= 0) & (above < fine // radial), source_gain, 0.0).astype(BF16)
    binned = dot(fine_hi[...], bins) + dot(fine_lo[...], bins)
    own_ref[...] = binned
    hi, lo = split(binned)
    most = pick_ref.shape[0] // 4
    for d, out in enumerate((to_xa, to_xb, to_za, to_zb)):
        pick = pick_ref[d * most : (d + 1) * most]
        tile = out.shape[1]
        out[0 : most // tile] = (dot(pick, hi) + dot(pick, lo)).reshape(most // tile, tile, radial)
        out[most // tile] = jnp.concatenate([cells_ref[d]] * (tile // 8), axis=0)


def gather_body(binned_ref, own_ref, xa, xb, za, zb, q_ref, to_xa, to_xb):
    rows, cols, radial = q_ref.shape
    cells = rows * cols
    most = binned_ref.shape[0] // 2
    even = is_even("ax")

    def onehot(row):
        at = lax.broadcasted_iota(jnp.int32, (cells, row.shape[1]), 0)
        return jnp.where(at == row, 1.0, 0.0).astype(BF16)

    mats = [onehot(own_ref[...])]
    packets = [binned_ref[...]]
    for got in (xa, xb, za, zb):
        layers, tile = got.shape[0], got.shape[1]
        mats.append(onehot(got[layers - 1, 0:1, 0:most].astype(jnp.int32)))
        packets.append(got[layers - 1 - most // tile : layers - 1].reshape(most, radial))
    mat = jnp.concatenate(mats, axis=1)
    hi, lo = split(jnp.concatenate(packets, axis=0))
    q_ref[...] = (dot(mat, hi) + dot(mat, lo)).reshape(rows, cols, radial)
    first, last = q_ref[0:REACH], q_ref[rows - REACH :]
    to_xa[...] = jnp.where(even, last, first)
    to_xb[...] = jnp.where(even, first, last)


def join_last(ut, p):
    low = lax.broadcasted_iota(jnp.int32, ut.shape, 0) < 4
    return jnp.where(low, pltpu.roll(ut, 3, 0), pltpu.roll(p, 7, 0))


def join_first(ut, p):
    low = lax.broadcasted_iota(jnp.int32, ut.shape, 0) < 4
    return jnp.where(low, ut, pltpu.roll(p, 4, 0))


def write_x(state, to_xa, to_xb):
    even = is_even("ax")
    fields, rows = state.shape[:2]
    for f in range(fields):
        first, last = state[f, 0:3], state[f, rows - 3 : rows]
        to_xa[3 * f : 3 * f + 3] = jnp.where(even, last, first)
        to_xb[3 * f : 3 * f + 3] = jnp.where(even, first, last)


def write_z(state, to_za, to_zb):
    even = is_even("az")
    for x in range(state.shape[1]):
        last = join_last(state[2, x, 8:16], state[4, x, 8:16])
        first = join_first(state[2, x, 0:8], state[4, x, 0:8])
        to_za[x] = jnp.where(even, last, first)[0 : to_za.shape[1]]
        to_zb[x] = jnp.where(even, first, last)[0 : to_zb.shape[1]]


def fill_side(side, za, zb):
    even = is_even("az")
    rows = side.shape[0]
    a, b = za[0:rows, 0:7], zb[0:rows, 0:7]
    side[:, 0:7] = jnp.where(even, b, a)
    side[:, 8:15] = jnp.where(even, a, b)
    blank = jnp.zeros((rows, 1, side.shape[2]), F32)
    side[:, 7:8] = blank
    side[:, 15:16] = blank


def inverse_step(cols, radial):
    base = cols * lax.axis_size("az") / (2.0 * math.pi)
    at = lax.broadcasted_iota(jnp.int32, (1, radial), 1).astype(F32)
    return base / (base / hub_ratio + radial_step * (at + 0.5))


def outward(rmat, which, hi, lo):
    return dot(hi, rmat[which, 0]) + dot(lo, rmat[which, 0]) + dot(hi, rmat[which, 1])


def along(row, x):
    total = drp_coeffs[0] * (row(x + 1) - row(x - 1))
    for s in (2, 3):
        total = total + drp_coeffs[s - 1] * (row(x + s) - row(x - s))
    return total


def apply_operator(state, row, side, tmat, rmat, finish):
    _, rows, cols, radial = state.shape
    inv_h = inverse_step(cols, radial)
    size = GROUP * cols
    for g in range(rows // GROUP):
        at = slice(g * GROUP, (g + 1) * GROUP)
        halo_hi, halo_lo = split(side[at].reshape(GROUP * 16, radial))
        p_hi, p_lo = split(state[4, at].reshape(size, radial))
        ut_hi, ut_lo = split(state[2, at].reshape(size, radial))
        ur_hi, ur_lo = split(state[3, at].reshape(size, radial))

        def across(which, hi, lo):
            hi = jnp.concatenate([hi, halo_hi], axis=0)
            lo = jnp.concatenate([lo, halo_lo], axis=0)
            return dot(tmat[which, 0], hi) + dot(tmat[which, 0], lo) + dot(tmat[which, 1], hi)

        div_tr = across(0, ut_hi, ut_lo) * inv_h + outward(rmat, 0, ur_hi, ur_lo)
        p_t = across(1, p_hi, p_lo) * inv_h
        p_r = outward(rmat, 1, p_hi, p_lo)
        for i in range(GROUP):
            x = g * GROUP + i
            part = slice(i * cols, (i + 1) * cols)
            d = [along(lambda y: row(f, y), x) for f in range(5)]
            div = d[1] + div_tr[part]
            finish(
                x,
                [
                    -mach_number * d[0] - div,
                    -mach_number * d[1] - d[4],
                    -mach_number * d[2] - p_t[part],
                    -mach_number * d[3] - p_r[part],
                    -mach_number * d[4] - div,
                ],
            )


def fill_halo(halo, xa, xb):
    n_ax, ax = lax.axis_size("ax"), lax.axis_index("ax")
    even = is_even("ax")
    for f in range(halo.shape[1]):
        a, b = xa[3 * f : 3 * f + 3], xb[3 * f : 3 * f + 3]
        halo[0, f] = jnp.where(ax > 0, jnp.where(even, b, a), 0.0)
        halo[1, f] = jnp.where(ax < n_ax - 1, jnp.where(even, a, b), 0.0)


def with_halos(state, halo):
    rows = state.shape[1]

    def row(f, x):
        if x < 0:
            return halo[0, f, x + 3]
        if x >= rows:
            return halo[1, f, x - rows]
        return state[f, x]

    return row


def start_body(state, za, zb, xa, xb, tmat, rmat, px_a, px_b, pz_a, pz_b, out, to_xa, to_xb, to_za, to_zb, halo, side):
    fill_halo(halo, xa, xb)
    fill_side(side, za, zb)

    def finish(x, tend):
        for f in range(5):
            out[f, x] = tend[f]

    apply_operator(state, with_halos(state, halo), side, tmat, rmat, finish)
    write_x(out, to_xa, to_xb)
    write_z(out, to_za, to_zb)
    for ref in (to_xa, to_xb):
        ref[15] = jnp.zeros(ref.shape[1:], F32)
    for packet, out_ref in ((px_a, to_xa), (px_b, to_xb), (pz_a, to_za), (pz_b, to_zb)):
        out_ref[out_ref.shape[0] - packet.shape[0] :] = packet[...]


def stage_body(factor, state, za, zb, xa, xb, tmat, rmat, base, out, to_xa, to_xb, to_za, to_zb, halo, side):
    fill_halo(halo, xa, xb)
    fill_side(side, za, zb)

    def finish(x, tend):
        for f in range(5):
            out[f, x] = base[f, x] + factor * tend[f]

    apply_operator(state, with_halos(state, halo), side, tmat, rmat, finish)
    write_x(out, to_xa, to_xb)
    write_z(out, to_za, to_zb)


def last_body(
    state, za, zb, xa, xb, tmat, rmat, k, fields, extra, extra_side, q, out, halo, side, both, result, sems
):
    _, rows, cols, radial = state.shape
    fill_halo(halo, xa, xb)
    fill_side(side, za, zb)
    side[...] = side[...] + extra_side[...]
    for f in range(5):
        halo[0, f] = halo[0, f] + extra[f, 0:3]
        halo[1, f] = halo[1, f] + extra[f, rows + 3 : rows + 6]
        for x in range(rows):
            both[f, x] = state[f, x] + extra[f, x + 3]

    def finish(x, tend):
        for f in range(5):
            slope = k[f, x] + q[x] if f == 4 else k[f, x]
            result[f, x] = fields[f, x] + time_step * slope + (0.5 * time_step * time_step) * tend[f]
        if x % GROUP == GROUP - 1:
            copy(x // GROUP).start()

    def copy(g):
        at = pl.ds(g * GROUP, GROUP)
        return pltpu.make_async_copy(result.at[:, at], out.at[:, at], sems.at[g])

    apply_operator(both, with_halos(both, halo), side, tmat, rmat, finish)
    for g in range(rows // GROUP):
        copy(g).wait()


COST = 1 << 27
REACH = 9


def widen_body(q, xa, xb, wide, to_za, to_zb):
    n_ax, ax = lax.axis_size("ax"), lax.axis_index("ax")
    even_x, even_z = is_even("ax"), is_even("az")
    rows, _, radial = q.shape
    wide[0:REACH] = jnp.where(ax > 0, jnp.where(even_x, xb[...], xa[...]), 0.0)
    wide[REACH : REACH + rows] = q[...]
    wide[REACH + rows :] = jnp.where(ax < n_ax - 1, jnp.where(even_x, xa[...], xb[...]), 0.0)
    total = rows + 2 * REACH
    place = lax.broadcasted_iota(jnp.int32, (8, radial), 0)
    for start in range(0, total, 8):
        last, first = jnp.zeros((8, radial), F32), jnp.zeros((8, radial), F32)
        for x in range(start, min(start + 8, total)):
            low, high = wide[x, 0:8], wide[x, 8:16]
            to_za[x] = jnp.where(even_z, high, low)
            to_zb[x] = jnp.where(even_z, low, high)
            at = x - start
            last = jnp.where(place == at, pltpu.roll(low, (at + 1) % 8, 0), last)
            first = jnp.where(place == at, pltpu.roll(high, at, 0) if at else high, first)
        to_za[total + start // 8] = jnp.where(even_z, last, first)
        to_zb[total + start // 8] = jnp.where(even_z, first, last)


def source_body(wide, za, zb, tmat, rmat, out, out_side, full, far, w3):
    n_ax, ax = lax.axis_size("ax"), lax.axis_index("ax")
    even = is_even("az")
    total, cols, radial = wide.shape
    rows = total - 2 * REACH

    def inside(value, x):
        if x < 0:
            return jnp.where(ax > 0, value, 0.0)
        if x >= rows:
            return jnp.where(ax < n_ax - 1, value, 0.0)
        return value

    before, after = 8, 8 + cols
    full[:, 0:8] = jnp.where(even, zb[0:total], za[0:total])
    full[:, 8:after] = wide[...]
    full[:, after : after + 8] = jnp.where(even, za[0:total], zb[0:total])
    far[0] = jnp.where(even, zb[total:], za[total:])
    far[1] = jnp.where(even, za[total:], zb[total:])
    inv_h = inverse_step(cols, radial)
    span = cols + 16
    size = GROUP * span
    place = lax.broadcasted_iota(jnp.int32, (8, radial), 0)
    edge = drp_coeffs[2]

    def across(hi, lo):
        return dot(tmat[0], hi) + dot(tmat[0], lo) + dot(tmat[1], hi)

    def groups(start, count):
        done = start
        while done < start + count:
            at = min(done, start + count - GROUP)
            yield at, range(done, at + GROUP)
            done = at + GROUP

    c = time_step / 4.0
    for at, todo in groups(3, rows + 12):
        hi, lo = split(full[at : at + GROUP].reshape(size, radial))
        q_t = across(hi, lo)
        q_r = outward(rmat, 1, hi, lo)
        for x in todo:
            part = slice((x - at) * span, (x - at + 1) * span)
            d = along(lambda y: full[y], x)
            w3[0, x - 3] = inside(-c * d, x - REACH)
            turn = q_t[part]
            low = jnp.where(place == 2, -edge * far[0, x // 8, x % 8 : x % 8 + 1], 0.0)
            high = jnp.where(place == 5, edge * far[1, x // 8, x % 8 : x % 8 + 1], 0.0)
            turn = jnp.concatenate([turn[0:8] + low, turn[8:after], turn[after:span] + high], axis=0)
            w3[1, x - 3] = inside((-c) * inv_h * turn, x - REACH)
            w3[2, x - 3] = inside(-c * q_r[part], x - REACH)
            w3[3, x - 3] = inside(full[x] - (c * mach_number) * d, x - REACH)

    c = time_step / 3.0
    for at, todo in groups(3, rows + 6):
        ut_hi, ut_lo = split(w3[1, at : at + GROUP].reshape(size, radial))
        ur_hi, ur_lo = split(w3[2, at : at + GROUP].reshape(size, radial))
        p_hi, p_lo = split(w3[3, at : at + GROUP].reshape(size, radial))
        div_tr = across(ut_hi, ut_lo) * inv_h + outward(rmat, 0, ur_hi, ur_lo)
        p_t = across(p_hi, p_lo) * inv_h
        p_r = outward(rmat, 1, p_hi, p_lo)
        for x in todo:
            o = x - 3
            begin = (x - at) * span
            part = slice(begin + 8, begin + 8 + cols)
            d = [along(lambda y: w3[f, y, 8:after], x) for f in range(4)]
            div = d[0] + div_tr[part]
            out[0, o] = inside(-c * div, o - 3)
            out[1, o] = inside(-c * (mach_number * d[0] + d[3]), o - 3)
            out[2, o] = inside(-c * (mach_number * d[1] + p_t[part]), o - 3)
            out[3, o] = inside(-c * (mach_number * d[2] + p_r[part]), o - 3)
            out[4, o] = inside(full[x + 3, 8:after] - c * (mach_number * d[3] + div), o - 3)
            if 3 <= o < 3 + rows:
                tiles = []
                for lanes in (slice(0, 8), slice(after, after + 8)):
                    part = slice(begin + lanes.start, begin + lanes.stop)
                    d0, d1, d3 = [along(lambda y: w3[f, y, lanes], x) for f in (0, 1, 3)]
                    ut = -c * (mach_number * d1 + p_t[part])
                    p = full[x + 3, lanes] - c * (mach_number * d3 + d0 + div_tr[part])
                    tiles.append((ut, p))
                out_side[o - 3, 0:8] = jnp.where(place == 7, 0.0, join_last(*tiles[0]))
                out_side[o - 3, 8:16] = jnp.where(place == 7, 0.0, join_first(*tiles[1]))


def local(noise, half_width, owner, target_cell, fields):
    px, pa, fine = noise.shape
    cx, ca, radial = fields.shape[1:]
    ncols = px * pa
    most = ncols // 2
    n_az = lax.axis_size("az")
    block = ((px, pa, fine), F32)
    even = is_even("ax")
    to_a = jnp.where(even, noise[px - HMAX :], noise[:HMAX])
    to_b = jnp.where(even, noise[:HMAX], noise[px - HMAX :])
    noise_a, noise_b = swap(to_a, to_b, "ax")
    send_x, send_z = ((15, ca, radial), F32), ((cx, 7, radial), F32)
    to_xa, to_xb = full_specs(write_x, [send_x, send_x], [fields], name="edges", after=[to_a])
    uxa, uxb = swap(to_xa, to_xb, "ax")
    inner, half_width = full_specs(
        inner_body, [block, ((px, pa, fine), jnp.int32)], [noise, half_width], name="filter_inner", after=[to_xa]
    )
    filtered, to_a, to_b = full_specs(
        first_body,
        [((px, pa, fine), F32), ((px // 2, 8, fine), F32), ((px // 2, 8, fine), F32)],
        [inner, half_width, noise_a, noise_b],
        [((2, HMAX, pa, fine), F32)],
        name="filter_axial",
    )
    got_a, got_b = swap(to_a, to_b, "az")
    uza, uzb = full_specs(write_z, [send_z, send_z], [fields], name="late_edges", after=[filtered])
    pick, cells, own = full_specs(
        route_body,
        [((4 * most, ncols), BF16), ((4, 8, radial), F32), ((1, ncols), jnp.int32)],
        [owner.reshape(1, ncols), target_cell.reshape(1, ncols)],
        name="route",
        after=[uzb],
    )
    uza, uzb = swap(uza, uzb, "az")
    tmat = jnp.asarray(azimuth_matrices(ca))
    rmat = jnp.asarray(radial_matrices(float(ca * n_az), radial))
    state = ((5, cx, ca, radial), F32)
    spare = [((2, 5, 3, ca, radial), F32), ((cx, 16, radial), F32)]

    packet_x = ((most // ca + 1, ca, radial), F32)
    packet_z = ((most // 8 + 1, 8, radial), F32)
    binned, *packets = full_specs(
        second_body,
        [((ncols, radial), F32), packet_x, packet_x, packet_z, packet_z],
        [filtered, half_width, got_a, got_b, pick, cells],
        [((px, 32, fine), F32), ((ncols, fine), BF16), ((ncols, fine), BF16)],
        name="filter_rest",
    )
    long_x = ((16 + packet_x[0][0], ca, radial), F32)
    long_z = ((cx + packet_z[0][0], 8, radial), F32)
    k, xa, xb, za, zb = full_specs(
        start_body,
        [state, long_x, long_x, long_z, long_z],
        [fields, uza, uzb, uxa, uxb, tmat, rmat, *packets],
        spare,
        name="operator",
    )
    xa, xb = swap(xa, xb, "ax")
    za, zb = swap(za, zb, "az")
    edge = ((REACH, ca, radial), F32)
    q, qxa, qxb = full_specs(
        gather_body,
        [((cx, ca, radial), F32), edge, edge],
        [binned, own, xa, xb, za, zb],
        name="gather",
    )

    def stage(factor, level, halos, name, after, cost=0):
        def body(*refs):
            stage_body(factor, *refs)

        return full_specs(
            body,
            [state, send_x, send_x, send_z, send_z],
            [level, *halos, tmat, rmat, k],
            spare,
            name=name,
            after=after,
            cost=cost,
        )

    level, xa, xb, za, zb = stage(time_step / 4.0, k, (za, zb, xa, xb), "stage_3", [qxa])
    qxa, qxb = swap(qxa, qxb, "ax")
    total = cx + 2 * REACH
    count = total + pl.cdiv(total, 8)
    xa, xb = swap(xa, xb, "ax")
    wide, qza, qzb = full_specs(
        widen_body,
        [((total, ca, radial), F32), ((count, 8, radial), F32), ((count, 8, radial), F32)],
        [q, qxa, qxb],
        name="widen",
    )
    za, zb = swap(za, zb, "az")
    qza_sent = qza
    qza, qzb = swap(qza, qzb, "az")
    level, xa, xb, za, zb = stage(time_step / 3.0, level, (za, zb, xa, xb), "stage_2", [qza_sent], COST)
    halos = (*swap(za, zb, "az"), *swap(xa, xb, "ax"))

    span = ca + 16
    extra, extra_side = full_specs(
        source_body,
        [((5, cx + 6, ca, radial), F32), ((cx, 16, radial), F32)],
        [wide, qza, qzb, jnp.asarray(window_matrices(span)), rmat],
        [
            ((total, span, radial), F32),
            ((2, pl.cdiv(total, 8), 8, radial), F32),
            ((4, cx + 12, span, radial), F32),
        ],
        name="source",
        after=[level],
    )
    (out,) = full_specs(
        last_body,
        [state],
        [level, *halos, tmat, rmat, k, fields, extra, extra_side, q],
        spare + [state, state, pltpu.SemaphoreType.DMA((cx // GROUP,))],
        name="final",
        out_specs=[ANY],
    )
    return out


def solution(mesh):
    return jax.shard_map(
        local,
        mesh=mesh,
        in_specs=(
            P("ax", "az", None),
            P("ax", "az", None),
            P(("ax", "az")),
            P(("ax", "az")),
            P(None, "ax", "az", None),
        ),
        out_specs=P(None, "ax", "az", None),
        check_vma=False,
    )
```

```python
import math

import numpy as np

import jax
import jax.numpy as jnp
from jax import lax
from jax.experimental import pallas as pl
from jax.experimental.pallas import tpu as pltpu
from jax.sharding import PartitionSpec as P

HMAX = 4
drp_coeffs = (0.770882380518, -0.166705904415, 0.02084314277)
mach_number = 0.5
time_step = 0.7
source_gain = 4.0
radial_step = 2.0
hub_ratio = 1.6

F32 = jnp.float32
BF16 = jnp.bfloat16
VM = pl.BlockSpec(memory_space=pltpu.VMEM)
ANY = pl.BlockSpec(memory_space=pl.ANY)
PARAMS = pltpu.CompilerParams(vmem_limit_bytes=24 * 1024 * 1024)
GROUP = 8
RIM = 4
COST = 1 << 27


def np_split(matrix):
    hi = matrix.astype(np.float32).astype(BF16)
    lo = (matrix - hi.astype(np.float64)).astype(np.float32).astype(BF16)
    return hi, lo


def filter_table():
    table = np.zeros((HMAX + 1, HMAX))
    for h in range(1, HMAX + 1):
        weights = [math.exp(-2.0 * k * k / (h * h)) if k <= h else 0.0 for k in range(HMAX + 1)]
        total = weights[0] + 2.0 * sum(weights[1:])
        table[:, h - 1] = [w / total for w in weights]
    return table


def radial_rows(na_total, radial):
    base = na_total / (2.0 * math.pi)
    radius = base / hub_ratio + radial_step * (np.arange(radial) + 0.5)
    return base / radius, 1.0 / radius


def radial_matrices(na_total, radial):
    diff = np.zeros((radial, radial))
    for s, a in zip((1, 2, 3), drp_coeffs):
        for j in range(radial):
            if j + s < radial:
                diff[j + s, j] += a / radial_step
            if j - s >= 0:
                diff[j - s, j] -= a / radial_step
    with_r = diff + np.diag(radial_rows(na_total, radial)[1])
    return np.stack([np.stack(np_split(with_r)), np.stack(np_split(diff))])


def azimuth_matrices(cols):
    packed = GROUP * 6
    full = np.zeros((2, GROUP * cols, GROUP * cols + 2 * packed))
    for which in range(2):
        for x in range(GROUP):
            for i in range(cols):
                for s, a in zip((1, 2, 3), drp_coeffs):
                    for j, sign in ((i + s, 1.0), (i - s, -1.0)):
                        if 0 <= j < cols:
                            at = x * cols + j
                        else:
                            m = j + 3 if j < 0 else j - cols
                            tile, row = (x % 4, m) if x % 4 < 3 else (m, 3)
                            at = GROUP * cols + (x // 4 * 3 + tile) * 8 + row + 4 * which
                            at += packed if j >= cols else 0
                        full[which, x * cols + i, at] += sign * a
    return np.stack([np.stack(np_split(full[w])) for w in range(2)])


def split(x):
    hi = x.astype(BF16)
    return hi, (x - hi.astype(F32)).astype(BF16)


def dot(a, b):
    return lax.dot_general(a, b, (((1,), (0,)), ((), ())), preferred_element_type=F32)


def is_even(axis):
    return lax.rem(lax.axis_index(axis), 2) == 0


def swap(to_a, to_b, axis):
    devices = lax.axis_size(axis)
    pairs_a = [(i, i ^ 1) for i in range(devices)]
    pairs_b = [(i, (i - 1) % devices if i % 2 == 0 else (i + 1) % devices) for i in range(devices)]
    return lax.ppermute(to_a, axis, pairs_a), lax.ppermute(to_b, axis, pairs_b)


def swap_b(value, axis):
    devices = lax.axis_size(axis)
    pairs = [(i, (i - 1) % devices if i % 2 == 0 else (i + 1) % devices) for i in range(devices)]
    return (lax.ppermute(value, axis, pairs),)


def full_specs(body, outs, args, scratch=(), name=None, in_specs=None, out_specs=None, after=(), cost=0, alias=None):
    skip = len(args)

    def run(*refs):
        body(*refs[:skip], *refs[skip + len(after) :])

    return pl.pallas_call(
        run,
        out_shape=[jax.ShapeDtypeStruct(s, d) for s, d in outs],
        in_specs=(in_specs or [VM] * skip) + [ANY] * len(after),
        input_output_aliases=alias or {},
        out_specs=out_specs or [VM] * len(outs),
        scratch_shapes=[pltpu.VMEM(*s) if isinstance(s, tuple) else s for s in scratch],
        compiler_params=PARAMS,
        name=name,
        cost_estimate=pl.CostEstimate(flops=0, bytes_accessed=cost, transcendentals=0),
    )(*args, *after)


def route_body(owner_ref, target_ref, pick_ref, cells_ref, own_ref):
    n_ax, n_az = lax.axis_size("ax"), lax.axis_size("az")
    ax, az = lax.axis_index("ax"), lax.axis_index("az")
    step_x = jnp.where(lax.rem(ax, 2) == 0, 1, -1)
    step_z = jnp.where(lax.rem(az, 2) == 0, 1, -1)
    me = ax * n_az + az
    b_x = ax - step_x
    ids = [
        (ax + step_x) * n_az + az,
        jnp.where((b_x >= 0) & (b_x < n_ax), b_x * n_az + az, -1),
        ax * n_az + lax.rem(az + step_z + n_az, n_az),
        ax * n_az + lax.rem(az - step_z + n_az, n_az),
    ]
    owner = owner_ref[...]
    target = target_ref[...]
    ncols = owner.shape[1]
    most = ncols // 2
    own_ref[...] = jnp.where(owner == me, target, -1)
    row = lax.broadcasted_iota(jnp.int32, (8, ncols), 0)
    marks = jnp.zeros((8, ncols), F32)
    for d, i in enumerate(ids):
        marks = jnp.where((row == d) & (owner == i), 1.0, marks)
    before = lax.broadcasted_iota(jnp.int32, (ncols, ncols), 0) < lax.broadcasted_iota(jnp.int32, (ncols, ncols), 1)
    rank = dot(marks.astype(BF16), jnp.where(before, 1.0, 0.0).astype(BF16))
    coarse = (target // 32).astype(F32)
    fine = (target % 32).astype(F32)
    digits = jnp.where(row == 0, coarse, jnp.where(row == 1, fine, 0.0)).astype(BF16)
    slot = lax.broadcasted_iota(jnp.int32, (most, ncols), 0).astype(F32)
    for d in range(4):
        wanted = jnp.where(marks[d : d + 1] > 0.0, rank[d : d + 1], -1.0)
        pick = jnp.where(slot == wanted, 1.0, 0.0).astype(BF16)
        pick_ref[d * most : (d + 1) * most, :] = pick
        found = lax.dot_general(digits, pick, (((1,), (1,)), ((), ())), preferred_element_type=F32)
        cells_ref[d, :, :] = jnp.zeros(cells_ref.shape[1:], F32)
        cells_ref[d, 0:1, 0:most] = found[0:1] * 32.0 + found[1:2]


def weights_of(h):
    table = filter_table()
    le = [h <= 1, h <= 2, h <= 3]
    out = []
    for k in range(HMAX + 1):
        value = jnp.full(h.shape, table[k, 3], F32)
        for j in (2, 1, 0):
            if j > 0 and table[k, j] == 0.0 and table[k, j - 1] == 0.0:
                value = jnp.where(le[j], 0.0, value)
                break
            value = jnp.where(le[j], table[k, j], value)
        out.append(value)
    return out


def inner_body(noise_ref, half_ref, first_ref, kept_ref):
    rows = noise_ref.shape[0]
    kept_ref[...] = half_ref[...]
    for x in range(rows):
        w = weights_of(half_ref[x])
        total = w[0] * noise_ref[x]
        for k in range(1, HMAX + 1):
            near = [noise_ref[y] for y in (x - k, x + k) if 0 <= y < rows]
            if near:
                total = total + w[k] * (near[0] + near[1] if len(near) == 2 else near[0])
        first_ref[x] = total


def first_body(inner_ref, half_ref, got_a_ref, got_b_ref, edge_a_ref, first_ref, to_a_ref, to_b_ref, halo):
    n_ax, ax = lax.axis_size("ax"), lax.axis_index("ax")
    even_x, even_z = is_even("ax"), is_even("az")
    rows, _, fine = half_ref.shape
    halo[0] = jnp.where(ax > 0, jnp.where(even_x, got_b_ref[...], got_a_ref[...]), 0.0)
    halo[1] = jnp.where(ax < n_ax - 1, jnp.where(even_x, got_a_ref[...], got_b_ref[...]), 0.0)
    for x in range(HMAX, rows - HMAX):
        first_ref[x] = inner_ref[x]
    for i in range(HMAX):
        w = weights_of(half_ref[i])
        total = inner_ref[i]
        for k in range(i + 1, HMAX + 1):
            total = total + w[k] * halo[0, HMAX + i - k]
        first_ref[i] = total
        x = rows - 1 - i
        w = weights_of(half_ref[x])
        total = inner_ref[x]
        for k in range(i + 1, HMAX + 1):
            total = total + w[k] * halo[1, k - i - 1]
        first_ref[x] = total
    half = rows // 2
    low = lax.broadcasted_iota(jnp.int32, (8, fine), 0) < 4
    for x in range(half):
        last = jnp.where(low, pltpu.roll(first_ref[x, 8:16], 4, 0), first_ref[x + half, 8:16])
        begin = jnp.where(low, first_ref[x, 0:8], pltpu.roll(first_ref[x + half, 0:8], 4, 0))
        to_a = jnp.where(even_z, last, begin)
        to_a_ref[x] = to_a[:, : fine // 2]
        to_a_ref[half + x] = to_a[:, fine // 2 :]
        to_b_ref[x] = jnp.where(even_z, begin, last)
    to_a_ref[2 * half :] = edge_a_ref[...]


def second_body(
    first_ref, half_ref, got_a_ref, got_b_ref, pick_ref, cells_ref,
    own_ref, to_xa, to_xb, to_za, to_zb, wide, fine_hi, fine_lo,
):
    even = is_even("az")
    rows, cols, fine = first_ref.shape
    half = rows // 2
    for x in range(half):
        got_a, got_b = jnp.concatenate([got_a_ref[x], got_a_ref[half + x]], axis=1), got_b_ref[x]
        before = jnp.where(even, got_b, got_a)
        after = jnp.where(even, got_a, got_b)
        wide[x, 0:8] = pltpu.roll(before, 4, 0)
        wide[x + half, 0:8] = before
        wide[x, 24:32] = after
        wide[x + half, 24:32] = pltpu.roll(after, 4, 0)
    lane = lax.broadcasted_iota(jnp.int32, (cols, fine), 1)
    for x in range(rows):
        wide[x, 8:24] = first_ref[x]
    for x in range(rows):
        w = weights_of(half_ref[x])
        total = w[0] * first_ref[x]
        for k in range(1, HMAX + 1):
            total = total + w[k] * (wide[x, 8 - k : 24 - k] + wide[x, 8 + k : 24 + k])
        result = w[0] * total
        for k in range(1, HMAX + 1):
            up = jnp.where(lane < fine - k, pltpu.roll(total, fine - k, 1), 0.0)
            down = jnp.where(lane >= k, pltpu.roll(total, k, 1), 0.0)
            result = result + w[k] * (up + down)
        hi, lo = split(result)
        fine_hi[x * cols : (x + 1) * cols] = hi
        fine_lo[x * cols : (x + 1) * cols] = lo
    radial = own_ref.shape[1]
    above = lax.broadcasted_iota(jnp.int32, (fine, radial), 0) - lax.broadcasted_iota(
        jnp.int32, (fine, radial), 1
    ) * (fine // radial)
    bins = jnp.where((above >= 0) & (above < fine // radial), source_gain, 0.0).astype(BF16)
    binned = dot(fine_hi[...], bins) + dot(fine_lo[...], bins)
    own_ref[...] = binned
    hi, lo = split(binned)
    most = pick_ref.shape[0] // 4
    for d, out in enumerate((to_xa, to_xb, to_za, to_zb)):
        pick = pick_ref[d * most : (d + 1) * most]
        out[0:most] = dot(pick, hi) + dot(pick, lo)
        out[most : most + 8] = cells_ref[d]


def gather_body(
    binned_ref, own_ref, xa, xb, za, zb, k_mid, k_rim, p_mid, p_rim, to_xa, to_xb, to_za, to_zb
):
    mid, cols, radial = p_mid.shape
    cells = (mid + 2 * RIM) * cols
    most = xa.shape[0] - 8

    def onehot(row):
        at = lax.broadcasted_iota(jnp.int32, (cells, row.shape[1]), 0)
        return jnp.where(at == row, 1.0, 0.0).astype(BF16)

    mats = [onehot(own_ref[...])]
    packets = [binned_ref[...]]
    for got in (xa, xb, za, zb):
        mats.append(onehot(got[most : most + 1, 0:most].astype(jnp.int32)))
        packets.append(got[0:most])
    mat = jnp.concatenate(mats, axis=1)
    hi, lo = split(jnp.concatenate(packets, axis=0))
    q = (dot(mat, hi) + dot(mat, lo)).reshape(mid + 2 * RIM, cols, radial)
    p_rim[0:RIM] = k_rim[4, 0:RIM] + q[0:RIM]
    p_mid[...] = k_mid[4] + q[RIM : RIM + mid]
    p_rim[RIM:] = k_rim[4, RIM:] + q[RIM + mid :]
    level = Parts(k_mid, k_rim, p_mid, p_rim)
    write_x(level, to_xa, to_xb)
    write_z(level, to_za, to_zb)


class Whole:
    def __init__(self, ref):
        self.ref = ref
        self.rows = ref.shape[1]

    def row(self, f, x):
        return self.ref[f, x]

    def group(self, f, g):
        if g is None:
            return jnp.concatenate([self.ref[f, 0:RIM], self.ref[f, self.rows - RIM :]], axis=0)
        return self.ref[f, RIM + g * GROUP : RIM + (g + 1) * GROUP]


class Parts:
    def __init__(self, mid, rim, p_mid=None, p_rim=None):
        self.arrays = (mid, rim, p_mid, p_rim)
        self.rows = mid.shape[1] + 2 * RIM

    def pick(self, f):
        mid, rim, p_mid, p_rim = self.arrays
        if f == 4 and p_mid is not None:
            return p_mid, p_rim
        return mid.at[f], rim.at[f]

    def row(self, f, x):
        mid, rim = self.pick(f)
        if RIM <= x < self.rows - RIM:
            return mid[x - RIM]
        return rim[x if x < RIM else x - self.rows + 2 * RIM]

    def group(self, f, g):
        mid, rim = self.pick(f)
        return rim[...] if g is None else mid[g * GROUP : (g + 1) * GROUP]

    def store(self, f, x, value):
        mid, rim = self.pick(f)
        if RIM <= x < self.rows - RIM:
            mid[x - RIM] = value
        else:
            rim[x if x < RIM else x - self.rows + 2 * RIM] = value


def join_last(ut, p):
    low = lax.broadcasted_iota(jnp.int32, ut.shape, 0) < 4
    return jnp.where(low, pltpu.roll(ut, 3, 0), pltpu.roll(p, 7, 0))


def join_first(ut, p):
    low = lax.broadcasted_iota(jnp.int32, ut.shape, 0) < 4
    return jnp.where(low, ut, pltpu.roll(p, 4, 0))


def write_x(level, to_xa, to_xb):
    even = is_even("ax")
    for f in range(5):
        for i in range(3):
            first, last = level.row(f, i), level.row(f, level.rows - 3 + i)
            to_xa[3 * f + i] = jnp.where(even, last, first)
            to_xb[3 * f + i] = jnp.where(even, first, last)


def write_z(level, to_za, to_zb):
    even = is_even("az")
    row = None
    for x in range(0, level.rows, 4):
        first, last = [], []
        for y in range(x, x + 4):
            ut, p = level.row(2, y), level.row(4, y)
            first.append(join_first(ut[0:8], p[0:8]))
            last.append(join_last(ut[8:16], p[8:16]))
        if row is None:
            row = lax.broadcasted_iota(jnp.int32, first[0].shape, 0) % 4 == 3
        for t in range(3):
            shift = 3 - t
            one = jnp.where(row, pltpu.roll(first[3], shift, 0), first[t])
            two = jnp.where(row, pltpu.roll(last[3], shift, 0), last[t])
            to_za[x // 4 * 3 + t] = jnp.where(even, two, one)
            to_zb[x // 4 * 3 + t] = jnp.where(even, one, two)


def edges_body(state, to_xa, to_xb, to_za, to_zb):
    level = Whole(state)
    write_x(level, to_xa, to_xb)
    write_z(level, to_za, to_zb)


def fill_halo(halo, xa, xb):
    n_ax, ax = lax.axis_size("ax"), lax.axis_index("ax")
    even = is_even("ax")
    for f in range(halo.shape[1]):
        a, b = xa[3 * f : 3 * f + 3], xb[3 * f : 3 * f + 3]
        halo[0, f] = jnp.where(ax > 0, jnp.where(even, b, a), 0.0)
        halo[1, f] = jnp.where(ax < n_ax - 1, jnp.where(even, a, b), 0.0)


def inverse_step(cols, radial):
    base = cols * lax.axis_size("az") / (2.0 * math.pi)
    at = lax.broadcasted_iota(jnp.int32, (1, radial), 1).astype(F32)
    return base / (base / hub_ratio + radial_step * (at + 0.5))


def along(row, x):
    total = drp_coeffs[0] * (row(x + 1) - row(x - 1))
    for s in (2, 3):
        total = total + drp_coeffs[s - 1] * (row(x + s) - row(x - s))
    return total


def apply_operator(level, groups, za, zb, tmat, rmat, finish, halo=None):
    even = is_even("az")
    tiles = level.rows // 4 * 3
    rim = RIM // 4 * 3

    def row(f, x):
        if x < 0:
            return halo[0, f, x + 3]
        if x >= level.rows:
            return halo[1, f, x - level.rows]
        return level.row(f, x)

    def beside(g):
        spans = [(0, rim), (tiles - rim, tiles)] if g is None else [(rim + 6 * g, rim + 6 * g + 6)]
        start = za.shape[0] - tiles
        sides = []
        for swap_ab in (False, True):
            for a, b in spans:
                got_a, got_b = za[start + a : start + b], zb[a:b]
                pair = (got_a, got_b) if swap_ab else (got_b, got_a)
                sides.append(jnp.where(even, *pair).reshape((b - a) * 8, za.shape[2]))
        return split(jnp.concatenate(sides, axis=0))

    for g in groups:
        if g is None:
            xs = [*range(RIM), *range(level.rows - RIM, level.rows)]
        else:
            xs = range(RIM + g * GROUP, RIM + (g + 1) * GROUP)
        ut, ur, p = [level.group(f, g) for f in (2, 3, 4)]
        _, cols, radial = ut.shape
        inv_h = inverse_step(cols, radial)
        side_hi, side_lo = beside(g)
        p_hi, p_lo = split(p.reshape(GROUP * cols, radial))
        ut_hi, ut_lo = split(ut.reshape(GROUP * cols, radial))
        ur_hi, ur_lo = split(ur.reshape(GROUP * cols, radial))

        def across(which, hi, lo):
            hi = jnp.concatenate([hi, side_hi], axis=0)
            lo = jnp.concatenate([lo, side_lo], axis=0)
            return dot(tmat[which, 0], hi) + dot(tmat[which, 0], lo) + dot(tmat[which, 1], hi)

        def outward(which, hi, lo):
            return dot(hi, rmat[which, 0]) + dot(lo, rmat[which, 0]) + dot(hi, rmat[which, 1])

        div_tr = across(0, ut_hi, ut_lo) * inv_h + outward(0, ur_hi, ur_lo)
        p_t = across(1, p_hi, p_lo) * inv_h
        p_r = outward(1, p_hi, p_lo)
        for i, x in enumerate(xs):
            part = slice(i * cols, (i + 1) * cols)
            d = [along(lambda y: row(f, y), x) for f in range(5)]
            div = d[1] + div_tr[part]
            finish(
                x,
                [
                    -mach_number * d[0] - div,
                    -mach_number * d[1] - d[4],
                    -mach_number * d[2] - p_t[part],
                    -mach_number * d[3] - p_r[part],
                    -mach_number * d[4] - div,
                ],
            )


def start_body(state, za, zb, xa, xb, tmat, rmat, k_mid, k_rim, halo):
    fill_halo(halo, xa, xb)
    level, out = Whole(state), Parts(k_mid, k_rim)

    def finish(x, tend):
        for f in range(5):
            out.store(f, x, tend[f])

    apply_operator(level, [*range(k_mid.shape[1] // GROUP), None], za, zb, tmat, rmat, finish, halo)


def inner_stage_body(factor, level, base, za, zb, tmat, rmat, out_mid):
    def finish(x, tend):
        for f in range(5):
            out_mid[f, x - RIM] = base.row(f, x) + factor * tend[f]

    apply_operator(level, range(out_mid.shape[1] // GROUP), za, zb, tmat, rmat, finish)


def rim_stage_body(factor, level, base, za, zb, xa, xb, tmat, rmat, out_mid, out_rim, to_xa, to_xb, to_za, to_zb, halo):
    fill_halo(halo, xa, xb)
    out = Parts(out_mid, out_rim)

    def finish(x, tend):
        for f in range(5):
            out.store(f, x, base.row(f, x) + factor * tend[f])

    apply_operator(level, [None], za, zb, tmat, rmat, finish, halo)
    write_x(out, to_xa, to_xb)
    write_z(out, to_za, to_zb)


def last_finish(fields, k, store):
    def finish(x, tend):
        for f in range(5):
            store(f, x, fields[f, x] + time_step * k.row(f, x) + (0.5 * time_step * time_step) * tend[f])

    return finish


def inner_last_body(level, k, fields, za, zb, tmat, rmat, out, result, sems):
    def store(f, x, value):
        result[f, x - RIM] = value

    def copy(g):
        at = g * GROUP
        return pltpu.make_async_copy(
            result.at[:, at : at + GROUP], out.at[:, RIM + at : RIM + at + GROUP], sems.at[g]
        )

    groups = range(result.shape[1] // GROUP)
    for g in groups:
        apply_operator(level, [g], za, zb, tmat, rmat, last_finish(fields, k, store))
        copy(g).start()
    for g in groups:
        copy(g).wait()


def rim_last_body(level, k, fields, za, zb, xa, xb, tmat, rmat, out, halo, result, sems):
    fill_halo(halo, xa, xb)
    rows = level.rows

    def store(f, x, value):
        result[f, x if x < RIM else x - rows + 2 * RIM] = value

    apply_operator(level, [None], za, zb, tmat, rmat, last_finish(fields, k, store), halo)
    copies = [
        pltpu.make_async_copy(result.at[:, 0:RIM], out.at[:, 0:RIM], sems.at[0]),
        pltpu.make_async_copy(result.at[:, RIM:], out.at[:, rows - RIM :], sems.at[1]),
    ]
    for copy in copies:
        copy.start()
    for copy in copies:
        copy.wait()


def local(noise, half_width, owner, target_cell, fields):
    px, pa, fine = noise.shape
    cx, ca, radial = fields.shape[1:]
    ncols = px * pa
    most = ncols // 2
    n_az = lax.axis_size("az")
    inner = cx - 2 * RIM

    block = ((px, pa, fine), F32)
    even = is_even("ax")
    to_a = jnp.where(even, noise[px - HMAX :], noise[:HMAX])
    to_b = jnp.where(even, noise[:HMAX], noise[px - HMAX :])
    noise_a, noise_b = swap(to_a, to_b, "ax")
    send_x, send_z = ((15, ca, radial), F32), ((cx // 4 * 3, 8, radial), F32)
    sends = [send_x, send_x, send_z, send_z]
    xa, xb, za, zb = full_specs(edges_body, sends, [fields], name="edges", after=[to_a])
    uxa, uxb = swap(xa, xb, "ax")
    partial, half_width = full_specs(
        inner_body, [block, ((px, pa, fine), jnp.int32)], [noise, half_width], name="filter_inner", after=[za]
    )
    filtered, to_a, to_b = full_specs(
        first_body,
        [block, ((px + send_z[0][0], 8, fine // 2), F32), ((px // 2, 8, fine), F32)],
        [partial, half_width, noise_a, noise_b, za],
        [((2, HMAX, pa, fine), F32)],
        name="filter_axial",
    )
    got_a, got_b = swap(to_a, to_b, "az")
    (uzb,) = swap_b(zb, "az")
    pick, cells, own = full_specs(
        route_body,
        [((4 * most, ncols), BF16), ((4, 8, radial), F32), ((1, ncols), jnp.int32)],
        [owner.reshape(1, ncols), target_cell.reshape(1, ncols)],
        name="route",
        after=[filtered],
    )
    packet = ((most + 8, radial), F32)
    binned, xa, xb, za, zb = full_specs(
        second_body,
        [((ncols, radial), F32), packet, packet, packet, packet],
        [filtered, half_width, got_a, got_b, pick, cells],
        [((px, 32, fine), F32), ((ncols, fine), BF16), ((ncols, fine), BF16)],
        name="filter_rest",
        cost=COST,
    )
    packets = (*swap(xa, xb, "ax"), *swap(za, zb, "az"))

    tmat = jnp.asarray(azimuth_matrices(ca))
    rmat = jnp.asarray(radial_matrices(float(ca * n_az), radial))
    mid, rim = ((5, inner, ca, radial), F32), ((5, 2 * RIM, ca, radial), F32)
    halo = ((2, 5, 3, ca, radial), F32)
    k_mid, k_rim = full_specs(
        start_body, [mid, rim], [fields, got_a, uzb, uxa, uxb, tmat, rmat], [halo], name="operator", after=[binned]
    )
    p_mid, p_rim, *edges = full_specs(
        gather_body,
        [((inner, ca, radial), F32), ((2 * RIM, ca, radial), F32), *sends],
        [binned, own, *packets, k_mid, k_rim],
        name="gather",
    )
    k = [k_mid, k_rim, p_mid, p_rim]
    level = k
    for factor in (time_step / 4.0, time_step / 3.0):
        size = len(level)
        xa, xb = swap(edges[0], edges[1], "ax")
        za, zb = swap(edges[2], edges[3], "az")

        def body(*refs, factor=factor, size=size):
            inner_stage_body(factor, Parts(*refs[:size]), Parts(*refs[size : size + 4]), *refs[size + 4 :])

        (new_mid,) = full_specs(body, [mid], [*level, *k, za, zb, tmat, rmat], name="stage_inner")

        def body(*refs, factor=factor, size=size):
            rim_stage_body(factor, Parts(*refs[:size]), Parts(*refs[size : size + 4]), *refs[size + 4 :])

        new_rim, *edges = full_specs(
            body, [rim, *sends], [*level, *k, za, zb, xa, xb, tmat, rmat, new_mid], [halo], name="stage_rim"
        )
        level = [new_mid, new_rim]
    xa, xb = swap(edges[0], edges[1], "ax")
    za, zb = swap(edges[2], edges[3], "az")

    def body(*refs):
        inner_last_body(Parts(*refs[:2]), Parts(*refs[2:6]), *refs[6:])

    whole = ((5, cx, ca, radial), F32)
    (out,) = full_specs(
        body,
        [whole],
        [*level, *k, fields, za, zb, tmat, rmat],
        [mid, pltpu.SemaphoreType.DMA((inner // GROUP,))],
        name="final_inner",
        out_specs=[ANY],
    )

    def body(out_in, *refs):
        rim_last_body(Parts(*refs[:2]), Parts(*refs[2:6]), *refs[6:])

    (out,) = full_specs(
        body,
        [whole],
        [out, *level, *k, fields, za, zb, xa, xb, tmat, rmat],
        [halo, rim, pltpu.SemaphoreType.DMA((2,))],
        name="final_rim",
        out_specs=[ANY],
        in_specs=[ANY] + [VM] * 13,
        alias={0: 0},
    )
    return out


def solution(mesh):
    return jax.shard_map(
        local,
        mesh=mesh,
        in_specs=(
            P("ax", "az", None),
            P("ax", "az", None),
            P(("ax", "az")),
            P(("ax", "az")),
            P(None, "ax", "az", None),
        ),
        out_specs=P(None, "ax", "az", None),
        check_vma=False,
    )
```

```python
import math

import numpy as np

import jax
import jax.numpy as jnp
from jax import lax
from jax.experimental import pallas as pl
from jax.experimental.pallas import tpu as pltpu
from jax.sharding import PartitionSpec as P

HMAX = 4
drp_coeffs = (0.770882380518, -0.166705904415, 0.02084314277)
mach_number = 0.5
time_step = 0.7
source_gain = 4.0
radial_step = 2.0
hub_ratio = 1.6

F32 = jnp.float32
BF16 = jnp.bfloat16
VM = pl.BlockSpec(memory_space=pltpu.VMEM)
ANY = pl.BlockSpec(memory_space=pl.ANY)
PARAMS = pltpu.CompilerParams(vmem_limit_bytes=24 * 1024 * 1024)
GROUP = 8
RIM = 4
COST = 1 << 27


def np_split(matrix):
    hi = matrix.astype(np.float32).astype(BF16)
    lo = (matrix - hi.astype(np.float64)).astype(np.float32).astype(BF16)
    return hi, lo


def filter_table():
    table = np.zeros((HMAX + 1, HMAX))
    for h in range(1, HMAX + 1):
        weights = [math.exp(-2.0 * k * k / (h * h)) if k <= h else 0.0 for k in range(HMAX + 1)]
        total = weights[0] + 2.0 * sum(weights[1:])
        table[:, h - 1] = [w / total for w in weights]
    return table


def radial_rows(na_total, radial):
    base = na_total / (2.0 * math.pi)
    radius = base / hub_ratio + radial_step * (np.arange(radial) + 0.5)
    return base / radius, 1.0 / radius


def radial_matrices(na_total, radial):
    diff = np.zeros((radial, radial))
    for s, a in zip((1, 2, 3), drp_coeffs):
        for j in range(radial):
            if j + s < radial:
                diff[j + s, j] += a / radial_step
            if j - s >= 0:
                diff[j - s, j] -= a / radial_step
    with_r = diff + np.diag(radial_rows(na_total, radial)[1])
    return np.stack([np.stack(np_split(with_r)), np.stack(np_split(diff))])


def azimuth_matrices(cols):
    packed = GROUP * 6
    full = np.zeros((2, GROUP * cols, GROUP * cols + 2 * packed))
    for which in range(2):
        for x in range(GROUP):
            for i in range(cols):
                for s, a in zip((1, 2, 3), drp_coeffs):
                    for j, sign in ((i + s, 1.0), (i - s, -1.0)):
                        if 0 <= j < cols:
                            at = x * cols + j
                        else:
                            m = j + 3 if j < 0 else j - cols
                            tile, row = (x % 4, m) if x % 4 < 3 else (m, 3)
                            at = GROUP * cols + (x // 4 * 3 + tile) * 8 + row + 4 * which
                            at += packed if j >= cols else 0
                        full[which, x * cols + i, at] += sign * a
    return np.stack([np.stack(np_split(full[w])) for w in range(2)])


def split(x):
    hi = x.astype(BF16)
    return hi, (x - hi.astype(F32)).astype(BF16)


def dot(a, b):
    return lax.dot_general(a, b, (((1,), (0,)), ((), ())), preferred_element_type=F32)


def is_even(axis):
    return lax.rem(lax.axis_index(axis), 2) == 0


def swap(to_a, to_b, axis):
    devices = lax.axis_size(axis)
    pairs_a = [(i, i ^ 1) for i in range(devices)]
    pairs_b = [(i, (i - 1) % devices if i % 2 == 0 else (i + 1) % devices) for i in range(devices)]
    return lax.ppermute(to_a, axis, pairs_a), lax.ppermute(to_b, axis, pairs_b)


def swap_b(value, axis):
    devices = lax.axis_size(axis)
    pairs = [(i, (i - 1) % devices if i % 2 == 0 else (i + 1) % devices) for i in range(devices)]
    return (lax.ppermute(value, axis, pairs),)


def full_specs(body, outs, args, scratch=(), name=None, out_specs=None, after=(), cost=0):
    skip = len(args)

    def run(*refs):
        body(*refs[:skip], *refs[skip + len(after) :])

    return pl.pallas_call(
        run,
        out_shape=[jax.ShapeDtypeStruct(s, d) for s, d in outs],
        in_specs=[VM] * skip + [ANY] * len(after),
        out_specs=out_specs or [VM] * len(outs),
        scratch_shapes=[pltpu.VMEM(*s) if isinstance(s, tuple) else s for s in scratch],
        compiler_params=PARAMS,
        name=name,
        cost_estimate=pl.CostEstimate(flops=0, bytes_accessed=cost, transcendentals=0),
    )(*args, *after)


def route_body(owner_ref, target_ref, pick_ref, cells_ref, own_ref):
    n_ax, n_az = lax.axis_size("ax"), lax.axis_size("az")
    ax, az = lax.axis_index("ax"), lax.axis_index("az")
    step_x = jnp.where(lax.rem(ax, 2) == 0, 1, -1)
    step_z = jnp.where(lax.rem(az, 2) == 0, 1, -1)
    me = ax * n_az + az
    b_x = ax - step_x
    ids = [
        (ax + step_x) * n_az + az,
        jnp.where((b_x >= 0) & (b_x < n_ax), b_x * n_az + az, -1),
        ax * n_az + lax.rem(az + step_z + n_az, n_az),
        ax * n_az + lax.rem(az - step_z + n_az, n_az),
    ]
    owner = owner_ref[...]
    target = target_ref[...]
    ncols = owner.shape[1]
    most = ncols // 2
    own_ref[...] = jnp.where(owner == me, target, -1)
    row = lax.broadcasted_iota(jnp.int32, (8, ncols), 0)
    marks = jnp.zeros((8, ncols), F32)
    for d, i in enumerate(ids):
        marks = jnp.where((row == d) & (owner == i), 1.0, marks)
    before = lax.broadcasted_iota(jnp.int32, (ncols, ncols), 0) < lax.broadcasted_iota(jnp.int32, (ncols, ncols), 1)
    rank = dot(marks.astype(BF16), jnp.where(before, 1.0, 0.0).astype(BF16))
    coarse = (target // 32).astype(F32)
    fine = (target % 32).astype(F32)
    digits = jnp.where(row == 0, coarse, jnp.where(row == 1, fine, 0.0)).astype(BF16)
    slot = lax.broadcasted_iota(jnp.int32, (most, ncols), 0).astype(F32)
    for d in range(4):
        wanted = jnp.where(marks[d : d + 1] > 0.0, rank[d : d + 1], -1.0)
        pick = jnp.where(slot == wanted, 1.0, 0.0).astype(BF16)
        pick_ref[d * most : (d + 1) * most, :] = pick
        found = lax.dot_general(digits, pick, (((1,), (1,)), ((), ())), preferred_element_type=F32)
        cells_ref[d, :, :] = jnp.zeros(cells_ref.shape[1:], F32)
        cells_ref[d, 0:1, 0:most] = found[0:1] * 32.0 + found[1:2]


def weights_of(h):
    table = filter_table()
    le = [h <= 1, h <= 2, h <= 3]
    out = []
    for k in range(HMAX + 1):
        value = jnp.full(h.shape, table[k, 3], F32)
        for j in (2, 1, 0):
            if j > 0 and table[k, j] == 0.0 and table[k, j - 1] == 0.0:
                value = jnp.where(le[j], 0.0, value)
                break
            value = jnp.where(le[j], table[k, j], value)
        out.append(value)
    return out


def inner_body(noise_ref, half_ref, first_ref, kept_ref):
    rows = noise_ref.shape[0]
    kept_ref[...] = half_ref[...]
    for x in range(rows):
        w = weights_of(half_ref[x])
        total = w[0] * noise_ref[x]
        for k in range(1, HMAX + 1):
            near = [noise_ref[y] for y in (x - k, x + k) if 0 <= y < rows]
            if near:
                total = total + w[k] * (near[0] + near[1] if len(near) == 2 else near[0])
        first_ref[x] = total


def first_body(inner_ref, half_ref, got_a_ref, got_b_ref, first_ref, to_a_ref, to_b_ref, halo):
    n_ax, ax = lax.axis_size("ax"), lax.axis_index("ax")
    even_x, even_z = is_even("ax"), is_even("az")
    rows, _, fine = half_ref.shape
    halo[0] = jnp.where(ax > 0, jnp.where(even_x, got_b_ref[...], got_a_ref[...]), 0.0)
    halo[1] = jnp.where(ax < n_ax - 1, jnp.where(even_x, got_a_ref[...], got_b_ref[...]), 0.0)
    for x in range(HMAX, rows - HMAX):
        first_ref[x] = inner_ref[x]
    for i in range(HMAX):
        w = weights_of(half_ref[i])
        total = inner_ref[i]
        for k in range(i + 1, HMAX + 1):
            total = total + w[k] * halo[0, HMAX + i - k]
        first_ref[i] = total
        x = rows - 1 - i
        w = weights_of(half_ref[x])
        total = inner_ref[x]
        for k in range(i + 1, HMAX + 1):
            total = total + w[k] * halo[1, k - i - 1]
        first_ref[x] = total
    half = rows // 2
    low = lax.broadcasted_iota(jnp.int32, (8, fine), 0) < 4
    for x in range(half):
        last = jnp.where(low, pltpu.roll(first_ref[x, 8:16], 4, 0), first_ref[x + half, 8:16])
        begin = jnp.where(low, first_ref[x, 0:8], pltpu.roll(first_ref[x + half, 0:8], 4, 0))
        to_a_ref[x] = jnp.where(even_z, last, begin)
        to_b_ref[x] = jnp.where(even_z, begin, last)


def second_body(
    first_ref, half_ref, got_a_ref, got_b_ref, pick_ref, cells_ref, edge_a_ref,
    own_ref, to_xa, to_xb, to_za, to_zb, wide, fine_hi, fine_lo,
):
    even = is_even("az")
    rows, cols, fine = first_ref.shape
    half = rows // 2
    for x in range(half):
        got_a, got_b = got_a_ref[x], got_b_ref[x]
        before = jnp.where(even, got_b, got_a)
        after = jnp.where(even, got_a, got_b)
        wide[x, 0:8] = pltpu.roll(before, 4, 0)
        wide[x + half, 0:8] = before
        wide[x, 24:32] = after
        wide[x + half, 24:32] = pltpu.roll(after, 4, 0)
    lane = lax.broadcasted_iota(jnp.int32, (cols, fine), 1)
    for x in range(rows):
        wide[x, 8:24] = first_ref[x]
    for x in range(rows):
        w = weights_of(half_ref[x])
        total = w[0] * first_ref[x]
        for k in range(1, HMAX + 1):
            total = total + w[k] * (wide[x, 8 - k : 24 - k] + wide[x, 8 + k : 24 + k])
        result = w[0] * total
        for k in range(1, HMAX + 1):
            up = jnp.where(lane < fine - k, pltpu.roll(total, fine - k, 1), 0.0)
            down = jnp.where(lane >= k, pltpu.roll(total, k, 1), 0.0)
            result = result + w[k] * (up + down)
        hi, lo = split(result)
        fine_hi[x * cols : (x + 1) * cols] = hi
        fine_lo[x * cols : (x + 1) * cols] = lo
    radial = own_ref.shape[1]
    above = lax.broadcasted_iota(jnp.int32, (fine, radial), 0) - lax.broadcasted_iota(
        jnp.int32, (fine, radial), 1
    ) * (fine // radial)
    bins = jnp.where((above >= 0) & (above < fine // radial), source_gain, 0.0).astype(BF16)
    binned = dot(fine_hi[...], bins) + dot(fine_lo[...], bins)
    own_ref[...] = binned
    hi, lo = split(binned)
    most = pick_ref.shape[0] // 4
    for d, out in enumerate((to_xa, to_xb, to_za, to_zb)):
        pick = pick_ref[d * most : (d + 1) * most]
        tiles = most // 8
        out[0:tiles] = (dot(pick, hi) + dot(pick, lo)).reshape(tiles, 8, radial)
        out[tiles] = cells_ref[d]
    to_za[most // 8 + 1 :] = edge_a_ref[...]


def gather_body(
    binned_ref, own_ref, xa, xb, za, zb, k_mid, k_rim, p_mid, p_rim, to_xa, to_xb, to_za, to_zb
):
    mid, cols, radial = p_mid.shape
    cells = (mid + 2 * RIM) * cols
    most = 8 * (xa.shape[0] - 1)

    def onehot(row):
        at = lax.broadcasted_iota(jnp.int32, (cells, row.shape[1]), 0)
        return jnp.where(at == row, 1.0, 0.0).astype(BF16)

    mats = [onehot(own_ref[...])]
    packets = [binned_ref[...]]
    for got in (xa, xb, za, zb):
        tiles = most // 8
        mats.append(onehot(got[tiles, 0:1, 0:most].astype(jnp.int32)))
        packets.append(got[0:tiles].reshape(most, radial))
    mat = jnp.concatenate(mats, axis=1)
    hi, lo = split(jnp.concatenate(packets, axis=0))
    q = (dot(mat, hi) + dot(mat, lo)).reshape(mid + 2 * RIM, cols, radial)
    p_rim[0:RIM] = k_rim[4, 0:RIM] + q[0:RIM]
    p_mid[...] = k_mid[4] + q[RIM : RIM + mid]
    p_rim[RIM:] = k_rim[4, RIM:] + q[RIM + mid :]
    level = Parts(k_mid, k_rim, p_mid, p_rim)
    write_x(level, to_xa, to_xb)
    write_z(level, to_za, to_zb)


class Whole:
    def __init__(self, ref):
        self.ref = ref
        self.rows = ref.shape[1]

    def row(self, f, x):
        return self.ref[f, x]

    def group(self, f, g):
        if g is None:
            return jnp.concatenate([self.ref[f, 0:RIM], self.ref[f, self.rows - RIM :]], axis=0)
        return self.ref[f, RIM + g * GROUP : RIM + (g + 1) * GROUP]


class Parts:
    def __init__(self, mid, rim, p_mid=None, p_rim=None):
        self.arrays = (mid, rim, p_mid, p_rim)
        self.rows = mid.shape[1] + 2 * RIM

    def pick(self, f):
        mid, rim, p_mid, p_rim = self.arrays
        if f == 4 and p_mid is not None:
            return p_mid, p_rim
        return mid.at[f], rim.at[f]

    def row(self, f, x):
        mid, rim = self.pick(f)
        if RIM <= x < self.rows - RIM:
            return mid[x - RIM]
        return rim[x if x < RIM else x - self.rows + 2 * RIM]

    def group(self, f, g):
        mid, rim = self.pick(f)
        return rim[...] if g is None else mid[g * GROUP : (g + 1) * GROUP]

    def store(self, f, x, value):
        mid, rim = self.pick(f)
        if RIM <= x < self.rows - RIM:
            mid[x - RIM] = value
        else:
            rim[x if x < RIM else x - self.rows + 2 * RIM] = value


def join_last(ut, p):
    low = lax.broadcasted_iota(jnp.int32, ut.shape, 0) < 4
    return jnp.where(low, pltpu.roll(ut, 3, 0), pltpu.roll(p, 7, 0))


def join_first(ut, p):
    low = lax.broadcasted_iota(jnp.int32, ut.shape, 0) < 4
    return jnp.where(low, ut, pltpu.roll(p, 4, 0))


def write_x(level, to_xa, to_xb):
    even = is_even("ax")
    for f in range(5):
        for i in range(3):
            first, last = level.row(f, i), level.row(f, level.rows - 3 + i)
            to_xa[3 * f + i] = jnp.where(even, last, first)
            to_xb[3 * f + i] = jnp.where(even, first, last)


def write_z(level, to_za, to_zb):
    even = is_even("az")
    row = None
    for x in range(0, level.rows, 4):
        first, last = [], []
        for y in range(x, x + 4):
            ut, p = level.row(2, y), level.row(4, y)
            first.append(join_first(ut[0:8], p[0:8]))
            last.append(join_last(ut[8:16], p[8:16]))
        if row is None:
            row = lax.broadcasted_iota(jnp.int32, first[0].shape, 0) % 4 == 3
        for t in range(3):
            shift = 3 - t
            one = jnp.where(row, pltpu.roll(first[3], shift, 0), first[t])
            two = jnp.where(row, pltpu.roll(last[3], shift, 0), last[t])
            to_za[x // 4 * 3 + t] = jnp.where(even, two, one)
            to_zb[x // 4 * 3 + t] = jnp.where(even, one, two)


def edges_body(state, to_xa, to_xb, to_za, to_zb):
    level = Whole(state)
    write_x(level, to_xa, to_xb)
    write_z(level, to_za, to_zb)


def fill_halo(halo, xa, xb):
    n_ax, ax = lax.axis_size("ax"), lax.axis_index("ax")
    even = is_even("ax")
    for f in range(halo.shape[1]):
        a, b = xa[3 * f : 3 * f + 3], xb[3 * f : 3 * f + 3]
        halo[0, f] = jnp.where(ax > 0, jnp.where(even, b, a), 0.0)
        halo[1, f] = jnp.where(ax < n_ax - 1, jnp.where(even, a, b), 0.0)


def inverse_step(cols, radial):
    base = cols * lax.axis_size("az") / (2.0 * math.pi)
    at = lax.broadcasted_iota(jnp.int32, (1, radial), 1).astype(F32)
    return base / (base / hub_ratio + radial_step * (at + 0.5))


def along(row, x):
    total = drp_coeffs[0] * (row(x + 1) - row(x - 1))
    for s in (2, 3):
        total = total + drp_coeffs[s - 1] * (row(x + s) - row(x - s))
    return total


def apply_operator(level, groups, za, zb, tmat, rmat, finish, halo=None):
    even = is_even("az")
    tiles = level.rows // 4 * 3
    rim = RIM // 4 * 3

    def row(f, x):
        if x < 0:
            return halo[0, f, x + 3]
        if x >= level.rows:
            return halo[1, f, x - level.rows]
        return level.row(f, x)

    def beside(g):
        spans = [(0, rim), (tiles - rim, tiles)] if g is None else [(rim + 6 * g, rim + 6 * g + 6)]
        start = za.shape[0] - tiles
        sides = []
        for swap_ab in (False, True):
            for a, b in spans:
                got_a, got_b = za[start + a : start + b], zb[a:b]
                pair = (got_a, got_b) if swap_ab else (got_b, got_a)
                sides.append(jnp.where(even, *pair).reshape((b - a) * 8, za.shape[2]))
        return split(jnp.concatenate(sides, axis=0))

    for g in groups:
        if g is None:
            xs = [*range(RIM), *range(level.rows - RIM, level.rows)]
        else:
            xs = range(RIM + g * GROUP, RIM + (g + 1) * GROUP)
        ut, ur, p = [level.group(f, g) for f in (2, 3, 4)]
        _, cols, radial = ut.shape
        inv_h = inverse_step(cols, radial)
        side_hi, side_lo = beside(g)
        p_hi, p_lo = split(p.reshape(GROUP * cols, radial))
        ut_hi, ut_lo = split(ut.reshape(GROUP * cols, radial))
        ur_hi, ur_lo = split(ur.reshape(GROUP * cols, radial))

        def across(which, hi, lo):
            hi = jnp.concatenate([hi, side_hi], axis=0)
            lo = jnp.concatenate([lo, side_lo], axis=0)
            return dot(tmat[which, 0], hi) + dot(tmat[which, 0], lo) + dot(tmat[which, 1], hi)

        def outward(which, hi, lo):
            return dot(hi, rmat[which, 0]) + dot(lo, rmat[which, 0]) + dot(hi, rmat[which, 1])

        div_tr = across(0, ut_hi, ut_lo) * inv_h + outward(0, ur_hi, ur_lo)
        p_t = across(1, p_hi, p_lo) * inv_h
        p_r = outward(1, p_hi, p_lo)
        for i, x in enumerate(xs):
            part = slice(i * cols, (i + 1) * cols)
            d = [along(lambda y: row(f, y), x) for f in range(5)]
            div = d[1] + div_tr[part]
            finish(
                x,
                [
                    -mach_number * d[0] - div,
                    -mach_number * d[1] - d[4],
                    -mach_number * d[2] - p_t[part],
                    -mach_number * d[3] - p_r[part],
                    -mach_number * d[4] - div,
                ],
            )


def start_body(state, za, zb, xa, xb, tmat, rmat, k_mid, k_rim, halo):
    fill_halo(halo, xa, xb)
    level, out = Whole(state), Parts(k_mid, k_rim)

    def finish(x, tend):
        for f in range(5):
            out.store(f, x, tend[f])

    apply_operator(level, [*range(k_mid.shape[1] // GROUP), None], za, zb, tmat, rmat, finish, halo)


def inner_stage_body(factor, level, base, za, zb, tmat, rmat, out_mid):
    def finish(x, tend):
        for f in range(5):
            out_mid[f, x - RIM] = base.row(f, x) + factor * tend[f]

    apply_operator(level, range(out_mid.shape[1] // GROUP), za, zb, tmat, rmat, finish)


def rim_stage_body(factor, level, base, za, zb, xa, xb, tmat, rmat, out_mid, out_rim, to_xa, to_xb, to_za, to_zb, halo):
    fill_halo(halo, xa, xb)
    out = Parts(out_mid, out_rim)

    def finish(x, tend):
        for f in range(5):
            out.store(f, x, base.row(f, x) + factor * tend[f])

    apply_operator(level, [None], za, zb, tmat, rmat, finish, halo)
    write_x(out, to_xa, to_xb)
    write_z(out, to_za, to_zb)


def last_finish(fields, k, store):
    def finish(x, tend):
        for f in range(5):
            store(f, x, fields[f, x] + time_step * k.row(f, x) + (0.5 * time_step * time_step) * tend[f])

    return finish


def inner_last_body(level, k, fields, za, zb, tmat, rmat, out_mid):
    def store(f, x, value):
        out_mid[f, x - RIM] = value

    groups = range(out_mid.shape[1] // GROUP)
    apply_operator(level, groups, za, zb, tmat, rmat, last_finish(fields, k, store))


def rim_last_body(level, k, fields, za, zb, xa, xb, tmat, rmat, out_mid, out, halo, result, sems):
    rows = level.rows
    inner = pltpu.make_async_copy(out_mid, out.at[:, RIM : rows - RIM], sems.at[0])
    inner.start()
    fill_halo(halo, xa, xb)

    def store(f, x, value):
        result[f, x if x < RIM else x - rows + 2 * RIM] = value

    apply_operator(level, [None], za, zb, tmat, rmat, last_finish(fields, k, store), halo)
    copies = [
        pltpu.make_async_copy(result.at[:, 0:RIM], out.at[:, 0:RIM], sems.at[1]),
        pltpu.make_async_copy(result.at[:, RIM:], out.at[:, rows - RIM :], sems.at[2]),
    ]
    for copy in copies:
        copy.start()
    for copy in (inner, *copies):
        copy.wait()


def local(noise, half_width, owner, target_cell, fields):
    px, pa, fine = noise.shape
    cx, ca, radial = fields.shape[1:]
    ncols = px * pa
    most = ncols // 2
    n_az = lax.axis_size("az")
    inner = cx - 2 * RIM

    block = ((px, pa, fine), F32)
    even = is_even("ax")
    to_a = jnp.where(even, noise[px - HMAX :], noise[:HMAX])
    to_b = jnp.where(even, noise[:HMAX], noise[px - HMAX :])
    noise_a, noise_b = swap(to_a, to_b, "ax")
    send_x, send_z = ((15, ca, radial), F32), ((cx // 4 * 3, 8, radial), F32)
    sends = [send_x, send_x, send_z, send_z]
    xa, xb, za, zb = full_specs(edges_body, sends, [fields], name="edges", after=[to_a])
    uxa, uxb = swap(xa, xb, "ax")
    partial, half_width = full_specs(
        inner_body, [block, ((px, pa, fine), jnp.int32)], [noise, half_width], name="filter_inner", after=[za]
    )
    filtered, to_a, to_b = full_specs(
        first_body,
        [block, ((px // 2, 8, fine), F32), ((px // 2, 8, fine), F32)],
        [partial, half_width, noise_a, noise_b],
        [((2, HMAX, pa, fine), F32)],
        name="filter_axial",
    )
    got_a, got_b = swap(to_a, to_b, "az")
    (uzb,) = swap_b(zb, "az")
    uza = za
    pick, cells, own = full_specs(
        route_body,
        [((4 * most, ncols), BF16), ((4, 8, radial), F32), ((1, ncols), jnp.int32)],
        [owner.reshape(1, ncols), target_cell.reshape(1, ncols)],
        name="route",
        after=[filtered, uxa, uxb, uzb],
    )
    tiles = most // 8 + 1
    packet = ((tiles, 8, radial), F32)
    binned, xa, xb, za, zb = full_specs(
        second_body,
        [((ncols, radial), F32), packet, packet, ((tiles + send_z[0][0], 8, radial), F32), packet],
        [filtered, half_width, got_a, got_b, pick, cells, uza],
        [((px, 32, fine), F32), ((ncols, fine), BF16), ((ncols, fine), BF16)],
        name="filter_rest",
    )
    packets = (*swap(xa, xb, "ax"), *swap(za, zb, "az"))

    tmat = jnp.asarray(azimuth_matrices(ca))
    rmat = jnp.asarray(radial_matrices(float(ca * n_az), radial))
    mid, rim = ((5, inner, ca, radial), F32), ((5, 2 * RIM, ca, radial), F32)
    halo = ((2, 5, 3, ca, radial), F32)
    k_mid, k_rim = full_specs(
        start_body, [mid, rim], [fields, packets[2], uzb, uxa, uxb, tmat, rmat], [halo], name="operator", after=[binned]
    )
    p_mid, p_rim, *edges = full_specs(
        gather_body,
        [((inner, ca, radial), F32), ((2 * RIM, ca, radial), F32), *sends],
        [binned, own, *packets, k_mid, k_rim],
        name="gather",
    )
    k = [k_mid, k_rim, p_mid, p_rim]
    level = k
    for factor in (time_step / 4.0, time_step / 3.0):
        size = len(level)
        xa, xb = swap(edges[0], edges[1], "ax")
        za, zb = swap(edges[2], edges[3], "az")

        def body(*refs, factor=factor, size=size):
            inner_stage_body(factor, Parts(*refs[:size]), Parts(*refs[size : size + 4]), *refs[size + 4 :])

        (new_mid,) = full_specs(body, [mid], [*level, *k, za, zb, tmat, rmat], name="stage_inner", cost=COST)

        def body(*refs, factor=factor, size=size):
            rim_stage_body(factor, Parts(*refs[:size]), Parts(*refs[size : size + 4]), *refs[size + 4 :])

        new_rim, *edges = full_specs(
            body, [rim, *sends], [*level, *k, za, zb, xa, xb, tmat, rmat, new_mid], [halo], name="stage_rim"
        )
        level = [new_mid, new_rim]
    xa, xb = swap(edges[0], edges[1], "ax")
    za, zb = swap(edges[2], edges[3], "az")

    def body(*refs):
        inner_last_body(Parts(*refs[:2]), Parts(*refs[2:6]), *refs[6:])

    (new_mid,) = full_specs(body, [mid], [*level, *k, fields, za, zb, tmat, rmat], name="final_inner", cost=COST)

    def body(*refs):
        rim_last_body(Parts(*refs[:2]), Parts(*refs[2:6]), *refs[6:])

    (out,) = full_specs(
        body,
        [((5, cx, ca, radial), F32)],
        [*level, *k, fields, za, zb, xa, xb, tmat, rmat, new_mid],
        [halo, rim, pltpu.SemaphoreType.DMA((3,))],
        name="final_rim",
        out_specs=[ANY],
    )
    return out


def solution(mesh):
    return jax.shard_map(
        local,
        mesh=mesh,
        in_specs=(
            P("ax", "az", None),
            P("ax", "az", None),
            P(("ax", "az")),
            P(("ax", "az")),
            P(None, "ax", "az", None),
        ),
        out_specs=P(None, "ax", "az", None),
        check_vma=False,
    )
```

```python
import math

import numpy as np

import jax
import jax.numpy as jnp
from jax import lax
from jax.experimental import pallas as pl
from jax.experimental.pallas import tpu as pltpu
from jax.sharding import PartitionSpec as P

HMAX = 4
drp_coeffs = (0.770882380518, -0.166705904415, 0.02084314277)
mach_number = 0.5
time_step = 0.7
source_gain = 4.0
radial_step = 2.0
hub_ratio = 1.6

F32 = jnp.float32
BF16 = jnp.bfloat16
VM = pl.BlockSpec(memory_space=pltpu.VMEM)
ANY = pl.BlockSpec(memory_space=pl.ANY)
PARAMS = pltpu.CompilerParams(vmem_limit_bytes=24 * 1024 * 1024)
GROUP = 8
RIM = 4
COST = 1 << 37


def np_split(matrix):
    hi = matrix.astype(np.float32).astype(BF16)
    lo = (matrix - hi.astype(np.float64)).astype(np.float32).astype(BF16)
    return hi, lo


def filter_table():
    table = np.zeros((HMAX + 1, HMAX))
    for h in range(1, HMAX + 1):
        weights = [math.exp(-2.0 * k * k / (h * h)) if k <= h else 0.0 for k in range(HMAX + 1)]
        total = weights[0] + 2.0 * sum(weights[1:])
        table[:, h - 1] = [w / total for w in weights]
    return table


def radial_rows(na_total, radial):
    base = na_total / (2.0 * math.pi)
    radius = base / hub_ratio + radial_step * (np.arange(radial) + 0.5)
    return base / radius, 1.0 / radius


def radial_matrices(na_total, radial):
    diff = np.zeros((radial, radial))
    for s, a in zip((1, 2, 3), drp_coeffs):
        for j in range(radial):
            if j + s < radial:
                diff[j + s, j] += a / radial_step
            if j - s >= 0:
                diff[j - s, j] -= a / radial_step
    with_r = diff + np.diag(radial_rows(na_total, radial)[1])
    return np.stack([np.stack(np_split(with_r)), np.stack(np_split(diff))])


def azimuth_matrices(cols):
    packed = GROUP * 6
    full = np.zeros((2, GROUP * cols, GROUP * cols + 2 * packed))
    for which in range(2):
        for x in range(GROUP):
            for i in range(cols):
                for s, a in zip((1, 2, 3), drp_coeffs):
                    for j, sign in ((i + s, 1.0), (i - s, -1.0)):
                        if 0 <= j < cols:
                            at = x * cols + j
                        else:
                            m = j + 3 if j < 0 else j - cols
                            tile, row = (x % 4, m) if x % 4 < 3 else (m, 3)
                            at = GROUP * cols + (x // 4 * 3 + tile) * 8 + row + 4 * which
                            at += packed if j >= cols else 0
                        full[which, x * cols + i, at] += sign * a
    return np.stack([np.stack(np_split(full[w])) for w in range(2)])


def split(x):
    hi = x.astype(BF16)
    return hi, (x - hi.astype(F32)).astype(BF16)


def dot(a, b):
    return lax.dot_general(a, b, (((1,), (0,)), ((), ())), preferred_element_type=F32)


def is_even(axis):
    return lax.rem(lax.axis_index(axis), 2) == 0


def swap(to_a, to_b, axis):
    devices = lax.axis_size(axis)
    pairs_a = [(i, i ^ 1) for i in range(devices)]
    pairs_b = [(i, (i - 1) % devices if i % 2 == 0 else (i + 1) % devices) for i in range(devices)]
    if axis == "ax":
        pairs_b = [(i, j if abs(i - j) == 1 else i) for i, j in pairs_b]
    return lax.ppermute(to_a, axis, pairs_a), lax.ppermute(to_b, axis, pairs_b)


def swap_b(value, axis):
    devices = lax.axis_size(axis)
    pairs = [(i, (i - 1) % devices if i % 2 == 0 else (i + 1) % devices) for i in range(devices)]
    return (lax.ppermute(value, axis, pairs),)


def full_specs(body, outs, args, scratch=(), name=None, out_specs=None, after=(), cost=0):
    skip = len(args)

    def run(*refs):
        body(*refs[:skip], *refs[skip + len(after) :])

    return pl.pallas_call(
        run,
        out_shape=[jax.ShapeDtypeStruct(s, d) for s, d in outs],
        in_specs=[VM] * skip + [ANY] * len(after),
        out_specs=out_specs or [VM] * len(outs),
        scratch_shapes=[pltpu.VMEM(*s) if isinstance(s, tuple) else s for s in scratch],
        compiler_params=PARAMS,
        name=name,
        cost_estimate=pl.CostEstimate(flops=cost, bytes_accessed=0, transcendentals=0),
    )(*args, *after)


def route_body(owner_ref, target_ref, pick_ref, cells_ref, own_ref):
    n_ax, n_az = lax.axis_size("ax"), lax.axis_size("az")
    ax, az = lax.axis_index("ax"), lax.axis_index("az")
    step_x = jnp.where(lax.rem(ax, 2) == 0, 1, -1)
    step_z = jnp.where(lax.rem(az, 2) == 0, 1, -1)
    me = ax * n_az + az
    b_x = ax - step_x
    ids = [
        (ax + step_x) * n_az + az,
        jnp.where((b_x >= 0) & (b_x < n_ax), b_x * n_az + az, -1),
        ax * n_az + lax.rem(az + step_z + n_az, n_az),
        ax * n_az + lax.rem(az - step_z + n_az, n_az),
    ]
    owner = owner_ref[...]
    target = target_ref[...]
    ncols = owner.shape[1]
    most = ncols // 2
    own_ref[...] = jnp.where(owner == me, target, -1)
    row = lax.broadcasted_iota(jnp.int32, (8, ncols), 0)
    marks = jnp.zeros((8, ncols), F32)
    for d, i in enumerate(ids):
        marks = jnp.where((row == d) & (owner == i), 1.0, marks)
    before = lax.broadcasted_iota(jnp.int32, (ncols, ncols), 0) < lax.broadcasted_iota(jnp.int32, (ncols, ncols), 1)
    rank = dot(marks.astype(BF16), jnp.where(before, 1.0, 0.0).astype(BF16))
    coarse = (target // 32).astype(F32)
    fine = (target % 32).astype(F32)
    digits = jnp.where(row == 0, coarse, jnp.where(row == 1, fine, 0.0)).astype(BF16)
    slot = lax.broadcasted_iota(jnp.int32, (most, ncols), 0).astype(F32)
    for d in range(4):
        wanted = jnp.where(marks[d : d + 1] > 0.0, rank[d : d + 1], -1.0)
        pick = jnp.where(slot == wanted, 1.0, 0.0).astype(BF16)
        pick_ref[d * most : (d + 1) * most, :] = pick
        found = lax.dot_general(digits, pick, (((1,), (1,)), ((), ())), preferred_element_type=F32)
        cells_ref[d, :, :] = jnp.zeros(cells_ref.shape[1:], F32)
        cells_ref[d, 0:1, 0:most] = found[0:1] * 32.0 + found[1:2]


def weights_of(h):
    table = filter_table()
    le = [h <= 1, h <= 2, h <= 3]
    out = []
    for k in range(HMAX + 1):
        value = jnp.full(h.shape, table[k, 3], F32)
        for j in (2, 1, 0):
            if j > 0 and table[k, j] == 0.0 and table[k, j - 1] == 0.0:
                value = jnp.where(le[j], 0.0, value)
                break
            value = jnp.where(le[j], table[k, j], value)
        out.append(value)
    return out


def inner_body(noise_ref, half_ref, first_ref, kept_ref):
    rows = noise_ref.shape[0]
    kept_ref[...] = half_ref[...]
    for x in range(rows):
        w = weights_of(half_ref[x])
        total = w[0] * noise_ref[x]
        for k in range(1, HMAX + 1):
            near = [noise_ref[y] for y in (x - k, x + k) if 0 <= y < rows]
            if near:
                total = total + w[k] * (near[0] + near[1] if len(near) == 2 else near[0])
        first_ref[x] = total


def first_body(inner_ref, half_ref, got_a_ref, got_b_ref, first_ref, to_a_ref, to_b_ref, halo):
    n_ax, ax = lax.axis_size("ax"), lax.axis_index("ax")
    even_x, even_z = is_even("ax"), is_even("az")
    rows, _, fine = half_ref.shape
    halo[0] = jnp.where(ax > 0, jnp.where(even_x, got_b_ref[...], got_a_ref[...]), 0.0)
    halo[1] = jnp.where(ax < n_ax - 1, jnp.where(even_x, got_a_ref[...], got_b_ref[...]), 0.0)
    for x in range(HMAX, rows - HMAX):
        first_ref[x] = inner_ref[x]
    for i in range(HMAX):
        w = weights_of(half_ref[i])
        total = inner_ref[i]
        for k in range(i + 1, HMAX + 1):
            total = total + w[k] * halo[0, HMAX + i - k]
        first_ref[i] = total
        x = rows - 1 - i
        w = weights_of(half_ref[x])
        total = inner_ref[x]
        for k in range(i + 1, HMAX + 1):
            total = total + w[k] * halo[1, k - i - 1]
        first_ref[x] = total
    half = rows // 2
    low = lax.broadcasted_iota(jnp.int32, (8, fine), 0) < 4
    for x in range(half):
        last = jnp.where(low, pltpu.roll(first_ref[x, 8:16], 4, 0), first_ref[x + half, 8:16])
        begin = jnp.where(low, first_ref[x, 0:8], pltpu.roll(first_ref[x + half, 0:8], 4, 0))
        to_a_ref[x] = jnp.where(even_z, last, begin)
        to_b_ref[x] = jnp.where(even_z, begin, last)


def second_body(
    first_ref, half_ref, got_a_ref, got_b_ref, pick_ref, cells_ref, edge_a_ref,
    own_ref, to_xa, to_xb, to_za, to_zb, wide, fine_hi, fine_lo,
):
    even = is_even("az")
    rows, cols, fine = first_ref.shape
    half = rows // 2
    for x in range(half):
        got_a, got_b = got_a_ref[x], got_b_ref[x]
        before = jnp.where(even, got_b, got_a)
        after = jnp.where(even, got_a, got_b)
        wide[x, 0:8] = pltpu.roll(before, 4, 0)
        wide[x + half, 0:8] = before
        wide[x, 24:32] = after
        wide[x + half, 24:32] = pltpu.roll(after, 4, 0)
    lane = lax.broadcasted_iota(jnp.int32, (cols, fine), 1)
    for x in range(rows):
        wide[x, 8:24] = first_ref[x]
    for x in range(rows):
        w = weights_of(half_ref[x])
        total = w[0] * first_ref[x]
        for k in range(1, HMAX + 1):
            total = total + w[k] * (wide[x, 8 - k : 24 - k] + wide[x, 8 + k : 24 + k])
        result = w[0] * total
        for k in range(1, HMAX + 1):
            up = jnp.where(lane < fine - k, pltpu.roll(total, fine - k, 1), 0.0)
            down = jnp.where(lane >= k, pltpu.roll(total, k, 1), 0.0)
            result = result + w[k] * (up + down)
        hi, lo = split(result)
        fine_hi[x * cols : (x + 1) * cols] = hi
        fine_lo[x * cols : (x + 1) * cols] = lo
    radial = own_ref.shape[1]
    above = lax.broadcasted_iota(jnp.int32, (fine, radial), 0) - lax.broadcasted_iota(
        jnp.int32, (fine, radial), 1
    ) * (fine // radial)
    bins = jnp.where((above >= 0) & (above < fine // radial), source_gain, 0.0).astype(BF16)
    binned = dot(fine_hi[...], bins) + dot(fine_lo[...], bins)
    own_ref[...] = binned
    hi, lo = split(binned)
    most = pick_ref.shape[0] // 4
    for d, out in enumerate((to_xa, to_xb, to_za, to_zb)):
        pick = pick_ref[d * most : (d + 1) * most]
        tiles = most // 8
        out[0:tiles] = (dot(pick, hi) + dot(pick, lo)).reshape(tiles, 8, radial)
        out[tiles] = cells_ref[d]
    to_za[most // 8 + 1 :] = edge_a_ref[...]


def gather_body(
    binned_ref, own_ref, xa, xb, za, zb, k_mid, k_rim, p_mid, p_rim, to_xa, to_xb, to_za, to_zb
):
    mid, cols, radial = p_mid.shape
    cells = (mid + 2 * RIM) * cols
    most = 8 * (xa.shape[0] - 1)

    def onehot(row):
        at = lax.broadcasted_iota(jnp.int32, (cells, row.shape[1]), 0)
        return jnp.where(at == row, 1.0, 0.0).astype(BF16)

    mats = [onehot(own_ref[...])]
    packets = [binned_ref[...]]
    for got in (xa, xb, za, zb):
        tiles = most // 8
        mats.append(onehot(got[tiles, 0:1, 0:most].astype(jnp.int32)))
        packets.append(got[0:tiles].reshape(most, radial))
    mat = jnp.concatenate(mats, axis=1)
    hi, lo = split(jnp.concatenate(packets, axis=0))
    q = (dot(mat, hi) + dot(mat, lo)).reshape(mid + 2 * RIM, cols, radial)
    p_rim[0:RIM] = k_rim[4, 0:RIM] + q[0:RIM]
    p_mid[...] = k_mid[4] + q[RIM : RIM + mid]
    p_rim[RIM:] = k_rim[4, RIM:] + q[RIM + mid :]
    level = Parts(k_mid, k_rim, p_mid, p_rim)
    write_x(level, to_xa, to_xb)
    write_z(level, to_za, to_zb)


class Whole:
    def __init__(self, ref):
        self.ref = ref
        self.rows = ref.shape[1]

    def row(self, f, x):
        return self.ref[f, x]

    def group(self, f, g):
        if g is None:
            return jnp.concatenate([self.ref[f, 0:RIM], self.ref[f, self.rows - RIM :]], axis=0)
        return self.ref[f, RIM + g * GROUP : RIM + (g + 1) * GROUP]


class Parts:
    def __init__(self, mid, rim, p_mid=None, p_rim=None):
        self.arrays = (mid, rim, p_mid, p_rim)
        self.rows = mid.shape[1] + 2 * RIM

    def pick(self, f):
        mid, rim, p_mid, p_rim = self.arrays
        if f == 4 and p_mid is not None:
            return p_mid, p_rim
        return mid.at[f], rim.at[f]

    def row(self, f, x):
        mid, rim = self.pick(f)
        if RIM <= x < self.rows - RIM:
            return mid[x - RIM]
        return rim[x if x < RIM else x - self.rows + 2 * RIM]

    def group(self, f, g):
        mid, rim = self.pick(f)
        return rim[...] if g is None else mid[g * GROUP : (g + 1) * GROUP]

    def store(self, f, x, value):
        mid, rim = self.pick(f)
        if RIM <= x < self.rows - RIM:
            mid[x - RIM] = value
        else:
            rim[x if x < RIM else x - self.rows + 2 * RIM] = value


def join_last(ut, p):
    low = lax.broadcasted_iota(jnp.int32, ut.shape, 0) < 4
    return jnp.where(low, pltpu.roll(ut, 3, 0), pltpu.roll(p, 7, 0))


def join_first(ut, p):
    low = lax.broadcasted_iota(jnp.int32, ut.shape, 0) < 4
    return jnp.where(low, ut, pltpu.roll(p, 4, 0))


def write_x(level, to_xa, to_xb):
    even = is_even("ax")
    for f in range(5):
        for i in range(3):
            first, last = level.row(f, i), level.row(f, level.rows - 3 + i)
            to_xa[3 * f + i] = jnp.where(even, last, first)
            to_xb[3 * f + i] = jnp.where(even, first, last)


def write_z(level, to_za, to_zb):
    even = is_even("az")
    row = None
    for x in range(0, level.rows, 4):
        first, last = [], []
        for y in range(x, x + 4):
            ut, p = level.row(2, y), level.row(4, y)
            first.append(join_first(ut[0:8], p[0:8]))
            last.append(join_last(ut[8:16], p[8:16]))
        if row is None:
            row = lax.broadcasted_iota(jnp.int32, first[0].shape, 0) % 4 == 3
        for t in range(3):
            shift = 3 - t
            one = jnp.where(row, pltpu.roll(first[3], shift, 0), first[t])
            two = jnp.where(row, pltpu.roll(last[3], shift, 0), last[t])
            to_za[x // 4 * 3 + t] = jnp.where(even, two, one)
            to_zb[x // 4 * 3 + t] = jnp.where(even, one, two)


def edges_body(state, to_xa, to_xb, to_za, to_zb):
    level = Whole(state)
    write_x(level, to_xa, to_xb)
    write_z(level, to_za, to_zb)


def fill_halo(halo, xa, xb):
    n_ax, ax = lax.axis_size("ax"), lax.axis_index("ax")
    even = is_even("ax")
    for f in range(halo.shape[1]):
        a, b = xa[3 * f : 3 * f + 3], xb[3 * f : 3 * f + 3]
        halo[0, f] = jnp.where(ax > 0, jnp.where(even, b, a), 0.0)
        halo[1, f] = jnp.where(ax < n_ax - 1, jnp.where(even, a, b), 0.0)


def inverse_step(cols, radial):
    base = cols * lax.axis_size("az") / (2.0 * math.pi)
    at = lax.broadcasted_iota(jnp.int32, (1, radial), 1).astype(F32)
    return base / (base / hub_ratio + radial_step * (at + 0.5))


def along(row, x):
    total = drp_coeffs[0] * (row(x + 1) - row(x - 1))
    for s in (2, 3):
        total = total + drp_coeffs[s - 1] * (row(x + s) - row(x - s))
    return total


def apply_operator(level, groups, za, zb, tmat, rmat, finish, halo=None):
    even = is_even("az")
    tiles = level.rows // 4 * 3
    rim = RIM // 4 * 3

    def row(f, x):
        if x < 0:
            return halo[0, f, x + 3]
        if x >= level.rows:
            return halo[1, f, x - level.rows]
        return level.row(f, x)

    def beside(g):
        spans = [(0, rim), (tiles - rim, tiles)] if g is None else [(rim + 6 * g, rim + 6 * g + 6)]
        start = za.shape[0] - tiles
        sides = []
        for swap_ab in (False, True):
            for a, b in spans:
                got_a, got_b = za[start + a : start + b], zb[a:b]
                pair = (got_a, got_b) if swap_ab else (got_b, got_a)
                sides.append(jnp.where(even, *pair).reshape((b - a) * 8, za.shape[2]))
        return split(jnp.concatenate(sides, axis=0))

    for g in groups:
        if g is None:
            xs = [*range(RIM), *range(level.rows - RIM, level.rows)]
        else:
            xs = range(RIM + g * GROUP, RIM + (g + 1) * GROUP)
        ut, ur, p = [level.group(f, g) for f in (2, 3, 4)]
        _, cols, radial = ut.shape
        inv_h = inverse_step(cols, radial)
        side_hi, side_lo = beside(g)
        p_hi, p_lo = split(p.reshape(GROUP * cols, radial))
        ut_hi, ut_lo = split(ut.reshape(GROUP * cols, radial))
        ur_hi, ur_lo = split(ur.reshape(GROUP * cols, radial))

        def across(which, hi, lo):
            hi = jnp.concatenate([hi, side_hi], axis=0)
            lo = jnp.concatenate([lo, side_lo], axis=0)
            return dot(tmat[which, 0], hi) + dot(tmat[which, 0], lo) + dot(tmat[which, 1], hi)

        def outward(which, hi, lo):
            return dot(hi, rmat[which, 0]) + dot(lo, rmat[which, 0]) + dot(hi, rmat[which, 1])

        div_tr = across(0, ut_hi, ut_lo) * inv_h + outward(0, ur_hi, ur_lo)
        p_t = across(1, p_hi, p_lo) * inv_h
        p_r = outward(1, p_hi, p_lo)
        for i, x in enumerate(xs):
            part = slice(i * cols, (i + 1) * cols)
            d = [along(lambda y: row(f, y), x) for f in range(5)]
            div = d[1] + div_tr[part]
            finish(
                x,
                [
                    -mach_number * d[0] - div,
                    -mach_number * d[1] - d[4],
                    -mach_number * d[2] - p_t[part],
                    -mach_number * d[3] - p_r[part],
                    -mach_number * d[4] - div,
                ],
            )


def start_body(state, za, zb, xa, xb, tmat, rmat, k_mid, k_rim, halo):
    fill_halo(halo, xa, xb)
    level, out = Whole(state), Parts(k_mid, k_rim)

    def finish(x, tend):
        for f in range(5):
            out.store(f, x, tend[f])

    apply_operator(level, [*range(k_mid.shape[1] // GROUP), None], za, zb, tmat, rmat, finish, halo)


def inner_stage_body(factor, level, base, za, zb, tmat, rmat, out_mid):
    def finish(x, tend):
        for f in range(5):
            out_mid[f, x - RIM] = base.row(f, x) + factor * tend[f]

    apply_operator(level, range(out_mid.shape[1] // GROUP), za, zb, tmat, rmat, finish)


def rim_stage_body(factor, level, base, za, zb, xa, xb, tmat, rmat, out_mid, out_rim, to_xa, to_xb, to_za, to_zb, halo):
    fill_halo(halo, xa, xb)
    out = Parts(out_mid, out_rim)

    def finish(x, tend):
        for f in range(5):
            out.store(f, x, base.row(f, x) + factor * tend[f])

    apply_operator(level, [None], za, zb, tmat, rmat, finish, halo)
    write_x(out, to_xa, to_xb)
    write_z(out, to_za, to_zb)


def last_finish(fields, k, store):
    def finish(x, tend):
        for f in range(5):
            store(f, x, fields[f, x] + time_step * k.row(f, x) + (0.5 * time_step * time_step) * tend[f])

    return finish


def inner_last_body(level, k, fields, za, zb, tmat, rmat, out_mid):
    def store(f, x, value):
        out_mid[f, x - RIM] = value

    groups = range(out_mid.shape[1] // GROUP)
    apply_operator(level, groups, za, zb, tmat, rmat, last_finish(fields, k, store))


def rim_last_body(level, k, fields, za, zb, xa, xb, tmat, rmat, out_mid, out, halo, result, sems):
    rows = level.rows
    inner = pltpu.make_async_copy(out_mid, out.at[:, RIM : rows - RIM], sems.at[0])
    inner.start()
    fill_halo(halo, xa, xb)

    def store(f, x, value):
        result[f, x if x < RIM else x - rows + 2 * RIM] = value

    apply_operator(level, [None], za, zb, tmat, rmat, last_finish(fields, k, store), halo)
    copies = [
        pltpu.make_async_copy(result.at[:, 0:RIM], out.at[:, 0:RIM], sems.at[1]),
        pltpu.make_async_copy(result.at[:, RIM:], out.at[:, rows - RIM :], sems.at[2]),
    ]
    for copy in copies:
        copy.start()
    for copy in (inner, *copies):
        copy.wait()


def local(noise, half_width, owner, target_cell, fields):
    px, pa, fine = noise.shape
    cx, ca, radial = fields.shape[1:]
    ncols = px * pa
    most = ncols // 2
    n_az = lax.axis_size("az")
    inner = cx - 2 * RIM

    block = ((px, pa, fine), F32)
    even = is_even("ax")
    to_a = jnp.where(even, noise[px - HMAX :], noise[:HMAX])
    to_b = jnp.where(even, noise[:HMAX], noise[px - HMAX :])
    noise_a, noise_b = swap(to_a, to_b, "ax")
    send_x, send_z = ((15, ca, radial), F32), ((cx // 4 * 3, 8, radial), F32)
    sends = [send_x, send_x, send_z, send_z]
    xa, xb, za, zb = full_specs(edges_body, sends, [fields], name="edges", after=[to_a])
    uxa, uxb = swap(xa, xb, "ax")
    partial, half_width = full_specs(
        inner_body, [block, ((px, pa, fine), jnp.int32)], [noise, half_width], name="filter_inner", after=[za]
    )
    filtered, to_a, to_b = full_specs(
        first_body,
        [block, ((px // 2, 8, fine), F32), ((px // 2, 8, fine), F32)],
        [partial, half_width, noise_a, noise_b],
        [((2, HMAX, pa, fine), F32)],
        name="filter_axial",
    )
    got_a, got_b = swap(to_a, to_b, "az")
    (uzb,) = swap_b(zb, "az")
    uza = za
    pick, cells, own = full_specs(
        route_body,
        [((4 * most, ncols), BF16), ((4, 8, radial), F32), ((1, ncols), jnp.int32)],
        [owner.reshape(1, ncols), target_cell.reshape(1, ncols)],
        name="route",
        after=[filtered, uxa, uxb, uzb],
    )
    tiles = most // 8 + 1
    packet = ((tiles, 8, radial), F32)
    binned, xa, xb, za, zb = full_specs(
        second_body,
        [((ncols, radial), F32), packet, packet, ((tiles + send_z[0][0], 8, radial), F32), packet],
        [filtered, half_width, got_a, got_b, pick, cells, uza],
        [((px, 32, fine), F32), ((ncols, fine), BF16), ((ncols, fine), BF16)],
        name="filter_rest",
    )
    packets = (*swap(xa, xb, "ax"), *swap(za, zb, "az"))

    tmat = jnp.asarray(azimuth_matrices(ca))
    rmat = jnp.asarray(radial_matrices(float(ca * n_az), radial))
    mid, rim = ((5, inner, ca, radial), F32), ((5, 2 * RIM, ca, radial), F32)
    halo = ((2, 5, 3, ca, radial), F32)
    k_mid, k_rim = full_specs(
        start_body, [mid, rim], [fields, packets[2], uzb, uxa, uxb, tmat, rmat], [halo], name="operator", after=[binned]
    )
    p_mid, p_rim, *edges = full_specs(
        gather_body,
        [((inner, ca, radial), F32), ((2 * RIM, ca, radial), F32), *sends],
        [binned, own, *packets, k_mid, k_rim],
        name="gather",
    )
    k = [k_mid, k_rim, p_mid, p_rim]
    level = k
    for factor in (time_step / 4.0, time_step / 3.0):
        size = len(level)
        xa, xb = swap(edges[0], edges[1], "ax")
        za, zb = swap(edges[2], edges[3], "az")

        def body(*refs, factor=factor, size=size):
            inner_stage_body(factor, Parts(*refs[:size]), Parts(*refs[size : size + 4]), *refs[size + 4 :])

        (new_mid,) = full_specs(body, [mid], [*level, *k, za, zb, tmat, rmat], name="stage_inner", cost=COST)

        def body(*refs, factor=factor, size=size):
            rim_stage_body(factor, Parts(*refs[:size]), Parts(*refs[size : size + 4]), *refs[size + 4 :])

        new_rim, *edges = full_specs(
            body, [rim, *sends], [*level, *k, za, zb, xa, xb, tmat, rmat, new_mid], [halo], name="stage_rim"
        )
        level = [new_mid, new_rim]
    xa, xb = swap(edges[0], edges[1], "ax")
    za, zb = swap(edges[2], edges[3], "az")

    def body(*refs):
        inner_last_body(Parts(*refs[:2]), Parts(*refs[2:6]), *refs[6:])

    (new_mid,) = full_specs(body, [mid], [*level, *k, fields, za, zb, tmat, rmat], name="final_inner", cost=COST)

    def body(*refs):
        rim_last_body(Parts(*refs[:2]), Parts(*refs[2:6]), *refs[6:])

    (out,) = full_specs(
        body,
        [((5, cx, ca, radial), F32)],
        [*level, *k, fields, za, zb, xa, xb, tmat, rmat, new_mid],
        [halo, rim, pltpu.SemaphoreType.DMA((3,))],
        name="final_rim",
        out_specs=[ANY],
    )
    return out


def solution(mesh):
    return jax.shard_map(
        local,
        mesh=mesh,
        in_specs=(
            P("ax", "az", None),
            P("ax", "az", None),
            P(("ax", "az")),
            P(("ax", "az")),
            P(None, "ax", "az", None),
        ),
        out_specs=P(None, "ax", "az", None),
        check_vma=False,
    )
```

```python
import math

import numpy as np

import jax
import jax.numpy as jnp
from jax import lax
from jax.experimental import pallas as pl
from jax.experimental.pallas import tpu as pltpu
from jax.sharding import PartitionSpec as P

HMAX = 4
drp_coeffs = (0.770882380518, -0.166705904415, 0.02084314277)
mach_number = 0.5
time_step = 0.7
source_gain = 4.0
radial_step = 2.0
hub_ratio = 1.6

F32 = jnp.float32
BF16 = jnp.bfloat16
VM = pl.BlockSpec(memory_space=pltpu.VMEM)
ANY = pl.BlockSpec(memory_space=pl.ANY)
PARAMS = pltpu.CompilerParams(vmem_limit_bytes=24 * 1024 * 1024)
GROUP = 8
RIM = 4
COST = 1 << 37


def np_split(matrix):
    hi = matrix.astype(np.float32).astype(BF16)
    lo = (matrix - hi.astype(np.float64)).astype(np.float32).astype(BF16)
    return hi, lo


def filter_table():
    table = np.zeros((HMAX + 1, HMAX))
    for h in range(1, HMAX + 1):
        weights = [math.exp(-2.0 * k * k / (h * h)) if k <= h else 0.0 for k in range(HMAX + 1)]
        total = weights[0] + 2.0 * sum(weights[1:])
        table[:, h - 1] = [w / total for w in weights]
    return table


def radial_rows(na_total, radial):
    base = na_total / (2.0 * math.pi)
    radius = base / hub_ratio + radial_step * (np.arange(radial) + 0.5)
    return base / radius, 1.0 / radius


def radial_matrices(na_total, radial):
    diff = np.zeros((radial, radial))
    for s, a in zip((1, 2, 3), drp_coeffs):
        for j in range(radial):
            if j + s < radial:
                diff[j + s, j] += a / radial_step
            if j - s >= 0:
                diff[j - s, j] -= a / radial_step
    with_r = diff + np.diag(radial_rows(na_total, radial)[1])
    return np.stack([np.stack(np_split(with_r)), np.stack(np_split(diff))])


def azimuth_matrices(cols):
    packed = GROUP * 6
    full = np.zeros((2, GROUP * cols, GROUP * cols + 2 * packed))
    for which in range(2):
        for x in range(GROUP):
            for i in range(cols):
                for s, a in zip((1, 2, 3), drp_coeffs):
                    for j, sign in ((i + s, 1.0), (i - s, -1.0)):
                        if 0 <= j < cols:
                            at = x * cols + j
                        else:
                            m = j + 3 if j < 0 else j - cols
                            tile, row = (x % 4, m) if x % 4 < 3 else (m, 3)
                            at = GROUP * cols + (x // 4 * 3 + tile) * 8 + row + 4 * which
                            at += packed if j >= cols else 0
                        full[which, x * cols + i, at] += sign * a
    return np.stack([np.stack(np_split(full[w])) for w in range(2)])


def split(x):
    hi = x.astype(BF16)
    return hi, (x - hi.astype(F32)).astype(BF16)


def dot(a, b):
    return lax.dot_general(a, b, (((1,), (0,)), ((), ())), preferred_element_type=F32)


def is_even(axis):
    return lax.rem(lax.axis_index(axis), 2) == 0


def swap(to_a, to_b, axis):
    devices = lax.axis_size(axis)
    pairs_a = [(i, i ^ 1) for i in range(devices)]
    pairs_b = [(i, (i - 1) % devices if i % 2 == 0 else (i + 1) % devices) for i in range(devices)]
    return lax.ppermute(to_a, axis, pairs_a), lax.ppermute(to_b, axis, pairs_b)


def full_specs(body, outs, args, scratch=(), name=None, out_specs=None, after=(), cost=0):
    skip = len(args)

    def run(*refs):
        body(*refs[:skip], *refs[skip + len(after) :])

    return pl.pallas_call(
        run,
        out_shape=[jax.ShapeDtypeStruct(s, d) for s, d in outs],
        in_specs=[VM] * skip + [ANY] * len(after),
        out_specs=out_specs or [VM] * len(outs),
        scratch_shapes=[pltpu.VMEM(*s) if isinstance(s, tuple) else s for s in scratch],
        compiler_params=PARAMS,
        name=name,
        cost_estimate=pl.CostEstimate(flops=cost, bytes_accessed=0, transcendentals=0),
    )(*args, *after)


def route_body(owner_ref, target_ref, pick_ref, cells_ref, own_ref):
    n_ax, n_az = lax.axis_size("ax"), lax.axis_size("az")
    ax, az = lax.axis_index("ax"), lax.axis_index("az")
    step_x = jnp.where(lax.rem(ax, 2) == 0, 1, -1)
    step_z = jnp.where(lax.rem(az, 2) == 0, 1, -1)
    me = ax * n_az + az
    b_x = ax - step_x
    ids = [
        (ax + step_x) * n_az + az,
        jnp.where((b_x >= 0) & (b_x < n_ax), b_x * n_az + az, -1),
        ax * n_az + lax.rem(az + step_z + n_az, n_az),
        ax * n_az + lax.rem(az - step_z + n_az, n_az),
    ]
    owner = owner_ref[...]
    target = target_ref[...]
    ncols = owner.shape[1]
    most = ncols // 2
    own_ref[...] = jnp.where(owner == me, target, -1)
    row = lax.broadcasted_iota(jnp.int32, (8, ncols), 0)
    marks = jnp.zeros((8, ncols), F32)
    for d, i in enumerate(ids):
        marks = jnp.where((row == d) & (owner == i), 1.0, marks)
    before = lax.broadcasted_iota(jnp.int32, (ncols, ncols), 0) < lax.broadcasted_iota(jnp.int32, (ncols, ncols), 1)
    rank = dot(marks.astype(BF16), jnp.where(before, 1.0, 0.0).astype(BF16))
    coarse = (target // 32).astype(F32)
    fine = (target % 32).astype(F32)
    digits = jnp.where(row == 0, coarse, jnp.where(row == 1, fine, 0.0)).astype(BF16)
    slot = lax.broadcasted_iota(jnp.int32, (most, ncols), 0).astype(F32)
    for d in range(4):
        wanted = jnp.where(marks[d : d + 1] > 0.0, rank[d : d + 1], -1.0)
        pick = jnp.where(slot == wanted, 1.0, 0.0).astype(BF16)
        pick_ref[d * most : (d + 1) * most, :] = pick
        found = lax.dot_general(digits, pick, (((1,), (1,)), ((), ())), preferred_element_type=F32)
        cells_ref[d, :, :] = jnp.zeros(cells_ref.shape[1:], F32)
        cells_ref[d, 0:1, 0:most] = found[0:1] * 32.0 + found[1:2]


def weights_of(h):
    table = filter_table()
    le = [h <= 1, h <= 2, h <= 3]
    out = []
    for k in range(HMAX + 1):
        value = jnp.full(h.shape, table[k, 3], F32)
        for j in (2, 1, 0):
            if j > 0 and table[k, j] == 0.0 and table[k, j - 1] == 0.0:
                value = jnp.where(le[j], 0.0, value)
                break
            value = jnp.where(le[j], table[k, j], value)
        out.append(value)
    return out


def inner_body(noise_ref, half_ref, first_ref, kept_ref):
    rows = noise_ref.shape[0]
    kept_ref[...] = half_ref[...]
    for x in range(rows):
        w = weights_of(half_ref[x])
        total = w[0] * noise_ref[x]
        for k in range(1, HMAX + 1):
            near = [noise_ref[y] for y in (x - k, x + k) if 0 <= y < rows]
            if near:
                total = total + w[k] * (near[0] + near[1] if len(near) == 2 else near[0])
        first_ref[x] = total


def first_body(
    inner_ref, half_ref, got_a_ref, got_b_ref, edge_a_ref, edge_b_ref, first_ref, to_a_ref, to_b_ref, halo
):
    n_ax, ax = lax.axis_size("ax"), lax.axis_index("ax")
    even_x, even_z = is_even("ax"), is_even("az")
    rows, _, fine = half_ref.shape
    halo[0] = jnp.where(ax > 0, jnp.where(even_x, got_b_ref[...], got_a_ref[...]), 0.0)
    halo[1] = jnp.where(ax < n_ax - 1, jnp.where(even_x, got_a_ref[...], got_b_ref[...]), 0.0)
    for x in range(HMAX, rows - HMAX):
        first_ref[x] = inner_ref[x]
    for i in range(HMAX):
        w = weights_of(half_ref[i])
        total = inner_ref[i]
        for k in range(i + 1, HMAX + 1):
            total = total + w[k] * halo[0, HMAX + i - k]
        first_ref[i] = total
        x = rows - 1 - i
        w = weights_of(half_ref[x])
        total = inner_ref[x]
        for k in range(i + 1, HMAX + 1):
            total = total + w[k] * halo[1, k - i - 1]
        first_ref[x] = total
    half = rows // 2
    low = lax.broadcasted_iota(jnp.int32, (8, fine), 0) < 4
    for x in range(half):
        last = jnp.where(low, pltpu.roll(first_ref[x, 8:16], 4, 0), first_ref[x + half, 8:16])
        begin = jnp.where(low, first_ref[x, 0:8], pltpu.roll(first_ref[x + half, 0:8], 4, 0))
        for ref, value in ((to_a_ref, jnp.where(even_z, last, begin)), (to_b_ref, jnp.where(even_z, begin, last))):
            ref[x] = value[:, : fine // 2]
            ref[half + x] = value[:, fine // 2 :]
    to_a_ref[rows:] = edge_a_ref[...]
    to_b_ref[rows:] = edge_b_ref[...]


def second_body(
    first_ref, half_ref, got_a_ref, got_b_ref, pick_ref, cells_ref,
    own_ref, to_xa, to_xb, to_za, to_zb, wide, fine_hi, fine_lo,
):
    even = is_even("az")
    rows, cols, fine = first_ref.shape
    half = rows // 2
    for x in range(half):
        got_a, got_b = [jnp.concatenate([got[x], got[half + x]], axis=1) for got in (got_a_ref, got_b_ref)]
        before = jnp.where(even, got_b, got_a)
        after = jnp.where(even, got_a, got_b)
        wide[x, 0:8] = pltpu.roll(before, 4, 0)
        wide[x + half, 0:8] = before
        wide[x, 24:32] = after
        wide[x + half, 24:32] = pltpu.roll(after, 4, 0)
    lane = lax.broadcasted_iota(jnp.int32, (cols, fine), 1)
    for x in range(rows):
        wide[x, 8:24] = first_ref[x]
    for x in range(rows):
        w = weights_of(half_ref[x])
        total = w[0] * first_ref[x]
        for k in range(1, HMAX + 1):
            total = total + w[k] * (wide[x, 8 - k : 24 - k] + wide[x, 8 + k : 24 + k])
        result = w[0] * total
        for k in range(1, HMAX + 1):
            up = jnp.where(lane < fine - k, pltpu.roll(total, fine - k, 1), 0.0)
            down = jnp.where(lane >= k, pltpu.roll(total, k, 1), 0.0)
            result = result + w[k] * (up + down)
        hi, lo = split(result)
        fine_hi[x * cols : (x + 1) * cols] = hi
        fine_lo[x * cols : (x + 1) * cols] = lo
    radial = own_ref.shape[1]
    above = lax.broadcasted_iota(jnp.int32, (fine, radial), 0) - lax.broadcasted_iota(
        jnp.int32, (fine, radial), 1
    ) * (fine // radial)
    bins = jnp.where((above >= 0) & (above < fine // radial), source_gain, 0.0).astype(BF16)
    binned = dot(fine_hi[...], bins) + dot(fine_lo[...], bins)
    own_ref[...] = binned
    hi, lo = split(binned)
    most = pick_ref.shape[0] // 4
    for d, out in enumerate((to_xa, to_xb, to_za, to_zb)):
        pick = pick_ref[d * most : (d + 1) * most]
        tiles = most // 8
        out[0:tiles] = (dot(pick, hi) + dot(pick, lo)).reshape(tiles, 8, radial)
        out[tiles] = cells_ref[d]
    for out in (to_za, to_zb):
        out[most // 8 + 1] = jnp.zeros(out.shape[1:], F32)


def gather_body(
    binned_ref, own_ref, xa, xb, za, zb, k_mid, k_rim, p_mid, p_rim, to_xa, to_xb, to_za, to_zb
):
    mid, cols, radial = p_mid.shape
    cells = (mid + 2 * RIM) * cols
    most = 8 * (xa.shape[0] - 1)

    def onehot(row):
        at = lax.broadcasted_iota(jnp.int32, (cells, row.shape[1]), 0)
        return jnp.where(at == row, 1.0, 0.0).astype(BF16)

    mats = [onehot(own_ref[...])]
    packets = [binned_ref[...]]
    for got in (xa, xb, za, zb):
        tiles = most // 8
        mats.append(onehot(got[tiles, 0:1, 0:most].astype(jnp.int32)))
        packets.append(got[0:tiles].reshape(most, radial))
    mat = jnp.concatenate(mats, axis=1)
    hi, lo = split(jnp.concatenate(packets, axis=0))
    q = (dot(mat, hi) + dot(mat, lo)).reshape(mid + 2 * RIM, cols, radial)
    p_rim[0:RIM] = k_rim[4, 0:RIM] + q[0:RIM]
    p_mid[...] = k_mid[4] + q[RIM : RIM + mid]
    p_rim[RIM:] = k_rim[4, RIM:] + q[RIM + mid :]
    level = Parts(k_mid, k_rim, p_mid, p_rim)
    write_x(level, to_xa, to_xb)
    write_z(level, to_za, to_zb)


class Whole:
    def __init__(self, ref):
        self.ref = ref
        self.rows = ref.shape[1]

    def row(self, f, x):
        return self.ref[f, x]

    def group(self, f, g):
        if g is None:
            return jnp.concatenate([self.ref[f, 0:RIM], self.ref[f, self.rows - RIM :]], axis=0)
        return self.ref[f, RIM + g * GROUP : RIM + (g + 1) * GROUP]


class Parts:
    def __init__(self, mid, rim, p_mid=None, p_rim=None):
        self.arrays = (mid, rim, p_mid, p_rim)
        self.rows = mid.shape[1] + 2 * RIM

    def pick(self, f):
        mid, rim, p_mid, p_rim = self.arrays
        if f == 4 and p_mid is not None:
            return p_mid, p_rim
        return mid.at[f], rim.at[f]

    def row(self, f, x):
        mid, rim = self.pick(f)
        if RIM <= x < self.rows - RIM:
            return mid[x - RIM]
        return rim[x if x < RIM else x - self.rows + 2 * RIM]

    def group(self, f, g):
        mid, rim = self.pick(f)
        return rim[...] if g is None else mid[g * GROUP : (g + 1) * GROUP]

    def store(self, f, x, value):
        mid, rim = self.pick(f)
        if RIM <= x < self.rows - RIM:
            mid[x - RIM] = value
        else:
            rim[x if x < RIM else x - self.rows + 2 * RIM] = value


def join_last(ut, p):
    low = lax.broadcasted_iota(jnp.int32, ut.shape, 0) < 4
    return jnp.where(low, pltpu.roll(ut, 3, 0), pltpu.roll(p, 7, 0))


def join_first(ut, p):
    low = lax.broadcasted_iota(jnp.int32, ut.shape, 0) < 4
    return jnp.where(low, ut, pltpu.roll(p, 4, 0))


def write_x(level, to_xa, to_xb):
    even = is_even("ax")
    for f in range(5):
        for i in range(3):
            first, last = level.row(f, i), level.row(f, level.rows - 3 + i)
            to_xa[3 * f + i] = jnp.where(even, last, first)
            to_xb[3 * f + i] = jnp.where(even, first, last)


def write_z(level, to_za, to_zb):
    even = is_even("az")
    row = None
    for x in range(0, level.rows, 4):
        first, last = [], []
        for y in range(x, x + 4):
            ut, p = level.row(2, y), level.row(4, y)
            first.append(join_first(ut[0:8], p[0:8]))
            last.append(join_last(ut[8:16], p[8:16]))
        if row is None:
            row = lax.broadcasted_iota(jnp.int32, first[0].shape, 0) % 4 == 3
        for t in range(3):
            shift = 3 - t
            one = jnp.where(row, pltpu.roll(first[3], shift, 0), first[t])
            two = jnp.where(row, pltpu.roll(last[3], shift, 0), last[t])
            to_za[x // 4 * 3 + t] = jnp.where(even, two, one)
            to_zb[x // 4 * 3 + t] = jnp.where(even, one, two)


def edges_body(state, to_xa, to_xb, to_za, to_zb):
    level = Whole(state)
    write_x(level, to_xa, to_xb)
    write_z(level, to_za, to_zb)


def fill_halo(halo, xa, xb):
    n_ax, ax = lax.axis_size("ax"), lax.axis_index("ax")
    even = is_even("ax")
    for f in range(halo.shape[1]):
        a, b = xa[3 * f : 3 * f + 3], xb[3 * f : 3 * f + 3]
        halo[0, f] = jnp.where(ax > 0, jnp.where(even, b, a), 0.0)
        halo[1, f] = jnp.where(ax < n_ax - 1, jnp.where(even, a, b), 0.0)


def inverse_step(cols, radial):
    base = cols * lax.axis_size("az") / (2.0 * math.pi)
    at = lax.broadcasted_iota(jnp.int32, (1, radial), 1).astype(F32)
    return base / (base / hub_ratio + radial_step * (at + 0.5))


def along(row, x):
    total = drp_coeffs[0] * (row(x + 1) - row(x - 1))
    for s in (2, 3):
        total = total + drp_coeffs[s - 1] * (row(x + s) - row(x - s))
    return total


def apply_operator(level, groups, za, zb, tmat, rmat, finish, halo=None):
    even = is_even("az")
    tiles = level.rows // 4 * 3
    rim = RIM // 4 * 3

    def row(f, x):
        if x < 0:
            return halo[0, f, x + 3]
        if x >= level.rows:
            return halo[1, f, x - level.rows]
        return level.row(f, x)

    def beside(g):
        spans = [(0, rim), (tiles - rim, tiles)] if g is None else [(rim + 6 * g, rim + 6 * g + 6)]
        start = za.shape[0] - tiles
        sides = []
        for swap_ab in (False, True):
            for a, b in spans:
                got_a, got_b = za[start + a : start + b], zb[start + a : start + b]
                pair = (got_a, got_b) if swap_ab else (got_b, got_a)
                sides.append(jnp.where(even, *pair).reshape((b - a) * 8, za.shape[2]))
        return split(jnp.concatenate(sides, axis=0))

    for g in groups:
        if g is None:
            xs = [*range(RIM), *range(level.rows - RIM, level.rows)]
        else:
            xs = range(RIM + g * GROUP, RIM + (g + 1) * GROUP)
        ut, ur, p = [level.group(f, g) for f in (2, 3, 4)]
        _, cols, radial = ut.shape
        inv_h = inverse_step(cols, radial)
        side_hi, side_lo = beside(g)
        p_hi, p_lo = split(p.reshape(GROUP * cols, radial))
        ut_hi, ut_lo = split(ut.reshape(GROUP * cols, radial))
        ur_hi, ur_lo = split(ur.reshape(GROUP * cols, radial))

        def across(which, hi, lo):
            hi = jnp.concatenate([hi, side_hi], axis=0)
            lo = jnp.concatenate([lo, side_lo], axis=0)
            return dot(tmat[which, 0], hi) + dot(tmat[which, 0], lo) + dot(tmat[which, 1], hi)

        def outward(which, hi, lo):
            return dot(hi, rmat[which, 0]) + dot(lo, rmat[which, 0]) + dot(hi, rmat[which, 1])

        div_tr = across(0, ut_hi, ut_lo) * inv_h + outward(0, ur_hi, ur_lo)
        p_t = across(1, p_hi, p_lo) * inv_h
        p_r = outward(1, p_hi, p_lo)
        for i, x in enumerate(xs):
            part = slice(i * cols, (i + 1) * cols)
            d = [along(lambda y: row(f, y), x) for f in range(5)]
            div = d[1] + div_tr[part]
            finish(
                x,
                [
                    -mach_number * d[0] - div,
                    -mach_number * d[1] - d[4],
                    -mach_number * d[2] - p_t[part],
                    -mach_number * d[3] - p_r[part],
                    -mach_number * d[4] - div,
                ],
            )


def start_body(state, za, zb, xa, xb, tmat, rmat, k_mid, k_rim, halo):
    fill_halo(halo, xa, xb)
    level, out = Whole(state), Parts(k_mid, k_rim)

    def finish(x, tend):
        for f in range(5):
            out.store(f, x, tend[f])

    apply_operator(level, [*range(k_mid.shape[1] // GROUP), None], za, zb, tmat, rmat, finish, halo)


def inner_stage_body(factor, level, base, za, zb, tmat, rmat, out_mid):
    def finish(x, tend):
        for f in range(5):
            out_mid[f, x - RIM] = base.row(f, x) + factor * tend[f]

    apply_operator(level, range(out_mid.shape[1] // GROUP), za, zb, tmat, rmat, finish)


def rim_stage_body(factor, level, base, za, zb, xa, xb, tmat, rmat, out_mid, out_rim, to_xa, to_xb, to_za, to_zb, halo):
    fill_halo(halo, xa, xb)
    out = Parts(out_mid, out_rim)

    def finish(x, tend):
        for f in range(5):
            out.store(f, x, base.row(f, x) + factor * tend[f])

    apply_operator(level, [None], za, zb, tmat, rmat, finish, halo)
    write_x(out, to_xa, to_xb)
    write_z(out, to_za, to_zb)


def last_finish(fields, k, store):
    def finish(x, tend):
        for f in range(5):
            store(f, x, fields[f, x] + time_step * k.row(f, x) + (0.5 * time_step * time_step) * tend[f])

    return finish


def inner_last_body(level, k, fields, za, zb, tmat, rmat, out_mid):
    def store(f, x, value):
        out_mid[f, x - RIM] = value

    groups = range(out_mid.shape[1] // GROUP)
    apply_operator(level, groups, za, zb, tmat, rmat, last_finish(fields, k, store))


def rim_last_body(level, k, fields, za, zb, xa, xb, tmat, rmat, out_mid, out, halo, result, sems):
    rows = level.rows
    inner = pltpu.make_async_copy(out_mid, out.at[:, RIM : rows - RIM], sems.at[0])
    inner.start()
    fill_halo(halo, xa, xb)

    def store(f, x, value):
        result[f, x if x < RIM else x - rows + 2 * RIM] = value

    apply_operator(level, [None], za, zb, tmat, rmat, last_finish(fields, k, store), halo)
    copies = [
        pltpu.make_async_copy(result.at[:, 0:RIM], out.at[:, 0:RIM], sems.at[1]),
        pltpu.make_async_copy(result.at[:, RIM:], out.at[:, rows - RIM :], sems.at[2]),
    ]
    for copy in copies:
        copy.start()
    for copy in (inner, *copies):
        copy.wait()


def local(noise, half_width, owner, target_cell, fields):
    px, pa, fine = noise.shape
    cx, ca, radial = fields.shape[1:]
    ncols = px * pa
    most = ncols // 2
    n_az = lax.axis_size("az")
    inner = cx - 2 * RIM

    block = ((px, pa, fine), F32)
    even = is_even("ax")
    to_a = jnp.where(even, noise[px - HMAX :], noise[:HMAX])
    to_b = jnp.where(even, noise[:HMAX], noise[px - HMAX :])
    noise_a, noise_b = swap(to_a, to_b, "ax")
    send_x, send_z = ((15, ca, radial), F32), ((cx // 4 * 3, 8, radial), F32)
    sends = [send_x, send_x, send_z, send_z]
    xa, xb, za, zb = full_specs(edges_body, sends, [fields], name="edges", after=[to_a])
    uxa, uxb = swap(xa, xb, "ax")
    partial, half_width = full_specs(
        inner_body, [block, ((px, pa, fine), jnp.int32)], [noise, half_width], name="filter_inner", after=[za]
    )
    long_z = ((px + send_z[0][0], 8, fine // 2), F32)
    filtered, to_a, to_b = full_specs(
        first_body,
        [block, long_z, long_z],
        [partial, half_width, noise_a, noise_b, za, zb],
        [((2, HMAX, pa, fine), F32)],
        name="filter_axial",
    )
    got_a, got_b = swap(to_a, to_b, "az")
    pick, cells, own = full_specs(
        route_body,
        [((4 * most, ncols), BF16), ((4, 8, radial), F32), ((1, ncols), jnp.int32)],
        [owner.reshape(1, ncols), target_cell.reshape(1, ncols)],
        name="route",
        after=[filtered],
    )
    tiles = most // 8 + 1
    packet, packet_z = ((tiles, 8, radial), F32), ((tiles + 1, 8, radial), F32)
    binned, xa, xb, za, zb = full_specs(
        second_body,
        [((ncols, radial), F32), packet, packet, packet_z, packet_z],
        [filtered, half_width, got_a, got_b, pick, cells],
        [((px, 32, fine), F32), ((ncols, fine), BF16), ((ncols, fine), BF16)],
        name="filter_rest",
    )
    packets = (*swap(xa, xb, "ax"), *swap(za, zb, "az"))

    tmat = jnp.asarray(azimuth_matrices(ca))
    rmat = jnp.asarray(radial_matrices(float(ca * n_az), radial))
    mid, rim = ((5, inner, ca, radial), F32), ((5, 2 * RIM, ca, radial), F32)
    halo = ((2, 5, 3, ca, radial), F32)
    k_mid, k_rim = full_specs(
        start_body, [mid, rim], [fields, got_a, got_b, uxa, uxb, tmat, rmat], [halo], name="operator", after=[binned]
    )
    p_mid, p_rim, *edges = full_specs(
        gather_body,
        [((inner, ca, radial), F32), ((2 * RIM, ca, radial), F32), *sends],
        [binned, own, *packets, k_mid, k_rim],
        name="gather",
    )
    k = [k_mid, k_rim, p_mid, p_rim]
    level = k
    for factor in (time_step / 4.0, time_step / 3.0):
        size = len(level)
        xa, xb = swap(edges[0], edges[1], "ax")
        za, zb = swap(edges[2], edges[3], "az")

        def body(*refs, factor=factor, size=size):
            inner_stage_body(factor, Parts(*refs[:size]), Parts(*refs[size : size + 4]), *refs[size + 4 :])

        (new_mid,) = full_specs(body, [mid], [*level, *k, za, zb, tmat, rmat], name="stage_inner", cost=COST)

        def body(*refs, factor=factor, size=size):
            rim_stage_body(factor, Parts(*refs[:size]), Parts(*refs[size : size + 4]), *refs[size + 4 :])

        new_rim, *edges = full_specs(
            body, [rim, *sends], [*level, *k, za, zb, xa, xb, tmat, rmat, new_mid], [halo], name="stage_rim"
        )
        level = [new_mid, new_rim]
    xa, xb = swap(edges[0], edges[1], "ax")
    za, zb = swap(edges[2], edges[3], "az")

    def body(*refs):
        inner_last_body(Parts(*refs[:2]), Parts(*refs[2:6]), *refs[6:])

    (new_mid,) = full_specs(body, [mid], [*level, *k, fields, za, zb, tmat, rmat], name="final_inner", cost=COST)

    def body(*refs):
        rim_last_body(Parts(*refs[:2]), Parts(*refs[2:6]), *refs[6:])

    (out,) = full_specs(
        body,
        [((5, cx, ca, radial), F32)],
        [*level, *k, fields, za, zb, xa, xb, tmat, rmat, new_mid],
        [halo, rim, pltpu.SemaphoreType.DMA((3,))],
        name="final_rim",
        out_specs=[ANY],
    )
    return out


def solution(mesh):
    return jax.shard_map(
        local,
        mesh=mesh,
        in_specs=(
            P("ax", "az", None),
            P("ax", "az", None),
            P(("ax", "az")),
            P(("ax", "az")),
            P(None, "ax", "az", None),
        ),
        out_specs=P(None, "ax", "az", None),
        check_vma=False,
    )
```

```python
import math

import numpy as np

import jax
import jax.numpy as jnp
from jax import lax
from jax.experimental import pallas as pl
from jax.experimental.pallas import tpu as pltpu
from jax.sharding import PartitionSpec as P

HMAX = 4
drp_coeffs = (0.770882380518, -0.166705904415, 0.02084314277)
mach_number = 0.5
time_step = 0.7
source_gain = 4.0
radial_step = 2.0
hub_ratio = 1.6

F32 = jnp.float32
BF16 = jnp.bfloat16
VM = pl.BlockSpec(memory_space=pltpu.VMEM)
ANY = pl.BlockSpec(memory_space=pl.ANY)
PARAMS = pltpu.CompilerParams(vmem_limit_bytes=24 * 1024 * 1024)
GROUP = 8
RIM = 4
COST = 1 << 37


def np_split(matrix):
    hi = matrix.astype(np.float32).astype(BF16)
    lo = (matrix - hi.astype(np.float64)).astype(np.float32).astype(BF16)
    return hi, lo


def filter_table():
    table = np.zeros((HMAX + 1, HMAX))
    for h in range(1, HMAX + 1):
        weights = [math.exp(-2.0 * k * k / (h * h)) if k <= h else 0.0 for k in range(HMAX + 1)]
        total = weights[0] + 2.0 * sum(weights[1:])
        table[:, h - 1] = [w / total for w in weights]
    return table


def radial_rows(na_total, radial):
    base = na_total / (2.0 * math.pi)
    radius = base / hub_ratio + radial_step * (np.arange(radial) + 0.5)
    return base / radius, 1.0 / radius


def radial_matrices(na_total, radial):
    diff = np.zeros((radial, radial))
    for s, a in zip((1, 2, 3), drp_coeffs):
        for j in range(radial):
            if j + s < radial:
                diff[j + s, j] += a / radial_step
            if j - s >= 0:
                diff[j - s, j] -= a / radial_step
    with_r = diff + np.diag(radial_rows(na_total, radial)[1])
    return np.stack([np.stack(np_split(with_r)), np.stack(np_split(diff))])


def azimuth_matrices(cols):
    packed = GROUP * 6
    full = np.zeros((2, GROUP * cols, GROUP * cols + 2 * packed))
    for which in range(2):
        for x in range(GROUP):
            for i in range(cols):
                for s, a in zip((1, 2, 3), drp_coeffs):
                    for j, sign in ((i + s, 1.0), (i - s, -1.0)):
                        if 0 <= j < cols:
                            at = x * cols + j
                        else:
                            m = j + 3 if j < 0 else j - cols
                            tile, row = (x % 4, m) if x % 4 < 3 else (m, 3)
                            at = GROUP * cols + (x // 4 * 3 + tile) * 8 + row + 4 * which
                            at += packed if j >= cols else 0
                        full[which, x * cols + i, at] += sign * a
    return np.stack([np.stack(np_split(full[w])) for w in range(2)])


def split(x):
    hi = x.astype(BF16)
    return hi, (x - hi.astype(F32)).astype(BF16)


def dot(a, b):
    return lax.dot_general(a, b, (((1,), (0,)), ((), ())), preferred_element_type=F32)


def is_even(axis):
    return lax.rem(lax.axis_index(axis), 2) == 0


def swap(to_a, to_b, axis):
    devices = lax.axis_size(axis)
    pairs_a = [(i, i ^ 1) for i in range(devices)]
    pairs_b = [(i, (i - 1) % devices if i % 2 == 0 else (i + 1) % devices) for i in range(devices)]
    return lax.ppermute(to_a, axis, pairs_a), lax.ppermute(to_b, axis, pairs_b)


def full_specs(body, outs, args, scratch=(), name=None, in_specs=None, out_specs=None, after=(), cost=0, alias=None):
    skip = len(args)

    def run(*refs):
        body(*refs[:skip], *refs[skip + len(after) :])

    return pl.pallas_call(
        run,
        out_shape=[jax.ShapeDtypeStruct(s, d) for s, d in outs],
        in_specs=(in_specs or [VM] * skip) + [ANY] * len(after),
        input_output_aliases=alias or {},
        out_specs=out_specs or [VM] * len(outs),
        scratch_shapes=[pltpu.VMEM(*s) if isinstance(s, tuple) else s for s in scratch],
        compiler_params=PARAMS,
        name=name,
        cost_estimate=pl.CostEstimate(flops=cost, bytes_accessed=0, transcendentals=0),
    )(*args, *after)


def route_body(owner_ref, target_ref, pick_ref, cells_ref, own_ref):
    n_ax, n_az = lax.axis_size("ax"), lax.axis_size("az")
    ax, az = lax.axis_index("ax"), lax.axis_index("az")
    step_x = jnp.where(lax.rem(ax, 2) == 0, 1, -1)
    step_z = jnp.where(lax.rem(az, 2) == 0, 1, -1)
    me = ax * n_az + az
    b_x = ax - step_x
    ids = [
        (ax + step_x) * n_az + az,
        jnp.where((b_x >= 0) & (b_x < n_ax), b_x * n_az + az, -1),
        ax * n_az + lax.rem(az + step_z + n_az, n_az),
        ax * n_az + lax.rem(az - step_z + n_az, n_az),
    ]
    owner = owner_ref[...]
    target = target_ref[...]
    ncols = owner.shape[1]
    most = ncols // 2
    own_ref[...] = jnp.where(owner == me, target, -1)
    row = lax.broadcasted_iota(jnp.int32, (8, ncols), 0)
    marks = jnp.zeros((8, ncols), F32)
    for d, i in enumerate(ids):
        marks = jnp.where((row == d) & (owner == i), 1.0, marks)
    before = lax.broadcasted_iota(jnp.int32, (ncols, ncols), 0) < lax.broadcasted_iota(jnp.int32, (ncols, ncols), 1)
    rank = dot(marks.astype(BF16), jnp.where(before, 1.0, 0.0).astype(BF16))
    coarse = (target // 32).astype(F32)
    fine = (target % 32).astype(F32)
    digits = jnp.where(row == 0, coarse, jnp.where(row == 1, fine, 0.0)).astype(BF16)
    slot = lax.broadcasted_iota(jnp.int32, (most, ncols), 0).astype(F32)
    for d in range(4):
        wanted = jnp.where(marks[d : d + 1] > 0.0, rank[d : d + 1], -1.0)
        pick = jnp.where(slot == wanted, 1.0, 0.0).astype(BF16)
        pick_ref[d * most : (d + 1) * most, :] = pick
        found = lax.dot_general(digits, pick, (((1,), (1,)), ((), ())), preferred_element_type=F32)
        cells_ref[d, :, :] = jnp.zeros(cells_ref.shape[1:], F32)
        cells_ref[d, 0:1, 0:most] = found[0:1] * 32.0 + found[1:2]


def weights_of(h):
    table = filter_table()
    le = [h <= 1, h <= 2, h <= 3]
    out = []
    for k in range(HMAX + 1):
        value = jnp.full(h.shape, table[k, 3], F32)
        for j in (2, 1, 0):
            if j > 0 and table[k, j] == 0.0 and table[k, j - 1] == 0.0:
                value = jnp.where(le[j], 0.0, value)
                break
            value = jnp.where(le[j], table[k, j], value)
        out.append(value)
    return out


def inner_body(noise_ref, half_ref, first_ref, kept_ref):
    rows = noise_ref.shape[0]
    kept_ref[...] = half_ref[...]
    for x in range(rows):
        w = weights_of(half_ref[x])
        total = w[0] * noise_ref[x]
        for k in range(1, HMAX + 1):
            near = [noise_ref[y] for y in (x - k, x + k) if 0 <= y < rows]
            if near:
                total = total + w[k] * (near[0] + near[1] if len(near) == 2 else near[0])
        first_ref[x] = total


def first_body(
    inner_ref, half_ref, got_a_ref, got_b_ref, edge_a_ref, edge_b_ref, first_ref, to_a_ref, to_b_ref, halo
):
    n_ax, ax = lax.axis_size("ax"), lax.axis_index("ax")
    even_x, even_z = is_even("ax"), is_even("az")
    rows, _, fine = half_ref.shape
    halo[0] = jnp.where(ax > 0, jnp.where(even_x, got_b_ref[...], got_a_ref[...]), 0.0)
    halo[1] = jnp.where(ax < n_ax - 1, jnp.where(even_x, got_a_ref[...], got_b_ref[...]), 0.0)
    for x in range(HMAX, rows - HMAX):
        first_ref[x] = inner_ref[x]
    for i in range(HMAX):
        w = weights_of(half_ref[i])
        total = inner_ref[i]
        for k in range(i + 1, HMAX + 1):
            total = total + w[k] * halo[0, HMAX + i - k]
        first_ref[i] = total
        x = rows - 1 - i
        w = weights_of(half_ref[x])
        total = inner_ref[x]
        for k in range(i + 1, HMAX + 1):
            total = total + w[k] * halo[1, k - i - 1]
        first_ref[x] = total
    half = rows // 2
    low = lax.broadcasted_iota(jnp.int32, (8, fine), 0) < 4
    for x in range(half):
        last = jnp.where(low, pltpu.roll(first_ref[x, 8:16], 4, 0), first_ref[x + half, 8:16])
        begin = jnp.where(low, first_ref[x, 0:8], pltpu.roll(first_ref[x + half, 0:8], 4, 0))
        for ref, value in ((to_a_ref, jnp.where(even_z, last, begin)), (to_b_ref, jnp.where(even_z, begin, last))):
            ref[x] = value[:, : fine // 2]
            ref[half + x] = value[:, fine // 2 :]
    to_a_ref[rows:] = edge_a_ref[...]
    to_b_ref[rows:] = edge_b_ref[...]


def second_body(
    first_ref, half_ref, got_a_ref, got_b_ref, pick_ref, cells_ref,
    own_ref, to_xa, to_xb, to_za, to_zb, wide, fine_hi, fine_lo,
):
    even = is_even("az")
    rows, cols, fine = first_ref.shape
    half = rows // 2
    for x in range(half):
        got_a, got_b = [jnp.concatenate([got[x], got[half + x]], axis=1) for got in (got_a_ref, got_b_ref)]
        before = jnp.where(even, got_b, got_a)
        after = jnp.where(even, got_a, got_b)
        wide[x, 0:8] = pltpu.roll(before, 4, 0)
        wide[x + half, 0:8] = before
        wide[x, 24:32] = after
        wide[x + half, 24:32] = pltpu.roll(after, 4, 0)
    lane = lax.broadcasted_iota(jnp.int32, (cols, fine), 1)
    for x in range(rows):
        wide[x, 8:24] = first_ref[x]
    for x in range(rows):
        w = weights_of(half_ref[x])
        total = w[0] * first_ref[x]
        for k in range(1, HMAX + 1):
            total = total + w[k] * (wide[x, 8 - k : 24 - k] + wide[x, 8 + k : 24 + k])
        result = w[0] * total
        for k in range(1, HMAX + 1):
            up = jnp.where(lane < fine - k, pltpu.roll(total, fine - k, 1), 0.0)
            down = jnp.where(lane >= k, pltpu.roll(total, k, 1), 0.0)
            result = result + w[k] * (up + down)
        hi, lo = split(result)
        fine_hi[x * cols : (x + 1) * cols] = hi
        fine_lo[x * cols : (x + 1) * cols] = lo
    radial = own_ref.shape[1]
    above = lax.broadcasted_iota(jnp.int32, (fine, radial), 0) - lax.broadcasted_iota(
        jnp.int32, (fine, radial), 1
    ) * (fine // radial)
    bins = jnp.where((above >= 0) & (above < fine // radial), source_gain, 0.0).astype(BF16)
    binned = dot(fine_hi[...], bins) + dot(fine_lo[...], bins)
    own_ref[...] = binned
    hi, lo = split(binned)
    most = pick_ref.shape[0] // 4
    for d, out in enumerate((to_xa, to_xb, to_za, to_zb)):
        pick = pick_ref[d * most : (d + 1) * most]
        tiles = most // 8
        out[0:tiles] = (dot(pick, hi) + dot(pick, lo)).reshape(tiles, 8, radial)
        out[tiles] = cells_ref[d]
    for out in (to_za, to_zb):
        out[most // 8 + 1] = jnp.zeros(out.shape[1:], F32)


def gather_body(
    binned_ref, own_ref, xa, xb, za, zb, k_mid, k_rim, p_mid, p_rim, to_xa, to_xb, to_za, to_zb
):
    mid, cols, radial = p_mid.shape
    cells = (mid + 2 * RIM) * cols
    most = 8 * (xa.shape[0] - 1)

    def onehot(row):
        at = lax.broadcasted_iota(jnp.int32, (cells, row.shape[1]), 0)
        return jnp.where(at == row, 1.0, 0.0).astype(BF16)

    mats = [onehot(own_ref[...])]
    packets = [binned_ref[...]]
    for got in (xa, xb, za, zb):
        tiles = most // 8
        mats.append(onehot(got[tiles, 0:1, 0:most].astype(jnp.int32)))
        packets.append(got[0:tiles].reshape(most, radial))
    mat = jnp.concatenate(mats, axis=1)
    hi, lo = split(jnp.concatenate(packets, axis=0))
    q = (dot(mat, hi) + dot(mat, lo)).reshape(mid + 2 * RIM, cols, radial)
    p_rim[0:RIM] = k_rim[4, 0:RIM] + q[0:RIM]
    p_mid[...] = k_mid[4] + q[RIM : RIM + mid]
    p_rim[RIM:] = k_rim[4, RIM:] + q[RIM + mid :]
    level = Parts(k_mid, k_rim, p_mid, p_rim)
    write_x(level, to_xa, to_xb)
    write_z(level, range(0, level.rows, 4), to_za, to_zb)


class Whole:
    def __init__(self, ref):
        self.ref = ref
        self.rows = ref.shape[1]

    def row(self, f, x):
        return self.ref[f, x]

    def group(self, f, g):
        if g is None:
            return jnp.concatenate([self.ref[f, 0:RIM], self.ref[f, self.rows - RIM :]], axis=0)
        return self.ref[f, RIM + g * GROUP : RIM + (g + 1) * GROUP]


class Parts:
    def __init__(self, mid, rim, p_mid=None, p_rim=None, rows=None):
        self.arrays = (mid, rim, p_mid, p_rim)
        self.rows = rows or mid.shape[1] + 2 * RIM

    def pick(self, f):
        mid, rim, p_mid, p_rim = self.arrays
        if f == 4 and p_mid is not None:
            return p_mid, p_rim
        return mid if mid is None else mid.at[f], rim if rim is None else rim.at[f]

    def row(self, f, x):
        mid, rim = self.pick(f)
        if RIM <= x < self.rows - RIM:
            return mid[x - RIM]
        return rim[x if x < RIM else x - self.rows + 2 * RIM]

    def group(self, f, g):
        mid, rim = self.pick(f)
        return rim[...] if g is None else mid[g * GROUP : (g + 1) * GROUP]

    def store(self, f, x, value):
        mid, rim = self.pick(f)
        if RIM <= x < self.rows - RIM:
            mid[x - RIM] = value
        else:
            rim[x if x < RIM else x - self.rows + 2 * RIM] = value


def join_last(ut, p):
    low = lax.broadcasted_iota(jnp.int32, ut.shape, 0) < 4
    return jnp.where(low, pltpu.roll(ut, 3, 0), pltpu.roll(p, 7, 0))


def join_first(ut, p):
    low = lax.broadcasted_iota(jnp.int32, ut.shape, 0) < 4
    return jnp.where(low, ut, pltpu.roll(p, 4, 0))


def write_x(level, to_xa, to_xb):
    even = is_even("ax")
    for f in range(5):
        for i in range(3):
            first, last = level.row(f, i), level.row(f, level.rows - 3 + i)
            to_xa[3 * f + i] = jnp.where(even, last, first)
            to_xb[3 * f + i] = jnp.where(even, first, last)


def write_z(level, starts, to_za, to_zb):
    even = is_even("az")
    row = None
    for i, x in enumerate(starts):
        first, last = [], []
        for y in range(x, x + 4):
            ut, p = level.row(2, y), level.row(4, y)
            first.append(join_first(ut[0:8], p[0:8]))
            last.append(join_last(ut[8:16], p[8:16]))
        if row is None:
            row = lax.broadcasted_iota(jnp.int32, first[0].shape, 0) % 4 == 3
        for t in range(3):
            shift = 3 - t
            one = jnp.where(row, pltpu.roll(first[3], shift, 0), first[t])
            two = jnp.where(row, pltpu.roll(last[3], shift, 0), last[t])
            to_za[3 * i + t] = jnp.where(even, two, one)
            to_zb[3 * i + t] = jnp.where(even, one, two)


def edges_body(state, to_xa, to_xb, to_za, to_zb):
    level = Whole(state)
    write_x(level, to_xa, to_xb)
    write_z(level, range(0, level.rows, 4), to_za, to_zb)


def fill_halo(halo, xa, xb):
    n_ax, ax = lax.axis_size("ax"), lax.axis_index("ax")
    even = is_even("ax")
    for f in range(halo.shape[1]):
        a, b = xa[3 * f : 3 * f + 3], xb[3 * f : 3 * f + 3]
        halo[0, f] = jnp.where(ax > 0, jnp.where(even, b, a), 0.0)
        halo[1, f] = jnp.where(ax < n_ax - 1, jnp.where(even, a, b), 0.0)


def inverse_step(cols, radial):
    base = cols * lax.axis_size("az") / (2.0 * math.pi)
    at = lax.broadcasted_iota(jnp.int32, (1, radial), 1).astype(F32)
    return base / (base / hub_ratio + radial_step * (at + 0.5))


def along(row, x):
    total = drp_coeffs[0] * (row(x + 1) - row(x - 1))
    for s in (2, 3):
        total = total + drp_coeffs[s - 1] * (row(x + s) - row(x - s))
    return total


def apply_operator(level, groups, za, zb, tmat, rmat, finish, halo=None):
    even = is_even("az")
    tiles = level.rows // 4 * 3
    rim = RIM // 4 * 3

    def row(f, x):
        if x < 0:
            return halo[0, f, x + 3]
        if x >= level.rows:
            return halo[1, f, x - level.rows]
        return level.row(f, x)

    def beside(g):
        spans = [(0, rim), (tiles - rim, tiles)] if g is None else [(rim + 6 * g, rim + 6 * g + 6)]
        start = za.shape[0] - tiles
        if za.shape[0] == 2 * rim:
            spans, start = [(0, rim), (rim, 2 * rim)], 0
        elif za.shape[0] == tiles - 2 * rim:
            start = -rim
        sides = []
        for swap_ab in (False, True):
            for a, b in spans:
                got_a, got_b = za[start + a : start + b], zb[start + a : start + b]
                pair = (got_a, got_b) if swap_ab else (got_b, got_a)
                sides.append(jnp.where(even, *pair).reshape((b - a) * 8, za.shape[2]))
        return split(jnp.concatenate(sides, axis=0))

    for g in groups:
        if g is None:
            xs = [*range(RIM), *range(level.rows - RIM, level.rows)]
        else:
            xs = range(RIM + g * GROUP, RIM + (g + 1) * GROUP)
        ut, ur, p = [level.group(f, g) for f in (2, 3, 4)]
        _, cols, radial = ut.shape
        inv_h = inverse_step(cols, radial)
        side_hi, side_lo = beside(g)
        p_hi, p_lo = split(p.reshape(GROUP * cols, radial))
        ut_hi, ut_lo = split(ut.reshape(GROUP * cols, radial))
        ur_hi, ur_lo = split(ur.reshape(GROUP * cols, radial))

        def across(which, hi, lo):
            hi = jnp.concatenate([hi, side_hi], axis=0)
            lo = jnp.concatenate([lo, side_lo], axis=0)
            return dot(tmat[which, 0], hi) + dot(tmat[which, 0], lo) + dot(tmat[which, 1], hi)

        def outward(which, hi, lo):
            return dot(hi, rmat[which, 0]) + dot(lo, rmat[which, 0]) + dot(hi, rmat[which, 1])

        div_tr = across(0, ut_hi, ut_lo) * inv_h + outward(0, ur_hi, ur_lo)
        p_t = across(1, p_hi, p_lo) * inv_h
        p_r = outward(1, p_hi, p_lo)
        for i, x in enumerate(xs):
            part = slice(i * cols, (i + 1) * cols)
            d = [along(lambda y: row(f, y), x) for f in range(5)]
            div = d[1] + div_tr[part]
            finish(
                x,
                [
                    -mach_number * d[0] - div,
                    -mach_number * d[1] - d[4],
                    -mach_number * d[2] - p_t[part],
                    -mach_number * d[3] - p_r[part],
                    -mach_number * d[4] - div,
                ],
            )


def start_body(state, za, zb, xa, xb, tmat, rmat, k_mid, k_rim, halo):
    fill_halo(halo, xa, xb)
    level, out = Whole(state), Parts(k_mid, k_rim)

    def finish(x, tend):
        for f in range(5):
            out.store(f, x, tend[f])

    apply_operator(level, [*range(k_mid.shape[1] // GROUP), None], za, zb, tmat, rmat, finish, halo)


def inner_stage_body(factor, level, base, za, zb, tmat, rmat, out_mid, to_za, to_zb):
    def finish(x, tend):
        for f in range(5):
            out_mid[f, x - RIM] = base.row(f, x) + factor * tend[f]

    apply_operator(level, range(out_mid.shape[1] // GROUP), za, zb, tmat, rmat, finish)
    write_z(Parts(out_mid, None, rows=level.rows), range(RIM, level.rows - RIM, 4), to_za, to_zb)


def rim_stage_body(factor, level, base, za, zb, xa, xb, tmat, rmat, out_rim, to_xa, to_xb, to_za, to_zb, halo):
    fill_halo(halo, xa, xb)
    out = Parts(None, out_rim, rows=level.rows)

    def finish(x, tend):
        for f in range(5):
            out.store(f, x, base.row(f, x) + factor * tend[f])

    apply_operator(level, [None], za, zb, tmat, rmat, finish, halo)
    write_x(out, to_xa, to_xb)
    write_z(out, [0, level.rows - RIM], to_za, to_zb)


def last_finish(fields, k, store):
    def finish(x, tend):
        for f in range(5):
            store(f, x, fields[f, x] + time_step * k.row(f, x) + (0.5 * time_step * time_step) * tend[f])

    return finish


def inner_last_body(level, k, fields, za, zb, tmat, rmat, out, result, sems):
    def store(f, x, value):
        result[f, x - RIM] = value

    def copy(g):
        at = g * GROUP
        return pltpu.make_async_copy(
            result.at[:, at : at + GROUP], out.at[:, RIM + at : RIM + at + GROUP], sems.at[g]
        )

    groups = range(result.shape[1] // GROUP)
    for g in groups:
        apply_operator(level, [g], za, zb, tmat, rmat, last_finish(fields, k, store))
        copy(g).start()
    for g in groups:
        copy(g).wait()


def rim_last_body(level, k, fields, za, zb, xa, xb, tmat, rmat, out, halo, result, sems):
    rows = level.rows
    fill_halo(halo, xa, xb)

    def store(f, x, value):
        result[f, x if x < RIM else x - rows + 2 * RIM] = value

    apply_operator(level, [None], za, zb, tmat, rmat, last_finish(fields, k, store), halo)
    copies = [
        pltpu.make_async_copy(result.at[:, 0:RIM], out.at[:, 0:RIM], sems.at[0]),
        pltpu.make_async_copy(result.at[:, RIM:], out.at[:, rows - RIM :], sems.at[1]),
    ]
    for copy in copies:
        copy.start()
    for copy in copies:
        copy.wait()


def local(noise, half_width, owner, target_cell, fields):
    px, pa, fine = noise.shape
    cx, ca, radial = fields.shape[1:]
    ncols = px * pa
    most = ncols // 2
    n_az = lax.axis_size("az")
    inner = cx - 2 * RIM

    block = ((px, pa, fine), F32)
    even = is_even("ax")
    to_a = jnp.where(even, noise[px - HMAX :], noise[:HMAX])
    to_b = jnp.where(even, noise[:HMAX], noise[px - HMAX :])
    noise_a, noise_b = swap(to_a, to_b, "ax")
    send_x, send_z = ((15, ca, radial), F32), ((cx // 4 * 3, 8, radial), F32)
    sends = [send_x, send_x, send_z, send_z]
    xa, xb, za, zb = full_specs(edges_body, sends, [fields], name="edges", after=[to_a])
    uxa, uxb = swap(xa, xb, "ax")
    partial, half_width = full_specs(
        inner_body, [block, ((px, pa, fine), jnp.int32)], [noise, half_width], name="filter_inner", after=[za]
    )
    long_z = ((px + send_z[0][0], 8, fine // 2), F32)
    filtered, to_a, to_b = full_specs(
        first_body,
        [block, long_z, long_z],
        [partial, half_width, noise_a, noise_b, za, zb],
        [((2, HMAX, pa, fine), F32)],
        name="filter_axial",
    )
    got_a, got_b = swap(to_a, to_b, "az")
    pick, cells, own = full_specs(
        route_body,
        [((4 * most, ncols), BF16), ((4, 8, radial), F32), ((1, ncols), jnp.int32)],
        [owner.reshape(1, ncols), target_cell.reshape(1, ncols)],
        name="route",
        after=[filtered],
    )
    tiles = most // 8 + 1
    packet, packet_z = ((tiles, 8, radial), F32), ((tiles + 1, 8, radial), F32)
    binned, xa, xb, za, zb = full_specs(
        second_body,
        [((ncols, radial), F32), packet, packet, packet_z, packet_z],
        [filtered, half_width, got_a, got_b, pick, cells],
        [((px, 32, fine), F32), ((ncols, fine), BF16), ((ncols, fine), BF16)],
        name="filter_rest",
    )
    packets = (*swap(xa, xb, "ax"), *swap(za, zb, "az"))

    tmat = jnp.asarray(azimuth_matrices(ca))
    rmat = jnp.asarray(radial_matrices(float(ca * n_az), radial))
    mid, rim = ((5, inner, ca, radial), F32), ((5, 2 * RIM, ca, radial), F32)
    halo = ((2, 5, 3, ca, radial), F32)
    k_mid, k_rim = full_specs(
        start_body, [mid, rim], [fields, got_a, got_b, uxa, uxb, tmat, rmat], [halo], name="operator", after=[binned]
    )
    p_mid, p_rim, *edges = full_specs(
        gather_body,
        [((inner, ca, radial), F32), ((2 * RIM, ca, radial), F32), *sends],
        [binned, own, *packets, k_mid, k_rim],
        name="gather",
    )
    k = [k_mid, k_rim, p_mid, p_rim]
    inner_z, rim_z = ((inner // 4 * 3, 8, radial), F32), ((RIM // 2 * 3, 8, radial), F32)
    za, zb = swap(edges[2], edges[3], "az")
    xa, xb = swap(edges[0], edges[1], "ax")
    level, rim_a, rim_b = k, za, zb
    for factor in (time_step / 4.0, time_step / 3.0):
        size = len(level)

        def body(*refs, factor=factor, size=size):
            inner_stage_body(factor, Parts(*refs[:size]), Parts(*refs[size : size + 4]), *refs[size + 4 :])

        new_mid, to_za, to_zb = full_specs(
            body, [mid, inner_z, inner_z], [*level, *k, za, zb, tmat, rmat], name="stage_inner", cost=COST if level is k else 0
        )
        za, zb = swap(to_za, to_zb, "az")

        def body(*refs, factor=factor, size=size):
            rim_stage_body(factor, Parts(*refs[:size]), Parts(*refs[size : size + 4]), *refs[size + 4 :])

        new_rim, to_xa, to_xb, to_za, to_zb = full_specs(
            body,
            [rim, send_x, send_x, rim_z, rim_z],
            [*level, *k, rim_a, rim_b, xa, xb, tmat, rmat],
            [halo],
            name="stage_rim",
            after=[new_mid],
            cost=COST,
        )
        xa, xb = swap(to_xa, to_xb, "ax")
        rim_a, rim_b = swap(to_za, to_zb, "az")
        level = [new_mid, new_rim]

    def body(*refs):
        inner_last_body(Parts(*refs[:2]), Parts(*refs[2:6]), *refs[6:])

    whole = ((5, cx, ca, radial), F32)
    (out,) = full_specs(
        body,
        [whole],
        [*level, *k, fields, za, zb, tmat, rmat],
        [mid, pltpu.SemaphoreType.DMA((inner // GROUP,))],
        name="final_inner",
        out_specs=[ANY],
    )

    def body(out_in, *refs):
        rim_last_body(Parts(*refs[:2]), Parts(*refs[2:6]), *refs[6:])

    (out,) = full_specs(
        body,
        [whole],
        [out, *level, *k, fields, rim_a, rim_b, xa, xb, tmat, rmat],
        [halo, rim, pltpu.SemaphoreType.DMA((2,))],
        name="final_rim",
        in_specs=[ANY] + [VM] * 13,
        out_specs=[ANY],
        alias={0: 0},
    )
    return out


def solution(mesh):
    return jax.shard_map(
        local,
        mesh=mesh,
        in_specs=(
            P("ax", "az", None),
            P("ax", "az", None),
            P(("ax", "az")),
            P(("ax", "az")),
            P(None, "ax", "az", None),
        ),
        out_specs=P(None, "ax", "az", None),
        check_vma=False,
    )
```

```python
import math

import numpy as np

import jax
import jax.numpy as jnp
from jax import lax
from jax.experimental import pallas as pl
from jax.experimental.pallas import tpu as pltpu
from jax.sharding import PartitionSpec as P

HMAX = 4
drp_coeffs = (0.770882380518, -0.166705904415, 0.02084314277)
mach_number = 0.5
time_step = 0.7
source_gain = 4.0
radial_step = 2.0
hub_ratio = 1.6

F32 = jnp.float32
BF16 = jnp.bfloat16
VM = pl.BlockSpec(memory_space=pltpu.VMEM)
ANY = pl.BlockSpec(memory_space=pl.ANY)
PARAMS = pltpu.CompilerParams(vmem_limit_bytes=24 * 1024 * 1024)
GROUP = 8
RIM = 4
SOME = 2_000_000_000
COST = 1 << 37


def np_split(matrix):
    hi = matrix.astype(np.float32).astype(BF16)
    lo = (matrix - hi.astype(np.float64)).astype(np.float32).astype(BF16)
    return hi, lo


def filter_table():
    table = np.zeros((HMAX + 1, HMAX))
    for h in range(1, HMAX + 1):
        weights = [math.exp(-2.0 * k * k / (h * h)) if k <= h else 0.0 for k in range(HMAX + 1)]
        total = weights[0] + 2.0 * sum(weights[1:])
        table[:, h - 1] = [w / total for w in weights]
    return table


def radial_rows(na_total, radial):
    base = na_total / (2.0 * math.pi)
    radius = base / hub_ratio + radial_step * (np.arange(radial) + 0.5)
    return base / radius, 1.0 / radius


def radial_matrices(na_total, radial):
    diff = np.zeros((radial, radial))
    for s, a in zip((1, 2, 3), drp_coeffs):
        for j in range(radial):
            if j + s < radial:
                diff[j + s, j] += a / radial_step
            if j - s >= 0:
                diff[j - s, j] -= a / radial_step
    with_r = diff + np.diag(radial_rows(na_total, radial)[1])
    return np.stack([np.stack(np_split(with_r)), np.stack(np_split(diff))])


def azimuth_matrices(cols):
    packed = GROUP * 6
    full = np.zeros((2, GROUP * cols, GROUP * cols + 2 * packed))
    for which in range(2):
        for x in range(GROUP):
            for i in range(cols):
                for s, a in zip((1, 2, 3), drp_coeffs):
                    for j, sign in ((i + s, 1.0), (i - s, -1.0)):
                        if 0 <= j < cols:
                            at = x * cols + j
                        else:
                            m = j + 3 if j < 0 else j - cols
                            tile, row = (x % 4, m) if x % 4 < 3 else (m, 3)
                            at = GROUP * cols + (x // 4 * 3 + tile) * 8 + row + 4 * which
                            at += packed if j >= cols else 0
                        full[which, x * cols + i, at] += sign * a
    return np.stack([np.stack(np_split(full[w])) for w in range(2)])


def split(x):
    hi = x.astype(BF16)
    return hi, (x - hi.astype(F32)).astype(BF16)


def dot(a, b):
    return lax.dot_general(a, b, (((1,), (0,)), ((), ())), preferred_element_type=F32)


def is_even(axis):
    return lax.rem(lax.axis_index(axis), 2) == 0


def swap(to_a, to_b, axis):
    devices = lax.axis_size(axis)
    pairs_a = [(i, i ^ 1) for i in range(devices)]
    pairs_b = [(i, (i - 1) % devices if i % 2 == 0 else (i + 1) % devices) for i in range(devices)]
    return lax.ppermute(to_a, axis, pairs_a), lax.ppermute(to_b, axis, pairs_b)


def full_specs(body, outs, args, scratch=(), name=None, in_specs=None, out_specs=None, after=(), cost=0, alias=None):
    skip = len(args)

    def run(*refs):
        body(*refs[:skip], *refs[skip + len(after) :])

    return pl.pallas_call(
        run,
        out_shape=[jax.ShapeDtypeStruct(s, d) for s, d in outs],
        in_specs=(in_specs or [VM] * skip) + [ANY] * len(after),
        input_output_aliases=alias or {},
        out_specs=out_specs or [VM] * len(outs),
        scratch_shapes=[pltpu.VMEM(*s) if isinstance(s, tuple) else s for s in scratch],
        compiler_params=PARAMS,
        name=name,
        cost_estimate=pl.CostEstimate(flops=cost, bytes_accessed=0, transcendentals=0),
    )(*args, *after)


def route_body(owner_ref, target_ref, pick_ref, cells_ref, own_ref):
    n_ax, n_az = lax.axis_size("ax"), lax.axis_size("az")
    ax, az = lax.axis_index("ax"), lax.axis_index("az")
    step_x = jnp.where(lax.rem(ax, 2) == 0, 1, -1)
    step_z = jnp.where(lax.rem(az, 2) == 0, 1, -1)
    me = ax * n_az + az
    b_x = ax - step_x
    ids = [
        (ax + step_x) * n_az + az,
        jnp.where((b_x >= 0) & (b_x < n_ax), b_x * n_az + az, -1),
        ax * n_az + lax.rem(az + step_z + n_az, n_az),
        ax * n_az + lax.rem(az - step_z + n_az, n_az),
    ]
    owner = owner_ref[...]
    target = target_ref[...]
    ncols = owner.shape[1]
    most = ncols // 2
    own_ref[...] = jnp.where(owner == me, target, -1)
    row = lax.broadcasted_iota(jnp.int32, (8, ncols), 0)
    marks = jnp.zeros((8, ncols), F32)
    for d, i in enumerate(ids):
        marks = jnp.where((row == d) & (owner == i), 1.0, marks)
    before = lax.broadcasted_iota(jnp.int32, (ncols, ncols), 0) < lax.broadcasted_iota(jnp.int32, (ncols, ncols), 1)
    rank = dot(marks.astype(BF16), jnp.where(before, 1.0, 0.0).astype(BF16))
    coarse = (target // 32).astype(F32)
    fine = (target % 32).astype(F32)
    digits = jnp.where(row == 0, coarse, jnp.where(row == 1, fine, 0.0)).astype(BF16)
    slot = lax.broadcasted_iota(jnp.int32, (most, ncols), 0).astype(F32)
    for d in range(4):
        wanted = jnp.where(marks[d : d + 1] > 0.0, rank[d : d + 1], -1.0)
        pick = jnp.where(slot == wanted, 1.0, 0.0).astype(BF16)
        pick_ref[d * most : (d + 1) * most, :] = pick
        found = lax.dot_general(digits, pick, (((1,), (1,)), ((), ())), preferred_element_type=F32)
        cells_ref[d, :, :] = jnp.zeros(cells_ref.shape[1:], F32)
        cells_ref[d, 0:1, 0:most] = found[0:1] * 32.0 + found[1:2]


def weights_of(h):
    table = filter_table()
    le = [h <= 1, h <= 2, h <= 3]
    out = []
    for k in range(HMAX + 1):
        value = jnp.full(h.shape, table[k, 3], F32)
        for j in (2, 1, 0):
            if j > 0 and table[k, j] == 0.0 and table[k, j - 1] == 0.0:
                value = jnp.where(le[j], 0.0, value)
                break
            value = jnp.where(le[j], table[k, j], value)
        out.append(value)
    return out


def inner_body(noise_ref, half_ref, first_ref, kept_ref):
    rows = noise_ref.shape[0]
    kept_ref[...] = half_ref[...]
    for x in range(rows):
        w = weights_of(half_ref[x])
        total = w[0] * noise_ref[x]
        for k in range(1, HMAX + 1):
            near = [noise_ref[y] for y in (x - k, x + k) if 0 <= y < rows]
            if near:
                total = total + w[k] * (near[0] + near[1] if len(near) == 2 else near[0])
        first_ref[x] = total


def first_body(
    inner_ref, half_ref, got_a_ref, got_b_ref, edge_a_ref, edge_b_ref, first_ref, to_a_ref, to_b_ref, halo
):
    n_ax, ax = lax.axis_size("ax"), lax.axis_index("ax")
    even_x, even_z = is_even("ax"), is_even("az")
    rows, _, fine = half_ref.shape
    halo[0] = jnp.where(ax > 0, jnp.where(even_x, got_b_ref[...], got_a_ref[...]), 0.0)
    halo[1] = jnp.where(ax < n_ax - 1, jnp.where(even_x, got_a_ref[...], got_b_ref[...]), 0.0)
    for x in range(HMAX, rows - HMAX):
        first_ref[x] = inner_ref[x]
    for i in range(HMAX):
        w = weights_of(half_ref[i])
        total = inner_ref[i]
        for k in range(i + 1, HMAX + 1):
            total = total + w[k] * halo[0, HMAX + i - k]
        first_ref[i] = total
        x = rows - 1 - i
        w = weights_of(half_ref[x])
        total = inner_ref[x]
        for k in range(i + 1, HMAX + 1):
            total = total + w[k] * halo[1, k - i - 1]
        first_ref[x] = total
    half = rows // 2
    low = lax.broadcasted_iota(jnp.int32, (8, fine), 0) < 4
    for x in range(half):
        last = jnp.where(low, pltpu.roll(first_ref[x, 8:16], 4, 0), first_ref[x + half, 8:16])
        begin = jnp.where(low, first_ref[x, 0:8], pltpu.roll(first_ref[x + half, 0:8], 4, 0))
        for ref, value in ((to_a_ref, jnp.where(even_z, last, begin)), (to_b_ref, jnp.where(even_z, begin, last))):
            ref[x] = value[:, : fine // 2]
            ref[half + x] = value[:, fine // 2 :]
    to_a_ref[rows:] = edge_a_ref[...]
    to_b_ref[rows:] = edge_b_ref[...]


def second_body(
    first_ref, half_ref, got_a_ref, got_b_ref, pick_ref, cells_ref,
    own_ref, to_xa, to_xb, to_za, to_zb, wide, fine_hi, fine_lo,
):
    even = is_even("az")
    rows, cols, fine = first_ref.shape
    half = rows // 2
    for x in range(half):
        got_a, got_b = [jnp.concatenate([got[x], got[half + x]], axis=1) for got in (got_a_ref, got_b_ref)]
        before = jnp.where(even, got_b, got_a)
        after = jnp.where(even, got_a, got_b)
        wide[x, 0:8] = pltpu.roll(before, 4, 0)
        wide[x + half, 0:8] = before
        wide[x, 24:32] = after
        wide[x + half, 24:32] = pltpu.roll(after, 4, 0)
    lane = lax.broadcasted_iota(jnp.int32, (cols, fine), 1)
    for x in range(rows):
        wide[x, 8:24] = first_ref[x]
    for x in range(rows):
        w = weights_of(half_ref[x])
        total = w[0] * first_ref[x]
        for k in range(1, HMAX + 1):
            total = total + w[k] * (wide[x, 8 - k : 24 - k] + wide[x, 8 + k : 24 + k])
        result = w[0] * total
        for k in range(1, HMAX + 1):
            up = jnp.where(lane < fine - k, pltpu.roll(total, fine - k, 1), 0.0)
            down = jnp.where(lane >= k, pltpu.roll(total, k, 1), 0.0)
            result = result + w[k] * (up + down)
        hi, lo = split(result)
        fine_hi[x * cols : (x + 1) * cols] = hi
        fine_lo[x * cols : (x + 1) * cols] = lo
    radial = own_ref.shape[1]
    above = lax.broadcasted_iota(jnp.int32, (fine, radial), 0) - lax.broadcasted_iota(
        jnp.int32, (fine, radial), 1
    ) * (fine // radial)
    bins = jnp.where((above >= 0) & (above < fine // radial), source_gain, 0.0).astype(BF16)
    binned = dot(fine_hi[...], bins) + dot(fine_lo[...], bins)
    own_ref[...] = binned
    hi, lo = split(binned)
    most = pick_ref.shape[0] // 4
    for d, out in enumerate((to_xa, to_xb, to_za, to_zb)):
        pick = pick_ref[d * most : (d + 1) * most]
        tiles = most // 8
        out[0:tiles] = (dot(pick, hi) + dot(pick, lo)).reshape(tiles, 8, radial)
        out[tiles] = cells_ref[d]
    for out in (to_za, to_zb):
        out[most // 8 + 1] = jnp.zeros(out.shape[1:], F32)


def gather_body(
    binned_ref, own_ref, xa, xb, za, zb, k_mid, k_rim, p_mid, p_rim, to_xa, to_xb, to_za, to_zb
):
    mid, cols, radial = p_mid.shape
    cells = (mid + 2 * RIM) * cols
    most = 8 * (xa.shape[0] - 1)

    def onehot(row):
        at = lax.broadcasted_iota(jnp.int32, (cells, row.shape[1]), 0)
        return jnp.where(at == row, 1.0, 0.0).astype(BF16)

    mats = [onehot(own_ref[...])]
    packets = [binned_ref[...]]
    for got in (xa, xb, za, zb):
        tiles = most // 8
        mats.append(onehot(got[tiles, 0:1, 0:most].astype(jnp.int32)))
        packets.append(got[0:tiles].reshape(most, radial))
    mat = jnp.concatenate(mats, axis=1)
    hi, lo = split(jnp.concatenate(packets, axis=0))
    q = (dot(mat, hi) + dot(mat, lo)).reshape(mid + 2 * RIM, cols, radial)
    p_rim[0:RIM] = k_rim[4, 0:RIM] + q[0:RIM]
    p_mid[...] = k_mid[4] + q[RIM : RIM + mid]
    p_rim[RIM:] = k_rim[4, RIM:] + q[RIM + mid :]
    level = Parts(k_mid, k_rim, p_mid, p_rim)
    write_x(level, to_xa, to_xb)
    write_z(level, range(0, level.rows, 4), to_za, to_zb)


class Whole:
    def __init__(self, ref):
        self.ref = ref
        self.rows = ref.shape[1]

    def row(self, f, x):
        return self.ref[f, x]

    def group(self, f, g):
        if g is None:
            return jnp.concatenate([self.ref[f, 0:RIM], self.ref[f, self.rows - RIM :]], axis=0)
        return self.ref[f, RIM + g * GROUP : RIM + (g + 1) * GROUP]


class Parts:
    def __init__(self, mid, rim, p_mid=None, p_rim=None, rows=None):
        self.arrays = (mid, rim, p_mid, p_rim)
        self.rows = rows or mid.shape[1] + 2 * RIM

    def pick(self, f):
        mid, rim, p_mid, p_rim = self.arrays
        if f == 4 and p_mid is not None:
            return p_mid, p_rim
        return mid if mid is None else mid.at[f], rim if rim is None else rim.at[f]

    def row(self, f, x):
        mid, rim = self.pick(f)
        if RIM <= x < self.rows - RIM:
            return mid[x - RIM]
        return rim[x if x < RIM else x - self.rows + 2 * RIM]

    def group(self, f, g):
        mid, rim = self.pick(f)
        return rim[...] if g is None else mid[g * GROUP : (g + 1) * GROUP]

    def store(self, f, x, value):
        mid, rim = self.pick(f)
        if RIM <= x < self.rows - RIM:
            mid[x - RIM] = value
        else:
            rim[x if x < RIM else x - self.rows + 2 * RIM] = value


def join_last(ut, p):
    low = lax.broadcasted_iota(jnp.int32, ut.shape, 0) < 4
    return jnp.where(low, pltpu.roll(ut, 3, 0), pltpu.roll(p, 7, 0))


def join_first(ut, p):
    low = lax.broadcasted_iota(jnp.int32, ut.shape, 0) < 4
    return jnp.where(low, ut, pltpu.roll(p, 4, 0))


def write_x(level, to_xa, to_xb):
    even = is_even("ax")
    for f in range(5):
        for i in range(3):
            first, last = level.row(f, i), level.row(f, level.rows - 3 + i)
            to_xa[3 * f + i] = jnp.where(even, last, first)
            to_xb[3 * f + i] = jnp.where(even, first, last)


def write_z(level, starts, to_za, to_zb):
    even = is_even("az")
    row = None
    for i, x in enumerate(starts):
        first, last = [], []
        for y in range(x, x + 4):
            ut, p = level.row(2, y), level.row(4, y)
            first.append(join_first(ut[0:8], p[0:8]))
            last.append(join_last(ut[8:16], p[8:16]))
        if row is None:
            row = lax.broadcasted_iota(jnp.int32, first[0].shape, 0) % 4 == 3
        for t in range(3):
            shift = 3 - t
            one = jnp.where(row, pltpu.roll(first[3], shift, 0), first[t])
            two = jnp.where(row, pltpu.roll(last[3], shift, 0), last[t])
            to_za[3 * i + t] = jnp.where(even, two, one)
            to_zb[3 * i + t] = jnp.where(even, one, two)


def edges_body(state, to_xa, to_xb, to_za, to_zb):
    level = Whole(state)
    write_x(level, to_xa, to_xb)
    write_z(level, range(0, level.rows, 4), to_za, to_zb)


def fill_halo(halo, xa, xb):
    n_ax, ax = lax.axis_size("ax"), lax.axis_index("ax")
    even = is_even("ax")
    for f in range(halo.shape[1]):
        a, b = xa[3 * f : 3 * f + 3], xb[3 * f : 3 * f + 3]
        halo[0, f] = jnp.where(ax > 0, jnp.where(even, b, a), 0.0)
        halo[1, f] = jnp.where(ax < n_ax - 1, jnp.where(even, a, b), 0.0)


def inverse_step(cols, radial):
    base = cols * lax.axis_size("az") / (2.0 * math.pi)
    at = lax.broadcasted_iota(jnp.int32, (1, radial), 1).astype(F32)
    return base / (base / hub_ratio + radial_step * (at + 0.5))


def along(row, x):
    total = drp_coeffs[0] * (row(x + 1) - row(x - 1))
    for s in (2, 3):
        total = total + drp_coeffs[s - 1] * (row(x + s) - row(x - s))
    return total


def apply_operator(level, groups, za, zb, tmat, rmat, finish, halo=None):
    even = is_even("az")
    tiles = level.rows // 4 * 3
    rim = RIM // 4 * 3

    def row(f, x):
        if x < 0:
            return halo[0, f, x + 3]
        if x >= level.rows:
            return halo[1, f, x - level.rows]
        return level.row(f, x)

    def beside(g):
        spans = [(0, rim), (tiles - rim, tiles)] if g is None else [(rim + 6 * g, rim + 6 * g + 6)]
        start = za.shape[0] - tiles
        if za.shape[0] == 2 * rim:
            spans, start = [(0, rim), (rim, 2 * rim)], 0
        elif za.shape[0] == tiles - 2 * rim:
            start = -rim
        sides = []
        for swap_ab in (False, True):
            for a, b in spans:
                got_a, got_b = za[start + a : start + b], zb[start + a : start + b]
                pair = (got_a, got_b) if swap_ab else (got_b, got_a)
                sides.append(jnp.where(even, *pair).reshape((b - a) * 8, za.shape[2]))
        return split(jnp.concatenate(sides, axis=0))

    for g in groups:
        if g is None:
            xs = [*range(RIM), *range(level.rows - RIM, level.rows)]
        else:
            xs = range(RIM + g * GROUP, RIM + (g + 1) * GROUP)
        ut, ur, p = [level.group(f, g) for f in (2, 3, 4)]
        _, cols, radial = ut.shape
        inv_h = inverse_step(cols, radial)
        side_hi, side_lo = beside(g)
        p_hi, p_lo = split(p.reshape(GROUP * cols, radial))
        ut_hi, ut_lo = split(ut.reshape(GROUP * cols, radial))
        ur_hi, ur_lo = split(ur.reshape(GROUP * cols, radial))

        def across(which, hi, lo):
            hi = jnp.concatenate([hi, side_hi], axis=0)
            lo = jnp.concatenate([lo, side_lo], axis=0)
            return dot(tmat[which, 0], hi) + dot(tmat[which, 0], lo) + dot(tmat[which, 1], hi)

        def outward(which, hi, lo):
            return dot(hi, rmat[which, 0]) + dot(lo, rmat[which, 0]) + dot(hi, rmat[which, 1])

        div_tr = across(0, ut_hi, ut_lo) * inv_h + outward(0, ur_hi, ur_lo)
        p_t = across(1, p_hi, p_lo) * inv_h
        p_r = outward(1, p_hi, p_lo)
        for i, x in enumerate(xs):
            part = slice(i * cols, (i + 1) * cols)
            d = [along(lambda y: row(f, y), x) for f in range(5)]
            div = d[1] + div_tr[part]
            finish(
                x,
                [
                    -mach_number * d[0] - div,
                    -mach_number * d[1] - d[4],
                    -mach_number * d[2] - p_t[part],
                    -mach_number * d[3] - p_r[part],
                    -mach_number * d[4] - div,
                ],
            )


def start_body(state, za, zb, xa, xb, tmat, rmat, k_mid, k_rim, halo):
    fill_halo(halo, xa, xb)
    level, out = Whole(state), Parts(k_mid, k_rim)

    def finish(x, tend):
        for f in range(5):
            out.store(f, x, tend[f])

    apply_operator(level, [*range(k_mid.shape[1] // GROUP), None], za, zb, tmat, rmat, finish, halo)


def inner_stage_body(factor, level, base, za, zb, tmat, rmat, out_mid, to_za, to_zb):
    def finish(x, tend):
        for f in range(5):
            out_mid[f, x - RIM] = base.row(f, x) + factor * tend[f]

    apply_operator(level, range(out_mid.shape[1] // GROUP), za, zb, tmat, rmat, finish)
    write_z(Parts(out_mid, None, rows=level.rows), range(RIM, level.rows - RIM, 4), to_za, to_zb)


def rim_stage_body(factor, level, base, xa, xb, za, zb, tmat, rmat, out_rim, to_xa, to_xb, to_za, to_zb, halo):
    fill_halo(halo, xa, xb)
    out = Parts(None, out_rim, rows=level.rows)

    def finish(x, tend):
        for f in range(5):
            out.store(f, x, base.row(f, x) + factor * tend[f])

    apply_operator(level, [None], za, zb, tmat, rmat, finish, halo)
    write_x(out, to_xa, to_xb)
    write_z(out, [0, level.rows - RIM], to_za, to_zb)


def last_finish(fields, k, store):
    def finish(x, tend):
        for f in range(5):
            store(f, x, fields[f, x] + time_step * k.row(f, x) + (0.5 * time_step * time_step) * tend[f])

    return finish


def inner_last_body(level, k, fields, za, zb, tmat, rmat, out, result, sems):
    def store(f, x, value):
        result[f, x - RIM] = value

    def copy(g):
        at = g * GROUP
        return pltpu.make_async_copy(
            result.at[:, at : at + GROUP], out.at[:, RIM + at : RIM + at + GROUP], sems.at[g]
        )

    groups = range(result.shape[1] // GROUP)
    for g in groups:
        apply_operator(level, [g], za, zb, tmat, rmat, last_finish(fields, k, store))
        copy(g).start()
    for g in groups:
        copy(g).wait()


def rim_last_body(level, k, fields, xa, xb, za, zb, tmat, rmat, out, halo, result, sems):
    rows = level.rows
    fill_halo(halo, xa, xb)

    def store(f, x, value):
        result[f, x if x < RIM else x - rows + 2 * RIM] = value

    apply_operator(level, [None], za, zb, tmat, rmat, last_finish(fields, k, store), halo)
    copies = [
        pltpu.make_async_copy(result.at[:, 0:RIM], out.at[:, 0:RIM], sems.at[0]),
        pltpu.make_async_copy(result.at[:, RIM:], out.at[:, rows - RIM :], sems.at[1]),
    ]
    for copy in copies:
        copy.start()
    for copy in copies:
        copy.wait()


def local(noise, half_width, owner, target_cell, fields):
    px, pa, fine = noise.shape
    cx, ca, radial = fields.shape[1:]
    ncols = px * pa
    most = ncols // 2
    n_az = lax.axis_size("az")
    inner = cx - 2 * RIM

    block = ((px, pa, fine), F32)
    even = is_even("ax")
    to_a = jnp.where(even, noise[px - HMAX :], noise[:HMAX])
    to_b = jnp.where(even, noise[:HMAX], noise[px - HMAX :])
    noise_a, noise_b = swap(to_a, to_b, "ax")
    send_x, send_z = ((15, ca, radial), F32), ((cx // 4 * 3, 8, radial), F32)
    sends = [send_x, send_x, send_z, send_z]
    xa, xb, za, zb = full_specs(edges_body, sends, [fields], name="edges", after=[to_a])
    uxa, uxb = swap(xa, xb, "ax")
    partial, half_width = full_specs(
        inner_body, [block, ((px, pa, fine), jnp.int32)], [noise, half_width], name="filter_inner", after=[za]
    )
    long_z = ((px + send_z[0][0], 8, fine // 2), F32)
    filtered, to_a, to_b = full_specs(
        first_body,
        [block, long_z, long_z],
        [partial, half_width, noise_a, noise_b, za, zb],
        [((2, HMAX, pa, fine), F32)],
        name="filter_axial",
    )
    got_a, got_b = swap(to_a, to_b, "az")
    pick, cells, own = full_specs(
        route_body,
        [((4 * most, ncols), BF16), ((4, 8, radial), F32), ((1, ncols), jnp.int32)],
        [owner.reshape(1, ncols), target_cell.reshape(1, ncols)],
        name="route",
        after=[filtered],
    )
    tiles = most // 8 + 1
    packet, packet_z = ((tiles, 8, radial), F32), ((tiles + 1, 8, radial), F32)
    binned, xa, xb, za, zb = full_specs(
        second_body,
        [((ncols, radial), F32), packet, packet, packet_z, packet_z],
        [filtered, half_width, got_a, got_b, pick, cells],
        [((px, 32, fine), F32), ((ncols, fine), BF16), ((ncols, fine), BF16)],
        name="filter_rest",
    )
    packets = (*swap(xa, xb, "ax"), *swap(za, zb, "az"))

    tmat = jnp.asarray(azimuth_matrices(ca))
    rmat = jnp.asarray(radial_matrices(float(ca * n_az), radial))
    mid, rim = ((5, inner, ca, radial), F32), ((5, 2 * RIM, ca, radial), F32)
    halo = ((2, 5, 3, ca, radial), F32)
    k_mid, k_rim = full_specs(
        start_body, [mid, rim], [fields, got_a, got_b, uxa, uxb, tmat, rmat], [halo], name="operator", after=[binned]
    )
    p_mid, p_rim, *edges = full_specs(
        gather_body,
        [((inner, ca, radial), F32), ((2 * RIM, ca, radial), F32), *sends],
        [binned, own, *packets, k_mid, k_rim],
        name="gather",
    )
    k = [k_mid, k_rim, p_mid, p_rim]
    inner_z, rim_z = ((inner // 4 * 3, 8, radial), F32), ((RIM // 2 * 3, 8, radial), F32)
    za, zb = swap(edges[2], edges[3], "az")
    xa, xb = swap(edges[0], edges[1], "ax")
    level, rim_a, rim_b = k, za, zb
    for factor in (time_step / 4.0, time_step / 3.0):
        size = len(level)

        def body(*refs, factor=factor, size=size):
            inner_stage_body(factor, Parts(*refs[:size]), Parts(*refs[size : size + 4]), *refs[size + 4 :])

        new_mid, to_za, to_zb = full_specs(
            body, [mid, inner_z, inner_z], [*level, *k, za, zb, tmat, rmat], name="stage_inner", cost=COST if level is k else SOME
        )
        za, zb = swap(to_za, to_zb, "az")

        def body(*refs, factor=factor, size=size):
            rim_stage_body(factor, Parts(*refs[:size]), Parts(*refs[size : size + 4]), *refs[size + 4 :])

        new_rim, to_xa, to_xb, to_za, to_zb = full_specs(
            body,
            [rim, send_x, send_x, rim_z, rim_z],
            [*level, *k, xa, xb, rim_a, rim_b, tmat, rmat],
            [halo],
            name="stage_rim",
            after=[new_mid],
            cost=COST,
        )
        xa, xb = swap(to_xa, to_xb, "ax")
        rim_a, rim_b = swap(to_za, to_zb, "az")
        level = [new_mid, new_rim]

    def body(*refs):
        inner_last_body(Parts(*refs[:2]), Parts(*refs[2:6]), *refs[6:])

    whole = ((5, cx, ca, radial), F32)
    (out,) = full_specs(
        body,
        [whole],
        [*level, *k, fields, za, zb, tmat, rmat],
        [mid, pltpu.SemaphoreType.DMA((inner // GROUP,))],
        name="final_inner",
        out_specs=[ANY],
        cost=SOME,
    )

    def body(out_in, *refs):
        rim_last_body(Parts(*refs[:2]), Parts(*refs[2:6]), *refs[6:])

    (out,) = full_specs(
        body,
        [whole],
        [out, *level, *k, fields, xa, xb, rim_a, rim_b, tmat, rmat],
        [halo, rim, pltpu.SemaphoreType.DMA((2,))],
        name="final_rim",
        in_specs=[ANY] + [VM] * 13,
        out_specs=[ANY],
        alias={0: 0},
    )
    return out


def solution(mesh):
    return jax.shard_map(
        local,
        mesh=mesh,
        in_specs=(
            P("ax", "az", None),
            P("ax", "az", None),
            P(("ax", "az")),
            P(("ax", "az")),
            P(None, "ax", "az", None),
        ),
        out_specs=P(None, "ax", "az", None),
        check_vma=False,
    )
```

```python
import math

import numpy as np

import jax
import jax.numpy as jnp
from jax import lax
from jax.experimental import pallas as pl
from jax.experimental.pallas import tpu as pltpu
from jax.sharding import PartitionSpec as P

HMAX = 4
drp_coeffs = (0.770882380518, -0.166705904415, 0.02084314277)
mach_number = 0.5
time_step = 0.7
source_gain = 4.0
radial_step = 2.0
hub_ratio = 1.6

F32 = jnp.float32
BF16 = jnp.bfloat16
VM = pl.BlockSpec(memory_space=pltpu.VMEM)
ANY = pl.BlockSpec(memory_space=pl.ANY)
PARAMS = pltpu.CompilerParams(vmem_limit_bytes=24 * 1024 * 1024)
GROUP = 8
RIM = 4
SOME = 2_000_000_000
COST = 1 << 37


def np_split(matrix):
    hi = matrix.astype(np.float32).astype(BF16)
    lo = (matrix - hi.astype(np.float64)).astype(np.float32).astype(BF16)
    return hi, lo


def filter_table():
    table = np.zeros((HMAX + 1, HMAX))
    for h in range(1, HMAX + 1):
        weights = [math.exp(-2.0 * k * k / (h * h)) if k <= h else 0.0 for k in range(HMAX + 1)]
        total = weights[0] + 2.0 * sum(weights[1:])
        table[:, h - 1] = [w / total for w in weights]
    return table


def radial_rows(na_total, radial):
    base = na_total / (2.0 * math.pi)
    radius = base / hub_ratio + radial_step * (np.arange(radial) + 0.5)
    return base / radius, 1.0 / radius


def radial_matrices(na_total, radial):
    diff = np.zeros((radial, radial))
    for s, a in zip((1, 2, 3), drp_coeffs):
        for j in range(radial):
            if j + s < radial:
                diff[j + s, j] += a / radial_step
            if j - s >= 0:
                diff[j - s, j] -= a / radial_step
    with_r = diff + np.diag(radial_rows(na_total, radial)[1])
    return np.stack([np.stack(np_split(with_r)), np.stack(np_split(diff))])


def azimuth_matrices(cols):
    packed = GROUP * 6
    full = np.zeros((2, GROUP * cols, GROUP * cols + 2 * packed))
    for which in range(2):
        for x in range(GROUP):
            for i in range(cols):
                for s, a in zip((1, 2, 3), drp_coeffs):
                    for j, sign in ((i + s, 1.0), (i - s, -1.0)):
                        if 0 <= j < cols:
                            at = x * cols + j
                        else:
                            m = j + 3 if j < 0 else j - cols
                            tile, row = (x % 4, m) if x % 4 < 3 else (m, 3)
                            at = GROUP * cols + (x // 4 * 3 + tile) * 8 + row + 4 * which
                            at += packed if j >= cols else 0
                        full[which, x * cols + i, at] += sign * a
    return np.stack([np.stack(np_split(full[w])) for w in range(2)])


def split(x):
    hi = x.astype(BF16)
    return hi, (x - hi.astype(F32)).astype(BF16)


def dot(a, b):
    return lax.dot_general(a, b, (((1,), (0,)), ((), ())), preferred_element_type=F32)


def is_even(axis):
    return lax.rem(lax.axis_index(axis), 2) == 0


def swap(to_a, to_b, axis):
    devices = lax.axis_size(axis)
    pairs_a = [(i, i ^ 1) for i in range(devices)]
    pairs_b = [(i, (i - 1) % devices if i % 2 == 0 else (i + 1) % devices) for i in range(devices)]
    return lax.ppermute(to_a, axis, pairs_a), lax.ppermute(to_b, axis, pairs_b)


def swap_b(value, axis):
    devices = lax.axis_size(axis)
    pairs = [(i, (i - 1) % devices if i % 2 == 0 else (i + 1) % devices) for i in range(devices)]
    return (lax.ppermute(value, axis, pairs),)


def full_specs(body, outs, args, scratch=(), name=None, in_specs=None, out_specs=None, after=(), cost=0, alias=None):
    skip = len(args)

    def run(*refs):
        body(*refs[:skip], *refs[skip + len(after) :])

    return pl.pallas_call(
        run,
        out_shape=[jax.ShapeDtypeStruct(s, d) for s, d in outs],
        in_specs=(in_specs or [VM] * skip) + [ANY] * len(after),
        input_output_aliases=alias or {},
        out_specs=out_specs or [VM] * len(outs),
        scratch_shapes=[pltpu.VMEM(*s) if isinstance(s, tuple) else s for s in scratch],
        compiler_params=PARAMS,
        name=name,
        cost_estimate=pl.CostEstimate(flops=cost, bytes_accessed=0, transcendentals=0),
    )(*args, *after)


def route_body(owner_ref, target_ref, pick_ref, cells_ref, own_ref):
    n_ax, n_az = lax.axis_size("ax"), lax.axis_size("az")
    ax, az = lax.axis_index("ax"), lax.axis_index("az")
    step_x = jnp.where(lax.rem(ax, 2) == 0, 1, -1)
    step_z = jnp.where(lax.rem(az, 2) == 0, 1, -1)
    me = ax * n_az + az
    b_x = ax - step_x
    ids = [
        (ax + step_x) * n_az + az,
        jnp.where((b_x >= 0) & (b_x < n_ax), b_x * n_az + az, -1),
        ax * n_az + lax.rem(az + step_z + n_az, n_az),
        ax * n_az + lax.rem(az - step_z + n_az, n_az),
    ]
    owner = owner_ref[...]
    target = target_ref[...]
    ncols = owner.shape[1]
    most = ncols // 2
    own_ref[...] = jnp.where(owner == me, target, -1)
    row = lax.broadcasted_iota(jnp.int32, (8, ncols), 0)
    marks = jnp.zeros((8, ncols), F32)
    for d, i in enumerate(ids):
        marks = jnp.where((row == d) & (owner == i), 1.0, marks)
    before = lax.broadcasted_iota(jnp.int32, (ncols, ncols), 0) < lax.broadcasted_iota(jnp.int32, (ncols, ncols), 1)
    rank = dot(marks.astype(BF16), jnp.where(before, 1.0, 0.0).astype(BF16))
    coarse = (target // 32).astype(F32)
    fine = (target % 32).astype(F32)
    digits = jnp.where(row == 0, coarse, jnp.where(row == 1, fine, 0.0)).astype(BF16)
    slot = lax.broadcasted_iota(jnp.int32, (most, ncols), 0).astype(F32)
    for d in range(4):
        wanted = jnp.where(marks[d : d + 1] > 0.0, rank[d : d + 1], -1.0)
        pick = jnp.where(slot == wanted, 1.0, 0.0).astype(BF16)
        pick_ref[d * most : (d + 1) * most, :] = pick
        found = lax.dot_general(digits, pick, (((1,), (1,)), ((), ())), preferred_element_type=F32)
        cells_ref[d, :, :] = jnp.zeros(cells_ref.shape[1:], F32)
        cells_ref[d, 0:1, 0:most] = found[0:1] * 32.0 + found[1:2]


def weights_of(h):
    table = filter_table()
    le = [h <= 1, h <= 2, h <= 3]
    out = []
    for k in range(HMAX + 1):
        value = jnp.full(h.shape, table[k, 3], F32)
        for j in (2, 1, 0):
            if j > 0 and table[k, j] == 0.0 and table[k, j - 1] == 0.0:
                value = jnp.where(le[j], 0.0, value)
                break
            value = jnp.where(le[j], table[k, j], value)
        out.append(value)
    return out


def inner_body(noise_ref, half_ref, first_ref, kept_ref):
    rows = noise_ref.shape[0]
    kept_ref[...] = half_ref[...]
    for x in range(rows):
        w = weights_of(half_ref[x])
        total = w[0] * noise_ref[x]
        for k in range(1, HMAX + 1):
            near = [noise_ref[y] for y in (x - k, x + k) if 0 <= y < rows]
            if near:
                total = total + w[k] * (near[0] + near[1] if len(near) == 2 else near[0])
        first_ref[x] = total


def first_body(
    inner_ref, half_ref, got_a_ref, got_b_ref, edge_a_ref, first_ref, to_a_ref, to_b_ref, halo
):
    n_ax, ax = lax.axis_size("ax"), lax.axis_index("ax")
    even_x, even_z = is_even("ax"), is_even("az")
    rows, _, fine = half_ref.shape
    halo[0] = jnp.where(ax > 0, jnp.where(even_x, got_b_ref[...], got_a_ref[...]), 0.0)
    halo[1] = jnp.where(ax < n_ax - 1, jnp.where(even_x, got_a_ref[...], got_b_ref[...]), 0.0)
    for x in range(HMAX, rows - HMAX):
        first_ref[x] = inner_ref[x]
    for i in range(HMAX):
        w = weights_of(half_ref[i])
        total = inner_ref[i]
        for k in range(i + 1, HMAX + 1):
            total = total + w[k] * halo[0, HMAX + i - k]
        first_ref[i] = total
        x = rows - 1 - i
        w = weights_of(half_ref[x])
        total = inner_ref[x]
        for k in range(i + 1, HMAX + 1):
            total = total + w[k] * halo[1, k - i - 1]
        first_ref[x] = total
    half = rows // 2
    low = lax.broadcasted_iota(jnp.int32, (8, fine), 0) < 4
    for x in range(half):
        last = jnp.where(low, pltpu.roll(first_ref[x, 8:16], 4, 0), first_ref[x + half, 8:16])
        begin = jnp.where(low, first_ref[x, 0:8], pltpu.roll(first_ref[x + half, 0:8], 4, 0))
        for ref, value in ((to_a_ref, jnp.where(even_z, last, begin)), (to_b_ref, jnp.where(even_z, begin, last))):
            ref[x] = value[:, : fine // 2]
            ref[half + x] = value[:, fine // 2 :]
    to_a_ref[rows:] = edge_a_ref[...]


def middle_body(first_ref, half_ref, partial_ref, weight_ref, wide):
    rows, cols, fine = first_ref.shape
    blank = jnp.zeros((rows, 8, fine), F32)
    wide[:, 0:8] = blank
    wide[:, 24:32] = blank
    for x in range(rows):
        wide[x, 8:24] = first_ref[x]
    for x in range(rows):
        w = weights_of(half_ref[x])
        total = w[0] * first_ref[x]
        for k in range(1, HMAX + 1):
            total = total + w[k] * (wide[x, 8 - k : 24 - k] + wide[x, 8 + k : 24 + k])
        partial_ref[x] = total
        for k in range(HMAX + 1):
            weight_ref[k, x] = w[k]


def second_body(
    partial_ref, weight_ref, got_a_ref, got_b_ref, pick_ref, cells_ref,
    own_ref, to_xa, to_xb, to_za, to_zb, fine_hi, fine_lo,
):
    even = is_even("az")
    rows, cols, fine = partial_ref.shape
    half = rows // 2
    lane = lax.broadcasted_iota(jnp.int32, (cols, fine), 1)
    row = lax.broadcasted_iota(jnp.int32, (8, fine), 0)
    for x in range(rows):
        y = x % half
        got_a, got_b = [jnp.concatenate([got[y], got[half + y]], axis=1) for got in (got_a_ref, got_b_ref)]
        before, after = jnp.where(even, got_b, got_a), jnp.where(even, got_a, got_b)
        if x < half:
            before = pltpu.roll(before, 4, 0)
        else:
            after = pltpu.roll(after, 4, 0)
        w = [weight_ref[k, x] for k in range(HMAX + 1)]
        total = partial_ref[x]
        for k in range(1, HMAX + 1):
            low = jnp.where(row < k, pltpu.roll(before, k, 0), 0.0)
            high = jnp.where(row >= 8 - k, pltpu.roll(after, 8 - k, 0), 0.0)
            total = total + w[k] * jnp.concatenate([low, high], axis=0)
        result = w[0] * total
        for k in range(1, HMAX + 1):
            up = jnp.where(lane < fine - k, pltpu.roll(total, fine - k, 1), 0.0)
            down = jnp.where(lane >= k, pltpu.roll(total, k, 1), 0.0)
            result = result + w[k] * (up + down)
        hi, lo = split(result)
        fine_hi[x * cols : (x + 1) * cols] = hi
        fine_lo[x * cols : (x + 1) * cols] = lo
    radial = own_ref.shape[1]
    above = lax.broadcasted_iota(jnp.int32, (fine, radial), 0) - lax.broadcasted_iota(
        jnp.int32, (fine, radial), 1
    ) * (fine // radial)
    bins = jnp.where((above >= 0) & (above < fine // radial), source_gain, 0.0).astype(BF16)
    binned = dot(fine_hi[...], bins) + dot(fine_lo[...], bins)
    own_ref[...] = binned
    hi, lo = split(binned)
    most = pick_ref.shape[0] // 4
    for d, out in enumerate((to_xa, to_xb, to_za, to_zb)):
        pick = pick_ref[d * most : (d + 1) * most]
        tiles = most // 8
        out[0:tiles] = (dot(pick, hi) + dot(pick, lo)).reshape(tiles, 8, radial)
        out[tiles] = cells_ref[d]
    for out in (to_za, to_zb):
        out[most // 8 + 1] = jnp.zeros(out.shape[1:], F32)


def gather_body(
    binned_ref, own_ref, xa, xb, za, zb, k_mid, k_rim, p_mid, p_rim, to_xa, to_xb, to_za, to_zb
):
    mid, cols, radial = p_mid.shape
    cells = (mid + 2 * RIM) * cols
    most = 8 * (xa.shape[0] - 1)

    def onehot(row):
        at = lax.broadcasted_iota(jnp.int32, (cells, row.shape[1]), 0)
        return jnp.where(at == row, 1.0, 0.0).astype(BF16)

    mats = [onehot(own_ref[...])]
    packets = [binned_ref[...]]
    for got in (xa, xb, za, zb):
        tiles = most // 8
        mats.append(onehot(got[tiles, 0:1, 0:most].astype(jnp.int32)))
        packets.append(got[0:tiles].reshape(most, radial))
    mat = jnp.concatenate(mats, axis=1)
    hi, lo = split(jnp.concatenate(packets, axis=0))
    q = (dot(mat, hi) + dot(mat, lo)).reshape(mid + 2 * RIM, cols, radial)
    p_rim[0:RIM] = k_rim[4, 0:RIM] + q[0:RIM]
    p_mid[...] = k_mid[4] + q[RIM : RIM + mid]
    p_rim[RIM:] = k_rim[4, RIM:] + q[RIM + mid :]
    level = Parts(k_mid, k_rim, p_mid, p_rim)
    write_x(level, to_xa, to_xb)
    write_z(level, range(0, level.rows, 4), to_za, to_zb)


class Whole:
    def __init__(self, ref):
        self.ref = ref
        self.rows = ref.shape[1]

    def row(self, f, x):
        return self.ref[f, x]

    def group(self, f, g):
        if g is None:
            return jnp.concatenate([self.ref[f, 0:RIM], self.ref[f, self.rows - RIM :]], axis=0)
        return self.ref[f, RIM + g * GROUP : RIM + (g + 1) * GROUP]


class Parts:
    def __init__(self, mid, rim, p_mid=None, p_rim=None, rows=None):
        self.arrays = (mid, rim, p_mid, p_rim)
        self.rows = rows or mid.shape[1] + 2 * RIM

    def pick(self, f):
        mid, rim, p_mid, p_rim = self.arrays
        if f == 4 and p_mid is not None:
            return p_mid, p_rim
        return mid if mid is None else mid.at[f], rim if rim is None else rim.at[f]

    def row(self, f, x):
        mid, rim = self.pick(f)
        if RIM <= x < self.rows - RIM:
            return mid[x - RIM]
        return rim[x if x < RIM else x - self.rows + 2 * RIM]

    def group(self, f, g):
        mid, rim = self.pick(f)
        return rim[...] if g is None else mid[g * GROUP : (g + 1) * GROUP]

    def store(self, f, x, value):
        mid, rim = self.pick(f)
        if RIM <= x < self.rows - RIM:
            mid[x - RIM] = value
        else:
            rim[x if x < RIM else x - self.rows + 2 * RIM] = value


def join_last(ut, p):
    low = lax.broadcasted_iota(jnp.int32, ut.shape, 0) < 4
    return jnp.where(low, pltpu.roll(ut, 3, 0), pltpu.roll(p, 7, 0))


def join_first(ut, p):
    low = lax.broadcasted_iota(jnp.int32, ut.shape, 0) < 4
    return jnp.where(low, ut, pltpu.roll(p, 4, 0))


def write_x(level, to_xa, to_xb):
    even = is_even("ax")
    for f in range(5):
        for i in range(3):
            first, last = level.row(f, i), level.row(f, level.rows - 3 + i)
            to_xa[3 * f + i] = jnp.where(even, last, first)
            to_xb[3 * f + i] = jnp.where(even, first, last)


def write_z(level, starts, to_za, to_zb):
    even = is_even("az")
    row = None
    for i, x in enumerate(starts):
        first, last = [], []
        for y in range(x, x + 4):
            ut, p = level.row(2, y), level.row(4, y)
            first.append(join_first(ut[0:8], p[0:8]))
            last.append(join_last(ut[8:16], p[8:16]))
        if row is None:
            row = lax.broadcasted_iota(jnp.int32, first[0].shape, 0) % 4 == 3
        for t in range(3):
            shift = 3 - t
            one = jnp.where(row, pltpu.roll(first[3], shift, 0), first[t])
            two = jnp.where(row, pltpu.roll(last[3], shift, 0), last[t])
            to_za[3 * i + t] = jnp.where(even, two, one)
            to_zb[3 * i + t] = jnp.where(even, one, two)


def edges_body(state, to_xa, to_xb, to_za, to_zb):
    level = Whole(state)
    write_x(level, to_xa, to_xb)
    write_z(level, range(0, level.rows, 4), to_za, to_zb)


def fill_halo(halo, xa, xb):
    n_ax, ax = lax.axis_size("ax"), lax.axis_index("ax")
    even = is_even("ax")
    for f in range(halo.shape[1]):
        a, b = xa[3 * f : 3 * f + 3], xb[3 * f : 3 * f + 3]
        halo[0, f] = jnp.where(ax > 0, jnp.where(even, b, a), 0.0)
        halo[1, f] = jnp.where(ax < n_ax - 1, jnp.where(even, a, b), 0.0)


def inverse_step(cols, radial):
    base = cols * lax.axis_size("az") / (2.0 * math.pi)
    at = lax.broadcasted_iota(jnp.int32, (1, radial), 1).astype(F32)
    return base / (base / hub_ratio + radial_step * (at + 0.5))


def along(row, x):
    total = drp_coeffs[0] * (row(x + 1) - row(x - 1))
    for s in (2, 3):
        total = total + drp_coeffs[s - 1] * (row(x + s) - row(x - s))
    return total


def apply_operator(level, groups, za, zb, tmat, rmat, finish, halo=None):
    even = is_even("az")
    tiles = level.rows // 4 * 3
    rim = RIM // 4 * 3

    def row(f, x):
        if x < 0:
            return halo[0, f, x + 3]
        if x >= level.rows:
            return halo[1, f, x - level.rows]
        return level.row(f, x)

    def beside(g):
        spans = [(0, rim), (tiles - rim, tiles)] if g is None else [(rim + 6 * g, rim + 6 * g + 6)]
        start = za.shape[0] - tiles
        if za.shape[0] == 2 * rim:
            spans, start = [(0, rim), (rim, 2 * rim)], 0
        elif za.shape[0] == tiles - 2 * rim:
            start = -rim
        sides = []
        for swap_ab in (False, True):
            for a, b in spans:
                last_b = zb.shape[0] - za.shape[0] + start
                got_a, got_b = za[start + a : start + b], zb[last_b + a : last_b + b]
                pair = (got_a, got_b) if swap_ab else (got_b, got_a)
                sides.append(jnp.where(even, *pair).reshape((b - a) * 8, za.shape[2]))
        return split(jnp.concatenate(sides, axis=0))

    for g in groups:
        if g is None:
            xs = [*range(RIM), *range(level.rows - RIM, level.rows)]
        else:
            xs = range(RIM + g * GROUP, RIM + (g + 1) * GROUP)
        ut, ur, p = [level.group(f, g) for f in (2, 3, 4)]
        _, cols, radial = ut.shape
        inv_h = inverse_step(cols, radial)
        side_hi, side_lo = beside(g)
        p_hi, p_lo = split(p.reshape(GROUP * cols, radial))
        ut_hi, ut_lo = split(ut.reshape(GROUP * cols, radial))
        ur_hi, ur_lo = split(ur.reshape(GROUP * cols, radial))

        def across(which, hi, lo):
            hi = jnp.concatenate([hi, side_hi], axis=0)
            lo = jnp.concatenate([lo, side_lo], axis=0)
            return dot(tmat[which, 0], hi) + dot(tmat[which, 0], lo) + dot(tmat[which, 1], hi)

        def outward(which, hi, lo):
            return dot(hi, rmat[which, 0]) + dot(lo, rmat[which, 0]) + dot(hi, rmat[which, 1])

        div_tr = across(0, ut_hi, ut_lo) * inv_h + outward(0, ur_hi, ur_lo)
        p_t = across(1, p_hi, p_lo) * inv_h
        p_r = outward(1, p_hi, p_lo)
        for i, x in enumerate(xs):
            part = slice(i * cols, (i + 1) * cols)
            d = [along(lambda y: row(f, y), x) for f in range(5)]
            div = d[1] + div_tr[part]
            finish(
                x,
                [
                    -mach_number * d[0] - div,
                    -mach_number * d[1] - d[4],
                    -mach_number * d[2] - p_t[part],
                    -mach_number * d[3] - p_r[part],
                    -mach_number * d[4] - div,
                ],
            )


def start_body(state, za, zb, xa, xb, tmat, rmat, k_mid, k_rim, halo):
    fill_halo(halo, xa, xb)
    level, out = Whole(state), Parts(k_mid, k_rim)

    def finish(x, tend):
        for f in range(5):
            out.store(f, x, tend[f])

    apply_operator(level, [*range(k_mid.shape[1] // GROUP), None], za, zb, tmat, rmat, finish, halo)


def inner_stage_body(factor, level, base, za, zb, tmat, rmat, out_mid, to_za, to_zb):
    def finish(x, tend):
        for f in range(5):
            out_mid[f, x - RIM] = base.row(f, x) + factor * tend[f]

    apply_operator(level, range(out_mid.shape[1] // GROUP), za, zb, tmat, rmat, finish)
    write_z(Parts(out_mid, None, rows=level.rows), range(RIM, level.rows - RIM, 4), to_za, to_zb)


def rim_stage_body(factor, level, base, xa, xb, za, zb, tmat, rmat, out_rim, to_xa, to_xb, to_za, to_zb, halo):
    fill_halo(halo, xa, xb)
    out = Parts(None, out_rim, rows=level.rows)

    def finish(x, tend):
        for f in range(5):
            out.store(f, x, base.row(f, x) + factor * tend[f])

    apply_operator(level, [None], za, zb, tmat, rmat, finish, halo)
    write_x(out, to_xa, to_xb)
    write_z(out, [0, level.rows - RIM], to_za, to_zb)


def last_finish(fields, k, store):
    def finish(x, tend):
        for f in range(5):
            store(f, x, fields[f, x] + time_step * k.row(f, x) + (0.5 * time_step * time_step) * tend[f])

    return finish


def inner_last_body(level, k, fields, za, zb, tmat, rmat, out, result, sems):
    def store(f, x, value):
        result[f, x - RIM] = value

    def copy(g):
        at = g * GROUP
        return pltpu.make_async_copy(
            result.at[:, at : at + GROUP], out.at[:, RIM + at : RIM + at + GROUP], sems.at[g]
        )

    groups = range(result.shape[1] // GROUP)
    for g in groups:
        apply_operator(level, [g], za, zb, tmat, rmat, last_finish(fields, k, store))
        copy(g).start()
    for g in groups:
        copy(g).wait()


def rim_last_body(level, k, fields, xa, xb, za, zb, tmat, rmat, out, halo, result, sems):
    rows = level.rows
    fill_halo(halo, xa, xb)

    def store(f, x, value):
        result[f, x if x < RIM else x - rows + 2 * RIM] = value

    apply_operator(level, [None], za, zb, tmat, rmat, last_finish(fields, k, store), halo)
    copies = [
        pltpu.make_async_copy(result.at[:, 0:RIM], out.at[:, 0:RIM], sems.at[0]),
        pltpu.make_async_copy(result.at[:, RIM:], out.at[:, rows - RIM :], sems.at[1]),
    ]
    for copy in copies:
        copy.start()
    for copy in copies:
        copy.wait()


def local(noise, half_width, owner, target_cell, fields):
    px, pa, fine = noise.shape
    cx, ca, radial = fields.shape[1:]
    ncols = px * pa
    most = ncols // 2
    n_az = lax.axis_size("az")
    inner = cx - 2 * RIM

    block = ((px, pa, fine), F32)
    even = is_even("ax")
    to_a = jnp.where(even, noise[px - HMAX :], noise[:HMAX])
    to_b = jnp.where(even, noise[:HMAX], noise[px - HMAX :])
    noise_a, noise_b = swap(to_a, to_b, "ax")
    send_x, send_z = ((15, ca, radial), F32), ((cx // 4 * 3, 8, radial), F32)
    sends = [send_x, send_x, send_z, send_z]
    xa, xb, za, zb = full_specs(edges_body, sends, [fields], name="edges", after=[to_a])
    uxa, uxb = swap(xa, xb, "ax")
    partial, half_width = full_specs(
        inner_body, [block, ((px, pa, fine), jnp.int32)], [noise, half_width], name="filter_inner", after=[za]
    )
    long_z = ((px + send_z[0][0], 8, fine // 2), F32)
    filtered, to_a, to_b = full_specs(
        first_body,
        [block, long_z, ((px, 8, fine // 2), F32)],
        [partial, half_width, noise_a, noise_b, za],
        [((2, HMAX, pa, fine), F32)],
        name="filter_axial",
    )
    got_a, got_b = swap(to_a, to_b, "az")
    (uzb,) = swap_b(zb, "az")
    pick, cells, own = full_specs(
        route_body,
        [((4 * most, ncols), BF16), ((4, 8, radial), F32), ((1, ncols), jnp.int32)],
        [owner.reshape(1, ncols), target_cell.reshape(1, ncols)],
        name="route",
        after=[filtered],
    )
    partial, weights = full_specs(
        middle_body,
        [block, ((HMAX + 1, px, pa, fine), F32)],
        [filtered, half_width],
        [((px, 32, fine), F32)],
        name="filter_middle",
        after=[pick],
    )
    tiles = most // 8 + 1
    packet, packet_z = ((tiles, 8, radial), F32), ((tiles + 1, 8, radial), F32)
    binned, xa, xb, za, zb = full_specs(
        second_body,
        [((ncols, radial), F32), packet, packet, packet_z, packet_z],
        [partial, weights, got_a, got_b, pick, cells],
        [((ncols, fine), BF16), ((ncols, fine), BF16)],
        name="filter_rest",
        cost=COST,
    )
    packets = (*swap(xa, xb, "ax"), *swap(za, zb, "az"))

    tmat = jnp.asarray(azimuth_matrices(ca))
    rmat = jnp.asarray(radial_matrices(float(ca * n_az), radial))
    mid, rim = ((5, inner, ca, radial), F32), ((5, 2 * RIM, ca, radial), F32)
    halo = ((2, 5, 3, ca, radial), F32)
    k_mid, k_rim = full_specs(
        start_body, [mid, rim], [fields, got_a, uzb, uxa, uxb, tmat, rmat], [halo], name="operator", after=[binned]
    )
    p_mid, p_rim, *edges = full_specs(
        gather_body,
        [((inner, ca, radial), F32), ((2 * RIM, ca, radial), F32), *sends],
        [binned, own, *packets, k_mid, k_rim],
        name="gather",
    )
    k = [k_mid, k_rim, p_mid, p_rim]
    inner_z, rim_z = ((inner // 4 * 3, 8, radial), F32), ((RIM // 2 * 3, 8, radial), F32)
    za, zb = swap(edges[2], edges[3], "az")
    xa, xb = swap(edges[0], edges[1], "ax")
    level, rim_a, rim_b = k, za, zb
    for factor in (time_step / 4.0, time_step / 3.0):
        size = len(level)

        def body(*refs, factor=factor, size=size):
            inner_stage_body(factor, Parts(*refs[:size]), Parts(*refs[size : size + 4]), *refs[size + 4 :])

        new_mid, to_za, to_zb = full_specs(
            body, [mid, inner_z, inner_z], [*level, *k, za, zb, tmat, rmat], name="stage_inner", cost=COST if level is k else SOME
        )
        za, zb = swap(to_za, to_zb, "az")

        def body(*refs, factor=factor, size=size):
            rim_stage_body(factor, Parts(*refs[:size]), Parts(*refs[size : size + 4]), *refs[size + 4 :])

        new_rim, to_xa, to_xb, to_za, to_zb = full_specs(
            body,
            [rim, send_x, send_x, rim_z, rim_z],
            [*level, *k, xa, xb, rim_a, rim_b, tmat, rmat],
            [halo],
            name="stage_rim",
            after=[new_mid],
            cost=COST,
        )
        xa, xb = swap(to_xa, to_xb, "ax")
        rim_a, rim_b = swap(to_za, to_zb, "az")
        level = [new_mid, new_rim]

    def body(*refs):
        inner_last_body(Parts(*refs[:2]), Parts(*refs[2:6]), *refs[6:])

    whole = ((5, cx, ca, radial), F32)
    (out,) = full_specs(
        body,
        [whole],
        [*level, *k, fields, za, zb, tmat, rmat],
        [mid, pltpu.SemaphoreType.DMA((inner // GROUP,))],
        name="final_inner",
        out_specs=[ANY],
        cost=SOME,
    )

    def body(out_in, *refs):
        rim_last_body(Parts(*refs[:2]), Parts(*refs[2:6]), *refs[6:])

    (out,) = full_specs(
        body,
        [whole],
        [out, *level, *k, fields, xa, xb, rim_a, rim_b, tmat, rmat],
        [halo, rim, pltpu.SemaphoreType.DMA((2,))],
        name="final_rim",
        in_specs=[ANY] + [VM] * 13,
        out_specs=[ANY],
        alias={0: 0},
    )
    return out


def solution(mesh):
    return jax.shard_map(
        local,
        mesh=mesh,
        in_specs=(
            P("ax", "az", None),
            P("ax", "az", None),
            P(("ax", "az")),
            P(("ax", "az")),
            P(None, "ax", "az", None),
        ),
        out_specs=P(None, "ax", "az", None),
        check_vma=False,
    )
```

```python
import math

import numpy as np

import jax
import jax.numpy as jnp
from jax import lax
from jax.experimental import pallas as pl
from jax.experimental.pallas import tpu as pltpu
from jax.sharding import PartitionSpec as P

HMAX = 4
drp_coeffs = (0.770882380518, -0.166705904415, 0.02084314277)
mach_number = 0.5
time_step = 0.7
source_gain = 4.0
radial_step = 2.0
hub_ratio = 1.6

F32 = jnp.float32
BF16 = jnp.bfloat16
VM = pl.BlockSpec(memory_space=pltpu.VMEM)
ANY = pl.BlockSpec(memory_space=pl.ANY)
PARAMS = pltpu.CompilerParams(vmem_limit_bytes=24 * 1024 * 1024)
GROUP = 8
RIM = 4
SOME = 2_000_000_000
COST = 1 << 37


def np_split(matrix):
    hi = matrix.astype(np.float32).astype(BF16)
    lo = (matrix - hi.astype(np.float64)).astype(np.float32).astype(BF16)
    return hi, lo


def filter_table():
    table = np.zeros((HMAX + 1, HMAX))
    for h in range(1, HMAX + 1):
        weights = [math.exp(-2.0 * k * k / (h * h)) if k <= h else 0.0 for k in range(HMAX + 1)]
        total = weights[0] + 2.0 * sum(weights[1:])
        table[:, h - 1] = [w / total for w in weights]
    return table


def radial_rows(na_total, radial):
    base = na_total / (2.0 * math.pi)
    radius = base / hub_ratio + radial_step * (np.arange(radial) + 0.5)
    return base / radius, 1.0 / radius


def radial_matrices(na_total, radial):
    diff = np.zeros((radial, radial))
    for s, a in zip((1, 2, 3), drp_coeffs):
        for j in range(radial):
            if j + s < radial:
                diff[j + s, j] += a / radial_step
            if j - s >= 0:
                diff[j - s, j] -= a / radial_step
    with_r = diff + np.diag(radial_rows(na_total, radial)[1])
    return np.stack([np.stack(np_split(with_r)), np.stack(np_split(diff))])


def azimuth_matrices(cols):
    packed = GROUP * 6
    full = np.zeros((2, GROUP * cols, GROUP * cols + 2 * packed))
    for which in range(2):
        for x in range(GROUP):
            for i in range(cols):
                for s, a in zip((1, 2, 3), drp_coeffs):
                    for j, sign in ((i + s, 1.0), (i - s, -1.0)):
                        if 0 <= j < cols:
                            at = x * cols + j
                        else:
                            m = j + 3 if j < 0 else j - cols
                            tile, row = (x % 4, m) if x % 4 < 3 else (m, 3)
                            at = GROUP * cols + (x // 4 * 3 + tile) * 8 + row + 4 * which
                            at += packed if j >= cols else 0
                        full[which, x * cols + i, at] += sign * a
    return np.stack([np.stack(np_split(full[w])) for w in range(2)])


def split(x):
    hi = x.astype(BF16)
    return hi, (x - hi.astype(F32)).astype(BF16)


def dot(a, b):
    return lax.dot_general(a, b, (((1,), (0,)), ((), ())), preferred_element_type=F32)


def is_even(axis):
    return lax.rem(lax.axis_index(axis), 2) == 0


def swap(to_a, to_b, axis):
    devices = lax.axis_size(axis)
    pairs_a = [(i, i ^ 1) for i in range(devices)]
    pairs_b = [(i, (i - 1) % devices if i % 2 == 0 else (i + 1) % devices) for i in range(devices)]
    return lax.ppermute(to_a, axis, pairs_a), lax.ppermute(to_b, axis, pairs_b)


def swap_b(value, axis):
    devices = lax.axis_size(axis)
    pairs = [(i, (i - 1) % devices if i % 2 == 0 else (i + 1) % devices) for i in range(devices)]
    return (lax.ppermute(value, axis, pairs),)


def full_specs(body, outs, args, scratch=(), name=None, in_specs=None, out_specs=None, after=(), cost=0, alias=None):
    skip = len(args)

    def run(*refs):
        body(*refs[:skip], *refs[skip + len(after) :])

    return pl.pallas_call(
        run,
        out_shape=[jax.ShapeDtypeStruct(s, d) for s, d in outs],
        in_specs=(in_specs or [VM] * skip) + [ANY] * len(after),
        input_output_aliases=alias or {},
        out_specs=out_specs or [VM] * len(outs),
        scratch_shapes=[pltpu.VMEM(*s) if isinstance(s, tuple) else s for s in scratch],
        compiler_params=PARAMS,
        name=name,
        cost_estimate=pl.CostEstimate(flops=cost, bytes_accessed=0, transcendentals=0),
    )(*args, *after)


def route_body(owner_ref, target_ref, pick_ref, cells_ref, own_ref):
    n_ax, n_az = lax.axis_size("ax"), lax.axis_size("az")
    ax, az = lax.axis_index("ax"), lax.axis_index("az")
    step_x = jnp.where(lax.rem(ax, 2) == 0, 1, -1)
    step_z = jnp.where(lax.rem(az, 2) == 0, 1, -1)
    me = ax * n_az + az
    b_x = ax - step_x
    ids = [
        (ax + step_x) * n_az + az,
        jnp.where((b_x >= 0) & (b_x < n_ax), b_x * n_az + az, -1),
        ax * n_az + lax.rem(az + step_z + n_az, n_az),
        ax * n_az + lax.rem(az - step_z + n_az, n_az),
    ]
    owner = owner_ref[...]
    target = target_ref[...]
    ncols = owner.shape[1]
    most = ncols // 2
    own_ref[...] = jnp.where(owner == me, target, -1)
    row = lax.broadcasted_iota(jnp.int32, (8, ncols), 0)
    marks = jnp.zeros((8, ncols), F32)
    for d, i in enumerate(ids):
        marks = jnp.where((row == d) & (owner == i), 1.0, marks)
    before = lax.broadcasted_iota(jnp.int32, (ncols, ncols), 0) < lax.broadcasted_iota(jnp.int32, (ncols, ncols), 1)
    rank = dot(marks.astype(BF16), jnp.where(before, 1.0, 0.0).astype(BF16))
    coarse = (target // 32).astype(F32)
    fine = (target % 32).astype(F32)
    digits = jnp.where(row == 0, coarse, jnp.where(row == 1, fine, 0.0)).astype(BF16)
    slot = lax.broadcasted_iota(jnp.int32, (most, ncols), 0).astype(F32)
    for d in range(4):
        wanted = jnp.where(marks[d : d + 1] > 0.0, rank[d : d + 1], -1.0)
        pick = jnp.where(slot == wanted, 1.0, 0.0).astype(BF16)
        pick_ref[d * most : (d + 1) * most, :] = pick
        found = lax.dot_general(digits, pick, (((1,), (1,)), ((), ())), preferred_element_type=F32)
        cells_ref[d, :, :] = jnp.zeros(cells_ref.shape[1:], F32)
        cells_ref[d, 0:1, 0:most] = found[0:1] * 32.0 + found[1:2]


def weights_of(h):
    table = filter_table()
    le = [h <= 1, h <= 2, h <= 3]
    out = []
    for k in range(HMAX + 1):
        value = jnp.full(h.shape, table[k, 3], F32)
        for j in (2, 1, 0):
            if j > 0 and table[k, j] == 0.0 and table[k, j - 1] == 0.0:
                value = jnp.where(le[j], 0.0, value)
                break
            value = jnp.where(le[j], table[k, j], value)
        out.append(value)
    return out


def inner_body(noise_ref, half_ref, first_ref, kept_ref):
    rows = noise_ref.shape[0]
    kept_ref[...] = half_ref[...]
    for x in range(rows):
        w = weights_of(half_ref[x])
        total = w[0] * noise_ref[x]
        for k in range(1, HMAX + 1):
            near = [noise_ref[y] for y in (x - k, x + k) if 0 <= y < rows]
            if near:
                total = total + w[k] * (near[0] + near[1] if len(near) == 2 else near[0])
        first_ref[x] = total


def first_body(
    inner_ref, half_ref, got_a_ref, got_b_ref, edge_a_ref, first_ref, to_a_ref, to_b_ref, halo
):
    n_ax, ax = lax.axis_size("ax"), lax.axis_index("ax")
    even_x, even_z = is_even("ax"), is_even("az")
    rows, _, fine = half_ref.shape
    halo[0] = jnp.where(ax > 0, jnp.where(even_x, got_b_ref[...], got_a_ref[...]), 0.0)
    halo[1] = jnp.where(ax < n_ax - 1, jnp.where(even_x, got_a_ref[...], got_b_ref[...]), 0.0)
    for x in range(HMAX, rows - HMAX):
        first_ref[x] = inner_ref[x]
    for i in range(HMAX):
        w = weights_of(half_ref[i])
        total = inner_ref[i]
        for k in range(i + 1, HMAX + 1):
            total = total + w[k] * halo[0, HMAX + i - k]
        first_ref[i] = total
        x = rows - 1 - i
        w = weights_of(half_ref[x])
        total = inner_ref[x]
        for k in range(i + 1, HMAX + 1):
            total = total + w[k] * halo[1, k - i - 1]
        first_ref[x] = total
    half = rows // 2
    low = lax.broadcasted_iota(jnp.int32, (8, fine), 0) < 4
    for x in range(half):
        last = jnp.where(low, pltpu.roll(first_ref[x, 8:16], 4, 0), first_ref[x + half, 8:16])
        begin = jnp.where(low, first_ref[x, 0:8], pltpu.roll(first_ref[x + half, 0:8], 4, 0))
        for ref, value in ((to_a_ref, jnp.where(even_z, last, begin)), (to_b_ref, jnp.where(even_z, begin, last))):
            ref[x] = value[:, : fine // 2]
            ref[half + x] = value[:, fine // 2 :]
    to_a_ref[rows:] = edge_a_ref[...]


def middle_body(first_ref, half_ref, partial_ref, weight_ref, wide):
    rows, cols, fine = first_ref.shape
    blank = jnp.zeros((rows, 8, fine), F32)
    wide[:, 0:8] = blank
    wide[:, 24:32] = blank
    for x in range(rows):
        wide[x, 8:24] = first_ref[x]
    for x in range(rows):
        w = weights_of(half_ref[x])
        total = w[0] * first_ref[x]
        for k in range(1, HMAX + 1):
            total = total + w[k] * (wide[x, 8 - k : 24 - k] + wide[x, 8 + k : 24 + k])
        partial_ref[x] = total
        for k in range(HMAX + 1):
            weight_ref[k, x] = w[k]


def second_body(
    partial_ref, weight_ref, got_a_ref, got_b_ref, pick_ref, cells_ref,
    own_ref, to_xa, to_xb, to_za, to_zb, fine_hi, fine_lo,
):
    even = is_even("az")
    rows, cols, fine = partial_ref.shape
    half = rows // 2
    lane = lax.broadcasted_iota(jnp.int32, (cols, fine), 1)
    row = lax.broadcasted_iota(jnp.int32, (8, fine), 0)
    for x in range(rows):
        y = x % half
        got_a, got_b = [jnp.concatenate([got[y], got[half + y]], axis=1) for got in (got_a_ref, got_b_ref)]
        before, after = jnp.where(even, got_b, got_a), jnp.where(even, got_a, got_b)
        if x < half:
            before = pltpu.roll(before, 4, 0)
        else:
            after = pltpu.roll(after, 4, 0)
        w = [weight_ref[k, x] for k in range(HMAX + 1)]
        total = partial_ref[x]
        for k in range(1, HMAX + 1):
            low = jnp.where(row < k, pltpu.roll(before, k, 0), 0.0)
            high = jnp.where(row >= 8 - k, pltpu.roll(after, 8 - k, 0), 0.0)
            total = total + w[k] * jnp.concatenate([low, high], axis=0)
        result = w[0] * total
        for k in range(1, HMAX + 1):
            up = jnp.where(lane < fine - k, pltpu.roll(total, fine - k, 1), 0.0)
            down = jnp.where(lane >= k, pltpu.roll(total, k, 1), 0.0)
            result = result + w[k] * (up + down)
        hi, lo = split(result)
        fine_hi[x * cols : (x + 1) * cols] = hi
        fine_lo[x * cols : (x + 1) * cols] = lo
    radial = own_ref.shape[1]
    above = lax.broadcasted_iota(jnp.int32, (fine, radial), 0) - lax.broadcasted_iota(
        jnp.int32, (fine, radial), 1
    ) * (fine // radial)
    bins = jnp.where((above >= 0) & (above < fine // radial), source_gain, 0.0).astype(BF16)
    binned = dot(fine_hi[...], bins) + dot(fine_lo[...], bins)
    own_ref[...] = binned
    hi, lo = split(binned)
    most = pick_ref.shape[0] // 4
    for d, out in enumerate((to_xa, to_xb, to_za, to_zb)):
        pick = pick_ref[d * most : (d + 1) * most]
        tiles = most // 8
        out[0:tiles] = (dot(pick, hi) + dot(pick, lo)).reshape(tiles, 8, radial)
        out[tiles] = cells_ref[d]
    for out in (to_xa, to_xb):
        out[most // 8 + 1] = jnp.zeros(out.shape[1:], F32)


def gather_body(
    binned_ref, own_ref, xa, xb, za, zb, k_mid, k_rim, p_mid, p_rim, to_xa, to_xb, to_za, to_zb
):
    mid, cols, radial = p_mid.shape
    cells = (mid + 2 * RIM) * cols
    most = 8 * (za.shape[0] - 1)

    def onehot(row):
        at = lax.broadcasted_iota(jnp.int32, (cells, row.shape[1]), 0)
        return jnp.where(at == row, 1.0, 0.0).astype(BF16)

    mats = [onehot(own_ref[...])]
    packets = [binned_ref[...]]
    for got in (xa, xb, za, zb):
        tiles = most // 8
        mats.append(onehot(got[tiles, 0:1, 0:most].astype(jnp.int32)))
        packets.append(got[0:tiles].reshape(most, radial))
    mat = jnp.concatenate(mats, axis=1)
    hi, lo = split(jnp.concatenate(packets, axis=0))
    q = (dot(mat, hi) + dot(mat, lo)).reshape(mid + 2 * RIM, cols, radial)
    p_rim[0:RIM] = k_rim[4, 0:RIM] + q[0:RIM]
    p_mid[...] = k_mid[4] + q[RIM : RIM + mid]
    p_rim[RIM:] = k_rim[4, RIM:] + q[RIM + mid :]
    level = Parts(k_mid, k_rim, p_mid, p_rim)
    write_x(level, to_xa, to_xb)
    write_z(level, range(0, level.rows, 4), to_za, to_zb)


class Whole:
    def __init__(self, ref):
        self.ref = ref
        self.rows = ref.shape[1]

    def row(self, f, x):
        return self.ref[f, x]

    def group(self, f, g):
        if g is None:
            return jnp.concatenate([self.ref[f, 0:RIM], self.ref[f, self.rows - RIM :]], axis=0)
        return self.ref[f, RIM + g * GROUP : RIM + (g + 1) * GROUP]


class Parts:
    def __init__(self, mid, rim, p_mid=None, p_rim=None, rows=None):
        self.arrays = (mid, rim, p_mid, p_rim)
        self.rows = rows or mid.shape[1] + 2 * RIM

    def pick(self, f):
        mid, rim, p_mid, p_rim = self.arrays
        if f == 4 and p_mid is not None:
            return p_mid, p_rim
        return mid if mid is None else mid.at[f], rim if rim is None else rim.at[f]

    def row(self, f, x):
        mid, rim = self.pick(f)
        if RIM <= x < self.rows - RIM:
            return mid[x - RIM]
        return rim[x if x < RIM else x - self.rows + 2 * RIM]

    def group(self, f, g):
        mid, rim = self.pick(f)
        return rim[...] if g is None else mid[g * GROUP : (g + 1) * GROUP]

    def store(self, f, x, value):
        mid, rim = self.pick(f)
        if RIM <= x < self.rows - RIM:
            mid[x - RIM] = value
        else:
            rim[x if x < RIM else x - self.rows + 2 * RIM] = value


def join_last(ut, p):
    low = lax.broadcasted_iota(jnp.int32, ut.shape, 0) < 4
    return jnp.where(low, pltpu.roll(ut, 3, 0), pltpu.roll(p, 7, 0))


def join_first(ut, p):
    low = lax.broadcasted_iota(jnp.int32, ut.shape, 0) < 4
    return jnp.where(low, ut, pltpu.roll(p, 4, 0))


def write_x(level, to_xa, to_xb):
    even = is_even("ax")
    for f in range(5):
        for i in range(3):
            first, last = level.row(f, i), level.row(f, level.rows - 3 + i)
            to_xa[3 * f + i] = jnp.where(even, last, first)
            to_xb[3 * f + i] = jnp.where(even, first, last)


def write_z(level, starts, to_za, to_zb):
    even = is_even("az")
    row = None
    for i, x in enumerate(starts):
        first, last = [], []
        for y in range(x, x + 4):
            ut, p = level.row(2, y), level.row(4, y)
            first.append(join_first(ut[0:8], p[0:8]))
            last.append(join_last(ut[8:16], p[8:16]))
        if row is None:
            row = lax.broadcasted_iota(jnp.int32, first[0].shape, 0) % 4 == 3
        for t in range(3):
            shift = 3 - t
            one = jnp.where(row, pltpu.roll(first[3], shift, 0), first[t])
            two = jnp.where(row, pltpu.roll(last[3], shift, 0), last[t])
            to_za[3 * i + t] = jnp.where(even, two, one)
            to_zb[3 * i + t] = jnp.where(even, one, two)


def edges_body(state, to_xa, to_xb, to_za, to_zb):
    level = Whole(state)
    write_x(level, to_xa, to_xb)
    write_z(level, range(0, level.rows, 4), to_za, to_zb)


def fill_halo(halo, xa, xb):
    n_ax, ax = lax.axis_size("ax"), lax.axis_index("ax")
    even = is_even("ax")
    for f in range(halo.shape[1]):
        a, b = xa[3 * f : 3 * f + 3], xb[3 * f : 3 * f + 3]
        halo[0, f] = jnp.where(ax > 0, jnp.where(even, b, a), 0.0)
        halo[1, f] = jnp.where(ax < n_ax - 1, jnp.where(even, a, b), 0.0)


def inverse_step(cols, radial):
    base = cols * lax.axis_size("az") / (2.0 * math.pi)
    at = lax.broadcasted_iota(jnp.int32, (1, radial), 1).astype(F32)
    return base / (base / hub_ratio + radial_step * (at + 0.5))


def along(row, x):
    total = drp_coeffs[0] * (row(x + 1) - row(x - 1))
    for s in (2, 3):
        total = total + drp_coeffs[s - 1] * (row(x + s) - row(x - s))
    return total


def apply_operator(level, groups, za, zb, tmat, rmat, finish, halo=None):
    even = is_even("az")
    tiles = level.rows // 4 * 3
    rim = RIM // 4 * 3

    def row(f, x):
        if x < 0:
            return halo[0, f, x + 3]
        if x >= level.rows:
            return halo[1, f, x - level.rows]
        return level.row(f, x)

    def beside(g):
        spans = [(0, rim), (tiles - rim, tiles)] if g is None else [(rim + 6 * g, rim + 6 * g + 6)]
        start = za.shape[0] - tiles
        if za.shape[0] == 2 * rim:
            spans, start = [(0, rim), (rim, 2 * rim)], 0
        elif za.shape[0] == tiles - 2 * rim:
            start = -rim
        sides = []
        for swap_ab in (False, True):
            for a, b in spans:
                last_b = zb.shape[0] - za.shape[0] + start
                got_a, got_b = za[start + a : start + b], zb[last_b + a : last_b + b]
                pair = (got_a, got_b) if swap_ab else (got_b, got_a)
                sides.append(jnp.where(even, *pair).reshape((b - a) * 8, za.shape[2]))
        return split(jnp.concatenate(sides, axis=0))

    for g in groups:
        if g is None:
            xs = [*range(RIM), *range(level.rows - RIM, level.rows)]
        else:
            xs = range(RIM + g * GROUP, RIM + (g + 1) * GROUP)
        ut, ur, p = [level.group(f, g) for f in (2, 3, 4)]
        _, cols, radial = ut.shape
        inv_h = inverse_step(cols, radial)
        side_hi, side_lo = beside(g)
        p_hi, p_lo = split(p.reshape(GROUP * cols, radial))
        ut_hi, ut_lo = split(ut.reshape(GROUP * cols, radial))
        ur_hi, ur_lo = split(ur.reshape(GROUP * cols, radial))

        def across(which, hi, lo):
            hi = jnp.concatenate([hi, side_hi], axis=0)
            lo = jnp.concatenate([lo, side_lo], axis=0)
            return dot(tmat[which, 0], hi) + dot(tmat[which, 0], lo) + dot(tmat[which, 1], hi)

        def outward(which, hi, lo):
            return dot(hi, rmat[which, 0]) + dot(lo, rmat[which, 0]) + dot(hi, rmat[which, 1])

        div_tr = across(0, ut_hi, ut_lo) * inv_h + outward(0, ur_hi, ur_lo)
        p_t = across(1, p_hi, p_lo) * inv_h
        p_r = outward(1, p_hi, p_lo)
        for i, x in enumerate(xs):
            part = slice(i * cols, (i + 1) * cols)
            d = [along(lambda y: row(f, y), x) for f in range(5)]
            div = d[1] + div_tr[part]
            finish(
                x,
                [
                    -mach_number * d[0] - div,
                    -mach_number * d[1] - d[4],
                    -mach_number * d[2] - p_t[part],
                    -mach_number * d[3] - p_r[part],
                    -mach_number * d[4] - div,
                ],
            )


def start_body(state, za, zb, xa, xb, tmat, rmat, k_mid, k_rim, halo):
    fill_halo(halo, xa, xb)
    level, out = Whole(state), Parts(k_mid, k_rim)

    def finish(x, tend):
        for f in range(5):
            out.store(f, x, tend[f])

    apply_operator(level, [*range(k_mid.shape[1] // GROUP), None], za, zb, tmat, rmat, finish, halo)


def inner_stage_body(factor, level, base, za, zb, tmat, rmat, out_mid, to_za, to_zb):
    def finish(x, tend):
        for f in range(5):
            out_mid[f, x - RIM] = base.row(f, x) + factor * tend[f]

    apply_operator(level, range(out_mid.shape[1] // GROUP), za, zb, tmat, rmat, finish)
    write_z(Parts(out_mid, None, rows=level.rows), range(RIM, level.rows - RIM, 4), to_za, to_zb)


def rim_stage_body(factor, level, base, xa, xb, za, zb, tmat, rmat, out_rim, to_xa, to_xb, to_za, to_zb, halo):
    fill_halo(halo, xa, xb)
    out = Parts(None, out_rim, rows=level.rows)

    def finish(x, tend):
        for f in range(5):
            out.store(f, x, base.row(f, x) + factor * tend[f])

    apply_operator(level, [None], za, zb, tmat, rmat, finish, halo)
    write_x(out, to_xa, to_xb)
    write_z(out, [0, level.rows - RIM], to_za, to_zb)


def last_finish(fields, k, store):
    def finish(x, tend):
        for f in range(5):
            store(f, x, fields[f, x] + time_step * k.row(f, x) + (0.5 * time_step * time_step) * tend[f])

    return finish


def inner_last_body(level, k, fields, za, zb, tmat, rmat, out, result, sems):
    def store(f, x, value):
        result[f, x - RIM] = value

    def copy(g):
        at = g * GROUP
        return pltpu.make_async_copy(
            result.at[:, at : at + GROUP], out.at[:, RIM + at : RIM + at + GROUP], sems.at[g]
        )

    groups = range(result.shape[1] // GROUP)
    for g in groups:
        apply_operator(level, [g], za, zb, tmat, rmat, last_finish(fields, k, store))
        copy(g).start()
    for g in groups:
        copy(g).wait()


def rim_last_body(level, k, fields, xa, xb, za, zb, tmat, rmat, out, halo, result, sems):
    rows = level.rows
    fill_halo(halo, xa, xb)

    def store(f, x, value):
        result[f, x if x < RIM else x - rows + 2 * RIM] = value

    apply_operator(level, [None], za, zb, tmat, rmat, last_finish(fields, k, store), halo)
    copies = [
        pltpu.make_async_copy(result.at[:, 0:RIM], out.at[:, 0:RIM], sems.at[0]),
        pltpu.make_async_copy(result.at[:, RIM:], out.at[:, rows - RIM :], sems.at[1]),
    ]
    for copy in copies:
        copy.start()
    for copy in copies:
        copy.wait()


def local(noise, half_width, owner, target_cell, fields):
    px, pa, fine = noise.shape
    cx, ca, radial = fields.shape[1:]
    ncols = px * pa
    most = ncols // 2
    n_az = lax.axis_size("az")
    inner = cx - 2 * RIM

    block = ((px, pa, fine), F32)
    even = is_even("ax")
    to_a = jnp.where(even, noise[px - HMAX :], noise[:HMAX])
    to_b = jnp.where(even, noise[:HMAX], noise[px - HMAX :])
    noise_a, noise_b = swap(to_a, to_b, "ax")
    send_x, send_z = ((15, ca, radial), F32), ((cx // 4 * 3, 8, radial), F32)
    sends = [send_x, send_x, send_z, send_z]
    xa, xb, za, zb = full_specs(edges_body, sends, [fields], name="edges", after=[to_a])
    uxa, uxb = swap(xa, xb, "ax")
    partial, half_width = full_specs(
        inner_body, [block, ((px, pa, fine), jnp.int32)], [noise, half_width], name="filter_inner", after=[za]
    )
    long_z = ((px + send_z[0][0], 8, fine // 2), F32)
    filtered, to_a, to_b = full_specs(
        first_body,
        [block, long_z, ((px, 8, fine // 2), F32)],
        [partial, half_width, noise_a, noise_b, za],
        [((2, HMAX, pa, fine), F32)],
        name="filter_axial",
    )
    got_a, got_b = swap(to_a, to_b, "az")
    (uzb,) = swap_b(zb, "az")
    pick, cells, own = full_specs(
        route_body,
        [((4 * most, ncols), BF16), ((4, 8, radial), F32), ((1, ncols), jnp.int32)],
        [owner.reshape(1, ncols), target_cell.reshape(1, ncols)],
        name="route",
        after=[filtered],
    )
    partial, weights = full_specs(
        middle_body,
        [block, ((HMAX + 1, px, pa, fine), F32)],
        [filtered, half_width],
        [((px, 32, fine), F32)],
        name="filter_middle",
        after=[pick],
    )
    tiles = most // 8 + 1
    packet, packet_x = ((tiles, 8, radial), F32), ((tiles + 1, 8, radial), F32)
    binned, xa, xb, za, zb = full_specs(
        second_body,
        [((ncols, radial), F32), packet_x, packet_x, packet, packet],
        [partial, weights, got_a, got_b, pick, cells],
        [((ncols, fine), BF16), ((ncols, fine), BF16)],
        name="filter_rest",
        cost=COST,
    )
    packets = (*swap(xa, xb, "ax"), *swap(za, zb, "az"))

    tmat = jnp.asarray(azimuth_matrices(ca))
    rmat = jnp.asarray(radial_matrices(float(ca * n_az), radial))
    mid, rim = ((5, inner, ca, radial), F32), ((5, 2 * RIM, ca, radial), F32)
    halo = ((2, 5, 3, ca, radial), F32)
    k_mid, k_rim = full_specs(
        start_body, [mid, rim], [fields, got_a, uzb, uxa, uxb, tmat, rmat], [halo], name="operator", after=[binned]
    )
    p_mid, p_rim, *edges = full_specs(
        gather_body,
        [((inner, ca, radial), F32), ((2 * RIM, ca, radial), F32), *sends],
        [binned, own, *packets, k_mid, k_rim],
        name="gather",
    )
    k = [k_mid, k_rim, p_mid, p_rim]
    inner_z, rim_z = ((inner // 4 * 3, 8, radial), F32), ((RIM // 2 * 3, 8, radial), F32)
    za, zb = swap(edges[2], edges[3], "az")
    xa, xb = swap(edges[0], edges[1], "ax")
    level, rim_a, rim_b = k, za, zb
    for factor in (time_step / 4.0, time_step / 3.0):
        size = len(level)

        def body(*refs, factor=factor, size=size):
            inner_stage_body(factor, Parts(*refs[:size]), Parts(*refs[size : size + 4]), *refs[size + 4 :])

        new_mid, to_za, to_zb = full_specs(
            body, [mid, inner_z, inner_z], [*level, *k, za, zb, tmat, rmat], name="stage_inner", cost=COST if level is k else SOME
        )
        za, zb = swap(to_za, to_zb, "az")

        def body(*refs, factor=factor, size=size):
            rim_stage_body(factor, Parts(*refs[:size]), Parts(*refs[size : size + 4]), *refs[size + 4 :])

        new_rim, to_xa, to_xb, to_za, to_zb = full_specs(
            body,
            [rim, send_x, send_x, rim_z, rim_z],
            [*level, *k, xa, xb, rim_a, rim_b, tmat, rmat],
            [halo],
            name="stage_rim",
            after=[new_mid],
            cost=COST,
        )
        xa, xb = swap(to_xa, to_xb, "ax")
        rim_a, rim_b = swap(to_za, to_zb, "az")
        level = [new_mid, new_rim]

    def body(*refs):
        inner_last_body(Parts(*refs[:2]), Parts(*refs[2:6]), *refs[6:])

    whole = ((5, cx, ca, radial), F32)
    (out,) = full_specs(
        body,
        [whole],
        [*level, *k, fields, za, zb, tmat, rmat],
        [mid, pltpu.SemaphoreType.DMA((inner // GROUP,))],
        name="final_inner",
        out_specs=[ANY],
        cost=SOME,
    )

    def body(out_in, *refs):
        rim_last_body(Parts(*refs[:2]), Parts(*refs[2:6]), *refs[6:])

    (out,) = full_specs(
        body,
        [whole],
        [out, *level, *k, fields, xa, xb, rim_a, rim_b, tmat, rmat],
        [halo, rim, pltpu.SemaphoreType.DMA((2,))],
        name="final_rim",
        in_specs=[ANY] + [VM] * 13,
        out_specs=[ANY],
        alias={0: 0},
    )
    return out


def solution(mesh):
    return jax.shard_map(
        local,
        mesh=mesh,
        in_specs=(
            P("ax", "az", None),
            P("ax", "az", None),
            P(("ax", "az")),
            P(("ax", "az")),
            P(None, "ax", "az", None),
        ),
        out_specs=P(None, "ax", "az", None),
        check_vma=False,
    )
```

```python
import math

import numpy as np

import jax
import jax.numpy as jnp
from jax import lax
from jax.experimental import pallas as pl
from jax.experimental.pallas import tpu as pltpu
from jax.sharding import PartitionSpec as P

HMAX = 4
drp_coeffs = (0.770882380518, -0.166705904415, 0.02084314277)
mach_number = 0.5
time_step = 0.7
source_gain = 4.0
radial_step = 2.0
hub_ratio = 1.6

F32 = jnp.float32
BF16 = jnp.bfloat16
VM = pl.BlockSpec(memory_space=pltpu.VMEM)
ANY = pl.BlockSpec(memory_space=pl.ANY)
PARAMS = pltpu.CompilerParams(vmem_limit_bytes=24 * 1024 * 1024)
GROUP = 8
RIM = 4
MORE = 2_500_000_000
SOME = 2_000_000_000
COST = 1 << 37


def np_split(matrix):
    hi = matrix.astype(np.float32).astype(BF16)
    lo = (matrix - hi.astype(np.float64)).astype(np.float32).astype(BF16)
    return hi, lo


def filter_table():
    table = np.zeros((HMAX + 1, HMAX))
    for h in range(1, HMAX + 1):
        weights = [math.exp(-2.0 * k * k / (h * h)) if k <= h else 0.0 for k in range(HMAX + 1)]
        total = weights[0] + 2.0 * sum(weights[1:])
        table[:, h - 1] = [w / total for w in weights]
    return table


def radial_rows(na_total, radial):
    base = na_total / (2.0 * math.pi)
    radius = base / hub_ratio + radial_step * (np.arange(radial) + 0.5)
    return base / radius, 1.0 / radius


def radial_matrices(na_total, radial):
    diff = np.zeros((radial, radial))
    for s, a in zip((1, 2, 3), drp_coeffs):
        for j in range(radial):
            if j + s < radial:
                diff[j + s, j] += a / radial_step
            if j - s >= 0:
                diff[j - s, j] -= a / radial_step
    with_r = diff + np.diag(radial_rows(na_total, radial)[1])
    return np.stack([np.stack(np_split(with_r)), np.stack(np_split(diff))])


def azimuth_matrices(cols):
    packed = GROUP * 6
    full = np.zeros((2, GROUP * cols, GROUP * cols + 2 * packed))
    for which in range(2):
        for x in range(GROUP):
            for i in range(cols):
                for s, a in zip((1, 2, 3), drp_coeffs):
                    for j, sign in ((i + s, 1.0), (i - s, -1.0)):
                        if 0 <= j < cols:
                            at = x * cols + j
                        else:
                            m = j + 3 if j < 0 else j - cols
                            tile, row = (x % 4, m) if x % 4 < 3 else (m, 3)
                            at = GROUP * cols + (x // 4 * 3 + tile) * 8 + row + 4 * which
                            at += packed if j >= cols else 0
                        full[which, x * cols + i, at] += sign * a
    return np.stack([np.stack(np_split(full[w])) for w in range(2)])


def split(x):
    hi = x.astype(BF16)
    return hi, (x - hi.astype(F32)).astype(BF16)


def dot(a, b):
    return lax.dot_general(a, b, (((1,), (0,)), ((), ())), preferred_element_type=F32)


def is_even(axis):
    return lax.rem(lax.axis_index(axis), 2) == 0


def swap(to_a, to_b, axis):
    devices = lax.axis_size(axis)
    pairs_a = [(i, i ^ 1) for i in range(devices)]
    pairs_b = [(i, (i - 1) % devices if i % 2 == 0 else (i + 1) % devices) for i in range(devices)]
    return lax.ppermute(to_a, axis, pairs_a), lax.ppermute(to_b, axis, pairs_b)


def swap_b(value, axis):
    devices = lax.axis_size(axis)
    pairs = [(i, (i - 1) % devices if i % 2 == 0 else (i + 1) % devices) for i in range(devices)]
    return (lax.ppermute(value, axis, pairs),)


def full_specs(body, outs, args, scratch=(), name=None, in_specs=None, out_specs=None, after=(), cost=0, alias=None):
    skip = len(args)

    def run(*refs):
        body(*refs[:skip], *refs[skip + len(after) :])

    return pl.pallas_call(
        run,
        out_shape=[jax.ShapeDtypeStruct(s, d) for s, d in outs],
        in_specs=(in_specs or [VM] * skip) + [ANY] * len(after),
        input_output_aliases=alias or {},
        out_specs=out_specs or [VM] * len(outs),
        scratch_shapes=[pltpu.VMEM(*s) if isinstance(s, tuple) else s for s in scratch],
        compiler_params=PARAMS,
        name=name,
        cost_estimate=pl.CostEstimate(flops=cost, bytes_accessed=0, transcendentals=0),
    )(*args, *after)


def route_body(owner_ref, target_ref, pick_ref, cells_ref, own_ref):
    n_ax, n_az = lax.axis_size("ax"), lax.axis_size("az")
    ax, az = lax.axis_index("ax"), lax.axis_index("az")
    step_x = jnp.where(lax.rem(ax, 2) == 0, 1, -1)
    step_z = jnp.where(lax.rem(az, 2) == 0, 1, -1)
    me = ax * n_az + az
    b_x = ax - step_x
    ids = [
        (ax + step_x) * n_az + az,
        jnp.where((b_x >= 0) & (b_x < n_ax), b_x * n_az + az, -1),
        ax * n_az + lax.rem(az + step_z + n_az, n_az),
        ax * n_az + lax.rem(az - step_z + n_az, n_az),
    ]
    owner = owner_ref[...]
    target = target_ref[...]
    ncols = owner.shape[1]
    most = ncols // 2
    own_ref[...] = jnp.where(owner == me, target, -1)
    row = lax.broadcasted_iota(jnp.int32, (8, ncols), 0)
    marks = jnp.zeros((8, ncols), F32)
    for d, i in enumerate(ids):
        marks = jnp.where((row == d) & (owner == i), 1.0, marks)
    before = lax.broadcasted_iota(jnp.int32, (ncols, ncols), 0) < lax.broadcasted_iota(jnp.int32, (ncols, ncols), 1)
    rank = dot(marks.astype(BF16), jnp.where(before, 1.0, 0.0).astype(BF16))
    coarse = (target // 32).astype(F32)
    fine = (target % 32).astype(F32)
    digits = jnp.where(row == 0, coarse, jnp.where(row == 1, fine, 0.0)).astype(BF16)
    slot = lax.broadcasted_iota(jnp.int32, (most, ncols), 0).astype(F32)
    for d in range(4):
        wanted = jnp.where(marks[d : d + 1] > 0.0, rank[d : d + 1], -1.0)
        pick = jnp.where(slot == wanted, 1.0, 0.0).astype(BF16)
        pick_ref[d * most : (d + 1) * most, :] = pick
        found = lax.dot_general(digits, pick, (((1,), (1,)), ((), ())), preferred_element_type=F32)
        cells_ref[d, :, :] = jnp.zeros(cells_ref.shape[1:], F32)
        cells_ref[d, 0:1, 0:most] = found[0:1] * 32.0 + found[1:2]


def weights_of(h):
    table = filter_table()
    le = [h <= 1, h <= 2, h <= 3]
    out = []
    for k in range(HMAX + 1):
        value = jnp.full(h.shape, table[k, 3], F32)
        for j in (2, 1, 0):
            if j > 0 and table[k, j] == 0.0 and table[k, j - 1] == 0.0:
                value = jnp.where(le[j], 0.0, value)
                break
            value = jnp.where(le[j], table[k, j], value)
        out.append(value)
    return out


def inner_body(noise_ref, half_ref, first_ref, kept_ref):
    rows = noise_ref.shape[0]
    kept_ref[...] = half_ref[...]
    for x in range(rows):
        w = weights_of(half_ref[x])
        total = w[0] * noise_ref[x]
        for k in range(1, HMAX + 1):
            near = [noise_ref[y] for y in (x - k, x + k) if 0 <= y < rows]
            if near:
                total = total + w[k] * (near[0] + near[1] if len(near) == 2 else near[0])
        first_ref[x] = total


def first_body(
    inner_ref, half_ref, got_a_ref, got_b_ref, edge_a_ref, first_ref, to_a_ref, to_b_ref, halo
):
    n_ax, ax = lax.axis_size("ax"), lax.axis_index("ax")
    even_x, even_z = is_even("ax"), is_even("az")
    rows, _, fine = half_ref.shape
    halo[0] = jnp.where(ax > 0, jnp.where(even_x, got_b_ref[...], got_a_ref[...]), 0.0)
    halo[1] = jnp.where(ax < n_ax - 1, jnp.where(even_x, got_a_ref[...], got_b_ref[...]), 0.0)
    for x in range(HMAX, rows - HMAX):
        first_ref[x] = inner_ref[x]
    for i in range(HMAX):
        w = weights_of(half_ref[i])
        total = inner_ref[i]
        for k in range(i + 1, HMAX + 1):
            total = total + w[k] * halo[0, HMAX + i - k]
        first_ref[i] = total
        x = rows - 1 - i
        w = weights_of(half_ref[x])
        total = inner_ref[x]
        for k in range(i + 1, HMAX + 1):
            total = total + w[k] * halo[1, k - i - 1]
        first_ref[x] = total
    half = rows // 2
    low = lax.broadcasted_iota(jnp.int32, (8, fine), 0) < 4
    for x in range(half):
        last = jnp.where(low, pltpu.roll(first_ref[x, 8:16], 4, 0), first_ref[x + half, 8:16])
        begin = jnp.where(low, first_ref[x, 0:8], pltpu.roll(first_ref[x + half, 0:8], 4, 0))
        for ref, value in ((to_a_ref, jnp.where(even_z, last, begin)), (to_b_ref, jnp.where(even_z, begin, last))):
            ref[x] = value[:, : fine // 2]
            ref[half + x] = value[:, fine // 2 :]
    to_a_ref[rows:] = edge_a_ref[...]


def middle_body(first_ref, half_ref, partial_ref, weight_ref, wide):
    rows, cols, fine = first_ref.shape
    blank = jnp.zeros((rows, 8, fine), F32)
    wide[:, 0:8] = blank
    wide[:, 24:32] = blank
    for x in range(rows):
        wide[x, 8:24] = first_ref[x]
    for x in range(rows):
        w = weights_of(half_ref[x])
        total = w[0] * first_ref[x]
        for k in range(1, HMAX + 1):
            total = total + w[k] * (wide[x, 8 - k : 24 - k] + wide[x, 8 + k : 24 + k])
        partial_ref[x] = total
        for k in range(HMAX + 1):
            weight_ref[k, x] = w[k]


def unpack_body(got_ref, out_ref):
    half = out_ref.shape[0]
    for y in range(half):
        out_ref[y] = jnp.concatenate([got_ref[y], got_ref[half + y]], axis=1)


def second_body(
    partial_ref, weight_ref, got_a_ref, got_b_ref, pick_ref, cells_ref,
    own_ref, to_xa, to_xb, to_za, to_zb, fine_hi, fine_lo,
):
    even = is_even("az")
    rows, cols, fine = partial_ref.shape
    half = rows // 2
    lane = lax.broadcasted_iota(jnp.int32, (cols, fine), 1)
    row = lax.broadcasted_iota(jnp.int32, (8, fine), 0)
    for x in range(rows):
        y = x % half
        got_a, got_b = jnp.concatenate([got_a_ref[y], got_a_ref[half + y]], axis=1), got_b_ref[y]
        before, after = jnp.where(even, got_b, got_a), jnp.where(even, got_a, got_b)
        if x < half:
            before = pltpu.roll(before, 4, 0)
        else:
            after = pltpu.roll(after, 4, 0)
        w = [weight_ref[k, x] for k in range(HMAX + 1)]
        total = partial_ref[x]
        for k in range(1, HMAX + 1):
            low = jnp.where(row < k, pltpu.roll(before, k, 0), 0.0)
            high = jnp.where(row >= 8 - k, pltpu.roll(after, 8 - k, 0), 0.0)
            total = total + w[k] * jnp.concatenate([low, high], axis=0)
        result = w[0] * total
        for k in range(1, HMAX + 1):
            up = jnp.where(lane < fine - k, pltpu.roll(total, fine - k, 1), 0.0)
            down = jnp.where(lane >= k, pltpu.roll(total, k, 1), 0.0)
            result = result + w[k] * (up + down)
        hi, lo = split(result)
        fine_hi[x * cols : (x + 1) * cols] = hi
        fine_lo[x * cols : (x + 1) * cols] = lo
    radial = own_ref.shape[1]
    above = lax.broadcasted_iota(jnp.int32, (fine, radial), 0) - lax.broadcasted_iota(
        jnp.int32, (fine, radial), 1
    ) * (fine // radial)
    bins = jnp.where((above >= 0) & (above < fine // radial), source_gain, 0.0).astype(BF16)
    binned = dot(fine_hi[...], bins) + dot(fine_lo[...], bins)
    own_ref[...] = binned
    hi, lo = split(binned)
    most = pick_ref.shape[0] // 4
    for d, out in enumerate((to_xa, to_xb, to_za, to_zb)):
        pick = pick_ref[d * most : (d + 1) * most]
        tiles = most // 8
        out[0:tiles] = (dot(pick, hi) + dot(pick, lo)).reshape(tiles, 8, radial)
        out[tiles] = cells_ref[d]
    for out in (to_za, to_zb):
        out[most // 8 + 1] = jnp.zeros(out.shape[1:], F32)


def gather_body(
    binned_ref, own_ref, xa, xb, zb, za, k_mid, k_rim, p_mid, p_rim, to_xa, to_xb, to_za, to_zb
):
    mid, cols, radial = p_mid.shape
    cells = (mid + 2 * RIM) * cols
    most = 8 * (xa.shape[0] - 1)

    def onehot(row):
        at = lax.broadcasted_iota(jnp.int32, (cells, row.shape[1]), 0)
        return jnp.where(at == row, 1.0, 0.0).astype(BF16)

    mats = [onehot(own_ref[...])]
    packets = [binned_ref[...]]
    for got in (xa, xb, za, zb):
        tiles = most // 8
        mats.append(onehot(got[tiles, 0:1, 0:most].astype(jnp.int32)))
        packets.append(got[0:tiles].reshape(most, radial))
    mat = jnp.concatenate(mats, axis=1)
    hi, lo = split(jnp.concatenate(packets, axis=0))
    q = (dot(mat, hi) + dot(mat, lo)).reshape(mid + 2 * RIM, cols, radial)
    p_rim[0:RIM] = k_rim[4, 0:RIM] + q[0:RIM]
    p_mid[...] = k_mid[4] + q[RIM : RIM + mid]
    p_rim[RIM:] = k_rim[4, RIM:] + q[RIM + mid :]
    level = Parts(k_mid, k_rim, p_mid, p_rim)
    write_x(level, to_xa, to_xb)
    write_z(level, range(0, level.rows, 4), to_za, to_zb)


class Whole:
    def __init__(self, ref):
        self.ref = ref
        self.rows = ref.shape[1]

    def row(self, f, x):
        return self.ref[f, x]

    def group(self, f, g):
        if g is None:
            return jnp.concatenate([self.ref[f, 0:RIM], self.ref[f, self.rows - RIM :]], axis=0)
        return self.ref[f, RIM + g * GROUP : RIM + (g + 1) * GROUP]


class Parts:
    def __init__(self, mid, rim, p_mid=None, p_rim=None, rows=None):
        self.arrays = (mid, rim, p_mid, p_rim)
        self.rows = rows or mid.shape[1] + 2 * RIM

    def pick(self, f):
        mid, rim, p_mid, p_rim = self.arrays
        if f == 4 and p_mid is not None:
            return p_mid, p_rim
        return mid if mid is None else mid.at[f], rim if rim is None else rim.at[f]

    def row(self, f, x):
        mid, rim = self.pick(f)
        if RIM <= x < self.rows - RIM:
            return mid[x - RIM]
        return rim[x if x < RIM else x - self.rows + 2 * RIM]

    def group(self, f, g):
        mid, rim = self.pick(f)
        return rim[...] if g is None else mid[g * GROUP : (g + 1) * GROUP]

    def store(self, f, x, value):
        mid, rim = self.pick(f)
        if RIM <= x < self.rows - RIM:
            mid[x - RIM] = value
        else:
            rim[x if x < RIM else x - self.rows + 2 * RIM] = value


def join_last(ut, p):
    low = lax.broadcasted_iota(jnp.int32, ut.shape, 0) < 4
    return jnp.where(low, pltpu.roll(ut, 3, 0), pltpu.roll(p, 7, 0))


def join_first(ut, p):
    low = lax.broadcasted_iota(jnp.int32, ut.shape, 0) < 4
    return jnp.where(low, ut, pltpu.roll(p, 4, 0))


def write_x(level, to_xa, to_xb):
    even = is_even("ax")
    for f in range(5):
        for i in range(3):
            first, last = level.row(f, i), level.row(f, level.rows - 3 + i)
            to_xa[3 * f + i] = jnp.where(even, last, first)
            to_xb[3 * f + i] = jnp.where(even, first, last)


def write_z(level, starts, to_za, to_zb):
    even = is_even("az")
    row = None
    for i, x in enumerate(starts):
        first, last = [], []
        for y in range(x, x + 4):
            ut, p = level.row(2, y), level.row(4, y)
            first.append(join_first(ut[0:8], p[0:8]))
            last.append(join_last(ut[8:16], p[8:16]))
        if row is None:
            row = lax.broadcasted_iota(jnp.int32, first[0].shape, 0) % 4 == 3
        for t in range(3):
            shift = 3 - t
            one = jnp.where(row, pltpu.roll(first[3], shift, 0), first[t])
            two = jnp.where(row, pltpu.roll(last[3], shift, 0), last[t])
            to_za[3 * i + t] = jnp.where(even, two, one)
            to_zb[3 * i + t] = jnp.where(even, one, two)


def edges_body(state, to_xa, to_xb, to_za, to_zb):
    level = Whole(state)
    write_x(level, to_xa, to_xb)
    write_z(level, range(0, level.rows, 4), to_za, to_zb)


def fill_halo(halo, xa, xb):
    n_ax, ax = lax.axis_size("ax"), lax.axis_index("ax")
    even = is_even("ax")
    for f in range(halo.shape[1]):
        a, b = xa[3 * f : 3 * f + 3], xb[3 * f : 3 * f + 3]
        halo[0, f] = jnp.where(ax > 0, jnp.where(even, b, a), 0.0)
        halo[1, f] = jnp.where(ax < n_ax - 1, jnp.where(even, a, b), 0.0)


def inverse_step(cols, radial):
    base = cols * lax.axis_size("az") / (2.0 * math.pi)
    at = lax.broadcasted_iota(jnp.int32, (1, radial), 1).astype(F32)
    return base / (base / hub_ratio + radial_step * (at + 0.5))


def along(row, x):
    total = drp_coeffs[0] * (row(x + 1) - row(x - 1))
    for s in (2, 3):
        total = total + drp_coeffs[s - 1] * (row(x + s) - row(x - s))
    return total


def apply_operator(level, groups, za, zb, tmat, rmat, finish, halo=None):
    even = is_even("az")
    tiles = level.rows // 4 * 3
    rim = RIM // 4 * 3

    def row(f, x):
        if x < 0:
            return halo[0, f, x + 3]
        if x >= level.rows:
            return halo[1, f, x - level.rows]
        return level.row(f, x)

    def beside(g):
        spans = [(0, rim), (tiles - rim, tiles)] if g is None else [(rim + 6 * g, rim + 6 * g + 6)]
        start = za.shape[0] - tiles
        if za.shape[0] == 2 * rim:
            spans, start = [(0, rim), (rim, 2 * rim)], 0
        elif za.shape[0] == tiles - 2 * rim:
            start = -rim
        sides = []
        for swap_ab in (False, True):
            for a, b in spans:
                last_b = zb.shape[0] - za.shape[0] + start
                got_a, got_b = za[start + a : start + b], zb[last_b + a : last_b + b]
                pair = (got_a, got_b) if swap_ab else (got_b, got_a)
                sides.append(jnp.where(even, *pair).reshape((b - a) * 8, za.shape[2]))
        return split(jnp.concatenate(sides, axis=0))

    for g in groups:
        if g is None:
            xs = [*range(RIM), *range(level.rows - RIM, level.rows)]
        else:
            xs = range(RIM + g * GROUP, RIM + (g + 1) * GROUP)
        ut, ur, p = [level.group(f, g) for f in (2, 3, 4)]
        _, cols, radial = ut.shape
        inv_h = inverse_step(cols, radial)
        side_hi, side_lo = beside(g)
        p_hi, p_lo = split(p.reshape(GROUP * cols, radial))
        ut_hi, ut_lo = split(ut.reshape(GROUP * cols, radial))
        ur_hi, ur_lo = split(ur.reshape(GROUP * cols, radial))

        def across(which, hi, lo):
            hi = jnp.concatenate([hi, side_hi], axis=0)
            lo = jnp.concatenate([lo, side_lo], axis=0)
            return dot(tmat[which, 0], hi) + dot(tmat[which, 0], lo) + dot(tmat[which, 1], hi)

        def outward(which, hi, lo):
            return dot(hi, rmat[which, 0]) + dot(lo, rmat[which, 0]) + dot(hi, rmat[which, 1])

        div_tr = across(0, ut_hi, ut_lo) * inv_h + outward(0, ur_hi, ur_lo)
        p_t = across(1, p_hi, p_lo) * inv_h
        p_r = outward(1, p_hi, p_lo)
        for i, x in enumerate(xs):
            part = slice(i * cols, (i + 1) * cols)
            d = [along(lambda y: row(f, y), x) for f in range(5)]
            div = d[1] + div_tr[part]
            finish(
                x,
                [
                    -mach_number * d[0] - div,
                    -mach_number * d[1] - d[4],
                    -mach_number * d[2] - p_t[part],
                    -mach_number * d[3] - p_r[part],
                    -mach_number * d[4] - div,
                ],
            )


def start_body(state, za, zb, xa, xb, tmat, rmat, k_mid, k_rim, halo):
    fill_halo(halo, xa, xb)
    level, out = Whole(state), Parts(k_mid, k_rim)

    def finish(x, tend):
        for f in range(5):
            out.store(f, x, tend[f])

    apply_operator(level, [*range(k_mid.shape[1] // GROUP), None], za, zb, tmat, rmat, finish, halo)


def inner_stage_body(factor, level, base, zb, za, tmat, rmat, out_mid, to_za, to_zb):
    def finish(x, tend):
        for f in range(5):
            out_mid[f, x - RIM] = base.row(f, x) + factor * tend[f]

    apply_operator(level, range(out_mid.shape[1] // GROUP), za, zb, tmat, rmat, finish)
    write_z(Parts(out_mid, None, rows=level.rows), range(RIM, level.rows - RIM, 4), to_za, to_zb)


def rim_stage_body(factor, level, base, xa, xb, zb, za, tmat, rmat, out_rim, to_xa, to_xb, to_za, to_zb, halo):
    fill_halo(halo, xa, xb)
    out = Parts(None, out_rim, rows=level.rows)

    def finish(x, tend):
        for f in range(5):
            out.store(f, x, base.row(f, x) + factor * tend[f])

    apply_operator(level, [None], za, zb, tmat, rmat, finish, halo)
    write_x(out, to_xa, to_xb)
    write_z(out, [0, level.rows - RIM], to_za, to_zb)


def last_finish(fields, k, store):
    def finish(x, tend):
        for f in range(5):
            store(f, x, fields[f, x] + time_step * k.row(f, x) + (0.5 * time_step * time_step) * tend[f])

    return finish


def inner_last_body(level, k, fields, zb, za, tmat, rmat, out, result, sems):
    def store(f, x, value):
        result[f, x - RIM] = value

    def copy(g):
        at = g * GROUP
        return pltpu.make_async_copy(
            result.at[:, at : at + GROUP], out.at[:, RIM + at : RIM + at + GROUP], sems.at[g]
        )

    groups = range(result.shape[1] // GROUP)
    for g in groups:
        apply_operator(level, [g], za, zb, tmat, rmat, last_finish(fields, k, store))
        copy(g).start()
    for g in groups:
        copy(g).wait()


def rim_last_body(level, k, fields, xa, xb, zb, za, tmat, rmat, out, halo, result, sems):
    rows = level.rows
    fill_halo(halo, xa, xb)

    def store(f, x, value):
        result[f, x if x < RIM else x - rows + 2 * RIM] = value

    apply_operator(level, [None], za, zb, tmat, rmat, last_finish(fields, k, store), halo)
    copies = [
        pltpu.make_async_copy(result.at[:, 0:RIM], out.at[:, 0:RIM], sems.at[0]),
        pltpu.make_async_copy(result.at[:, RIM:], out.at[:, rows - RIM :], sems.at[1]),
    ]
    for copy in copies:
        copy.start()
    for copy in copies:
        copy.wait()


def local(noise, half_width, owner, target_cell, fields):
    px, pa, fine = noise.shape
    cx, ca, radial = fields.shape[1:]
    ncols = px * pa
    most = ncols // 2
    n_az = lax.axis_size("az")
    inner = cx - 2 * RIM

    block = ((px, pa, fine), F32)
    even = is_even("ax")
    to_a = jnp.where(even, noise[px - HMAX :], noise[:HMAX])
    to_b = jnp.where(even, noise[:HMAX], noise[px - HMAX :])
    noise_a, noise_b = swap(to_a, to_b, "ax")
    send_x, send_z = ((15, ca, radial), F32), ((cx // 4 * 3, 8, radial), F32)
    sends = [send_x, send_x, send_z, send_z]
    xa, xb, za, zb = full_specs(edges_body, sends, [fields], name="edges", after=[to_a])
    uxa, uxb = swap(xa, xb, "ax")
    partial, half_width = full_specs(
        inner_body, [block, ((px, pa, fine), jnp.int32)], [noise, half_width], name="filter_inner", after=[za]
    )
    long_z = ((px + send_z[0][0], 8, fine // 2), F32)
    filtered, to_a, to_b = full_specs(
        first_body,
        [block, long_z, ((px, 8, fine // 2), F32)],
        [partial, half_width, noise_a, noise_b, za],
        [((2, HMAX, pa, fine), F32)],
        name="filter_axial",
    )
    got_a, got_b = swap(to_a, to_b, "az")
    (uzb,) = swap_b(zb, "az")
    pick, cells, own = full_specs(
        route_body,
        [((4 * most, ncols), BF16), ((4, 8, radial), F32), ((1, ncols), jnp.int32)],
        [owner.reshape(1, ncols), target_cell.reshape(1, ncols)],
        name="route",
        after=[filtered],
    )
    partial, weights = full_specs(
        middle_body,
        [block, ((HMAX + 1, px, pa, fine), F32)],
        [filtered, half_width],
        [((px, 32, fine), F32)],
        name="filter_middle",
        after=[pick],
    )
    (got_b,) = full_specs(
        unpack_body, [((px // 2, 8, fine), F32)], [got_b], name="unpack", after=[weights], cost=MORE
    )
    tiles = most // 8 + 1
    packet, packet_z = ((tiles, 8, radial), F32), ((tiles + 1, 8, radial), F32)
    binned, xa, xb, za, zb = full_specs(
        second_body,
        [((ncols, radial), F32), packet, packet, packet_z, packet_z],
        [partial, weights, got_a, got_b, pick, cells],
        [((ncols, fine), BF16), ((ncols, fine), BF16)],
        name="filter_rest",
        cost=COST,
    )
    za, zb = swap(za, zb, "az")
    packets = (*swap(xa, xb, "ax"), zb, za)

    tmat = jnp.asarray(azimuth_matrices(ca))
    rmat = jnp.asarray(radial_matrices(float(ca * n_az), radial))
    mid, rim = ((5, inner, ca, radial), F32), ((5, 2 * RIM, ca, radial), F32)
    halo = ((2, 5, 3, ca, radial), F32)
    k_mid, k_rim = full_specs(
        start_body, [mid, rim], [fields, got_a, uzb, uxa, uxb, tmat, rmat], [halo], name="operator", after=[binned]
    )
    p_mid, p_rim, *edges = full_specs(
        gather_body,
        [((inner, ca, radial), F32), ((2 * RIM, ca, radial), F32), *sends],
        [binned, own, *packets, k_mid, k_rim],
        name="gather",
    )
    k = [k_mid, k_rim, p_mid, p_rim]
    inner_z, rim_z = ((inner // 4 * 3, 8, radial), F32), ((RIM // 2 * 3, 8, radial), F32)
    za, zb = swap(edges[2], edges[3], "az")
    xa, xb = swap(edges[0], edges[1], "ax")
    level, rim_a, rim_b = k, za, zb
    for factor in (time_step / 4.0, time_step / 3.0):
        size = len(level)

        def body(*refs, factor=factor, size=size):
            inner_stage_body(factor, Parts(*refs[:size]), Parts(*refs[size : size + 4]), *refs[size + 4 :])

        new_mid, to_za, to_zb = full_specs(
            body, [mid, inner_z, inner_z], [*level, *k, zb, za, tmat, rmat], name="stage_inner", cost=COST if level is k else SOME
        )
        za, zb = swap(to_za, to_zb, "az")

        def body(*refs, factor=factor, size=size):
            rim_stage_body(factor, Parts(*refs[:size]), Parts(*refs[size : size + 4]), *refs[size + 4 :])

        new_rim, to_xa, to_xb, to_za, to_zb = full_specs(
            body,
            [rim, send_x, send_x, rim_z, rim_z],
            [*level, *k, xa, xb, rim_b, rim_a, tmat, rmat],
            [halo],
            name="stage_rim",
            after=[new_mid],
            cost=COST,
        )
        xa, xb = swap(to_xa, to_xb, "ax")
        rim_a, rim_b = swap(to_za, to_zb, "az")
        level = [new_mid, new_rim]

    def body(*refs):
        inner_last_body(Parts(*refs[:2]), Parts(*refs[2:6]), *refs[6:])

    whole = ((5, cx, ca, radial), F32)
    (out,) = full_specs(
        body,
        [whole],
        [*level, *k, fields, zb, za, tmat, rmat],
        [mid, pltpu.SemaphoreType.DMA((inner // GROUP,))],
        name="final_inner",
        out_specs=[ANY],
        cost=SOME,
    )

    def body(out_in, *refs):
        rim_last_body(Parts(*refs[:2]), Parts(*refs[2:6]), *refs[6:])

    (out,) = full_specs(
        body,
        [whole],
        [out, *level, *k, fields, xa, xb, rim_b, rim_a, tmat, rmat],
        [halo, rim, pltpu.SemaphoreType.DMA((2,))],
        name="final_rim",
        in_specs=[ANY] + [VM] * 13,
        out_specs=[ANY],
        alias={0: 0},
    )
    return out


def solution(mesh):
    return jax.shard_map(
        local,
        mesh=mesh,
        in_specs=(
            P("ax", "az", None),
            P("ax", "az", None),
            P(("ax", "az")),
            P(("ax", "az")),
            P(None, "ax", "az", None),
        ),
        out_specs=P(None, "ax", "az", None),
        check_vma=False,
    )
```

```python
import math

import numpy as np

import jax
import jax.numpy as jnp
from jax import lax
from jax.experimental import pallas as pl
from jax.experimental.pallas import tpu as pltpu
from jax.sharding import PartitionSpec as P

HMAX = 4
drp_coeffs = (0.770882380518, -0.166705904415, 0.02084314277)
mach_number = 0.5
time_step = 0.7
source_gain = 4.0
radial_step = 2.0
hub_ratio = 1.6

F32 = jnp.float32
BF16 = jnp.bfloat16
VM = pl.BlockSpec(memory_space=pltpu.VMEM)
ANY = pl.BlockSpec(memory_space=pl.ANY)
PARAMS = pltpu.CompilerParams(vmem_limit_bytes=24 * 1024 * 1024)
GROUP = 8
RIM = 4
MORE = 2_500_000_000
SOME = 2_000_000_000
COST = 1 << 37


def np_split(matrix):
    hi = matrix.astype(np.float32).astype(BF16)
    lo = (matrix - hi.astype(np.float64)).astype(np.float32).astype(BF16)
    return hi, lo


def filter_table():
    table = np.zeros((HMAX + 1, HMAX))
    for h in range(1, HMAX + 1):
        weights = [math.exp(-2.0 * k * k / (h * h)) if k <= h else 0.0 for k in range(HMAX + 1)]
        total = weights[0] + 2.0 * sum(weights[1:])
        table[:, h - 1] = [w / total for w in weights]
    return table


def radial_rows(na_total, radial):
    base = na_total / (2.0 * math.pi)
    radius = base / hub_ratio + radial_step * (np.arange(radial) + 0.5)
    return base / radius, 1.0 / radius


def radial_matrices(na_total, radial):
    diff = np.zeros((radial, radial))
    for s, a in zip((1, 2, 3), drp_coeffs):
        for j in range(radial):
            if j + s < radial:
                diff[j + s, j] += a / radial_step
            if j - s >= 0:
                diff[j - s, j] -= a / radial_step
    with_r = diff + np.diag(radial_rows(na_total, radial)[1])
    return np.stack([np.stack(np_split(with_r)), np.stack(np_split(diff))])


def azimuth_matrices(cols):
    packed = GROUP * 6
    full = np.zeros((2, GROUP * cols, GROUP * cols + 2 * packed))
    for which in range(2):
        for x in range(GROUP):
            for i in range(cols):
                for s, a in zip((1, 2, 3), drp_coeffs):
                    for j, sign in ((i + s, 1.0), (i - s, -1.0)):
                        if 0 <= j < cols:
                            at = x * cols + j
                        else:
                            m = j + 3 if j < 0 else j - cols
                            tile, row = (x % 4, m) if x % 4 < 3 else (m, 3)
                            at = GROUP * cols + (x // 4 * 3 + tile) * 8 + row + 4 * which
                            at += packed if j >= cols else 0
                        full[which, x * cols + i, at] += sign * a
    return np.stack([np.stack(np_split(full[w])) for w in range(2)])


def split(x):
    hi = x.astype(BF16)
    return hi, (x - hi.astype(F32)).astype(BF16)


def dot(a, b):
    return lax.dot_general(a, b, (((1,), (0,)), ((), ())), preferred_element_type=F32)


def is_even(axis):
    return lax.rem(lax.axis_index(axis), 2) == 0


def swap(to_a, to_b, axis):
    devices = lax.axis_size(axis)
    pairs_a = [(i, i ^ 1) for i in range(devices)]
    pairs_b = [(i, (i - 1) % devices if i % 2 == 0 else (i + 1) % devices) for i in range(devices)]
    return lax.ppermute(to_a, axis, pairs_a), lax.ppermute(to_b, axis, pairs_b)


def swap_b(value, axis):
    devices = lax.axis_size(axis)
    pairs = [(i, (i - 1) % devices if i % 2 == 0 else (i + 1) % devices) for i in range(devices)]
    return (lax.ppermute(value, axis, pairs),)


def full_specs(body, outs, args, scratch=(), name=None, in_specs=None, out_specs=None, after=(), cost=0, alias=None):
    skip = len(args)

    def run(*refs):
        body(*refs[:skip], *refs[skip + len(after) :])

    return pl.pallas_call(
        run,
        out_shape=[jax.ShapeDtypeStruct(s, d) for s, d in outs],
        in_specs=(in_specs or [VM] * skip) + [ANY] * len(after),
        input_output_aliases=alias or {},
        out_specs=out_specs or [VM] * len(outs),
        scratch_shapes=[pltpu.VMEM(*s) if isinstance(s, tuple) else s for s in scratch],
        compiler_params=PARAMS,
        name=name,
        cost_estimate=pl.CostEstimate(flops=cost, bytes_accessed=0, transcendentals=0),
    )(*args, *after)


def route_body(owner_ref, target_ref, pick_ref, cells_ref, own_ref):
    n_ax, n_az = lax.axis_size("ax"), lax.axis_size("az")
    ax, az = lax.axis_index("ax"), lax.axis_index("az")
    step_x = jnp.where(lax.rem(ax, 2) == 0, 1, -1)
    step_z = jnp.where(lax.rem(az, 2) == 0, 1, -1)
    me = ax * n_az + az
    b_x = ax - step_x
    ids = [
        (ax + step_x) * n_az + az,
        jnp.where((b_x >= 0) & (b_x < n_ax), b_x * n_az + az, -1),
        ax * n_az + lax.rem(az + step_z + n_az, n_az),
        ax * n_az + lax.rem(az - step_z + n_az, n_az),
    ]
    owner = owner_ref[...]
    target = target_ref[...]
    ncols = owner.shape[1]
    most = ncols // 2
    own_ref[...] = jnp.where(owner == me, target, -1)
    row = lax.broadcasted_iota(jnp.int32, (8, ncols), 0)
    marks = jnp.zeros((8, ncols), F32)
    for d, i in enumerate(ids):
        marks = jnp.where((row == d) & (owner == i), 1.0, marks)
    before = lax.broadcasted_iota(jnp.int32, (ncols, ncols), 0) < lax.broadcasted_iota(jnp.int32, (ncols, ncols), 1)
    rank = dot(marks.astype(BF16), jnp.where(before, 1.0, 0.0).astype(BF16))
    coarse = (target // 32).astype(F32)
    fine = (target % 32).astype(F32)
    digits = jnp.where(row == 0, coarse, jnp.where(row == 1, fine, 0.0)).astype(BF16)
    slot = lax.broadcasted_iota(jnp.int32, (most, ncols), 0).astype(F32)
    for d in range(4):
        wanted = jnp.where(marks[d : d + 1] > 0.0, rank[d : d + 1], -1.0)
        pick = jnp.where(slot == wanted, 1.0, 0.0).astype(BF16)
        pick_ref[d * most : (d + 1) * most, :] = pick
        found = lax.dot_general(digits, pick, (((1,), (1,)), ((), ())), preferred_element_type=F32)
        cells_ref[d, :, :] = jnp.zeros(cells_ref.shape[1:], F32)
        cells_ref[d, 0:1, 0:most] = found[0:1] * 32.0 + found[1:2]


def weights_of(h):
    table = filter_table()
    le = [h <= 1, h <= 2, h <= 3]
    out = []
    for k in range(HMAX + 1):
        value = jnp.full(h.shape, table[k, 3], F32)
        for j in (2, 1, 0):
            if j > 0 and table[k, j] == 0.0 and table[k, j - 1] == 0.0:
                value = jnp.where(le[j], 0.0, value)
                break
            value = jnp.where(le[j], table[k, j], value)
        out.append(value)
    return out


def inner_body(noise_ref, half_ref, first_ref, kept_ref):
    rows = noise_ref.shape[0]
    kept_ref[...] = half_ref[...]
    for x in range(rows):
        w = weights_of(half_ref[x])
        total = w[0] * noise_ref[x]
        for k in range(1, HMAX + 1):
            near = [noise_ref[y] for y in (x - k, x + k) if 0 <= y < rows]
            if near:
                total = total + w[k] * (near[0] + near[1] if len(near) == 2 else near[0])
        first_ref[x] = total


def first_body(
    inner_ref, half_ref, got_a_ref, got_b_ref, edge_a_ref, first_ref, to_a_ref, to_b_ref, halo
):
    n_ax, ax = lax.axis_size("ax"), lax.axis_index("ax")
    even_x, even_z = is_even("ax"), is_even("az")
    rows, _, fine = half_ref.shape
    halo[0] = jnp.where(ax > 0, jnp.where(even_x, got_b_ref[...], got_a_ref[...]), 0.0)
    halo[1] = jnp.where(ax < n_ax - 1, jnp.where(even_x, got_a_ref[...], got_b_ref[...]), 0.0)
    for x in range(HMAX, rows - HMAX):
        first_ref[x] = inner_ref[x]
    for i in range(HMAX):
        w = weights_of(half_ref[i])
        total = inner_ref[i]
        for k in range(i + 1, HMAX + 1):
            total = total + w[k] * halo[0, HMAX + i - k]
        first_ref[i] = total
        x = rows - 1 - i
        w = weights_of(half_ref[x])
        total = inner_ref[x]
        for k in range(i + 1, HMAX + 1):
            total = total + w[k] * halo[1, k - i - 1]
        first_ref[x] = total
    half = rows // 2
    low = lax.broadcasted_iota(jnp.int32, (8, fine), 0) < 4
    for x in range(half):
        last = jnp.where(low, pltpu.roll(first_ref[x, 8:16], 4, 0), first_ref[x + half, 8:16])
        begin = jnp.where(low, first_ref[x, 0:8], pltpu.roll(first_ref[x + half, 0:8], 4, 0))
        for ref, value in ((to_a_ref, jnp.where(even_z, last, begin)), (to_b_ref, jnp.where(even_z, begin, last))):
            ref[x] = value[:, : fine // 2]
            ref[half + x] = value[:, fine // 2 :]
    to_a_ref[rows:] = edge_a_ref[...]


def middle_body(first_ref, half_ref, partial_ref, weight_ref, wide):
    rows, cols, fine = first_ref.shape
    blank = jnp.zeros((rows, 8, fine), F32)
    wide[:, 0:8] = blank
    wide[:, 24:32] = blank
    for x in range(rows):
        wide[x, 8:24] = first_ref[x]
    for x in range(rows):
        w = weights_of(half_ref[x])
        total = w[0] * first_ref[x]
        for k in range(1, HMAX + 1):
            total = total + w[k] * (wide[x, 8 - k : 24 - k] + wide[x, 8 + k : 24 + k])
        partial_ref[x] = total
        for k in range(HMAX + 1):
            weight_ref[k, x] = w[k]


def unpack_body(got_ref, out_ref):
    half = out_ref.shape[0]
    for y in range(half):
        out_ref[y] = jnp.concatenate([got_ref[y], got_ref[half + y]], axis=1)


def second_body(
    partial_ref, weight_ref, got_a_ref, got_b_ref, pick_ref, cells_ref,
    own_ref, to_xa, to_xb, to_za, to_zb, fine_hi, fine_lo,
):
    even = is_even("az")
    rows, cols, fine = partial_ref.shape
    half = rows // 2
    lane = lax.broadcasted_iota(jnp.int32, (cols, fine), 1)
    row = lax.broadcasted_iota(jnp.int32, (8, fine), 0)
    for x in range(rows):
        y = x % half
        got_a, got_b = jnp.concatenate([got_a_ref[y], got_a_ref[half + y]], axis=1), got_b_ref[y]
        before, after = jnp.where(even, got_b, got_a), jnp.where(even, got_a, got_b)
        if x < half:
            before = pltpu.roll(before, 4, 0)
        else:
            after = pltpu.roll(after, 4, 0)
        w = [weight_ref[k, x] for k in range(HMAX + 1)]
        total = partial_ref[x]
        for k in range(1, HMAX + 1):
            low = jnp.where(row < k, pltpu.roll(before, k, 0), 0.0)
            high = jnp.where(row >= 8 - k, pltpu.roll(after, 8 - k, 0), 0.0)
            total = total + w[k] * jnp.concatenate([low, high], axis=0)
        result = w[0] * total
        for k in range(1, HMAX + 1):
            up = jnp.where(lane < fine - k, pltpu.roll(total, fine - k, 1), 0.0)
            down = jnp.where(lane >= k, pltpu.roll(total, k, 1), 0.0)
            result = result + w[k] * (up + down)
        hi, lo = split(result)
        fine_hi[x * cols : (x + 1) * cols] = hi
        fine_lo[x * cols : (x + 1) * cols] = lo
    radial = own_ref.shape[1]
    above = lax.broadcasted_iota(jnp.int32, (fine, radial), 0) - lax.broadcasted_iota(
        jnp.int32, (fine, radial), 1
    ) * (fine // radial)
    bins = jnp.where((above >= 0) & (above < fine // radial), source_gain, 0.0).astype(BF16)
    binned = dot(fine_hi[...], bins) + dot(fine_lo[...], bins)
    own_ref[...] = binned
    hi, lo = split(binned)
    most = pick_ref.shape[0] // 4
    for d, out in enumerate((to_xa, to_xb, to_za, to_zb)):
        pick = pick_ref[d * most : (d + 1) * most]
        tiles = most // 8
        out[0:tiles] = (dot(pick, hi) + dot(pick, lo)).reshape(tiles, 8, radial)
        out[tiles] = cells_ref[d]
    for out in (to_za, to_zb):
        out[most // 8 + 1] = jnp.zeros(out.shape[1:], F32)


def gather_body(
    binned_ref, own_ref, xa, xb, zb, za, k_mid, k_rim, p_mid, p_rim, to_xa, to_xb, to_za, to_zb, rim_za, rim_zb
):
    mid, cols, radial = p_mid.shape
    cells = (mid + 2 * RIM) * cols
    most = 8 * (xa.shape[0] - 1)

    def onehot(row):
        at = lax.broadcasted_iota(jnp.int32, (cells, row.shape[1]), 0)
        return jnp.where(at == row, 1.0, 0.0).astype(BF16)

    mats = [onehot(own_ref[...])]
    packets = [binned_ref[...]]
    for got in (xa, xb, za, zb):
        tiles = most // 8
        mats.append(onehot(got[tiles, 0:1, 0:most].astype(jnp.int32)))
        packets.append(got[0:tiles].reshape(most, radial))
    mat = jnp.concatenate(mats, axis=1)
    hi, lo = split(jnp.concatenate(packets, axis=0))
    q = (dot(mat, hi) + dot(mat, lo)).reshape(mid + 2 * RIM, cols, radial)
    p_rim[0:RIM] = k_rim[4, 0:RIM] + q[0:RIM]
    p_mid[...] = k_mid[4] + q[RIM : RIM + mid]
    p_rim[RIM:] = k_rim[4, RIM:] + q[RIM + mid :]
    level = Parts(k_mid, k_rim, p_mid, p_rim)
    write_x(level, to_xa, to_xb)
    write_z(level, range(RIM, level.rows - RIM, 4), to_za, to_zb)
    write_z(level, [0, level.rows - RIM], rim_za, rim_zb)


class Whole:
    def __init__(self, ref):
        self.ref = ref
        self.rows = ref.shape[1]

    def row(self, f, x):
        return self.ref[f, x]

    def group(self, f, g):
        if g is None:
            return jnp.concatenate([self.ref[f, 0:RIM], self.ref[f, self.rows - RIM :]], axis=0)
        return self.ref[f, RIM + g * GROUP : RIM + (g + 1) * GROUP]


class Parts:
    def __init__(self, mid, rim, p_mid=None, p_rim=None, rows=None):
        self.arrays = (mid, rim, p_mid, p_rim)
        self.rows = rows or mid.shape[1] + 2 * RIM

    def pick(self, f):
        mid, rim, p_mid, p_rim = self.arrays
        if f == 4 and p_mid is not None:
            return p_mid, p_rim
        return mid if mid is None else mid.at[f], rim if rim is None else rim.at[f]

    def row(self, f, x):
        mid, rim = self.pick(f)
        if RIM <= x < self.rows - RIM:
            return mid[x - RIM]
        return rim[x if x < RIM else x - self.rows + 2 * RIM]

    def group(self, f, g):
        mid, rim = self.pick(f)
        return rim[...] if g is None else mid[g * GROUP : (g + 1) * GROUP]

    def store(self, f, x, value):
        mid, rim = self.pick(f)
        if RIM <= x < self.rows - RIM:
            mid[x - RIM] = value
        else:
            rim[x if x < RIM else x - self.rows + 2 * RIM] = value


def join_last(ut, p):
    low = lax.broadcasted_iota(jnp.int32, ut.shape, 0) < 4
    return jnp.where(low, pltpu.roll(ut, 3, 0), pltpu.roll(p, 7, 0))


def join_first(ut, p):
    low = lax.broadcasted_iota(jnp.int32, ut.shape, 0) < 4
    return jnp.where(low, ut, pltpu.roll(p, 4, 0))


def write_x(level, to_xa, to_xb):
    even = is_even("ax")
    for f in range(5):
        for i in range(3):
            first, last = level.row(f, i), level.row(f, level.rows - 3 + i)
            to_xa[3 * f + i] = jnp.where(even, last, first)
            to_xb[3 * f + i] = jnp.where(even, first, last)


def write_z(level, starts, to_za, to_zb):
    even = is_even("az")
    row = None
    for i, x in enumerate(starts):
        first, last = [], []
        for y in range(x, x + 4):
            ut, p = level.row(2, y), level.row(4, y)
            first.append(join_first(ut[0:8], p[0:8]))
            last.append(join_last(ut[8:16], p[8:16]))
        if row is None:
            row = lax.broadcasted_iota(jnp.int32, first[0].shape, 0) % 4 == 3
        for t in range(3):
            shift = 3 - t
            one = jnp.where(row, pltpu.roll(first[3], shift, 0), first[t])
            two = jnp.where(row, pltpu.roll(last[3], shift, 0), last[t])
            to_za[3 * i + t] = jnp.where(even, two, one)
            to_zb[3 * i + t] = jnp.where(even, one, two)


def edges_body(state, to_xa, to_xb, to_za, to_zb):
    level = Whole(state)
    write_x(level, to_xa, to_xb)
    write_z(level, range(0, level.rows, 4), to_za, to_zb)


def fill_halo(halo, xa, xb):
    n_ax, ax = lax.axis_size("ax"), lax.axis_index("ax")
    even = is_even("ax")
    for f in range(halo.shape[1]):
        a, b = xa[3 * f : 3 * f + 3], xb[3 * f : 3 * f + 3]
        halo[0, f] = jnp.where(ax > 0, jnp.where(even, b, a), 0.0)
        halo[1, f] = jnp.where(ax < n_ax - 1, jnp.where(even, a, b), 0.0)


def inverse_step(cols, radial):
    base = cols * lax.axis_size("az") / (2.0 * math.pi)
    at = lax.broadcasted_iota(jnp.int32, (1, radial), 1).astype(F32)
    return base / (base / hub_ratio + radial_step * (at + 0.5))


def along(row, x):
    total = drp_coeffs[0] * (row(x + 1) - row(x - 1))
    for s in (2, 3):
        total = total + drp_coeffs[s - 1] * (row(x + s) - row(x - s))
    return total


def apply_operator(level, groups, za, zb, tmat, rmat, finish, halo=None):
    even = is_even("az")
    tiles = level.rows // 4 * 3
    rim = RIM // 4 * 3

    def row(f, x):
        if x < 0:
            return halo[0, f, x + 3]
        if x >= level.rows:
            return halo[1, f, x - level.rows]
        return level.row(f, x)

    def beside(g):
        spans = [(0, rim), (tiles - rim, tiles)] if g is None else [(rim + 6 * g, rim + 6 * g + 6)]
        start = za.shape[0] - tiles
        if za.shape[0] == 2 * rim:
            spans, start = [(0, rim), (rim, 2 * rim)], 0
        elif za.shape[0] == tiles - 2 * rim:
            start = -rim
        sides = []
        for swap_ab in (False, True):
            for a, b in spans:
                last_b = zb.shape[0] - za.shape[0] + start
                got_a, got_b = za[start + a : start + b], zb[last_b + a : last_b + b]
                pair = (got_a, got_b) if swap_ab else (got_b, got_a)
                sides.append(jnp.where(even, *pair).reshape((b - a) * 8, za.shape[2]))
        return split(jnp.concatenate(sides, axis=0))

    for g in groups:
        if g is None:
            xs = [*range(RIM), *range(level.rows - RIM, level.rows)]
        else:
            xs = range(RIM + g * GROUP, RIM + (g + 1) * GROUP)
        ut, ur, p = [level.group(f, g) for f in (2, 3, 4)]
        _, cols, radial = ut.shape
        inv_h = inverse_step(cols, radial)
        side_hi, side_lo = beside(g)
        p_hi, p_lo = split(p.reshape(GROUP * cols, radial))
        ut_hi, ut_lo = split(ut.reshape(GROUP * cols, radial))
        ur_hi, ur_lo = split(ur.reshape(GROUP * cols, radial))

        def across(which, hi, lo):
            hi = jnp.concatenate([hi, side_hi], axis=0)
            lo = jnp.concatenate([lo, side_lo], axis=0)
            return dot(tmat[which, 0], hi) + dot(tmat[which, 0], lo) + dot(tmat[which, 1], hi)

        def outward(which, hi, lo):
            return dot(hi, rmat[which, 0]) + dot(lo, rmat[which, 0]) + dot(hi, rmat[which, 1])

        div_tr = across(0, ut_hi, ut_lo) * inv_h + outward(0, ur_hi, ur_lo)
        p_t = across(1, p_hi, p_lo) * inv_h
        p_r = outward(1, p_hi, p_lo)
        for i, x in enumerate(xs):
            part = slice(i * cols, (i + 1) * cols)
            d = [along(lambda y: row(f, y), x) for f in range(5)]
            div = d[1] + div_tr[part]
            finish(
                x,
                [
                    -mach_number * d[0] - div,
                    -mach_number * d[1] - d[4],
                    -mach_number * d[2] - p_t[part],
                    -mach_number * d[3] - p_r[part],
                    -mach_number * d[4] - div,
                ],
            )


def start_body(state, za, zb, xa, xb, tmat, rmat, k_mid, k_rim, halo):
    fill_halo(halo, xa, xb)
    level, out = Whole(state), Parts(k_mid, k_rim)

    def finish(x, tend):
        for f in range(5):
            out.store(f, x, tend[f])

    apply_operator(level, [*range(k_mid.shape[1] // GROUP), None], za, zb, tmat, rmat, finish, halo)


def inner_stage_body(factor, level, base, zb, za, tmat, rmat, out_mid, to_za, to_zb):
    def finish(x, tend):
        for f in range(5):
            out_mid[f, x - RIM] = base.row(f, x) + factor * tend[f]

    apply_operator(level, range(out_mid.shape[1] // GROUP), za, zb, tmat, rmat, finish)
    write_z(Parts(out_mid, None, rows=level.rows), range(RIM, level.rows - RIM, 4), to_za, to_zb)


def rim_stage_body(factor, level, base, xa, xb, zb, za, tmat, rmat, out_rim, to_xa, to_xb, to_za, to_zb, halo):
    fill_halo(halo, xa, xb)
    out = Parts(None, out_rim, rows=level.rows)

    def finish(x, tend):
        for f in range(5):
            out.store(f, x, base.row(f, x) + factor * tend[f])

    apply_operator(level, [None], za, zb, tmat, rmat, finish, halo)
    write_x(out, to_xa, to_xb)
    write_z(out, [0, level.rows - RIM], to_za, to_zb)


def last_finish(fields, k, store):
    def finish(x, tend):
        for f in range(5):
            store(f, x, fields[f, x] + time_step * k.row(f, x) + (0.5 * time_step * time_step) * tend[f])

    return finish


def inner_last_body(level, k, fields, zb, za, tmat, rmat, out, result, sems):
    def store(f, x, value):
        result[f, x - RIM] = value

    def copy(g):
        at = g * GROUP
        return pltpu.make_async_copy(
            result.at[:, at : at + GROUP], out.at[:, RIM + at : RIM + at + GROUP], sems.at[g]
        )

    groups = range(result.shape[1] // GROUP)
    for g in groups:
        apply_operator(level, [g], za, zb, tmat, rmat, last_finish(fields, k, store))
        copy(g).start()
    for g in groups:
        copy(g).wait()


def rim_last_body(level, k, fields, xa, xb, zb, za, tmat, rmat, out, halo, result, sems):
    rows = level.rows
    fill_halo(halo, xa, xb)

    copies = [
        pltpu.make_async_copy(result.at[:, 0:RIM], out.at[:, 0:RIM], sems.at[0]),
        pltpu.make_async_copy(result.at[:, RIM:], out.at[:, rows - RIM :], sems.at[1]),
    ]

    def store(f, x, value):
        result[f, x if x < RIM else x - rows + 2 * RIM] = value
        if f == 4 and x in (RIM - 1, rows - 1):
            copies[x // RIM > 0].start()

    apply_operator(level, [None], za, zb, tmat, rmat, last_finish(fields, k, store), halo)
    for copy in copies:
        copy.wait()


def local(noise, half_width, owner, target_cell, fields):
    px, pa, fine = noise.shape
    cx, ca, radial = fields.shape[1:]
    ncols = px * pa
    most = ncols // 2
    n_az = lax.axis_size("az")
    inner = cx - 2 * RIM

    block = ((px, pa, fine), F32)
    even = is_even("ax")
    to_a = jnp.where(even, noise[px - HMAX :], noise[:HMAX])
    to_b = jnp.where(even, noise[:HMAX], noise[px - HMAX :])
    noise_a, noise_b = swap(to_a, to_b, "ax")
    send_x, send_z = ((15, ca, radial), F32), ((cx // 4 * 3, 8, radial), F32)
    sends = [send_x, send_x, send_z, send_z]
    xa, xb, za, zb = full_specs(edges_body, sends, [fields], name="edges", after=[to_a])
    uxa, uxb = swap(xa, xb, "ax")
    partial, half_width = full_specs(
        inner_body, [block, ((px, pa, fine), jnp.int32)], [noise, half_width], name="filter_inner", after=[za]
    )
    long_z = ((px + send_z[0][0], 8, fine // 2), F32)
    filtered, to_a, to_b = full_specs(
        first_body,
        [block, long_z, ((px, 8, fine // 2), F32)],
        [partial, half_width, noise_a, noise_b, za],
        [((2, HMAX, pa, fine), F32)],
        name="filter_axial",
    )
    got_a, got_b = swap(to_a, to_b, "az")
    (uzb,) = swap_b(zb, "az")
    pick, cells, own = full_specs(
        route_body,
        [((4 * most, ncols), BF16), ((4, 8, radial), F32), ((1, ncols), jnp.int32)],
        [owner.reshape(1, ncols), target_cell.reshape(1, ncols)],
        name="route",
        after=[filtered],
    )
    partial, weights = full_specs(
        middle_body,
        [block, ((HMAX + 1, px, pa, fine), F32)],
        [filtered, half_width],
        [((px, 32, fine), F32)],
        name="filter_middle",
        after=[pick],
    )
    (got_b,) = full_specs(
        unpack_body, [((px // 2, 8, fine), F32)], [got_b], name="unpack", after=[weights], cost=MORE
    )
    tiles = most // 8 + 1
    packet, packet_z = ((tiles, 8, radial), F32), ((tiles + 1, 8, radial), F32)
    binned, xa, xb, za, zb = full_specs(
        second_body,
        [((ncols, radial), F32), packet, packet, packet_z, packet_z],
        [partial, weights, got_a, got_b, pick, cells],
        [((ncols, fine), BF16), ((ncols, fine), BF16)],
        name="filter_rest",
        cost=COST,
    )
    za, zb = swap(za, zb, "az")
    packets = (*swap(xa, xb, "ax"), zb, za)

    tmat = jnp.asarray(azimuth_matrices(ca))
    rmat = jnp.asarray(radial_matrices(float(ca * n_az), radial))
    mid, rim = ((5, inner, ca, radial), F32), ((5, 2 * RIM, ca, radial), F32)
    halo = ((2, 5, 3, ca, radial), F32)
    k_mid, k_rim = full_specs(
        start_body, [mid, rim], [fields, got_a, uzb, uxa, uxb, tmat, rmat], [halo], name="operator", after=[binned]
    )
    inner_z, rim_z = ((inner // 4 * 3, 8, radial), F32), ((RIM // 2 * 3, 8, radial), F32)
    p_mid, p_rim, *edges = full_specs(
        gather_body,
        [((inner, ca, radial), F32), ((2 * RIM, ca, radial), F32), send_x, send_x, inner_z, inner_z, rim_z, rim_z],
        [binned, own, *packets, k_mid, k_rim],
        name="gather",
    )
    k = [k_mid, k_rim, p_mid, p_rim]
    za, zb = swap(edges[2], edges[3], "az")
    xa, xb = swap(edges[0], edges[1], "ax")
    rim_a, rim_b = swap(edges[4], edges[5], "az")
    level = k
    for factor in (time_step / 4.0, time_step / 3.0):
        size = len(level)

        def body(*refs, factor=factor, size=size):
            inner_stage_body(factor, Parts(*refs[:size]), Parts(*refs[size : size + 4]), *refs[size + 4 :])

        new_mid, to_za, to_zb = full_specs(
            body, [mid, inner_z, inner_z], [*level, *k, zb, za, tmat, rmat], name="stage_inner", cost=SOME
        )
        za, zb = swap(to_za, to_zb, "az")

        def body(*refs, factor=factor, size=size):
            rim_stage_body(factor, Parts(*refs[:size]), Parts(*refs[size : size + 4]), *refs[size + 4 :])

        new_rim, to_xa, to_xb, to_za, to_zb = full_specs(
            body,
            [rim, send_x, send_x, rim_z, rim_z],
            [*level, *k, xa, xb, rim_b, rim_a, tmat, rmat],
            [halo],
            name="stage_rim",
            after=[new_mid],
            cost=COST,
        )
        xa, xb = swap(to_xa, to_xb, "ax")
        rim_a, rim_b = swap(to_za, to_zb, "az")
        level = [new_mid, new_rim]

    def body(*refs):
        inner_last_body(Parts(*refs[:2]), Parts(*refs[2:6]), *refs[6:])

    whole = ((5, cx, ca, radial), F32)
    (out,) = full_specs(
        body,
        [whole],
        [*level, *k, fields, zb, za, tmat, rmat],
        [mid, pltpu.SemaphoreType.DMA((inner // GROUP,))],
        name="final_inner",
        out_specs=[ANY],
        cost=SOME,
    )

    def body(out_in, *refs):
        rim_last_body(Parts(*refs[:2]), Parts(*refs[2:6]), *refs[6:])

    (out,) = full_specs(
        body,
        [whole],
        [out, *level, *k, fields, xa, xb, rim_b, rim_a, tmat, rmat],
        [halo, rim, pltpu.SemaphoreType.DMA((2,))],
        name="final_rim",
        in_specs=[ANY] + [VM] * 13,
        out_specs=[ANY],
        alias={0: 0},
    )
    return out


def solution(mesh):
    return jax.shard_map(
        local,
        mesh=mesh,
        in_specs=(
            P("ax", "az", None),
            P("ax", "az", None),
            P(("ax", "az")),
            P(("ax", "az")),
            P(None, "ax", "az", None),
        ),
        out_specs=P(None, "ax", "az", None),
        check_vma=False,
    )
```

```python
import math

import numpy as np

import jax
import jax.numpy as jnp
from jax import lax
from jax.experimental import pallas as pl
from jax.experimental.pallas import tpu as pltpu
from jax.sharding import PartitionSpec as P

HMAX = 4
drp_coeffs = (0.770882380518, -0.166705904415, 0.02084314277)
mach_number = 0.5
time_step = 0.7
source_gain = 4.0
radial_step = 2.0
hub_ratio = 1.6

F32 = jnp.float32
BF16 = jnp.bfloat16
VM = pl.BlockSpec(memory_space=pltpu.VMEM)
ANY = pl.BlockSpec(memory_space=pl.ANY)
PARAMS = pltpu.CompilerParams(vmem_limit_bytes=24 * 1024 * 1024)
GROUP = 8
RIM = 4
MORE = 2_500_000_000
SOME = 2_000_000_000
COST = 1 << 37


def np_split(matrix):
    hi = matrix.astype(np.float32).astype(BF16)
    lo = (matrix - hi.astype(np.float64)).astype(np.float32).astype(BF16)
    return hi, lo


def filter_table():
    table = np.zeros((HMAX + 1, HMAX))
    for h in range(1, HMAX + 1):
        weights = [math.exp(-2.0 * k * k / (h * h)) if k <= h else 0.0 for k in range(HMAX + 1)]
        total = weights[0] + 2.0 * sum(weights[1:])
        table[:, h - 1] = [w / total for w in weights]
    return table


def radial_rows(na_total, radial):
    base = na_total / (2.0 * math.pi)
    radius = base / hub_ratio + radial_step * (np.arange(radial) + 0.5)
    return base / radius, 1.0 / radius


def radial_matrices(na_total, radial):
    diff = np.zeros((radial, radial))
    for s, a in zip((1, 2, 3), drp_coeffs):
        for j in range(radial):
            if j + s < radial:
                diff[j + s, j] += a / radial_step
            if j - s >= 0:
                diff[j - s, j] -= a / radial_step
    with_r = diff + np.diag(radial_rows(na_total, radial)[1])
    return np.stack([np.stack(np_split(with_r)), np.stack(np_split(diff))])


def azimuth_matrices(cols):
    packed = GROUP * 6
    full = np.zeros((2, GROUP * cols, GROUP * cols + 2 * packed))
    for which in range(2):
        for x in range(GROUP):
            for i in range(cols):
                for s, a in zip((1, 2, 3), drp_coeffs):
                    for j, sign in ((i + s, 1.0), (i - s, -1.0)):
                        if 0 <= j < cols:
                            at = x * cols + j
                        else:
                            m = j + 3 if j < 0 else j - cols
                            tile, row = (x % 4, m) if x % 4 < 3 else (m, 3)
                            at = GROUP * cols + (x // 4 * 3 + tile) * 8 + row + 4 * which
                            at += packed if j >= cols else 0
                        full[which, x * cols + i, at] += sign * a
    return np.stack([np.stack(np_split(full[w])) for w in range(2)])


def split(x):
    hi = x.astype(BF16)
    return hi, (x - hi.astype(F32)).astype(BF16)


def dot(a, b):
    return lax.dot_general(a, b, (((1,), (0,)), ((), ())), preferred_element_type=F32)


def is_even(axis):
    return lax.rem(lax.axis_index(axis), 2) == 0


def swap(to_a, to_b, axis):
    devices = lax.axis_size(axis)
    pairs_a = [(i, i ^ 1) for i in range(devices)]
    pairs_b = [(i, (i - 1) % devices if i % 2 == 0 else (i + 1) % devices) for i in range(devices)]
    return lax.ppermute(to_a, axis, pairs_a), lax.ppermute(to_b, axis, pairs_b)


def swap_b(value, axis):
    devices = lax.axis_size(axis)
    pairs = [(i, (i - 1) % devices if i % 2 == 0 else (i + 1) % devices) for i in range(devices)]
    return (lax.ppermute(value, axis, pairs),)


def full_specs(body, outs, args, scratch=(), name=None, in_specs=None, out_specs=None, after=(), cost=0, alias=None):
    skip = len(args)

    def run(*refs):
        body(*refs[:skip], *refs[skip + len(after) :])

    return pl.pallas_call(
        run,
        out_shape=[jax.ShapeDtypeStruct(s, d) for s, d in outs],
        in_specs=(in_specs or [VM] * skip) + [ANY] * len(after),
        input_output_aliases=alias or {},
        out_specs=out_specs or [VM] * len(outs),
        scratch_shapes=[pltpu.VMEM(*s) if isinstance(s, tuple) else s for s in scratch],
        compiler_params=PARAMS,
        name=name,
        cost_estimate=pl.CostEstimate(flops=cost, bytes_accessed=0, transcendentals=0),
    )(*args, *after)


def route_body(owner_ref, target_ref, pick_ref, cells_ref, own_ref):
    n_ax, n_az = lax.axis_size("ax"), lax.axis_size("az")
    ax, az = lax.axis_index("ax"), lax.axis_index("az")
    step_x = jnp.where(lax.rem(ax, 2) == 0, 1, -1)
    step_z = jnp.where(lax.rem(az, 2) == 0, 1, -1)
    me = ax * n_az + az
    b_x = ax - step_x
    ids = [
        (ax + step_x) * n_az + az,
        jnp.where((b_x >= 0) & (b_x < n_ax), b_x * n_az + az, -1),
        ax * n_az + lax.rem(az + step_z + n_az, n_az),
        ax * n_az + lax.rem(az - step_z + n_az, n_az),
    ]
    owner = owner_ref[...]
    target = target_ref[...]
    ncols = owner.shape[1]
    most = ncols // 2
    own_ref[...] = jnp.where(owner == me, target, -1)
    row = lax.broadcasted_iota(jnp.int32, (8, ncols), 0)
    marks = jnp.zeros((8, ncols), F32)
    for d, i in enumerate(ids):
        marks = jnp.where((row == d) & (owner == i), 1.0, marks)
    before = lax.broadcasted_iota(jnp.int32, (ncols, ncols), 0) < lax.broadcasted_iota(jnp.int32, (ncols, ncols), 1)
    rank = dot(marks.astype(BF16), jnp.where(before, 1.0, 0.0).astype(BF16))
    coarse = (target // 32).astype(F32)
    fine = (target % 32).astype(F32)
    digits = jnp.where(row == 0, coarse, jnp.where(row == 1, fine, 0.0)).astype(BF16)
    slot = lax.broadcasted_iota(jnp.int32, (most, ncols), 0).astype(F32)
    for d in range(4):
        wanted = jnp.where(marks[d : d + 1] > 0.0, rank[d : d + 1], -1.0)
        pick = jnp.where(slot == wanted, 1.0, 0.0).astype(BF16)
        pick_ref[d * most : (d + 1) * most, :] = pick
        found = lax.dot_general(digits, pick, (((1,), (1,)), ((), ())), preferred_element_type=F32)
        cells_ref[d, :, :] = jnp.zeros(cells_ref.shape[1:], F32)
        cells_ref[d, 0:1, 0:most] = found[0:1] * 32.0 + found[1:2]


def weights_of(h):
    table = filter_table()
    le = [h <= 1, h <= 2, h <= 3]
    out = []
    for k in range(HMAX + 1):
        value = jnp.full(h.shape, table[k, 3], F32)
        for j in (2, 1, 0):
            if j > 0 and table[k, j] == 0.0 and table[k, j - 1] == 0.0:
                value = jnp.where(le[j], 0.0, value)
                break
            value = jnp.where(le[j], table[k, j], value)
        out.append(value)
    return out


def inner_body(noise_ref, half_ref, first_ref, kept_ref):
    rows = noise_ref.shape[0]
    kept_ref[...] = half_ref[...]
    for x in range(rows):
        w = weights_of(half_ref[x])
        total = w[0] * noise_ref[x]
        for k in range(1, HMAX + 1):
            near = [noise_ref[y] for y in (x - k, x + k) if 0 <= y < rows]
            if near:
                total = total + w[k] * (near[0] + near[1] if len(near) == 2 else near[0])
        first_ref[x] = total


def first_body(
    inner_ref, half_ref, got_a_ref, got_b_ref, edge_a_ref, first_ref, to_a_ref, to_b_ref, halo
):
    n_ax, ax = lax.axis_size("ax"), lax.axis_index("ax")
    even_x, even_z = is_even("ax"), is_even("az")
    rows, _, fine = half_ref.shape
    halo[0] = jnp.where(ax > 0, jnp.where(even_x, got_b_ref[...], got_a_ref[...]), 0.0)
    halo[1] = jnp.where(ax < n_ax - 1, jnp.where(even_x, got_a_ref[...], got_b_ref[...]), 0.0)
    for x in range(HMAX, rows - HMAX):
        first_ref[x] = inner_ref[x]
    for i in range(HMAX):
        w = weights_of(half_ref[i])
        total = inner_ref[i]
        for k in range(i + 1, HMAX + 1):
            total = total + w[k] * halo[0, HMAX + i - k]
        first_ref[i] = total
        x = rows - 1 - i
        w = weights_of(half_ref[x])
        total = inner_ref[x]
        for k in range(i + 1, HMAX + 1):
            total = total + w[k] * halo[1, k - i - 1]
        first_ref[x] = total
    half = rows // 2
    low = lax.broadcasted_iota(jnp.int32, (8, fine), 0) < 4
    for x in range(half):
        last = jnp.where(low, pltpu.roll(first_ref[x, 8:16], 4, 0), first_ref[x + half, 8:16])
        begin = jnp.where(low, first_ref[x, 0:8], pltpu.roll(first_ref[x + half, 0:8], 4, 0))
        for ref, value in ((to_a_ref, jnp.where(even_z, last, begin)), (to_b_ref, jnp.where(even_z, begin, last))):
            ref[x] = value[:, : fine // 2]
            ref[half + x] = value[:, fine // 2 :]
    to_a_ref[rows:] = edge_a_ref[...]


def middle_body(first_ref, half_ref, partial_ref, weight_ref, wide):
    rows, cols, fine = first_ref.shape
    blank = jnp.zeros((rows, 8, fine), F32)
    wide[:, 0:8] = blank
    wide[:, 24:32] = blank
    for x in range(rows):
        wide[x, 8:24] = first_ref[x]
    for x in range(rows):
        w = weights_of(half_ref[x])
        total = w[0] * first_ref[x]
        for k in range(1, HMAX + 1):
            total = total + w[k] * (wide[x, 8 - k : 24 - k] + wide[x, 8 + k : 24 + k])
        partial_ref[x] = total
        for k in range(HMAX + 1):
            weight_ref[k, x] = w[k]


def unpack_body(got_ref, out_ref):
    half = out_ref.shape[0]
    for y in range(half):
        out_ref[y] = jnp.concatenate([got_ref[y], got_ref[half + y]], axis=1)


def second_body(
    partial_ref, weight_ref, got_a_ref, got_b_ref, pick_ref, cells_ref,
    own_ref, to_xa, to_xb, to_za, to_zb, fine_hi, fine_lo,
):
    even = is_even("az")
    rows, cols, fine = partial_ref.shape
    half = rows // 2
    lane = lax.broadcasted_iota(jnp.int32, (cols, fine), 1)
    row = lax.broadcasted_iota(jnp.int32, (8, fine), 0)
    for x in range(rows):
        y = x % half
        got_a, got_b = jnp.concatenate([got_a_ref[y], got_a_ref[half + y]], axis=1), got_b_ref[y]
        before, after = jnp.where(even, got_b, got_a), jnp.where(even, got_a, got_b)
        if x < half:
            before = pltpu.roll(before, 4, 0)
        else:
            after = pltpu.roll(after, 4, 0)
        w = [weight_ref[k, x] for k in range(HMAX + 1)]
        total = partial_ref[x]
        for k in range(1, HMAX + 1):
            low = jnp.where(row < k, pltpu.roll(before, k, 0), 0.0)
            high = jnp.where(row >= 8 - k, pltpu.roll(after, 8 - k, 0), 0.0)
            total = total + w[k] * jnp.concatenate([low, high], axis=0)
        result = w[0] * total
        for k in range(1, HMAX + 1):
            up = jnp.where(lane < fine - k, pltpu.roll(total, fine - k, 1), 0.0)
            down = jnp.where(lane >= k, pltpu.roll(total, k, 1), 0.0)
            result = result + w[k] * (up + down)
        hi, lo = split(result)
        fine_hi[x * cols : (x + 1) * cols] = hi
        fine_lo[x * cols : (x + 1) * cols] = lo
    radial = own_ref.shape[1]
    above = lax.broadcasted_iota(jnp.int32, (fine, radial), 0) - lax.broadcasted_iota(
        jnp.int32, (fine, radial), 1
    ) * (fine // radial)
    bins = jnp.where((above >= 0) & (above < fine // radial), source_gain, 0.0).astype(BF16)
    binned = dot(fine_hi[...], bins) + dot(fine_lo[...], bins)
    own_ref[...] = binned
    hi, lo = split(binned)
    most = pick_ref.shape[0] // 4
    for d, out in enumerate((to_xa, to_xb, to_za, to_zb)):
        pick = pick_ref[d * most : (d + 1) * most]
        tiles = most // 8
        out[0:tiles] = (dot(pick, hi) + dot(pick, lo)).reshape(tiles, 8, radial)
        out[tiles] = cells_ref[d]
    for out in (to_xa, to_xb, to_zb):
        out[most // 8 + 1 :] = jnp.zeros((out.shape[0] - most // 8 - 1, *out.shape[1:]), F32)


def onehot(cells, row):
    at = lax.broadcasted_iota(jnp.int32, (cells, row.shape[1]), 0)
    return jnp.where(at == row, 1.0, 0.0).astype(BF16)


def gather_body(
    xa, xb, zb, za, k_mid, k_rim, p_mid, p_rim, to_xa, to_xb, to_za, to_zb, rim_za, rim_zb
):
    mid, cols, radial = p_mid.shape
    cells = (mid + 2 * RIM) * cols
    most = 8 * (za.shape[0] - 1)

    mats, packets = [], []
    for got in (xa, xb, za, zb):
        tiles = most // 8
        mats.append(onehot(cells, got[tiles, 0:1, 0:most].astype(jnp.int32)))
        packets.append(got[0:tiles].reshape(most, radial))
    mat = jnp.concatenate(mats, axis=1)
    hi, lo = split(jnp.concatenate(packets, axis=0))
    q = (dot(mat, hi) + dot(mat, lo)).reshape(mid + 2 * RIM, cols, radial)
    p_rim[0:RIM] = k_rim[4, 0:RIM] + q[0:RIM]
    p_mid[...] = k_mid[4] + q[RIM : RIM + mid]
    p_rim[RIM:] = k_rim[4, RIM:] + q[RIM + mid :]
    level = Parts(k_mid, k_rim, p_mid, p_rim)
    write_x(level, to_xa, to_xb)
    write_z(level, range(RIM, level.rows - RIM, 4), to_za, to_zb)
    write_z(level, [0, level.rows - RIM], rim_za, rim_zb)


class Whole:
    def __init__(self, ref):
        self.ref = ref
        self.rows = ref.shape[1]

    def row(self, f, x):
        return self.ref[f, x]

    def group(self, f, g):
        if g is None:
            return jnp.concatenate([self.ref[f, 0:RIM], self.ref[f, self.rows - RIM :]], axis=0)
        return self.ref[f, RIM + g * GROUP : RIM + (g + 1) * GROUP]


class Parts:
    def __init__(self, mid, rim, p_mid=None, p_rim=None, rows=None):
        self.arrays = (mid, rim, p_mid, p_rim)
        self.rows = rows or mid.shape[1] + 2 * RIM

    def pick(self, f):
        mid, rim, p_mid, p_rim = self.arrays
        if f == 4 and p_mid is not None:
            return p_mid, p_rim
        return mid if mid is None else mid.at[f], rim if rim is None else rim.at[f]

    def row(self, f, x):
        mid, rim = self.pick(f)
        if RIM <= x < self.rows - RIM:
            return mid[x - RIM]
        return rim[x if x < RIM else x - self.rows + 2 * RIM]

    def group(self, f, g):
        mid, rim = self.pick(f)
        return rim[...] if g is None else mid[g * GROUP : (g + 1) * GROUP]

    def store(self, f, x, value):
        mid, rim = self.pick(f)
        if RIM <= x < self.rows - RIM:
            mid[x - RIM] = value
        else:
            rim[x if x < RIM else x - self.rows + 2 * RIM] = value


def join_last(ut, p):
    low = lax.broadcasted_iota(jnp.int32, ut.shape, 0) < 4
    return jnp.where(low, pltpu.roll(ut, 3, 0), pltpu.roll(p, 7, 0))


def join_first(ut, p):
    low = lax.broadcasted_iota(jnp.int32, ut.shape, 0) < 4
    return jnp.where(low, ut, pltpu.roll(p, 4, 0))


def write_x(level, to_xa, to_xb):
    even = is_even("ax")
    for f in range(5):
        for i in range(3):
            first, last = level.row(f, i), level.row(f, level.rows - 3 + i)
            to_xa[3 * f + i] = jnp.where(even, last, first)
            to_xb[3 * f + i] = jnp.where(even, first, last)


def write_z(level, starts, to_za, to_zb):
    even = is_even("az")
    row = None
    for i, x in enumerate(starts):
        first, last = [], []
        for y in range(x, x + 4):
            ut, p = level.row(2, y), level.row(4, y)
            first.append(join_first(ut[0:8], p[0:8]))
            last.append(join_last(ut[8:16], p[8:16]))
        if row is None:
            row = lax.broadcasted_iota(jnp.int32, first[0].shape, 0) % 4 == 3
        for t in range(3):
            shift = 3 - t
            one = jnp.where(row, pltpu.roll(first[3], shift, 0), first[t])
            two = jnp.where(row, pltpu.roll(last[3], shift, 0), last[t])
            to_za[3 * i + t] = jnp.where(even, two, one)
            to_zb[3 * i + t] = jnp.where(even, one, two)


def edges_body(state, to_xa, to_xb, to_za, to_zb):
    level = Whole(state)
    write_x(level, to_xa, to_xb)
    write_z(level, range(0, level.rows, 4), to_za, to_zb)


def fill_halo(halo, xa, xb):
    n_ax, ax = lax.axis_size("ax"), lax.axis_index("ax")
    even = is_even("ax")
    for f in range(halo.shape[1]):
        a, b = xa[3 * f : 3 * f + 3], xb[3 * f : 3 * f + 3]
        halo[0, f] = jnp.where(ax > 0, jnp.where(even, b, a), 0.0)
        halo[1, f] = jnp.where(ax < n_ax - 1, jnp.where(even, a, b), 0.0)


def inverse_step(cols, radial):
    base = cols * lax.axis_size("az") / (2.0 * math.pi)
    at = lax.broadcasted_iota(jnp.int32, (1, radial), 1).astype(F32)
    return base / (base / hub_ratio + radial_step * (at + 0.5))


def along(row, x):
    total = drp_coeffs[0] * (row(x + 1) - row(x - 1))
    for s in (2, 3):
        total = total + drp_coeffs[s - 1] * (row(x + s) - row(x - s))
    return total


def apply_operator(level, groups, za, zb, tmat, rmat, finish, halo=None):
    even = is_even("az")
    tiles = level.rows // 4 * 3
    rim = RIM // 4 * 3

    def row(f, x):
        if x < 0:
            return halo[0, f, x + 3]
        if x >= level.rows:
            return halo[1, f, x - level.rows]
        return level.row(f, x)

    def beside(g):
        spans = [(0, rim), (tiles - rim, tiles)] if g is None else [(rim + 6 * g, rim + 6 * g + 6)]
        start = za.shape[0] - tiles
        if za.shape[0] == 2 * rim:
            spans, start = [(0, rim), (rim, 2 * rim)], 0
        elif za.shape[0] == tiles - 2 * rim:
            start = -rim
        sides = []
        for swap_ab in (False, True):
            for a, b in spans:
                last_b = zb.shape[0] - za.shape[0] + start
                got_a, got_b = za[start + a : start + b], zb[last_b + a : last_b + b]
                pair = (got_a, got_b) if swap_ab else (got_b, got_a)
                sides.append(jnp.where(even, *pair).reshape((b - a) * 8, za.shape[2]))
        return split(jnp.concatenate(sides, axis=0))

    for g in groups:
        if g is None:
            xs = [*range(RIM), *range(level.rows - RIM, level.rows)]
        else:
            xs = range(RIM + g * GROUP, RIM + (g + 1) * GROUP)
        ut, ur, p = [level.group(f, g) for f in (2, 3, 4)]
        _, cols, radial = ut.shape
        inv_h = inverse_step(cols, radial)
        side_hi, side_lo = beside(g)
        p_hi, p_lo = split(p.reshape(GROUP * cols, radial))
        ut_hi, ut_lo = split(ut.reshape(GROUP * cols, radial))
        ur_hi, ur_lo = split(ur.reshape(GROUP * cols, radial))

        def across(which, hi, lo):
            hi = jnp.concatenate([hi, side_hi], axis=0)
            lo = jnp.concatenate([lo, side_lo], axis=0)
            return dot(tmat[which, 0], hi) + dot(tmat[which, 0], lo) + dot(tmat[which, 1], hi)

        def outward(which, hi, lo):
            return dot(hi, rmat[which, 0]) + dot(lo, rmat[which, 0]) + dot(hi, rmat[which, 1])

        div_tr = across(0, ut_hi, ut_lo) * inv_h + outward(0, ur_hi, ur_lo)
        p_t = across(1, p_hi, p_lo) * inv_h
        p_r = outward(1, p_hi, p_lo)
        for i, x in enumerate(xs):
            part = slice(i * cols, (i + 1) * cols)
            d = [along(lambda y: row(f, y), x) for f in range(5)]
            div = d[1] + div_tr[part]
            finish(
                x,
                [
                    -mach_number * d[0] - div,
                    -mach_number * d[1] - d[4],
                    -mach_number * d[2] - p_t[part],
                    -mach_number * d[3] - p_r[part],
                    -mach_number * d[4] - div,
                ],
            )


def start_body(state, za, zb, xa, xb, tmat, rmat, binned, own, k_mid, k_rim, halo, source):
    rows, cols, radial = source.shape
    hi, lo = split(binned[...])
    mat = onehot(rows * cols, own[...])
    source[...] = (dot(mat, hi) + dot(mat, lo)).reshape(rows, cols, radial)
    fill_halo(halo, xa, xb)
    level, out = Whole(state), Parts(k_mid, k_rim)

    def finish(x, tend):
        for f in range(5):
            out.store(f, x, tend[f] + source[x] if f == 4 else tend[f])

    apply_operator(level, [*range(k_mid.shape[1] // GROUP), None], za, zb, tmat, rmat, finish, halo)


def inner_stage_body(factor, level, base, zb, za, tmat, rmat, out_mid, to_za, to_zb):
    def finish(x, tend):
        for f in range(5):
            out_mid[f, x - RIM] = base.row(f, x) + factor * tend[f]

    apply_operator(level, range(out_mid.shape[1] // GROUP), za, zb, tmat, rmat, finish)
    write_z(Parts(out_mid, None, rows=level.rows), range(RIM, level.rows - RIM, 4), to_za, to_zb)


def rim_stage_body(factor, level, base, xa, xb, zb, za, tmat, rmat, out_rim, to_xa, to_xb, to_za, to_zb, halo):
    fill_halo(halo, xa, xb)
    out = Parts(None, out_rim, rows=level.rows)

    def finish(x, tend):
        for f in range(5):
            out.store(f, x, base.row(f, x) + factor * tend[f])

    apply_operator(level, [None], za, zb, tmat, rmat, finish, halo)
    write_x(out, to_xa, to_xb)
    write_z(out, [0, level.rows - RIM], to_za, to_zb)


def last_finish(fields, k, store):
    def finish(x, tend):
        for f in range(5):
            store(f, x, fields[f, x] + time_step * k.row(f, x) + (0.5 * time_step * time_step) * tend[f])

    return finish


def inner_last_body(level, k, fields, zb, za, tmat, rmat, out, result, sems):
    def store(f, x, value):
        result[f, x - RIM] = value

    def copy(g):
        at = g * GROUP
        return pltpu.make_async_copy(
            result.at[:, at : at + GROUP], out.at[:, RIM + at : RIM + at + GROUP], sems.at[g]
        )

    groups = range(result.shape[1] // GROUP)
    for g in groups:
        apply_operator(level, [g], za, zb, tmat, rmat, last_finish(fields, k, store))
        copy(g).start()
    for g in groups:
        copy(g).wait()


def rim_last_body(level, k, fields, xa, xb, zb, za, tmat, rmat, out, halo, result, sems):
    rows = level.rows
    fill_halo(halo, xa, xb)

    copies = [
        pltpu.make_async_copy(result.at[:, 0:RIM], out.at[:, 0:RIM], sems.at[0]),
        pltpu.make_async_copy(result.at[:, RIM:], out.at[:, rows - RIM :], sems.at[1]),
    ]

    def store(f, x, value):
        result[f, x if x < RIM else x - rows + 2 * RIM] = value
        if f == 4 and x in (RIM - 1, rows - 1):
            copies[x // RIM > 0].start()

    apply_operator(level, [None], za, zb, tmat, rmat, last_finish(fields, k, store), halo)
    for copy in copies:
        copy.wait()


def local(noise, half_width, owner, target_cell, fields):
    px, pa, fine = noise.shape
    cx, ca, radial = fields.shape[1:]
    ncols = px * pa
    most = ncols // 2
    n_az = lax.axis_size("az")
    inner = cx - 2 * RIM

    block = ((px, pa, fine), F32)
    even = is_even("ax")
    to_a = jnp.where(even, noise[px - HMAX :], noise[:HMAX])
    to_b = jnp.where(even, noise[:HMAX], noise[px - HMAX :])
    noise_a, noise_b = swap(to_a, to_b, "ax")
    send_x, send_z = ((15, ca, radial), F32), ((cx // 4 * 3, 8, radial), F32)
    sends = [send_x, send_x, send_z, send_z]
    xa, xb, za, zb = full_specs(edges_body, sends, [fields], name="edges", after=[to_a])
    uxa, uxb = swap(xa, xb, "ax")
    partial, half_width = full_specs(
        inner_body, [block, ((px, pa, fine), jnp.int32)], [noise, half_width], name="filter_inner", after=[za]
    )
    long_z = ((px + send_z[0][0], 8, fine // 2), F32)
    filtered, to_a, to_b = full_specs(
        first_body,
        [block, long_z, ((px, 8, fine // 2), F32)],
        [partial, half_width, noise_a, noise_b, za],
        [((2, HMAX, pa, fine), F32)],
        name="filter_axial",
    )
    got_a, got_b = swap(to_a, to_b, "az")
    (uzb,) = swap_b(zb, "az")
    pick, cells, own = full_specs(
        route_body,
        [((4 * most, ncols), BF16), ((4, 8, radial), F32), ((1, ncols), jnp.int32)],
        [owner.reshape(1, ncols), target_cell.reshape(1, ncols)],
        name="route",
        after=[filtered],
    )
    partial, weights = full_specs(
        middle_body,
        [block, ((HMAX + 1, px, pa, fine), F32)],
        [filtered, half_width],
        [((px, 32, fine), F32)],
        name="filter_middle",
        after=[pick],
    )
    (got_b,) = full_specs(
        unpack_body, [((px // 2, 8, fine), F32)], [got_b], name="unpack", after=[weights], cost=MORE
    )
    tiles = most // 8 + 1
    packet, packet_x, packet_b = [((tiles + spare, 8, radial), F32) for spare in (0, 1, 2)]
    binned, xa, xb, za, zb = full_specs(
        second_body,
        [((ncols, radial), F32), packet_x, packet_x, packet, packet_b],
        [partial, weights, got_a, got_b, pick, cells],
        [((ncols, fine), BF16), ((ncols, fine), BF16)],
        name="filter_rest",
        cost=COST,
    )
    za, zb = swap(za, zb, "az")
    packets = (*swap(xa, xb, "ax"), zb, za)

    tmat = jnp.asarray(azimuth_matrices(ca))
    rmat = jnp.asarray(radial_matrices(float(ca * n_az), radial))
    mid, rim = ((5, inner, ca, radial), F32), ((5, 2 * RIM, ca, radial), F32)
    halo = ((2, 5, 3, ca, radial), F32)
    k_mid, k_rim = full_specs(
        start_body, [mid, rim], [fields, got_a, uzb, uxa, uxb, tmat, rmat, binned, own], [halo, ((cx, ca, radial), F32)], name="operator"
    )
    inner_z, rim_z = ((inner // 4 * 3, 8, radial), F32), ((RIM // 2 * 3, 8, radial), F32)
    p_mid, p_rim, *edges = full_specs(
        gather_body,
        [((inner, ca, radial), F32), ((2 * RIM, ca, radial), F32), send_x, send_x, inner_z, inner_z, rim_z, rim_z],
        [*packets, k_mid, k_rim],
        name="gather",
    )
    k = [k_mid, k_rim, p_mid, p_rim]
    za, zb = swap(edges[2], edges[3], "az")
    xa, xb = swap(edges[0], edges[1], "ax")
    rim_a, rim_b = swap(edges[4], edges[5], "az")
    level = k
    for factor in (time_step / 4.0, time_step / 3.0):
        size = len(level)

        def body(*refs, factor=factor, size=size):
            inner_stage_body(factor, Parts(*refs[:size]), Parts(*refs[size : size + 4]), *refs[size + 4 :])

        new_mid, to_za, to_zb = full_specs(
            body, [mid, inner_z, inner_z], [*level, *k, zb, za, tmat, rmat], name="stage_inner", cost=SOME
        )
        za, zb = swap(to_za, to_zb, "az")

        def body(*refs, factor=factor, size=size):
            rim_stage_body(factor, Parts(*refs[:size]), Parts(*refs[size : size + 4]), *refs[size + 4 :])

        new_rim, to_xa, to_xb, to_za, to_zb = full_specs(
            body,
            [rim, send_x, send_x, rim_z, rim_z],
            [*level, *k, xa, xb, rim_b, rim_a, tmat, rmat],
            [halo],
            name="stage_rim",
            after=[new_mid],
            cost=COST,
        )
        xa, xb = swap(to_xa, to_xb, "ax")
        rim_a, rim_b = swap(to_za, to_zb, "az")
        level = [new_mid, new_rim]

    def body(*refs):
        inner_last_body(Parts(*refs[:2]), Parts(*refs[2:6]), *refs[6:])

    whole = ((5, cx, ca, radial), F32)
    (out,) = full_specs(
        body,
        [whole],
        [*level, *k, fields, zb, za, tmat, rmat],
        [mid, pltpu.SemaphoreType.DMA((inner // GROUP,))],
        name="final_inner",
        out_specs=[ANY],
        cost=SOME,
    )

    def body(out_in, *refs):
        rim_last_body(Parts(*refs[:2]), Parts(*refs[2:6]), *refs[6:])

    (out,) = full_specs(
        body,
        [whole],
        [out, *level, *k, fields, xa, xb, rim_b, rim_a, tmat, rmat],
        [halo, rim, pltpu.SemaphoreType.DMA((2,))],
        name="final_rim",
        in_specs=[ANY] + [VM] * 13,
        out_specs=[ANY],
        alias={0: 0},
    )
    return out


def solution(mesh):
    return jax.shard_map(
        local,
        mesh=mesh,
        in_specs=(
            P("ax", "az", None),
            P("ax", "az", None),
            P(("ax", "az")),
            P(("ax", "az")),
            P(None, "ax", "az", None),
        ),
        out_specs=P(None, "ax", "az", None),
        check_vma=False,
    )
```

```python
import math

import numpy as np

import jax
import jax.numpy as jnp
from jax import lax
from jax.experimental import pallas as pl
from jax.experimental.pallas import tpu as pltpu
from jax.sharding import PartitionSpec as P

HMAX = 4
drp_coeffs = (0.770882380518, -0.166705904415, 0.02084314277)
mach_number = 0.5
time_step = 0.7
source_gain = 4.0
radial_step = 2.0
hub_ratio = 1.6

F32 = jnp.float32
BF16 = jnp.bfloat16
VM = pl.BlockSpec(memory_space=pltpu.VMEM)
ANY = pl.BlockSpec(memory_space=pl.ANY)
PARAMS = pltpu.CompilerParams(vmem_limit_bytes=24 * 1024 * 1024)
GROUP = 8
RIM = 4
MORE = 2_500_000_000
SOME = 2_000_000_000
COST = 1 << 37


def np_split(matrix):
    hi = matrix.astype(np.float32).astype(BF16)
    lo = (matrix - hi.astype(np.float64)).astype(np.float32).astype(BF16)
    return hi, lo


def filter_table():
    table = np.zeros((HMAX + 1, HMAX))
    for h in range(1, HMAX + 1):
        weights = [math.exp(-2.0 * k * k / (h * h)) if k <= h else 0.0 for k in range(HMAX + 1)]
        total = weights[0] + 2.0 * sum(weights[1:])
        table[:, h - 1] = [w / total for w in weights]
    return table


def radial_rows(na_total, radial):
    base = na_total / (2.0 * math.pi)
    radius = base / hub_ratio + radial_step * (np.arange(radial) + 0.5)
    return base / radius, 1.0 / radius


def radial_matrices(na_total, radial):
    diff = np.zeros((radial, radial))
    for s, a in zip((1, 2, 3), drp_coeffs):
        for j in range(radial):
            if j + s < radial:
                diff[j + s, j] += a / radial_step
            if j - s >= 0:
                diff[j - s, j] -= a / radial_step
    with_r = diff + np.diag(radial_rows(na_total, radial)[1])
    return np.stack([np.stack(np_split(with_r)), np.stack(np_split(diff))])


def azimuth_matrices(cols):
    packed = GROUP * 6
    full = np.zeros((2, GROUP * cols, GROUP * cols + 2 * packed))
    for which in range(2):
        for x in range(GROUP):
            for i in range(cols):
                for s, a in zip((1, 2, 3), drp_coeffs):
                    for j, sign in ((i + s, 1.0), (i - s, -1.0)):
                        if 0 <= j < cols:
                            at = x * cols + j
                        else:
                            m = j + 3 if j < 0 else j - cols
                            tile, row = (x % 4, m) if x % 4 < 3 else (m, 3)
                            at = GROUP * cols + (x // 4 * 3 + tile) * 8 + row + 4 * which
                            at += packed if j >= cols else 0
                        full[which, x * cols + i, at] += sign * a
    return np.stack([np.stack(np_split(full[w])) for w in range(2)])


def split(x):
    hi = x.astype(BF16)
    return hi, (x - hi.astype(F32)).astype(BF16)


def dot(a, b):
    return lax.dot_general(a, b, (((1,), (0,)), ((), ())), preferred_element_type=F32)


def is_even(axis):
    return lax.rem(lax.axis_index(axis), 2) == 0


def swap(to_a, to_b, axis):
    devices = lax.axis_size(axis)
    pairs_a = [(i, i ^ 1) for i in range(devices)]
    pairs_b = [(i, (i - 1) % devices if i % 2 == 0 else (i + 1) % devices) for i in range(devices)]
    return lax.ppermute(to_a, axis, pairs_a), lax.ppermute(to_b, axis, pairs_b)


def swap_b(value, axis):
    devices = lax.axis_size(axis)
    pairs = [(i, (i - 1) % devices if i % 2 == 0 else (i + 1) % devices) for i in range(devices)]
    return (lax.ppermute(value, axis, pairs),)


def full_specs(body, outs, args, scratch=(), name=None, in_specs=None, out_specs=None, after=(), cost=0, alias=None):
    skip = len(args)

    def run(*refs):
        body(*refs[:skip], *refs[skip + len(after) :])

    return pl.pallas_call(
        run,
        out_shape=[jax.ShapeDtypeStruct(s, d) for s, d in outs],
        in_specs=(in_specs or [VM] * skip) + [ANY] * len(after),
        input_output_aliases=alias or {},
        out_specs=out_specs or [VM] * len(outs),
        scratch_shapes=[pltpu.VMEM(*s) if isinstance(s, tuple) else s for s in scratch],
        compiler_params=PARAMS,
        name=name,
        cost_estimate=pl.CostEstimate(flops=cost, bytes_accessed=0, transcendentals=0),
    )(*args, *after)


def route_body(owner_ref, target_ref, pick_ref, cells_ref, own_ref):
    n_ax, n_az = lax.axis_size("ax"), lax.axis_size("az")
    ax, az = lax.axis_index("ax"), lax.axis_index("az")
    step_x = jnp.where(lax.rem(ax, 2) == 0, 1, -1)
    step_z = jnp.where(lax.rem(az, 2) == 0, 1, -1)
    me = ax * n_az + az
    b_x = ax - step_x
    ids = [
        (ax + step_x) * n_az + az,
        jnp.where((b_x >= 0) & (b_x < n_ax), b_x * n_az + az, -1),
        ax * n_az + lax.rem(az + step_z + n_az, n_az),
        ax * n_az + lax.rem(az - step_z + n_az, n_az),
    ]
    owner = owner_ref[...]
    target = target_ref[...]
    ncols = owner.shape[1]
    most = ncols // 2
    own_ref[...] = jnp.where(owner == me, target, -1)
    row = lax.broadcasted_iota(jnp.int32, (8, ncols), 0)
    marks = jnp.zeros((8, ncols), F32)
    for d, i in enumerate(ids):
        marks = jnp.where((row == d) & (owner == i), 1.0, marks)
    before = lax.broadcasted_iota(jnp.int32, (ncols, ncols), 0) < lax.broadcasted_iota(jnp.int32, (ncols, ncols), 1)
    rank = dot(marks.astype(BF16), jnp.where(before, 1.0, 0.0).astype(BF16))
    coarse = (target // 32).astype(F32)
    fine = (target % 32).astype(F32)
    digits = jnp.where(row == 0, coarse, jnp.where(row == 1, fine, 0.0)).astype(BF16)
    slot = lax.broadcasted_iota(jnp.int32, (most, ncols), 0).astype(F32)
    for d in range(4):
        wanted = jnp.where(marks[d : d + 1] > 0.0, rank[d : d + 1], -1.0)
        pick = jnp.where(slot == wanted, 1.0, 0.0).astype(BF16)
        pick_ref[d * most : (d + 1) * most, :] = pick
        found = lax.dot_general(digits, pick, (((1,), (1,)), ((), ())), preferred_element_type=F32)
        cells_ref[d, :, :] = jnp.zeros(cells_ref.shape[1:], F32)
        cells_ref[d, 0:1, 0:most] = found[0:1] * 32.0 + found[1:2]


def weights_of(h):
    table = filter_table()
    le = [h <= 1, h <= 2, h <= 3]
    out = []
    for k in range(HMAX + 1):
        value = jnp.full(h.shape, table[k, 3], F32)
        for j in (2, 1, 0):
            if j > 0 and table[k, j] == 0.0 and table[k, j - 1] == 0.0:
                value = jnp.where(le[j], 0.0, value)
                break
            value = jnp.where(le[j], table[k, j], value)
        out.append(value)
    return out


def inner_body(noise_ref, half_ref, first_ref, kept_ref):
    rows = noise_ref.shape[0]
    kept_ref[...] = half_ref[...]
    for x in range(rows):
        w = weights_of(half_ref[x])
        total = w[0] * noise_ref[x]
        for k in range(1, HMAX + 1):
            near = [noise_ref[y] for y in (x - k, x + k) if 0 <= y < rows]
            if near:
                total = total + w[k] * (near[0] + near[1] if len(near) == 2 else near[0])
        first_ref[x] = total


def first_body(
    inner_ref, half_ref, got_a_ref, got_b_ref, edge_a_ref, first_ref, to_a_ref, to_b_ref, halo
):
    n_ax, ax = lax.axis_size("ax"), lax.axis_index("ax")
    even_x, even_z = is_even("ax"), is_even("az")
    rows, _, fine = half_ref.shape
    halo[0] = jnp.where(ax > 0, jnp.where(even_x, got_b_ref[...], got_a_ref[...]), 0.0)
    halo[1] = jnp.where(ax < n_ax - 1, jnp.where(even_x, got_a_ref[...], got_b_ref[...]), 0.0)
    for x in range(HMAX, rows - HMAX):
        first_ref[x] = inner_ref[x]
    for i in range(HMAX):
        w = weights_of(half_ref[i])
        total = inner_ref[i]
        for k in range(i + 1, HMAX + 1):
            total = total + w[k] * halo[0, HMAX + i - k]
        first_ref[i] = total
        x = rows - 1 - i
        w = weights_of(half_ref[x])
        total = inner_ref[x]
        for k in range(i + 1, HMAX + 1):
            total = total + w[k] * halo[1, k - i - 1]
        first_ref[x] = total
    half = rows // 2
    low = lax.broadcasted_iota(jnp.int32, (8, fine), 0) < 4
    for x in range(half):
        last = jnp.where(low, pltpu.roll(first_ref[x, 8:16], 4, 0), first_ref[x + half, 8:16])
        begin = jnp.where(low, first_ref[x, 0:8], pltpu.roll(first_ref[x + half, 0:8], 4, 0))
        for ref, value in ((to_a_ref, jnp.where(even_z, last, begin)), (to_b_ref, jnp.where(even_z, begin, last))):
            ref[x] = value[:, : fine // 2]
            ref[half + x] = value[:, fine // 2 :]
    to_a_ref[rows:] = edge_a_ref[...]


def middle_body(first_ref, half_ref, partial_ref, weight_ref, wide):
    rows, cols, fine = first_ref.shape
    blank = jnp.zeros((rows, 8, fine), F32)
    wide[:, 0:8] = blank
    wide[:, 24:32] = blank
    for x in range(rows):
        wide[x, 8:24] = first_ref[x]
    for x in range(rows):
        w = weights_of(half_ref[x])
        total = w[0] * first_ref[x]
        for k in range(1, HMAX + 1):
            total = total + w[k] * (wide[x, 8 - k : 24 - k] + wide[x, 8 + k : 24 + k])
        partial_ref[x] = total
        for k in range(HMAX + 1):
            weight_ref[k, x] = w[k]


def unpack_body(got_ref, out_ref):
    half = out_ref.shape[0]
    for y in range(half):
        out_ref[y] = jnp.concatenate([got_ref[y], got_ref[half + y]], axis=1)


def second_body(
    partial_ref, weight_ref, got_a_ref, got_b_ref, pick_ref, cells_ref,
    own_ref, to_xa, to_xb, to_za, to_zb, fine_hi, fine_lo,
):
    even = is_even("az")
    rows, cols, fine = partial_ref.shape
    half = rows // 2
    lane = lax.broadcasted_iota(jnp.int32, (cols, fine), 1)
    row = lax.broadcasted_iota(jnp.int32, (8, fine), 0)
    for x in range(rows):
        y = x % half
        got_a, got_b = jnp.concatenate([got_a_ref[y], got_a_ref[half + y]], axis=1), got_b_ref[y]
        before, after = jnp.where(even, got_b, got_a), jnp.where(even, got_a, got_b)
        if x < half:
            before = pltpu.roll(before, 4, 0)
        else:
            after = pltpu.roll(after, 4, 0)
        w = [weight_ref[k, x] for k in range(HMAX + 1)]
        total = partial_ref[x]
        for k in range(1, HMAX + 1):
            low = jnp.where(row < k, pltpu.roll(before, k, 0), 0.0)
            high = jnp.where(row >= 8 - k, pltpu.roll(after, 8 - k, 0), 0.0)
            total = total + w[k] * jnp.concatenate([low, high], axis=0)
        result = w[0] * total
        for k in range(1, HMAX + 1):
            up = jnp.where(lane < fine - k, pltpu.roll(total, fine - k, 1), 0.0)
            down = jnp.where(lane >= k, pltpu.roll(total, k, 1), 0.0)
            result = result + w[k] * (up + down)
        hi, lo = split(result)
        fine_hi[x * cols : (x + 1) * cols] = hi
        fine_lo[x * cols : (x + 1) * cols] = lo
    radial = own_ref.shape[1]
    above = lax.broadcasted_iota(jnp.int32, (fine, radial), 0) - lax.broadcasted_iota(
        jnp.int32, (fine, radial), 1
    ) * (fine // radial)
    bins = jnp.where((above >= 0) & (above < fine // radial), source_gain, 0.0).astype(BF16)
    binned = dot(fine_hi[...], bins) + dot(fine_lo[...], bins)
    own_ref[...] = binned
    hi, lo = split(binned)
    most = pick_ref.shape[0] // 4
    for d, out in enumerate((to_xa, to_xb, to_za, to_zb)):
        pick = pick_ref[d * most : (d + 1) * most]
        tiles = most // 8
        out[0:tiles] = (dot(pick, hi) + dot(pick, lo)).reshape(tiles, 8, radial)
        out[tiles] = cells_ref[d]
    for out in (to_xa, to_xb, to_zb):
        out[most // 8 + 1 :] = jnp.zeros((out.shape[0] - most // 8 - 1, *out.shape[1:]), F32)


def onehot(cells, row):
    at = lax.broadcasted_iota(jnp.int32, (cells, row.shape[1]), 0)
    return jnp.where(at == row, 1.0, 0.0).astype(BF16)


def gather_body(
    xa, xb, zb, za, k_mid, k_rim, p_mid, p_rim, to_xa, to_xb, to_za, to_zb, rim_za, rim_zb
):
    mid, cols, radial = p_mid.shape
    cells = (mid + 2 * RIM) * cols
    most = 8 * (za.shape[0] - 1)

    mats, packets = [], []
    for got in (xa, xb, za, zb):
        tiles = most // 8
        mats.append(onehot(cells, got[tiles, 0:1, 0:most].astype(jnp.int32)))
        packets.append(got[0:tiles].reshape(most, radial))
    mat = jnp.concatenate(mats, axis=1)
    hi, lo = split(jnp.concatenate(packets, axis=0))
    q = (dot(mat, hi) + dot(mat, lo)).reshape(mid + 2 * RIM, cols, radial)
    p_rim[0:RIM] = k_rim[4, 0:RIM] + q[0:RIM]
    p_mid[...] = k_mid[4] + q[RIM : RIM + mid]
    p_rim[RIM:] = k_rim[4, RIM:] + q[RIM + mid :]
    level = Parts(k_mid, k_rim, p_mid, p_rim)
    write_x(level, to_xa, to_xb)
    write_z(level, range(RIM, level.rows - RIM, 4), to_za, to_zb)
    write_z(level, [0, level.rows - RIM], rim_za, rim_zb)


class Whole:
    def __init__(self, ref):
        self.ref = ref
        self.rows = ref.shape[1]

    def row(self, f, x):
        return self.ref[f, x]

    def group(self, f, g):
        if g is None:
            return jnp.concatenate([self.ref[f, 0:RIM], self.ref[f, self.rows - RIM :]], axis=0)
        return self.ref[f, RIM + g * GROUP : RIM + (g + 1) * GROUP]


class Parts:
    def __init__(self, mid, rim, p_mid=None, p_rim=None, rows=None):
        self.arrays = (mid, rim, p_mid, p_rim)
        self.rows = rows or mid.shape[1] + 2 * RIM

    def pick(self, f):
        mid, rim, p_mid, p_rim = self.arrays
        if f == 4 and p_mid is not None:
            return p_mid, p_rim
        return mid if mid is None else mid.at[f], rim if rim is None else rim.at[f]

    def row(self, f, x):
        mid, rim = self.pick(f)
        if RIM <= x < self.rows - RIM:
            return mid[x - RIM]
        return rim[x if x < RIM else x - self.rows + 2 * RIM]

    def group(self, f, g):
        mid, rim = self.pick(f)
        return rim[...] if g is None else mid[g * GROUP : (g + 1) * GROUP]

    def store(self, f, x, value):
        mid, rim = self.pick(f)
        if RIM <= x < self.rows - RIM:
            mid[x - RIM] = value
        else:
            rim[x if x < RIM else x - self.rows + 2 * RIM] = value


def join_last(ut, p):
    low = lax.broadcasted_iota(jnp.int32, ut.shape, 0) < 4
    return jnp.where(low, pltpu.roll(ut, 3, 0), pltpu.roll(p, 7, 0))


def join_first(ut, p):
    low = lax.broadcasted_iota(jnp.int32, ut.shape, 0) < 4
    return jnp.where(low, ut, pltpu.roll(p, 4, 0))


def write_x(level, to_xa, to_xb):
    even = is_even("ax")
    for f in range(5):
        for i in range(3):
            first, last = level.row(f, i), level.row(f, level.rows - 3 + i)
            to_xa[3 * f + i] = jnp.where(even, last, first)
            to_xb[3 * f + i] = jnp.where(even, first, last)


def write_z(level, starts, to_za, to_zb):
    even = is_even("az")
    row = None
    for i, x in enumerate(starts):
        first, last = [], []
        for y in range(x, x + 4):
            ut, p = level.row(2, y), level.row(4, y)
            first.append(join_first(ut[0:8], p[0:8]))
            last.append(join_last(ut[8:16], p[8:16]))
        if row is None:
            row = lax.broadcasted_iota(jnp.int32, first[0].shape, 0) % 4 == 3
        for t in range(3):
            shift = 3 - t
            one = jnp.where(row, pltpu.roll(first[3], shift, 0), first[t])
            two = jnp.where(row, pltpu.roll(last[3], shift, 0), last[t])
            to_za[3 * i + t] = jnp.where(even, two, one)
            to_zb[3 * i + t] = jnp.where(even, one, two)


def edges_body(state, to_xa, to_xb, to_za, to_zb):
    level = Whole(state)
    write_x(level, to_xa, to_xb)
    write_z(level, range(0, level.rows, 4), to_za, to_zb)


def fill_halo(halo, xa, xb):
    n_ax, ax = lax.axis_size("ax"), lax.axis_index("ax")
    even = is_even("ax")
    for f in range(halo.shape[1]):
        a, b = xa[3 * f : 3 * f + 3], xb[3 * f : 3 * f + 3]
        halo[0, f] = jnp.where(ax > 0, jnp.where(even, b, a), 0.0)
        halo[1, f] = jnp.where(ax < n_ax - 1, jnp.where(even, a, b), 0.0)


def inverse_step(cols, radial):
    base = cols * lax.axis_size("az") / (2.0 * math.pi)
    at = lax.broadcasted_iota(jnp.int32, (1, radial), 1).astype(F32)
    return base / (base / hub_ratio + radial_step * (at + 0.5))


def along(row, x):
    total = drp_coeffs[0] * (row(x + 1) - row(x - 1))
    for s in (2, 3):
        total = total + drp_coeffs[s - 1] * (row(x + s) - row(x - s))
    return total


def apply_operator(level, groups, za, zb, tmat, rmat, finish, halo=None):
    even = is_even("az")
    tiles = level.rows // 4 * 3
    rim = RIM // 4 * 3

    def row(f, x):
        if x < 0:
            return halo[0, f, x + 3]
        if x >= level.rows:
            return halo[1, f, x - level.rows]
        return level.row(f, x)

    def beside(g):
        spans = [(0, rim), (tiles - rim, tiles)] if g is None else [(rim + 6 * g, rim + 6 * g + 6)]
        start = za.shape[0] - tiles
        if za.shape[0] == 2 * rim:
            spans, start = [(0, rim), (rim, 2 * rim)], 0
        elif za.shape[0] == tiles - 2 * rim:
            start = -rim
        sides = []
        for swap_ab in (False, True):
            for a, b in spans:
                last_b = zb.shape[0] - za.shape[0] + start
                got_a, got_b = za[start + a : start + b], zb[last_b + a : last_b + b]
                pair = (got_a, got_b) if swap_ab else (got_b, got_a)
                sides.append(jnp.where(even, *pair).reshape((b - a) * 8, za.shape[2]))
        return split(jnp.concatenate(sides, axis=0))

    for g in groups:
        if g is None:
            xs = [*range(RIM), *range(level.rows - RIM, level.rows)]
        else:
            xs = range(RIM + g * GROUP, RIM + (g + 1) * GROUP)
        ut, ur, p = [level.group(f, g) for f in (2, 3, 4)]
        _, cols, radial = ut.shape
        inv_h = inverse_step(cols, radial)
        side_hi, side_lo = beside(g)
        p_hi, p_lo = split(p.reshape(GROUP * cols, radial))
        ut_hi, ut_lo = split(ut.reshape(GROUP * cols, radial))
        ur_hi, ur_lo = split(ur.reshape(GROUP * cols, radial))

        def across(which, hi, lo):
            hi = jnp.concatenate([hi, side_hi], axis=0)
            lo = jnp.concatenate([lo, side_lo], axis=0)
            return dot(tmat[which, 0], hi) + dot(tmat[which, 0], lo) + dot(tmat[which, 1], hi)

        def outward(which, hi, lo):
            return dot(hi, rmat[which, 0]) + dot(lo, rmat[which, 0]) + dot(hi, rmat[which, 1])

        div_tr = across(0, ut_hi, ut_lo) * inv_h + outward(0, ur_hi, ur_lo)
        p_t = across(1, p_hi, p_lo) * inv_h
        p_r = outward(1, p_hi, p_lo)
        for i, x in enumerate(xs):
            part = slice(i * cols, (i + 1) * cols)
            d = [along(lambda y: row(f, y), x) for f in range(5)]
            div = d[1] + div_tr[part]
            finish(
                x,
                [
                    -mach_number * d[0] - div,
                    -mach_number * d[1] - d[4],
                    -mach_number * d[2] - p_t[part],
                    -mach_number * d[3] - p_r[part],
                    -mach_number * d[4] - div,
                ],
            )


def start_body(state, za, zb, xa, xb, tmat, rmat, binned, own, k_mid, k_rim, halo, source):
    rows, cols, radial = source.shape
    hi, lo = split(binned[...])
    mat = onehot(rows * cols, own[...])
    source[...] = (dot(mat, hi) + dot(mat, lo)).reshape(rows, cols, radial)
    fill_halo(halo, xa, xb)
    level, out = Whole(state), Parts(k_mid, k_rim)

    def finish(x, tend):
        for f in range(5):
            out.store(f, x, tend[f] + source[x] if f == 4 else tend[f])

    apply_operator(level, [*range(k_mid.shape[1] // GROUP), None], za, zb, tmat, rmat, finish, halo)


def inner_stage_body(factor, level, base, zb, za, tmat, rmat, out_mid, to_za, to_zb):
    def finish(x, tend):
        for f in range(5):
            out_mid[f, x - RIM] = base.row(f, x) + factor * tend[f]

    apply_operator(level, range(out_mid.shape[1] // GROUP), za, zb, tmat, rmat, finish)
    write_z(Parts(out_mid, None, rows=level.rows), range(RIM, level.rows - RIM, 4), to_za, to_zb)


def rim_stage_body(factor, level, base, xa, xb, zb, za, tmat, rmat, out_rim, to_xa, to_xb, to_za, to_zb, halo):
    fill_halo(halo, xa, xb)
    out = Parts(None, out_rim, rows=level.rows)

    def finish(x, tend):
        for f in range(5):
            out.store(f, x, base.row(f, x) + factor * tend[f])

    apply_operator(level, [None], za, zb, tmat, rmat, finish, halo)
    write_x(out, to_xa, to_xb)
    write_z(out, [0, level.rows - RIM], to_za, to_zb)


def last_finish(fields, k, store):
    def finish(x, tend):
        for f in range(5):
            store(f, x, fields[f, x] + time_step * k.row(f, x) + (0.5 * time_step * time_step) * tend[f])

    return finish


def inner_last_body(level, k, fields, zb, za, tmat, rmat, out, result, sems):
    def store(f, x, value):
        result[f, x - RIM] = value

    def copy(g):
        at = g * GROUP
        return pltpu.make_async_copy(
            result.at[:, at : at + GROUP], out.at[:, RIM + at : RIM + at + GROUP], sems.at[g]
        )

    groups = range(result.shape[1] // GROUP)
    for g in groups:
        apply_operator(level, [g], za, zb, tmat, rmat, last_finish(fields, k, store))
        copy(g).start()
    for g in groups:
        copy(g).wait()


def rim_last_body(level, k, fields, xa, xb, zb, za, tmat, rmat, out, halo, result, sems):
    rows = level.rows
    fill_halo(halo, xa, xb)

    copies = [
        pltpu.make_async_copy(result.at[:, 0:RIM], out.at[:, 0:RIM], sems.at[0]),
        pltpu.make_async_copy(result.at[:, RIM:], out.at[:, rows - RIM :], sems.at[1]),
    ]

    def store(f, x, value):
        result[f, x if x < RIM else x - rows + 2 * RIM] = value
        if f == 4 and x in (RIM - 1, rows - 1):
            copies[x // RIM > 0].start()

    apply_operator(level, [None], za, zb, tmat, rmat, last_finish(fields, k, store), halo)
    for copy in copies:
        copy.wait()


def local(noise, half_width, owner, target_cell, fields):
    px, pa, fine = noise.shape
    cx, ca, radial = fields.shape[1:]
    ncols = px * pa
    most = ncols // 2
    n_az = lax.axis_size("az")
    inner = cx - 2 * RIM

    block = ((px, pa, fine), F32)
    even = is_even("ax")
    to_a = jnp.where(even, noise[px - HMAX :], noise[:HMAX])
    to_b = jnp.where(even, noise[:HMAX], noise[px - HMAX :])
    noise_a, noise_b = swap(to_a, to_b, "ax")
    send_x, send_z = ((15, ca, radial), F32), ((cx // 4 * 3, 8, radial), F32)
    sends = [send_x, send_x, send_z, send_z]
    xa, xb, za, zb = full_specs(edges_body, sends, [fields], name="edges", after=[to_a])
    uxa, uxb = swap(xa, xb, "ax")
    partial, half_width = full_specs(
        inner_body, [block, ((px, pa, fine), jnp.int32)], [noise, half_width], name="filter_inner", after=[za]
    )
    pick, cells, own = full_specs(
        route_body,
        [((4 * most, ncols), BF16), ((4, 8, radial), F32), ((1, ncols), jnp.int32)],
        [owner.reshape(1, ncols), target_cell.reshape(1, ncols)],
        name="route",
        after=[partial],
    )
    long_z = ((px + send_z[0][0], 8, fine // 2), F32)
    filtered, to_a, to_b = full_specs(
        first_body,
        [block, long_z, ((px, 8, fine // 2), F32)],
        [partial, half_width, noise_a, noise_b, za],
        [((2, HMAX, pa, fine), F32)],
        name="filter_axial",
        after=[pick],
    )
    got_a, got_b = swap(to_a, to_b, "az")
    (uzb,) = swap_b(zb, "az")
    partial, weights = full_specs(
        middle_body,
        [block, ((HMAX + 1, px, pa, fine), F32)],
        [filtered, half_width],
        [((px, 32, fine), F32)],
        name="filter_middle",
        after=[pick],
    )
    (got_b,) = full_specs(
        unpack_body, [((px // 2, 8, fine), F32)], [got_b], name="unpack", after=[weights], cost=MORE
    )
    tiles = most // 8 + 1
    packet, packet_x, packet_b = [((tiles + spare, 8, radial), F32) for spare in (0, 1, 2)]
    binned, xa, xb, za, zb = full_specs(
        second_body,
        [((ncols, radial), F32), packet_x, packet_x, packet, packet_b],
        [partial, weights, got_a, got_b, pick, cells],
        [((ncols, fine), BF16), ((ncols, fine), BF16)],
        name="filter_rest",
        cost=COST,
    )
    za, zb = swap(za, zb, "az")
    packets = (*swap(xa, xb, "ax"), zb, za)

    tmat = jnp.asarray(azimuth_matrices(ca))
    rmat = jnp.asarray(radial_matrices(float(ca * n_az), radial))
    mid, rim = ((5, inner, ca, radial), F32), ((5, 2 * RIM, ca, radial), F32)
    halo = ((2, 5, 3, ca, radial), F32)
    k_mid, k_rim = full_specs(
        start_body, [mid, rim], [fields, got_a, uzb, uxa, uxb, tmat, rmat, binned, own], [halo, ((cx, ca, radial), F32)], name="operator"
    )
    inner_z, rim_z = ((inner // 4 * 3, 8, radial), F32), ((RIM // 2 * 3, 8, radial), F32)
    p_mid, p_rim, *edges = full_specs(
        gather_body,
        [((inner, ca, radial), F32), ((2 * RIM, ca, radial), F32), send_x, send_x, inner_z, inner_z, rim_z, rim_z],
        [*packets, k_mid, k_rim],
        name="gather",
    )
    k = [k_mid, k_rim, p_mid, p_rim]
    za, zb = swap(edges[2], edges[3], "az")
    xa, xb = swap(edges[0], edges[1], "ax")
    rim_a, rim_b = swap(edges[4], edges[5], "az")
    level = k
    for factor in (time_step / 4.0, time_step / 3.0):
        size = len(level)

        def body(*refs, factor=factor, size=size):
            inner_stage_body(factor, Parts(*refs[:size]), Parts(*refs[size : size + 4]), *refs[size + 4 :])

        new_mid, to_za, to_zb = full_specs(
            body, [mid, inner_z, inner_z], [*level, *k, zb, za, tmat, rmat], name="stage_inner", cost=SOME
        )
        za, zb = swap(to_za, to_zb, "az")

        def body(*refs, factor=factor, size=size):
            rim_stage_body(factor, Parts(*refs[:size]), Parts(*refs[size : size + 4]), *refs[size + 4 :])

        new_rim, to_xa, to_xb, to_za, to_zb = full_specs(
            body,
            [rim, send_x, send_x, rim_z, rim_z],
            [*level, *k, xa, xb, rim_b, rim_a, tmat, rmat],
            [halo],
            name="stage_rim",
            after=[new_mid],
            cost=COST,
        )
        xa, xb = swap(to_xa, to_xb, "ax")
        rim_a, rim_b = swap(to_za, to_zb, "az")
        level = [new_mid, new_rim]

    def body(*refs):
        inner_last_body(Parts(*refs[:2]), Parts(*refs[2:6]), *refs[6:])

    whole = ((5, cx, ca, radial), F32)
    (out,) = full_specs(
        body,
        [whole],
        [*level, *k, fields, zb, za, tmat, rmat],
        [mid, pltpu.SemaphoreType.DMA((inner // GROUP,))],
        name="final_inner",
        out_specs=[ANY],
        cost=SOME,
    )

    def body(out_in, *refs):
        rim_last_body(Parts(*refs[:2]), Parts(*refs[2:6]), *refs[6:])

    (out,) = full_specs(
        body,
        [whole],
        [out, *level, *k, fields, xa, xb, rim_b, rim_a, tmat, rmat],
        [halo, rim, pltpu.SemaphoreType.DMA((2,))],
        name="final_rim",
        in_specs=[ANY] + [VM] * 13,
        out_specs=[ANY],
        alias={0: 0},
    )
    return out


def solution(mesh):
    return jax.shard_map(
        local,
        mesh=mesh,
        in_specs=(
            P("ax", "az", None),
            P("ax", "az", None),
            P(("ax", "az")),
            P(("ax", "az")),
            P(None, "ax", "az", None),
        ),
        out_specs=P(None, "ax", "az", None),
        check_vma=False,
    )
```
